32 devices in a mesh: ctx: 16 (over z, y, core), tp: 2 (over x).
Axes of the slice: x: 2, y: 2, z: 4, core: 2. Of those that a mesh axis runs over, the one named last changes fastest.
Arguments:
- queries: bfloat16 [8192, 4096], P('ctx', 'tp'), may hold values from -5 to 5
- keys: bfloat16 [8192, 4096], P('ctx', 'tp'), may hold values from -5 to 5
- values: bfloat16 [8192, 4096], P('ctx', 'tp'), may hold values from -21 to 21
- log_decay: float32 [32, 8192], P('tp', 'ctx'), may hold values from -0.7 to 0
- gate: bfloat16 [8192, 4096], P('ctx', 'tp'), may hold values from -6 to 6
- gain: float32 [4096], P('tp'), may hold values from 0.5 to 1.5
- grad_out: bfloat16 [8192, 4096], P(('ctx', 'tp')), may hold values from -20 to 20
Outputs:
- query_grad: bfloat16 [8192, 4096], P('ctx', 'tp')
- key_grad: bfloat16 [8192, 4096], P('ctx', 'tp')
- value_grad: bfloat16 [8192, 4096], P('ctx', 'tp')
- gate_grad: bfloat16 [8192, 4096], P('ctx', 'tp')
- gain_grad: float32 [4096], P('tp')
The draws below stay inside these ranges and needn't reach their ends.
All inputs are finite; a program needn't handle non-finite values.
Results may differ from the reference program's by a relative error of at most 0.005.
Values may be sent and summed in bfloat16 or wider, within the bound.
No kernel may reach another device: no remote copies, remote signals or barrier semaphores. Data moves between devices by JAX's collectives and lax.ppermute only.
A program may use at most 128 MiB of HBM per device.

```python
import math
import jax
import jax.numpy as jnp
from jax import lax

HEAD = 128
HEADS = 32
BLOCK = 512
TOKEN_POSITIONS = 8192
HD_ALL = 4096


def draw_log_decay(key, part):
    sequence_lanes = jax.random.split(key, 6)
    fraction = 0.5
    is_fast = jax.random.uniform(sequence_lanes[0], (HEADS, 1), jnp.float32) < fraction
    fast_rate = jnp.exp(jax.random.uniform(sequence_lanes[1], (HEADS, 1), jnp.float32, minval=math.log(1.0 / 50.0), maxval=math.log(1.0 / 30.0)))
    slow_rate = jnp.exp(jax.random.uniform(sequence_lanes[2], (HEADS, 1), jnp.float32, minval=math.log(0.1), maxval=0.0)) / TOKEN_POSITIONS
    head_forget_rate = jnp.where(is_fast, fast_rate, slow_rate)
    segments = (TOKEN_POSITIONS + 127) // 128
    decay_factor = jnp.exp(jax.random.uniform(sequence_lanes[3], (HEADS, segments), jnp.float32, minval=-0.7, maxval=0.7))
    decay_factor = jnp.repeat(decay_factor, 128, axis=1)[:, :TOKEN_POSITIONS]
    grouped_segments = jax.random.uniform(sequence_lanes[4], (1, TOKEN_POSITIONS), jnp.float32) < 3.0 / TOKEN_POSITIONS
    excluded_terms = jnp.log(jax.random.uniform(sequence_lanes[5], (1, TOKEN_POSITIONS), jnp.float32, minval=0.5, maxval=0.8))
    return jnp.where(grouped_segments, excluded_terms, -head_forget_rate * decay_factor)


def draw_values(key, part):
    sequence_lanes = jax.random.split(key, 1)
    head_index = (jnp.arange(HEADS * HEAD) // HEAD).astype(jnp.float32)
    spread = 1.0 + 2.0 * head_index / (HEADS - 1)
    base = jnp.clip(jax.random.normal(sequence_lanes[0], (TOKEN_POSITIONS, HEADS * HEAD), jnp.float32), -5.0, 5.0)
    return (base * spread[None, :]).astype(jnp.bfloat16)


def draw_grad_out(key, part):
    sequence_lanes = jax.random.split(key, 1)
    position = jnp.arange(TOKEN_POSITIONS).astype(jnp.float32) / (TOKEN_POSITIONS - 1)
    rising = (1.0 + 2.0 * position)[:, None]
    base = jnp.clip(jax.random.normal(sequence_lanes[0], (TOKEN_POSITIONS, HEADS * HEAD), jnp.float32), -5.0, 5.0)
    return (base * rising).astype(jnp.bfloat16)


def levels(key, shape, shards, least, largest):
    def one(dim, shards_of):
        steps = jax.random.uniform(jax.random.fold_in(jax.random.fold_in(key, 6), dim), (shards_of,), jnp.float32, least / len(shards), largest / len(shards))
        return jnp.repeat(jnp.exp(steps), shape[dim] // shards_of).reshape((-1,) + (1,) * (len(shape) - dim - 1))

    level = one(*shards[0])
    for cut in shards[1:]:
        level = level * one(*cut)
    return level


def scatter_about(stream_key, shape, deviation, reach, cuts=(), kind=jnp.bfloat16):
    entries = deviation * jax.random.normal(stream_key, shape, jnp.float32)
    if cuts:
        entries = entries * levels(stream_key, shape, cuts, -0.22, 0.18)
    return jnp.clip(entries, -reach, reach).astype(kind)


def setup_inputs(seed: int = 0) -> dict:
    arg_keys = jax.random.split(jax.random.key(seed), 8)
    queries = scatter_about(arg_keys[0], (TOKEN_POSITIONS, HD_ALL), 1.0, 5.0, ((0, 16), (1, 2)))
    keys = scatter_about(arg_keys[1], (TOKEN_POSITIONS, HD_ALL), 1.0, 5.0, ((0, 16), (1, 2)))
    values = draw_values(jax.random.fold_in(arg_keys[7], 71), 0)
    log_decay = draw_log_decay(jax.random.fold_in(arg_keys[7], 71), 0)
    gate = scatter_about(arg_keys[4], (TOKEN_POSITIONS, HD_ALL), 1.5, 6.0, ((0, 16), (1, 2)))
    gain = jnp.clip(1.0 + 0.1 * jax.random.normal(arg_keys[5], (HD_ALL,), jnp.float32), 0.5, 1.5)
    grad_out = draw_grad_out(jax.random.fold_in(arg_keys[7], 71), 0)
    return {"queries": queries, "keys": keys, "values": values, "log_decay": log_decay, "gate": gate, "gain": gain, "grad_out": grad_out}


HIGH_PRECISION = lax.Precision.HIGHEST
EPSILON = 1e-06

def decay_mask(decay_block):
    by_head = jnp.transpose(decay_block, (1, 0))
    spread = by_head[:, :, None] - by_head[:, None, :]
    causal = jnp.tril(jnp.ones((BLOCK, BLOCK), dtype=bool))
    return jnp.where(causal[None], jnp.exp(jnp.minimum(spread, 0.0)), 0.0)

def block_forward(carried_state, element):
    query_block, key_block, value_block, decay_block = element
    full_query_rows = query_block.astype(jnp.float32)
    full_key_rows = key_block.astype(jnp.float32)
    full_value_rows = value_block.astype(jnp.float32)
    block_decay_rate = decay_block[-1]
    table = decay_mask(decay_block)
    attention_scores = jnp.einsum('rgs,fgs->grf', full_query_rows, full_key_rows)
    probs = lax.optimization_barrier((attention_scores * table).astype(jnp.bfloat16))
    intra = jnp.einsum('hlm,mhe->lhe', probs.astype(jnp.float32), full_value_rows)
    growth = jnp.exp(decay_block)[:, :, None]
    decay_shrink = jnp.exp(block_decay_rate[None, :] - decay_block)[:, :, None]
    inter = jnp.einsum('lhd,hde->lhe', full_query_rows * growth, carried_state, precision=HIGH_PRECISION)
    addend = jnp.einsum('lhd,lhe->hde', full_key_rows * decay_shrink, full_value_rows, precision=HIGH_PRECISION)
    updated = jnp.exp(block_decay_rate)[:, None, None] * carried_state + addend
    return (updated, (intra + inter, carried_state))

def block_backward(carried_state, element):
    query_block, key_block, value_block, decay_block, dattn_block, prev_state = element
    full_query_rows = query_block.astype(jnp.float32)
    full_key_rows = key_block.astype(jnp.float32)
    full_value_rows = value_block.astype(jnp.float32)
    wide_dattn = dattn_block.astype(jnp.float32)
    block_decay_rate = decay_block[-1]
    table = decay_mask(decay_block)
    attention_scores = jnp.einsum('rgs,fgs->grf', full_query_rows, full_key_rows)
    probs = lax.optimization_barrier((attention_scores * table).astype(jnp.bfloat16)).astype(jnp.float32)
    dprobs = jnp.einsum('lhe,mhe->hlm', wide_dattn, full_value_rows)
    scores_gradient = lax.optimization_barrier((dprobs * table).astype(jnp.bfloat16)).astype(jnp.float32)
    growth = jnp.exp(decay_block)[:, :, None]
    decay_shrink = jnp.exp(block_decay_rate[None, :] - decay_block)[:, :, None]
    query_portion = jnp.einsum('fxz,zfb->xfb', scores_gradient, full_key_rows)
    query_portion = query_portion + jnp.einsum('lhe,hde->lhd', wide_dattn * growth, prev_state, precision=HIGH_PRECISION)
    key_portion = jnp.einsum('fzu,zfj->ufj', scores_gradient, full_query_rows)
    key_portion = key_portion + jnp.einsum('bip,iup->biu', full_value_rows * decay_shrink, carried_state, precision=HIGH_PRECISION)
    value_portion = jnp.einsum('hlm,lhe->mhe', probs, wide_dattn)
    value_portion = value_portion + jnp.einsum('bfj,fjq->bfq', full_key_rows * decay_shrink, carried_state, precision=HIGH_PRECISION)
    backterm = jnp.einsum('lhd,lhe->hde', full_query_rows * growth, wide_dattn, precision=HIGH_PRECISION)
    updated = jnp.exp(block_decay_rate)[:, None, None] * carried_state + backterm
    return (updated, (query_portion.astype(jnp.bfloat16), key_portion.astype(jnp.bfloat16), value_portion.astype(jnp.bfloat16)))

def reference(queries, keys, values, log_decay, gate, gain, grad_out):
    count = TOKEN_POSITIONS // BLOCK
    shape4 = (count, BLOCK, HEADS, HEAD)
    query_blocks = queries.reshape(shape4)
    key_blocks = keys.reshape(shape4)
    value_blocks = values.reshape(shape4)
    rates = jnp.transpose(log_decay.reshape(HEADS, count, BLOCK), (1, 2, 0))
    decay_sum = jnp.cumsum(rates, axis=1)
    start = jnp.zeros((HEADS, HEAD, HEAD), jnp.float32)
    _, (attention, prev_states) = lax.scan(block_forward, start, (query_blocks, key_blocks, value_blocks, decay_sum))
    gate_blocks = gate.reshape(shape4).astype(jnp.float32)
    grad_blocks = grad_out.reshape(shape4).astype(jnp.float32)
    gain_heads = gain.reshape(HEADS, HEAD)
    opened = jax.nn.sigmoid(gate_blocks)
    dnorm = grad_blocks * opened
    dscaled = dnorm * gain_heads
    squares = lax.optimization_barrier(jnp.sum(attention * attention, axis=(2, 3)))
    inner = lax.optimization_barrier(jnp.sum(attention * dscaled, axis=(2, 3)))
    rscale = lax.rsqrt(squares / (HEADS * HEAD) + EPSILON)[:, :, None, None]
    normed = attention * rscale * gain_heads
    gate_grad = (grad_blocks * normed * opened * (1.0 - opened)).astype(jnp.bfloat16)
    gain_grad = lax.optimization_barrier(jnp.sum(dnorm * attention * rscale, axis=(0, 1))).reshape(HEADS * HEAD)
    dattn = (dscaled * rscale - attention * (inner[:, :, None, None] * rscale ** 3 / (HEADS * HEAD))).astype(jnp.bfloat16)
    _, (query_grad, key_grad, value_grad) = lax.scan(block_backward, start, (query_blocks, key_blocks, value_blocks, decay_sum, dattn, prev_states), reverse=True)
    flat = (TOKEN_POSITIONS, HEADS * HEAD)
    return (query_grad.reshape(flat), key_grad.reshape(flat), value_grad.reshape(flat), gate_grad.reshape(flat), gain_grad)
```

```python
import functools

import jax
import jax.numpy as jnp
from jax import lax
from jax.experimental import pallas as pl
from jax.experimental.pallas import tpu as pltpu
from jax.sharding import PartitionSpec as P

HEAD = 128
BLOCK = 512
TEAM = 4
EPSILON = 1e-06
F32 = jnp.float32
BF16 = jnp.bfloat16
VMEM_LIMIT = 48 * 1024 * 1024


def dot(a, b, ca, cb, precision=None):
    return lax.dot_general(
        a, b, (((ca,), (cb,)), ((), ())), preferred_element_type=F32, precision=precision
    )


def head_cols(j):
    return slice(j * HEAD, (j + 1) * HEAD)


def call(body, grid, info, inputs, in_specs, out_shape, out_specs, scratch, flops, name):
    nbytes = sum(x.size * x.dtype.itemsize for x in inputs)
    nbytes += sum(x.size * x.dtype.itemsize for x in out_shape)
    return pl.pallas_call(
        body,
        grid_spec=pltpu.PrefetchScalarGridSpec(
            num_scalar_prefetch=1,
            grid=grid,
            in_specs=in_specs,
            out_specs=out_specs,
            scratch_shapes=scratch,
        ),
        out_shape=out_shape,
        compiler_params=pltpu.CompilerParams(vmem_limit_bytes=VMEM_LIMIT),
        cost_estimate=pl.CostEstimate(flops=flops, bytes_accessed=nbytes, transcendentals=0),
        name=name,
    )(info, *inputs)


def ahead(d, s):
    return lax.rem(s[0] + d, TEAM)


def behind(d, s):
    return lax.rem(s[0] + TEAM - d, TEAM)


def cols_spec(rows, width, quarter):
    return pl.BlockSpec((rows, width), lambda d, s: (0, quarter(d, s)))


def row_spec(quarter):
    return pl.BlockSpec((1, 8, BLOCK), lambda d, s: (quarter(d, s), 0, 0))


def col_spec(quarter):
    return pl.BlockSpec((1, BLOCK, HEAD), lambda d, s: (quarter(d, s), 0, 0))


def whole(shape):
    return pl.BlockSpec(shape, lambda d, s: (0,) * len(shape))


def local_states_body(hq, s, k, v, ld, l0, l1, l2, l3, row, col):
    d = pl.program_id(0)
    outs = (l0, l1, l2, l3)
    rows = ld.shape[0]
    offset = lax.rem(ahead(d, s) * hq, rows)
    x = ld[0:hq, :]
    for c in range(hq, rows, hq):
        x = jnp.where(offset == c, ld[c : c + hq, :], x)
    x = jnp.concatenate([x, jnp.zeros((8 - hq, BLOCK), F32)], axis=0)
    lane = lax.broadcasted_iota(jnp.int32, (8, BLOCK), 1)
    step = 1
    while step < BLOCK:
        x = x + jnp.where(lane >= step, pltpu.roll(x, step, 1), 0.0)
        step *= 2
    row[0] = x
    spread = jnp.concatenate([x, jnp.zeros((HEAD - 8, BLOCK), F32)], axis=0).T
    col[0] = spread
    shrink = jnp.exp(spread[BLOCK - 1 : BLOCK, :] - spread)
    for j in range(hq):
        kd = (k[:, head_cols(j)].astype(F32) * shrink[:, j : j + 1]).astype(BF16)
        part = dot(kd, v[:, head_cols(j)], 0, 0).astype(BF16)
        for i in range(TEAM):

            @pl.when(d == i)
            def _():
                outs[i][j] = part


def table_block(col, row, j, i, half):
    t = jnp.exp(col[0, i * half : (i + 1) * half, j : j + 1] - row[0, j : j + 1, 0 : (i + 1) * half])
    shape = (half, (i + 1) * half)
    at = lax.broadcasted_iota(jnp.int32, shape, 0) + i * half
    other = lax.broadcasted_iota(jnp.int32, shape, 1)
    return jnp.where(at >= other, t, 0.0)


def intra_body(hq, s, q, k, v, row, col, intra):
    half = BLOCK // 2
    for j in range(hq):
        c = head_cols(j)
        for i in range(2):
            mine = slice(i * half, (i + 1) * half)
            upto = slice(0, (i + 1) * half)
            scores = dot(q[mine, c], k[upto, c], 1, 1)
            probs = (scores * table_block(col, row, j, i, half)).astype(BF16)
            intra[mine, c] = dot(probs, v[upto, c], 1, 0)


def attention_body(hq, s, q, intra, gate, own, got, gain, col, s0, s1, s2, s3, att, sums, state, sq, inn):
    d = pl.program_id(0)
    for i, ref in enumerate((s0, s1, s2, s3)):

        @pl.when(d == i)
        def _():
            state[...] = ref[...]

    @pl.when(d == 0)
    def _():
        sq[...] = jnp.zeros_like(sq)
        inn[...] = jnp.zeros_like(inn)

    part = own.shape[0]
    for j in range(hq):
        c = head_cols(j)
        a = intra[:, c] + dot(q[:, c], state[j], 1, 0) * jnp.exp(col[0, :, j : j + 1])
        att[:, c] = a
        sq[...] += a * a
    for where, ref in ((s[1], own), (1 - s[1], got)):
        rows = pl.ds(pl.multiple_of(where * part, part), part)
        for j in range(hq):
            c = head_cols(j)
            opened = jax.nn.sigmoid(gate[rows, c].astype(F32))
            inn[rows, :] += att[rows, c] * (ref[:, c].astype(F32) * opened * gain[:, c])

    @pl.when(d == TEAM - 1)
    def _():
        ones = jnp.ones((8, HEAD), F32)
        a = dot(ones, sq[...], 1, 1, lax.Precision.HIGHEST)
        b = dot(ones, inn[...], 1, 1, lax.Precision.HIGHEST)
        sums[...] = jnp.where(lax.broadcasted_iota(jnp.int32, (8, BLOCK), 0) == 0, a, b)


def dattn_body(hq, channels, s, att, q, gate, own, got, gain, col, sum_a, sum_b, dattn, gate_grad, gain_part,
               b0, b1, b2, b3, scale):
    d = pl.program_id(0)
    outs = (b0, b1, b2, b3)

    @pl.when(d == 0)
    def _():
        total = sum_a[...] + sum_b[...]
        rs = lax.rsqrt(total[0:1, :] / channels + EPSILON)
        coef = total[1:2, :] * (rs * rs * rs) / channels
        both = jnp.concatenate([rs, coef, jnp.zeros((HEAD - 2, BLOCK), F32)], axis=0)
        scale[...] = both.T

    part = own.shape[0]
    gain_part[...] = jnp.zeros_like(gain_part)
    for where, ref in ((s[1], own), (1 - s[1], got)):
        rows = pl.ds(pl.multiple_of(where * part, part), part)
        rs = scale[rows, 0:1]
        coef = scale[rows, 1:2]
        for j in range(hq):
            c = head_cols(j)
            a = att[rows, c]
            opened = jax.nn.sigmoid(gate[rows, c].astype(F32))
            dnorm = ref[:, c].astype(F32) * opened
            scaled = a * rs
            dscaled = dnorm * gain[:, c]
            gain_part[:, c] += jnp.sum(dnorm * scaled, axis=0, keepdims=True)
            gate_grad[rows, c] = (dscaled * scaled * (1.0 - opened)).astype(BF16)
            dattn[rows, c] = (dscaled * rs - a * coef).astype(BF16)
    for j in range(hq):
        c = head_cols(j)
        qd = (q[:, c].astype(F32) * jnp.exp(col[0, :, j : j + 1])).astype(BF16)
        back = dot(qd, dattn[:, c], 0, 0).astype(BF16)
        for i in range(TEAM):

            @pl.when(d == i)
            def _():
                outs[i][j] = back


def local_grads_body(hq, s, q, k, v, dattn, row, col, s0, s1, s2, s3, query_grad, dk, dv, state):
    d = pl.program_id(0)
    for i, ref in enumerate((s0, s1, s2, s3)):

        @pl.when(d == i)
        def _():
            state[...] = ref[...]

    half = BLOCK // 2
    for j in range(hq):
        c = head_cols(j)
        for i in (1, 0):
            mine = slice(i * half, (i + 1) * half)
            upto = slice(0, (i + 1) * half)
            table = table_block(col, row, j, i, half)
            probs = (dot(q[mine, c], k[upto, c], 1, 1) * table).astype(BF16)
            dscores = (dot(dattn[mine, c], v[upto, c], 1, 1) * table).astype(BF16)
            inter = dot(dattn[mine, c], state[j], 1, 1) * jnp.exp(col[0, mine, j : j + 1])
            query_grad[mine, c] = (dot(dscores, k[upto, c], 1, 0) + inter).astype(BF16)
            dkey = dot(dscores, q[mine, c], 0, 0)
            dvalue = dot(probs, dattn[mine, c], 0, 0)
            if i == 1:
                dk[:, c] = dkey
                dv[:, c] = dvalue
            else:
                dk[upto, c] += dkey
                dv[upto, c] += dvalue


def final_body(hq, s, k, v, dk, dv, col, r0, r1, r2, r3, key_grad, value_grad, state):
    d = pl.program_id(0)
    for i, ref in enumerate((r0, r1, r2, r3)):

        @pl.when(d == i)
        def _():
            state[...] = ref[...]

    for j in range(hq):
        c = head_cols(j)
        shrink = jnp.exp(col[0, BLOCK - 1 : BLOCK, j : j + 1] - col[0, :, j : j + 1])
        key_grad[:, c] = (dk[:, c] + dot(v[:, c], state[j], 1, 1) * shrink).astype(BF16)
        value_grad[:, c] = (dv[:, c] + dot(k[:, c], state[j], 1, 0) * shrink).astype(BF16)


def group_total_body(hq, base, w, a0, a1, a2, a3, out):
    for j in range(hq):
        total = a0[j].astype(F32) * w[base, j]
        for d, ref in ((1, a1), (2, a2), (3, a3)):
            total = total + ref[j].astype(F32) * w[base + d, j]
        out[j] = total.astype(BF16)


def entering_body(hq, base, groups, w, *refs):
    parts = refs[:TEAM]
    far = refs[TEAM : TEAM + groups - 1]
    outs = refs[TEAM + groups - 1 :]
    b_far = base + TEAM
    b_in = b_far + groups - 1
    b_mix = b_in + TEAM
    for j in range(hq):
        incoming = jnp.zeros((HEAD, HEAD), F32)
        for k in range(groups - 1):
            incoming = incoming + far[k][j].astype(F32) * w[b_far + k, j]
        for d in range(TEAM):
            total = incoming * w[b_in + d, j]
            for i in range(TEAM):
                total = total + parts[i][j].astype(F32) * w[b_mix + d * TEAM + i, j]
            outs[d][j] = total.astype(BF16)


def scan_weights(edges, place, team, groups, hq):
    r = lax.rem(place, team)
    p = place // team
    low, high, valid = [], [], []

    def add(a, b, ok=True):
        low.append(a)
        high.append(b)
        valid.append(jnp.asarray(ok))

    first = team * p
    for reverse in (False, True):
        source = [lax.rem(r + team - d, team) for d in range(team)]
        target = [lax.rem(r + d, team) for d in range(team)]
        for d in range(team):
            if reverse:
                add(first, first + source[d])
            else:
                add(first + source[d] + 1, first + team)
        for k in range(1, groups):
            if reverse:
                add(first + team, first + team * k)
            else:
                add(first - team * (k - 1), first)
        for d in range(team):
            if reverse:
                add(first + target[d] + 1, first + team)
            else:
                add(first, first + target[d])
        for d in range(team):
            for i in range(team):
                if reverse:
                    add(first + target[d] + 1, first + source[i], source[i] > target[d])
                else:
                    add(first + source[i] + 1, first + target[d], source[i] < target[d])
    low = jnp.stack(low)[:, None]
    high = jnp.stack(high)[:, None]
    valid = jnp.stack(valid)[:, None]
    at = jnp.arange(team * groups, dtype=jnp.int32)[None, :]
    inside = ((at >= low) & (at < high)).astype(F32)
    mine = lax.dynamic_slice_in_dim(edges, r * hq, hq, 1)
    total = jnp.sum(inside[:, :, None] * mine[None], axis=1)
    return jnp.where(valid, jnp.exp(total), 0.0)


def scan_states(parts, weights, base, groups, hq, reverse):
    n = TEAM * groups
    shape = jax.ShapeDtypeStruct((hq, HEAD, HEAD), BF16)
    vmem = pl.BlockSpec(memory_space=pltpu.VMEM)
    smem = pl.BlockSpec(memory_space=pltpu.SMEM)

    def around(d):
        return [(i, i - i % TEAM + (i + d) % TEAM) for i in range(n)]

    terms = [parts[0]] + [lax.ppermute(parts[d], "ctx", around(d)) for d in range(1, TEAM)]
    total = pl.pallas_call(
        functools.partial(group_total_body, hq, base),
        in_specs=[smem] + [vmem] * TEAM,
        out_specs=vmem,
        out_shape=shape,
        name="group_total",
    )(weights, *terms)
    far = []
    for k in range(1, groups):
        move = -TEAM * k if reverse else TEAM * k
        pairs = [(i, i + move) for i in range(n) if 0 <= i + move < n]
        far.append(lax.ppermute(total, "ctx", pairs))
    entering = pl.pallas_call(
        functools.partial(entering_body, hq, base, groups),
        in_specs=[smem] + [vmem] * (TEAM + groups - 1),
        out_specs=[vmem] * TEAM,
        out_shape=[shape] * TEAM,
        name="entering",
    )(weights, *terms, *far)
    return [entering[0]] + [lax.ppermute(entering[d], "ctx", around(d)) for d in range(1, TEAM)]


def local(queries, keys, values, log_decay, gate, gain, grad_out):
    rows, width = queries.shape
    heads = width // HEAD
    hq = heads // TEAM
    tp = lax.axis_size("tp")
    groups = lax.axis_size("ctx") // TEAM
    channels = width * tp
    place = lax.axis_index("ctx")
    mine = lax.axis_index("tp")
    w = hq * HEAD
    part = grad_out.shape[0]
    bf = lambda *shape: jax.ShapeDtypeStruct(shape, BF16)
    f32 = lambda *shape: jax.ShapeDtypeStruct(shape, F32)

    if tp == 2:
        away = lax.dynamic_slice_in_dim(grad_out, (1 - mine) * width, width, 1)
        got = lax.ppermute(away, "tp", [(0, 1), (1, 0)])
        own, own_base = grad_out, mine * TEAM
        half = mine
        part = grad_out.shape[0]
    else:
        every = lax.all_to_all(grad_out, "tp", split_axis=1, concat_axis=0, tiled=True)
        own, got = every[: rows // 2], every[rows // 2 :]
        own_base = jnp.int32(0)
        half = jnp.int32(0)
        part = rows // 2
    info = jnp.stack([lax.rem(place, TEAM), half, own_base]).astype(jnp.int32)

    edges = lax.all_gather(jnp.sum(log_decay, axis=1), "ctx")
    weights = scan_weights(edges, place, TEAM, groups, hq)
    reverse_base = weights.shape[0] // 2

    state_shape = [bf(hq, HEAD, HEAD)] * TEAM
    state_specs = [whole((hq, HEAD, HEAD))] * TEAM
    state_scratch = pltpu.VMEM((hq, HEAD, HEAD), BF16)
    decay_rows = 8 if heads % 8 == 0 else heads
    per = decay_rows // hq
    small = 2 * heads * rows * HEAD * HEAD
    large = 2 * heads * rows * rows * HEAD

    *parts, row, col = call(
        functools.partial(local_states_body, hq),
        (TEAM,),
        info,
        [keys, values, log_decay],
        [
            cols_spec(rows, w, ahead),
            cols_spec(rows, w, ahead),
            pl.BlockSpec((decay_rows, rows), lambda d, s: (ahead(d, s) // per, 0)),
        ],
        state_shape + [f32(TEAM, 8, rows), f32(TEAM, rows, HEAD)],
        state_specs + [row_spec(ahead), col_spec(ahead)],
        [],
        small,
        "local_states",
    )
    entering = scan_states(parts, weights, 0, groups, hq, False)

    own_spec = pl.BlockSpec((part, w), lambda d, s: (0, s[2] + behind(d, s)))
    own_spec_ahead = pl.BlockSpec((part, w), lambda d, s: (0, s[2] + ahead(d, s)))
    b_cols = cols_spec(rows, w, behind)
    a_cols = cols_spec(rows, w, ahead)
    (intra,) = call(
        functools.partial(intra_body, hq),
        (TEAM,),
        info,
        [queries, keys, values, row, col],
        [b_cols, b_cols, b_cols, row_spec(behind), col_spec(behind)],
        [f32(rows, width)],
        [b_cols],
        [],
        2 * large,
        "intra",
    )
    gain_row = gain.reshape(1, width)
    att, sums = call(
        functools.partial(attention_body, hq),
        (TEAM,),
        info,
        [queries, intra, gate, own, got, gain_row, col, *entering],
        [b_cols, b_cols, b_cols, own_spec, cols_spec(part, w, behind), cols_spec(1, w, behind), col_spec(behind)]
        + state_specs,
        [f32(rows, width), f32(8, rows)],
        [b_cols, whole((8, rows))],
        [state_scratch, pltpu.VMEM((rows, HEAD), F32), pltpu.VMEM((rows, HEAD), F32)],
        small,
        "attention",
    )
    if tp == 2:
        others = lax.ppermute(sums, "tp", [(0, 1), (1, 0)])
    else:
        others = lax.psum(sums, "tp") - sums
    dattn, gate_grad, gain_part, *parts = call(
        functools.partial(dattn_body, hq, channels),
        (TEAM,),
        info,
        [att, queries, gate, own, got, gain_row, col, sums, others],
        [a_cols, a_cols, a_cols, own_spec_ahead, cols_spec(part, w, ahead), cols_spec(1, w, ahead), col_spec(ahead)]
        + [whole((8, rows))] * 2,
        [bf(rows, width), bf(rows, width), f32(1, width)] + state_shape,
        [a_cols, a_cols, cols_spec(1, w, ahead)] + state_specs,
        [pltpu.VMEM((rows, HEAD), F32)],
        small,
        "dattn",
    )
    leaving = scan_states(parts, weights, reverse_base, groups, hq, True)
    gain_grad = lax.psum(gain_part.reshape(width), "ctx")
    query_grad, dk, dv = call(
        functools.partial(local_grads_body, hq),
        (TEAM,),
        info,
        [queries, keys, values, dattn, row, col, *entering],
        [b_cols] * 4 + [row_spec(behind), col_spec(behind)] + state_specs,
        [bf(rows, width), f32(rows, width), f32(rows, width)],
        [b_cols] * 3,
        [state_scratch],
        5 * large,
        "local_grads",
    )
    key_grad, value_grad = call(
        functools.partial(final_body, hq),
        (TEAM,),
        info,
        [keys, values, dk, dv, col, *leaving],
        [b_cols] * 4 + [col_spec(behind)] + state_specs,
        [bf(rows, width), bf(rows, width)],
        [b_cols] * 2,
        [state_scratch],
        2 * small,
        "final",
    )
    return query_grad, key_grad, value_grad, gate_grad, gain_grad


def solution(mesh):
    return jax.shard_map(
        local,
        mesh=mesh,
        in_specs=(
            P("ctx", "tp"),
            P("ctx", "tp"),
            P("ctx", "tp"),
            P("tp", "ctx"),
            P("ctx", "tp"),
            P("tp"),
            P(("ctx", "tp"), None),
        ),
        out_specs=(P("ctx", "tp"), P("ctx", "tp"), P("ctx", "tp"), P("ctx", "tp"), P("tp")),
        check_vma=False,
    )
```

```python
import functools

import jax
import jax.numpy as jnp
from jax import lax
from jax.experimental import pallas as pl
from jax.experimental.pallas import tpu as pltpu
from jax.sharding import PartitionSpec as P

HEAD = 128
BLOCK = 512
HALF = BLOCK // 2
EXTRA = 16
EPSILON = 1e-06
F32 = jnp.float32
BF16 = jnp.bfloat16
VMEM_LIMIT = 60 * 1024 * 1024


def nt(a, b, precision=None):
    return lax.dot_general(a, b, (((1,), (1,)), ((), ())), preferred_element_type=F32, precision=precision)


def nn(a, b):
    return lax.dot_general(a, b, (((1,), (0,)), ((), ())), preferred_element_type=F32)


def head_cols(j):
    return slice(j * HEAD, (j + 1) * HEAD)


def piece(i):
    return slice(i * HALF, (i + 1) * HALF)


def split_terms(x, count):
    terms = []
    for _ in range(count):
        term = x.astype(BF16)
        terms.append(term)
        x = x - term.astype(F32)
    return terms


def call(body, grid, info, inputs, in_specs, out_shape, out_specs, scratch, flops, name):
    nbytes = sum(x.size * x.dtype.itemsize for x in inputs)
    nbytes += sum(x.size * x.dtype.itemsize for x in out_shape)
    return pl.pallas_call(
        body,
        grid_spec=pltpu.PrefetchScalarGridSpec(
            num_scalar_prefetch=1,
            grid=grid,
            in_specs=in_specs,
            out_specs=out_specs,
            scratch_shapes=scratch,
        ),
        out_shape=out_shape,
        compiler_params=pltpu.CompilerParams(vmem_limit_bytes=VMEM_LIMIT),
        cost_estimate=pl.CostEstimate(flops=flops, bytes_accessed=nbytes, transcendentals=0),
        name=name,
    )(info, *inputs)


def cols_spec(rows, width):
    return pl.BlockSpec((rows, width), lambda d, s: (0, d))


def lead_spec(*shape):
    return pl.BlockSpec(shape, lambda d, s: (d,) + (0,) * (len(shape) - 1))


def whole(shape):
    return pl.BlockSpec(shape, lambda d, s: (0,) * len(shape))


def transposed(x):
    eye = (
        lax.broadcasted_iota(jnp.int32, (HEAD, HEAD), 0) == lax.broadcasted_iota(jnp.int32, (HEAD, HEAD), 1)
    ).astype(BF16)
    return nt(eye, x)


def local_states_body(hq, sends, s, k, v, ld, *refs):
    if sends:
        grad, parts, row, col, away, tri = refs
        away[...] = grad[...]
    else:
        parts, row, col, tri = refs
    d = pl.program_id(0)

    @pl.when(d == 0)
    def _():
        at = lax.broadcasted_iota(jnp.int32, (BLOCK, BLOCK), 0)
        other = lax.broadcasted_iota(jnp.int32, (BLOCK, BLOCK), 1)
        tri[...] = (at >= other).astype(BF16)

    rows = ld.shape[0]
    offset = lax.rem(d * hq, rows)
    x = ld[0:hq, :]
    for c in range(hq, rows, hq):
        x = jnp.where(offset == c, ld[c : c + hq, :], x)
    x = jnp.concatenate([x, jnp.zeros((EXTRA - hq, BLOCK), F32)], axis=0)
    terms = split_terms(x, 3)
    sums = jnp.zeros((EXTRA, BLOCK), F32)
    down = jnp.zeros((BLOCK, EXTRA), F32)
    for term in reversed(terms):
        sums = sums + nt(term, tri[...])
        down = down + nt(tri[...], term)
    row[0] = sums[0:8]
    col[0, :, 0:EXTRA] = down
    edge = sums[:, BLOCK - 1 : BLOCK]
    shrink = jnp.exp(edge - sums)
    at = lax.broadcasted_iota(jnp.int32, (EXTRA, HEAD), 0)
    for j in range(hq):
        kd = (transposed(k[:, head_cols(j)]) * shrink[j : j + 1, :]).astype(BF16)
        parts[j, 0:HEAD, :] = nn(kd, v[:, head_cols(j)]).astype(BF16)
        e = split_terms(jnp.broadcast_to(edge[j : j + 1, :], (EXTRA, HEAD)), 3)
        out = jnp.zeros((EXTRA, HEAD), F32)
        for i in range(3):
            out = jnp.where(at == i, e[i].astype(F32), out)
        parts[j, HEAD : HEAD + EXTRA, :] = out.astype(BF16)


def forward_scan_body(got, out):
    n, tall, _ = got.shape
    tall -= EXTRA
    state = jnp.zeros((tall, HEAD), F32)
    for j in range(n):
        out[j] = state.astype(BF16)
        decay = jnp.exp(jnp.sum(got[j, tall : tall + EXTRA, :].astype(F32), axis=0, keepdims=True))
        state = state * decay + got[j, 0:tall, :].astype(F32)


def reverse_scan_body(edges, got, out):
    n, tall, _ = got.shape
    tall -= EXTRA
    state = jnp.zeros((tall, HEAD), F32)
    gain = jnp.zeros((EXTRA, HEAD), F32)
    for j in reversed(range(n)):
        out[j, 0:tall, :] = state.astype(BF16)
        decay = jnp.exp(jnp.sum(edges[j, tall : tall + EXTRA, :].astype(F32), axis=0, keepdims=True))
        state = state * decay + got[j, 0:tall, :].astype(F32)
        gain = gain + got[j, tall : tall + EXTRA, :].astype(F32)
    rows = gain_rows(jnp.sum(gain, axis=0, keepdims=True))
    for j in range(n):
        out[j, tall : tall + EXTRA, :] = rows


def gain_rows(total):
    at = lax.broadcasted_iota(jnp.int32, (EXTRA, HEAD), 0)
    high, low = split_terms(jnp.broadcast_to(total, (EXTRA, HEAD)), 2)
    return jnp.where(at == 0, high.astype(F32), jnp.where(at == 1, low.astype(F32), 0.0)).astype(BF16)


def lower_mask():
    return lax.broadcasted_iota(jnp.int32, (HALF, HALF), 0) >= lax.broadcasted_iota(jnp.int32, (HALF, HALF), 1)


def upper_mask():
    return lax.broadcasted_iota(jnp.int32, (HALF, HALF), 0) <= lax.broadcasted_iota(jnp.int32, (HALF, HALF), 1)


def intra_body(hq, s, q, k, v, row, col, intra):
    mask = lower_mask()
    for j in range(hq):
        c = head_cols(j)
        for i in range(2):
            total = None
            for m in range(i + 1):
                table = jnp.exp(col[0, piece(i), j : j + 1] - row[0, j : j + 1, piece(m)])
                if m == i:
                    table = jnp.where(mask, table, 0.0)
                probs = (nt(q[piece(i), c], k[piece(m), c]) * table).astype(BF16)
                term = nn(probs, v[piece(m), c])
                total = term if total is None else total + term
            intra[piece(i), c] = total


def dscaled_body(hq, s, gate, own, got, gain, q, row, dscaled, turned):
    part = own.shape[0]
    for where, ref in ((s[0], own), (1 - s[0], got)):
        rows = pl.ds(pl.multiple_of(where * part, part), part)
        opened = jax.nn.sigmoid(gate[rows, :].astype(F32))
        dscaled[rows, :] = ref[...].astype(F32) * opened * gain[...]
    growth = jnp.exp(row[0])
    for j in range(hq):
        turned[j] = (transposed(q[:, head_cols(j)]) * growth[j : j + 1, :]).astype(BF16)


def attention_body(hq, s, q, intra, dscaled, col, state, att, sums, sq, inn):
    d = pl.program_id(0)

    @pl.when(d == 0)
    def _():
        sq[...] = jnp.zeros_like(sq)
        inn[...] = jnp.zeros_like(inn)

    for i in range(BLOCK // HEAD):
        r = head_cols(i)
        a_sq = sq[r, :]
        a_in = inn[r, :]
        for j in range(hq):
            c = head_cols(j)
            a = intra[r, c] + nn(q[r, c], state[j, 0:HEAD, :]) * jnp.exp(col[0, r, j : j + 1])
            att[r, c] = a
            a_sq = a_sq + a * a
            a_in = a_in + a * dscaled[r, c]
        sq[r, :] = a_sq
        inn[r, :] = a_in

    @pl.when(d == pl.num_programs(0) - 1)
    def _():
        ones = jnp.ones((8, HEAD), F32)
        a = nt(ones, sq[...], lax.Precision.HIGHEST)
        b = nt(ones, inn[...], lax.Precision.HIGHEST)
        sums[...] = jnp.where(lax.broadcasted_iota(jnp.int32, (8, BLOCK), 0) == 0, a, b)


def dattn_body(hq, channels, s, att, dscaled, turned, gain, sum_a, sum_b, dattn, parts, scale):
    d = pl.program_id(0)

    @pl.when(d == 0)
    def _():
        total = sum_a[...] + sum_b[...]
        rs = lax.rsqrt(total[0:1, :] / channels + EPSILON)
        coef = total[1:2, :] * (rs * rs * rs) / channels
        both = jnp.concatenate([rs, coef, jnp.zeros((HEAD - 2, BLOCK), F32)], axis=0)
        scale[...] = both.T

    for j in range(hq):
        c = head_cols(j)
        gsum = jnp.zeros((8, HEAD), F32)
        for i in range(BLOCK // HEAD):
            r = head_cols(i)
            a = att[r, c]
            t = dscaled[r, c] * scale[r, 0:1]
            dattn[r, c] = (t - a * scale[r, 1:2]).astype(BF16)
            gsum = gsum + jnp.sum((t * a).reshape(HEAD // 8, 8, HEAD), axis=0)
        parts[j, 0:HEAD, :] = nn(turned[j], dattn[:, c]).astype(BF16)
        total = jnp.sum(gsum, axis=0, keepdims=True) / gain[:, c]
        parts[j, HEAD : HEAD + EXTRA, :] = gain_rows(total)


def query_body(hq, s, k, v, dattn, row, col, state, gate, att, dscaled, scale, query_grad, gate_grad):
    mask = lower_mask()
    for j in range(hq):
        c = head_cols(j)
        for i in range(2):
            d = dattn[piece(i), c]
            total = nt(d, state[j, 0:HEAD, :]) * jnp.exp(col[0, piece(i), j : j + 1])
            for m in range(i + 1):
                table = jnp.exp(col[0, piece(i), j : j + 1] - row[0, j : j + 1, piece(m)])
                if m == i:
                    table = jnp.where(mask, table, 0.0)
                dscores = (nt(d, v[piece(m), c]) * table).astype(BF16)
                total = total + nn(dscores, k[piece(m), c])
            query_grad[piece(i), c] = total.astype(BF16)
        opened = jax.nn.sigmoid(gate[:, c].astype(F32))
        gate_grad[:, c] = (dscaled[:, c] * att[:, c] * scale[:, 0:1] * (1.0 - opened)).astype(BF16)


def key_value_body(hq, s, q, k, v, dattn, row, col, dk, dv):
    mask = upper_mask()
    for j in range(hq):
        c = head_cols(j)
        for i in range(2):
            dkey = dvalue = None
            for m in range(i, 2):
                table = jnp.exp(row[0, j : j + 1, piece(m)] - col[0, piece(i), j : j + 1])
                if m == i:
                    table = jnp.where(mask, table, 0.0)
                probs = (nt(k[piece(i), c], q[piece(m), c]) * table).astype(BF16)
                dscores = (nt(v[piece(i), c], dattn[piece(m), c]) * table).astype(BF16)
                a = nn(dscores, q[piece(m), c])
                b = nn(probs, dattn[piece(m), c])
                dkey, dvalue = (a, b) if dkey is None else (dkey + a, dvalue + b)
            dk[piece(i), c] = dkey
            dv[piece(i), c] = dvalue


def final_body(hq, s, k, v, dk, dv, col, state, key_grad, value_grad, gain_grad):
    for j in range(hq):
        c = head_cols(j)
        shrink = jnp.exp(col[0, BLOCK - 1 : BLOCK, j : j + 1] - col[0, :, j : j + 1])
        after = state[j, 0:HEAD, :]
        key_grad[:, c] = (dk[:, c] + nt(v[:, c], after) * shrink).astype(BF16)
        value_grad[:, c] = (dv[:, c] + nn(k[:, c], after) * shrink).astype(BF16)
        gain_grad[:, c] = jnp.sum(state[j, HEAD : HEAD + EXTRA, :].astype(F32), axis=0, keepdims=True)


def plain(body, inputs, out_shape, name):
    return pl.pallas_call(
        body,
        out_shape=out_shape,
        compiler_params=pltpu.CompilerParams(vmem_limit_bytes=VMEM_LIMIT),
        name=name,
    )(*inputs)


def local(queries, keys, values, log_decay, gate, gain, grad_out):
    rows, width = queries.shape
    heads = width // HEAD
    hq = min(4, heads)
    grid = (heads // hq,)
    tp = lax.axis_size("tp")
    n = lax.axis_size("ctx")
    channels = width * tp
    mine = lax.axis_index("tp")
    w = hq * HEAD
    bf = lambda *shape: jax.ShapeDtypeStruct(shape, BF16)
    f32 = lambda *shape: jax.ShapeDtypeStruct(shape, F32)
    tall = heads * HEAD // n
    copies = n // heads

    def spread(payload):
        if copies == 1:
            return payload
        body = payload[:, :HEAD].reshape(n, tall, HEAD)
        return jnp.concatenate([body, jnp.repeat(payload[:, HEAD:], copies, axis=0)], axis=1)

    def collect(chunks):
        if copies == 1:
            return chunks
        body = chunks[:, :tall].reshape(heads, HEAD, HEAD)
        return jnp.concatenate([body, chunks[::copies, tall:]], axis=1)

    def swap(x):
        return lax.all_to_all(x, "ctx", split_axis=0, concat_axis=0, tiled=True)

    swaps = tp == 2
    part = rows // 2
    if swaps:
        own = grad_out
        half = mine
        blocks = grid[0]
        info = jnp.stack([mine, mine * blocks, (1 - mine) * blocks]).astype(jnp.int32)
    else:
        every = lax.all_to_all(grad_out, "tp", split_axis=1, concat_axis=0, tiled=True)
        own, got = every[:part], every[part:]
        info = jnp.zeros((3,), jnp.int32)

    decay_rows = 8 if heads % 8 == 0 else heads
    per = decay_rows // hq
    small = 2 * heads * rows * HEAD * HEAD
    large = 2 * heads * rows * rows * HEAD
    cols = cols_spec(rows, w)
    row_spec = lead_spec(1, 8, BLOCK)
    col_spec = lead_spec(1, BLOCK, HEAD)
    state_spec = lead_spec(hq, HEAD + EXTRA, HEAD)
    narrow_spec = lead_spec(hq, HEAD, HEAD)
    half_spec = cols_spec(part, w)
    gain_spec = cols_spec(1, w)
    gain_row = gain.reshape(1, width)

    outs = call(
        functools.partial(local_states_body, hq, swaps),
        grid,
        info,
        [keys, values, log_decay] + [grad_out] * swaps,
        [cols, cols, pl.BlockSpec((decay_rows, rows), lambda d, s: (d // per, 0))]
        + [pl.BlockSpec((part, w), lambda d, s: (0, s[2] + d))] * swaps,
        [bf(heads, HEAD + EXTRA, HEAD), f32(grid[0], 8, rows), f32(grid[0], rows, HEAD)]
        + [bf(part, width)] * swaps,
        [state_spec, row_spec, col_spec] + [half_spec] * swaps,
        [pltpu.VMEM((BLOCK, BLOCK), BF16)],
        small,
        "local_states",
    )
    parts, row, col = outs[:3]
    received = swap(spread(parts))
    if swaps:
        got = lax.ppermute(outs[3], "tp", [(0, 1), (1, 0)])
    own_spec = pl.BlockSpec((part, w), lambda d, s: (0, s[1] + d))

    (intra,) = call(
        functools.partial(intra_body, hq),
        grid,
        info,
        [queries, keys, values, row, col],
        [cols] * 3 + [row_spec, col_spec],
        [f32(rows, width)],
        [cols],
        [],
        2 * large,
        "intra",
    )
    entering = plain(forward_scan_body, [received], bf(n, tall, HEAD), "forward_scan")
    entering = swap(entering)
    if copies > 1:
        entering = entering.reshape(heads, HEAD, HEAD)
    dscaled, turned = call(
        functools.partial(dscaled_body, hq),
        grid,
        info,
        [gate, own, got, gain_row, queries, row],
        [cols, own_spec, half_spec, gain_spec, cols, row_spec],
        [f32(rows, width), bf(heads, HEAD, rows)],
        [cols, lead_spec(hq, HEAD, rows)],
        [],
        small,
        "dscaled",
    )
    att, sums = call(
        functools.partial(attention_body, hq),
        grid,
        info,
        [queries, intra, dscaled, col, entering],
        [cols, cols, cols, col_spec, narrow_spec],
        [f32(rows, width), f32(8, rows)],
        [cols, whole((8, rows))],
        [pltpu.VMEM((rows, HEAD), F32), pltpu.VMEM((rows, HEAD), F32)],
        small,
        "attention",
    )
    if swaps:
        others = lax.ppermute(sums, "tp", [(0, 1), (1, 0)])
    else:
        others = lax.psum(sums, "tp") - sums
    dattn, parts, scale = call(
        functools.partial(dattn_body, hq, channels),
        grid,
        info,
        [att, dscaled, turned, gain_row, sums, others],
        [cols, cols, lead_spec(hq, HEAD, rows), gain_spec] + [whole((8, rows))] * 2,
        [bf(rows, width), bf(heads, HEAD + EXTRA, HEAD), f32(rows, HEAD)],
        [cols, state_spec, whole((rows, HEAD))],
        [],
        small,
        "dattn",
    )
    received_back = swap(spread(parts))
    query_grad, gate_grad = call(
        functools.partial(query_body, hq),
        grid,
        info,
        [keys, values, dattn, row, col, entering, gate, att, dscaled, scale],
        [cols] * 3 + [row_spec, col_spec, narrow_spec] + [cols] * 3 + [whole((rows, HEAD))],
        [bf(rows, width), bf(rows, width)],
        [cols] * 2,
        [],
        2 * large + small,
        "query",
    )
    leaving = plain(reverse_scan_body, [received, received_back], bf(n, tall + EXTRA, HEAD), "reverse_scan")
    leaving, late_dattn = lax.optimization_barrier((leaving, dattn))
    leaving = collect(swap(leaving))
    dk, dv = call(
        functools.partial(key_value_body, hq),
        grid,
        info,
        [queries, keys, values, late_dattn, row, col],
        [cols] * 4 + [row_spec, col_spec],
        [f32(rows, width), f32(rows, width)],
        [cols] * 2,
        [],
        4 * large,
        "key_value",
    )
    key_grad, value_grad, gain_grad = call(
        functools.partial(final_body, hq),
        grid,
        info,
        [keys, values, dk, dv, col, leaving],
        [cols] * 4 + [col_spec, state_spec],
        [bf(rows, width), bf(rows, width), f32(1, width)],
        [cols] * 2 + [gain_spec],
        [],
        2 * small,
        "final",
    )
    return query_grad, key_grad, value_grad, gate_grad, gain_grad.reshape(width)


def solution(mesh):
    return jax.shard_map(
        local,
        mesh=mesh,
        in_specs=(
            P("ctx", "tp"),
            P("ctx", "tp"),
            P("ctx", "tp"),
            P("tp", "ctx"),
            P("ctx", "tp"),
            P("tp"),
            P(("ctx", "tp"), None),
        ),
        out_specs=(P("ctx", "tp"), P("ctx", "tp"), P("ctx", "tp"), P("ctx", "tp"), P("tp")),
        check_vma=False,
    )
```

```python
import functools

import jax
import jax.numpy as jnp
from jax import lax
from jax.experimental import pallas as pl
from jax.experimental.pallas import tpu as pltpu
from jax.sharding import PartitionSpec as P

HEAD = 128
BLOCK = 512
HALF = BLOCK // 2
EXTRA = 16
TALL = HEAD + EXTRA
TEAM = 4
EPSILON = 1e-06
F32 = jnp.float32
BF16 = jnp.bfloat16
GRANT = 12 * 1024 * 1024
VMEM = pl.BlockSpec(memory_space=pltpu.VMEM)
ANY = pl.BlockSpec(memory_space=pl.ANY)


def nt(a, b, precision=None):
    return lax.dot_general(a, b, (((1,), (1,)), ((), ())), preferred_element_type=F32, precision=precision)


def nn(a, b):
    return lax.dot_general(a, b, (((1,), (0,)), ((), ())), preferred_element_type=F32)


def piece(i):
    return slice(i * HALF, (i + 1) * HALF)


def chunk(i):
    return slice(i * HEAD, (i + 1) * HEAD)


def split_terms(x, count):
    terms = []
    for _ in range(count):
        term = x.astype(BF16)
        terms.append(term)
        x = x - term.astype(F32)
    return terms


def term_rows(x, count):
    at = lax.broadcasted_iota(jnp.int32, (EXTRA, HEAD), 0)
    out = jnp.zeros((EXTRA, HEAD), F32)
    for i, term in enumerate(split_terms(jnp.broadcast_to(x, (EXTRA, HEAD)), count)):
        out = jnp.where(at == i, term.astype(F32), out)
    return out.astype(BF16)


def row_total(ref, j):
    return jnp.sum(ref[j, HEAD:TALL, :].astype(F32), axis=0, keepdims=True)


def seat():
    return lax.rem(lax.axis_index("ctx"), TEAM)


def ahead(d):
    return lax.rem(seat() + d, TEAM)


def behind(d):
    return lax.rem(seat() + TEAM - d, TEAM)


def head_at(quarter, hq, j):
    h = quarter * hq + j
    return h, pl.ds(pl.multiple_of(h * HEAD, HEAD), HEAD)


def transposed(x):
    eye = (
        lax.broadcasted_iota(jnp.int32, (HEAD, HEAD), 0) == lax.broadcasted_iota(jnp.int32, (HEAD, HEAD), 1)
    ).astype(BF16)
    return nt(eye, x)


def call(body, inputs, out_shape, name, scratch=(), flops=0, in_specs=None, out_specs=None):
    nbytes = sum(x.size * x.dtype.itemsize for x in inputs)
    nbytes += sum(x.size * x.dtype.itemsize for x in out_shape)
    return pl.pallas_call(
        body,
        in_specs=in_specs or [VMEM] * len(inputs),
        out_specs=out_specs or [VMEM] * len(out_shape),
        out_shape=out_shape,
        scratch_shapes=list(scratch),
        compiler_params=pltpu.CompilerParams(vmem_limit_bytes=GRANT),
        cost_estimate=pl.CostEstimate(flops=flops, bytes_accessed=nbytes, transcendentals=0),
        name=name,
    )(*inputs)


def local_states_body(heads, swaps, k_hbm, v_hbm, ld, *refs):
    hq = heads // TEAM
    w = hq * HEAD
    if swaps:
        grad, p0, p1, p2, p3, row, away, own, k, v, sems, grad_sems = refs
        width = heads * HEAD
        mine = lax.axis_index("tp")
        cols = lambda t: pl.ds(pl.multiple_of(t * width, HEAD), width)
        grad_copies = [
            pltpu.make_async_copy(grad.at[:, cols(1 - mine)], away, grad_sems.at[0]),
            pltpu.make_async_copy(grad.at[:, cols(mine)], own, grad_sems.at[1]),
        ]
    else:
        p0, p1, p2, p3, row, k, v, sems = refs
        grad_copies = []
    outs = (p0, p1, p2, p3)
    order = (1, 2, 3, 0)
    copies = []
    for d in order:
        cols_d = pl.ds(pl.multiple_of(ahead(d) * w, HEAD), w)
        pair = [
            pltpu.make_async_copy(k_hbm.at[:, cols_d], k.at[d], sems.at[0, d]),
            pltpu.make_async_copy(v_hbm.at[:, cols_d], v.at[d], sems.at[1, d]),
        ]
        for c in pair:
            c.start()
        copies.append(pair)
    for c in grad_copies:
        c.start()
    at = lax.broadcasted_iota(jnp.int32, (BLOCK, BLOCK), 0)
    other = lax.broadcasted_iota(jnp.int32, (BLOCK, BLOCK), 1)
    tri = (at <= other).astype(BF16)
    x = ld[...]
    if heads < EXTRA:
        x = jnp.concatenate([x, jnp.zeros((EXTRA - heads, BLOCK), F32)], axis=0)
    a, b, c = (nn(term, tri) for term in split_terms(x, 3))
    row[...] = a + (b + c)
    for d, pair in zip(order, copies):
        for c in pair:
            c.wait()
        for j in range(hq):
            h = ahead(d) * hq + j
            sums = row[pl.ds(h, 1), :]
            edge = sums[:, BLOCK - 1 : BLOCK]
            shrink = jnp.exp(edge - sums)
            kd = (transposed(k[d, :, chunk(j)]) * shrink).astype(BF16)
            outs[d][j, 0:HEAD, :] = nn(kd, v[d, :, chunk(j)]).astype(BF16)
            outs[d][j, HEAD:TALL, :] = term_rows(jnp.broadcast_to(edge, (1, HEAD)), 3)
    for c in grad_copies:
        c.wait()


def group_total_body(reverse, hq, a0, a1, a2, a3, *refs):
    if reverse:
        edges, out = refs
    else:
        out, edges = refs
    slots = (a0, a1, a2, a3)
    src = [behind(d) for d in range(TEAM)]
    for j in range(hq):
        if reverse:
            e = [edges[j, d : d + 1, :] for d in range(TEAM)]
        else:
            e = [row_total(slots[d], j) for d in range(TEAM)]
            for d in range(TEAM):
                edges[j, d : d + 1, :] = e[d]
            edges[j, TEAM : TEAM + 1, :] = (e[0] + e[1]) + (e[2] + e[3])
            for d in range(TEAM + 1, 8):
                edges[j, d : d + 1, :] = jnp.zeros((1, HEAD), F32)
        total = jnp.zeros((HEAD, HEAD), F32)
        for d in range(TEAM):
            expo = jnp.zeros((1, HEAD), F32)
            for i in range(TEAM):
                if i != d:
                    between = src[i] < src[d] if reverse else src[i] > src[d]
                    expo = expo + jnp.where(between, e[i], 0.0)
            total = total + slots[d][j, 0:HEAD, :].astype(F32) * jnp.exp(expo)
        out[j, 0:HEAD, :] = total.astype(BF16)
        rows = term_rows((e[0] + e[1]) + (e[2] + e[3]), 3)
        if reverse:
            gains = [row_total(slots[d], j) for d in range(TEAM)]
            gain = term_rows((gains[0] + gains[1]) + (gains[2] + gains[3]), 2).astype(F32)
            at = lax.broadcasted_iota(jnp.int32, (EXTRA, HEAD), 0)
            rows = jnp.where(at < 8, rows.astype(F32), jnp.concatenate([gain[8:], gain[:8]], axis=0))
            rows = rows.astype(BF16)
        out[j, HEAD:TALL, :] = rows


def entering_body(reverse, hq, groups, *refs):
    slots = refs[:TEAM]
    total, edges = refs[TEAM : TEAM + 2]
    far = refs[TEAM + 2 : TEAM + 1 + groups]
    outs = refs[TEAM + 1 + groups :]
    src = [behind(d) for d in range(TEAM)]
    dst = [ahead(d) for d in range(TEAM)]
    group = lax.axis_index("ctx") // TEAM
    for j in range(hq):
        e = [edges[j, d : d + 1, :] for d in range(TEAM)]
        incoming = jnp.zeros((HEAD, HEAD), F32)
        gain = total[j, HEAD + 8 : TALL, :].astype(F32)
        for k in reversed(range(1, groups)):
            ref = far[k - 1]
            there = group + k < groups if reverse else group - k >= 0
            decay = jnp.exp(jnp.sum(ref[j, HEAD : HEAD + 8, :].astype(F32), axis=0, keepdims=True))
            incoming = incoming * decay + ref[j, 0:HEAD, :].astype(F32)
            incoming = jnp.where(there, incoming, 0.0)
            gain = gain + ref[j, HEAD + 8 : TALL, :].astype(F32)
        parts = [slots[i][j, 0:HEAD, :].astype(F32) for i in range(TEAM)]
        for d in range(TEAM):
            def passed(i):
                return src[i] > dst[d] if reverse else src[i] < dst[d]

            def beyond(i, m):
                return src[m] < src[i] if reverse else src[m] > src[i]

            expo = jnp.zeros((1, HEAD), F32)
            for i in range(TEAM):
                expo = expo + jnp.where(passed(i), e[i], 0.0)
            state = incoming * jnp.exp(expo)
            for i in range(TEAM):
                if (i + d) % TEAM == 0:
                    continue
                expo = jnp.zeros((1, HEAD), F32)
                for m in range(TEAM):
                    if m != i:
                        expo = expo + jnp.where(jnp.logical_and(passed(m), beyond(i, m)), e[m], 0.0)
                state = state + parts[i] * jnp.where(passed(i), jnp.exp(expo), 0.0)
            outs[d][j, 0:HEAD, :] = state.astype(BF16)
            if reverse:
                outs[d][j, HEAD:TALL, :] = term_rows(jnp.sum(gain, axis=0, keepdims=True), 2)


def masked(lower):
    at = lax.broadcasted_iota(jnp.int32, (HALF, HALF), 0)
    other = lax.broadcasted_iota(jnp.int32, (HALF, HALF), 1)
    return at >= other if lower else at <= other


def intra_body(heads, q, k, v, row, intra, col, growth, shrink):
    hq = heads // TEAM
    mask = masked(True)
    for g in range(TEAM):
        rows = row[g * hq : (g + 1) * hq, :]
        across = jnp.concatenate([rows, jnp.zeros((HEAD - hq, BLOCK), F32)], axis=0).T
        col[g] = across
        growth[g] = jnp.exp(across)
        shrink[g] = jnp.exp(across[BLOCK - 1 : BLOCK, :] - across)

    def one(g, _):
        for j in range(hq):
            h, c = head_at(g, hq, j)
            line = row[pl.ds(h, 1), :]
            for i in range(2):
                total = None
                for m in range(i + 1):
                    table = jnp.exp(col[g, piece(i), j : j + 1] - line[:, piece(m)])
                    if m == i:
                        table = jnp.where(mask, table, 0.0)
                    probs = (nt(q[piece(i), c], k[piece(m), c]) * table).astype(BF16)
                    term = nn(probs, v[piece(m), c])
                    total = term if total is None else total + term
                intra[piece(i), c] = total
        return 0

    lax.fori_loop(0, TEAM, one, 0)


def dscaled_body(heads, swaps, gate, own, got, gain, q, row, dscaled, turned):
    hq = heads // TEAM
    part = own.shape[0]
    mine = lax.axis_index("tp") if swaps else 0

    def one(g, _):
        for j in range(hq):
            h, c = head_at(g, hq, j)
            for where, ref in ((mine, own), (1 - mine, got)):
                rows = pl.ds(pl.multiple_of(where * part, part), part)
                opened = jax.nn.sigmoid(gate[rows, c].astype(F32))
                dscaled[rows, c] = ref[:, c].astype(F32) * opened * gain[:, c]
            turned[h] = (transposed(q[:, c]) * jnp.exp(row[pl.ds(h, 1), :])).astype(BF16)
        return 0

    lax.fori_loop(0, TEAM, one, 0)


def attention_body(heads, q, intra, dscaled, growth, s0, s1, s2, s3, att, sums, sq, inn):
    hq = heads // TEAM
    for i in range(BLOCK // HEAD):
        r = chunk(i)
        a_sq = jnp.zeros((HEAD, HEAD), F32)
        a_in = jnp.zeros((HEAD, HEAD), F32)
        for d, state in enumerate((s0, s1, s2, s3)):
            grow = growth[behind(d), r, :]
            for j in range(hq):
                _, c = head_at(behind(d), hq, j)
                a = intra[r, c] + nn(q[r, c], state[j, 0:HEAD, :]) * grow[:, j : j + 1]
                att[r, c] = a
                a_sq = a_sq + a * a
                a_in = a_in + a * dscaled[r, c]
        sq[r, :] = a_sq
        inn[r, :] = a_in
    ones = jnp.ones((8, HEAD), F32)
    a = nt(ones, sq[...], lax.Precision.HIGHEST)
    b = nt(ones, inn[...], lax.Precision.HIGHEST)
    sums[...] = jnp.where(lax.broadcasted_iota(jnp.int32, (8, BLOCK), 0) == 0, a, b)


def dattn_body(heads, channels, att, dscaled, turned, gain, sum_a, sum_b, dattn, scale, p0, p1, p2, p3):
    hq = heads // TEAM
    total = sum_a[...] + sum_b[...]
    rs = lax.rsqrt(total[0:1, :] / channels + EPSILON)
    coef = total[1:2, :] * (rs * rs * rs) / channels
    scale[...] = jnp.concatenate([rs, coef, jnp.zeros((HEAD - 2, BLOCK), F32)], axis=0).T
    for d, out in ((1, p1), (2, p2), (3, p3), (0, p0)):
        for j in range(hq):
            h, c = head_at(ahead(d), hq, j)
            gsum = jnp.zeros((8, HEAD), F32)
            for i in range(BLOCK // HEAD):
                r = chunk(i)
                a = att[r, c]
                t = dscaled[r, c] * scale[r, 0:1]
                dattn[r, c] = (t - a * scale[r, 1:2]).astype(BF16)
                gsum = gsum + jnp.sum((t * a).reshape(HEAD // 8, 8, HEAD), axis=0)
            out[j, 0:HEAD, :] = nn(turned[h], dattn[:, c]).astype(BF16)
            out[j, HEAD:TALL, :] = term_rows(jnp.sum(gsum, axis=0, keepdims=True) / gain[:, c], 2)


def query_body(heads, k, v, dattn, row, col, growth, s0, s1, s2, s3, gate, att, dscaled, scale, query_grad, gate_grad):
    hq = heads // TEAM
    mask = masked(True)
    for slot, state in enumerate((s0, s1, s2, s3)):
        g = behind(slot)
        for j in range(hq):
            h, c = head_at(g, hq, j)
            line = row[pl.ds(h, 1), :]
            for i in range(2):
                d = dattn[piece(i), c]
                total = nt(d, state[j, 0:HEAD, :]) * growth[g, piece(i), j : j + 1]
                for m in range(i + 1):
                    table = jnp.exp(col[g, piece(i), j : j + 1] - line[:, piece(m)])
                    if m == i:
                        table = jnp.where(mask, table, 0.0)
                    dscores = (nt(d, v[piece(m), c]) * table).astype(BF16)
                    total = total + nn(dscores, k[piece(m), c])
                query_grad[piece(i), c] = total.astype(BF16)
            opened = jax.nn.sigmoid(gate[:, c].astype(F32))
            gate_grad[:, c] = (dscaled[:, c] * att[:, c] * scale[:, 0:1] * (1.0 - opened)).astype(BF16)


def key_value_body(heads, q, k, v, dattn, row, col, dk, dv):
    hq = heads // TEAM
    mask = masked(False)

    def one(g, _):
        for n in range(hq):
            h, c = head_at(g, hq, n)
            line = row[pl.ds(h, 1), :]
            for i in range(2):
                dkey = dvalue = None
                for m in range(i, 2):
                    table = jnp.exp(line[:, piece(m)] - col[g, piece(i), n : n + 1])
                    if m == i:
                        table = jnp.where(mask, table, 0.0)
                    probs = (nt(k[piece(i), c], q[piece(m), c]) * table).astype(BF16)
                    dscores = (nt(v[piece(i), c], dattn[piece(m), c]) * table).astype(BF16)
                    a = nn(dscores, q[piece(m), c])
                    b = nn(probs, dattn[piece(m), c])
                    dkey, dvalue = (a, b) if dkey is None else (dkey + a, dvalue + b)
                dk[piece(i), c] = dkey
                dv[piece(i), c] = dvalue
        return 0

    lax.fori_loop(0, TEAM, one, 0)


def final_body(heads, k, v, dk, dv, shrink, r0, r1, r2, r3, key_grad, value_grad, gain_grad, key_out, value_out, sems):
    hq = heads // TEAM
    w = hq * HEAD
    copies = []
    for d, state in enumerate((r0, r1, r2, r3)):
        g = behind(d)
        for j in range(hq):
            _, c = head_at(g, hq, j)
            fade = shrink[g, :, j : j + 1]
            after = state[j, 0:HEAD, :]
            key_out[d, :, chunk(j)] = (dk[:, c] + nt(v[:, c], after) * fade).astype(BF16)
            value_out[d, :, chunk(j)] = (dv[:, c] + nn(k[:, c], after) * fade).astype(BF16)
            gain_grad[:, c] = row_total(state, j)
        cols = pl.ds(pl.multiple_of(g * w, HEAD), w)
        for i, (src, dst) in enumerate(((key_out, key_grad), (value_out, value_grad))):
            copy = pltpu.make_async_copy(src.at[d], dst.at[:, cols], sems.at[i, d])
            copy.start()
            copies.append(copy)
    for copy in copies:
        copy.wait()


def around(x, d):
    n = lax.axis_size("ctx")
    return lax.ppermute(x, "ctx", [(i, i - i % TEAM + (i + d) % TEAM) for i in range(n)])


def across(x, k):
    n = lax.axis_size("ctx")
    return lax.ppermute(x, "ctx", [(i, (i + TEAM * k) % n) for i in range(n)])


def local(queries, keys, values, log_decay, gate, gain, grad_out):
    rows, width = queries.shape
    heads = width // HEAD
    hq = heads // TEAM
    tp = lax.axis_size("tp")
    n = lax.axis_size("ctx")
    groups = n // TEAM
    channels = width * tp
    bf = lambda *shape: jax.ShapeDtypeStruct(shape, BF16)
    f32 = lambda *shape: jax.ShapeDtypeStruct(shape, F32)
    swaps = tp == 2
    part = rows // 2
    small = 2 * heads * rows * HEAD * HEAD
    large = 2 * heads * rows * rows * HEAD
    packed = bf(hq, TALL, HEAD)
    plain = bf(hq, HEAD, HEAD)
    table = f32(TEAM, rows, HEAD)
    gain_row = gain.reshape(1, width)

    outs = call(
        functools.partial(local_states_body, heads, swaps),
        [keys, values, log_decay] + [grad_out] * swaps,
        [packed] * TEAM + [f32(EXTRA, rows)] + [bf(part, width)] * 2 * swaps,
        "local_states",
        [pltpu.VMEM((TEAM, rows, hq * HEAD), BF16)] * 2
        + [pltpu.SemaphoreType.DMA((2, TEAM))]
        + [pltpu.SemaphoreType.DMA((2,))] * swaps,
        small,
        [ANY, ANY, VMEM] + [ANY] * swaps,
        [VMEM] * (TEAM + 1) + [ANY, VMEM] * swaps,
    )
    parts, row = outs[:TEAM], outs[TEAM]
    slots = [parts[0]] + [around(parts[d], d) for d in range(1, TEAM)]
    if swaps:
        away, own = outs[TEAM + 1 :]
        got = lax.ppermute(away, "tp", [(0, 1), (1, 0)])
    else:
        every = lax.all_to_all(grad_out, "tp", split_axis=1, concat_axis=0, tiled=True)
        own, got = every[:part], every[part:]
    intra, col, growth, shrink = call(
        functools.partial(intra_body, heads),
        [queries, keys, values, row],
        [f32(rows, width), table, table, table],
        "intra",
        flops=2 * large,
    )
    total, edges = call(
        functools.partial(group_total_body, False, hq), slots, [packed, f32(hq, 8, HEAD)], "group_total"
    )
    far = [across(total, k) for k in range(1, groups)]
    entering = call(
        functools.partial(entering_body, False, hq, groups), [*slots, total, edges, *far], [plain] * TEAM, "entering"
    )
    entering = [entering[0]] + [around(entering[d], d) for d in range(1, TEAM)]
    dscaled, turned = call(
        functools.partial(dscaled_body, heads, swaps),
        [gate, own, got, gain_row, queries, row],
        [f32(rows, width), bf(heads, HEAD, rows)],
        "dscaled",
        flops=small,
    )
    att, sums = call(
        functools.partial(attention_body, heads),
        [queries, intra, dscaled, growth, *entering],
        [f32(rows, width), f32(8, rows)],
        "attention",
        [pltpu.VMEM((rows, HEAD), F32)] * 2,
        small,
    )
    if swaps:
        others = lax.ppermute(sums, "tp", [(0, 1), (1, 0)])
    else:
        others = lax.psum(sums, "tp") - sums
    dattn, scale, *parts = call(
        functools.partial(dattn_body, heads, channels),
        [att, dscaled, turned, gain_row, sums, others],
        [bf(rows, width), f32(rows, HEAD)] + [packed] * TEAM,
        "dattn",
        flops=small,
    )
    back = [parts[0]] + [around(parts[d], d) for d in range(1, TEAM)]
    query_grad, gate_grad = call(
        functools.partial(query_body, heads),
        [keys, values, dattn, row, col, growth, *entering, gate, att, dscaled, scale],
        [bf(rows, width), bf(rows, width)],
        "query",
        flops=2 * large + small,
    )
    (total,) = call(functools.partial(group_total_body, True, hq), [*back, edges], [packed], "group_total_back")
    far = [across(total, -k) for k in range(1, groups)]
    leaving = call(
        functools.partial(entering_body, True, hq, groups), [*back, total, edges, *far], [packed] * TEAM, "leaving"
    )
    leaving = [leaving[0]] + [around(leaving[d], d) for d in range(1, TEAM)]
    dk, dv = call(
        functools.partial(key_value_body, heads),
        [queries, keys, values, dattn, row, col],
        [f32(rows, width), f32(rows, width)],
        "key_value",
        flops=4 * large,
    )
    key_grad, value_grad, gain_grad = call(
        functools.partial(final_body, heads),
        [keys, values, dk, dv, shrink, *leaving],
        [bf(rows, width), bf(rows, width), f32(1, width)],
        "final",
        [pltpu.VMEM((TEAM, rows, hq * HEAD), BF16)] * 2 + [pltpu.SemaphoreType.DMA((2, TEAM))],
        2 * small,
        out_specs=[ANY, ANY, VMEM],
    )
    return query_grad, key_grad, value_grad, gate_grad, gain_grad.reshape(width)


def solution(mesh):
    return jax.shard_map(
        local,
        mesh=mesh,
        in_specs=(
            P("ctx", "tp"),
            P("ctx", "tp"),
            P("ctx", "tp"),
            P("tp", "ctx"),
            P("ctx", "tp"),
            P("tp"),
            P(("ctx", "tp"), None),
        ),
        out_specs=(P("ctx", "tp"), P("ctx", "tp"), P("ctx", "tp"), P("ctx", "tp"), P("tp")),
        check_vma=False,
    )
```

```python
import functools

import jax
import jax.numpy as jnp
from jax import lax
from jax.experimental import pallas as pl
from jax.experimental.pallas import tpu as pltpu
from jax.sharding import PartitionSpec as P

HEAD = 128
BLOCK = 512
WIDE = 2 * HEAD
TEAM = 4
SIDE = 8
EXTRA = 16
EPSILON = 1e-06
F32 = jnp.float32
BF16 = jnp.bfloat16
GRANT = 12 * 1024 * 1024
VMEM = pl.BlockSpec(memory_space=pltpu.VMEM)
HBM = pl.BlockSpec(memory_space=pltpu.HBM)
ANY = pl.BlockSpec(memory_space=pl.ANY)


def nt(a, b, precision=None):
    return lax.dot_general(a, b, (((1,), (1,)), ((), ())), preferred_element_type=F32, precision=precision)


def nn(a, b):
    return lax.dot_general(a, b, (((1,), (0,)), ((), ())), preferred_element_type=F32)


def chunk(i):
    return slice(i * HEAD, (i + 1) * HEAD)


def split_terms(x, count):
    terms = []
    for _ in range(count):
        term = x.astype(BF16)
        terms.append(term)
        x = x - term.astype(F32)
    return terms


def read_wide(ref, hq):
    base = hq * HEAD
    return [
        (ref[chunk(j), :], ref[base + j : base + j + 1, :], ref[base + TEAM + j : base + TEAM + j + 1, :])
        for j in range(hq)
    ]


def write_wide(ref, hq, items):
    base = hq * HEAD
    at = lax.broadcasted_iota(jnp.int32, (SIDE, HEAD), 0)
    side = jnp.zeros((SIDE, HEAD), F32)
    for j, (term, edge, gain) in enumerate(items):
        ref[chunk(j), :] = term
        side = jnp.where(at == j, edge, side)
        side = jnp.where(at == TEAM + j, gain, side)
    ref[base : base + SIDE, :] = side


def read_narrow(ref, hq):
    base = hq * HEAD
    side = ref[base : base + EXTRA, :].astype(F32)
    row = lambda i: side[i : i + 1, :] + side[i + 1 : i + 2, :]
    return [(ref[chunk(j), :].astype(F32), row(2 * j), row(2 * TEAM + 2 * j)) for j in range(hq)]


def write_narrow(ref, hq, items):
    base = hq * HEAD
    at = lax.broadcasted_iota(jnp.int32, (EXTRA, HEAD), 0)
    side = jnp.zeros((EXTRA, HEAD), F32)
    for j, (term, edge, gain) in enumerate(items):
        ref[chunk(j), :] = term.astype(BF16)
        for first, value in ((2 * j, edge), (2 * TEAM + 2 * j, gain)):
            for i, part in enumerate(split_terms(value, 2)):
                side = jnp.where(at == first + i, part.astype(F32), side)
    ref[base : base + EXTRA, :] = side.astype(BF16)


def core():
    return lax.rem(lax.axis_index("ctx"), 2)


def pair():
    return lax.rem(lax.axis_index("ctx") // 2, 2)


def group():
    return lax.axis_index("ctx") // TEAM


def quarter_of(y, same):
    return 2 * y + (core() if same else 1 - core())


def head_at(quarter, hq, j):
    h = quarter * hq + j
    return h, pl.ds(pl.multiple_of(h * HEAD, HEAD), HEAD)


def transposed(x):
    eye = (
        lax.broadcasted_iota(jnp.int32, (HEAD, HEAD), 0) == lax.broadcasted_iota(jnp.int32, (HEAD, HEAD), 1)
    ).astype(BF16)
    return nt(eye, x)


def call(body, inputs, out_shape, name, scratch=(), flops=0, in_specs=None, out_specs=None, alias=None):
    nbytes = sum(x.size * x.dtype.itemsize for x in inputs)
    nbytes += sum(x.size * x.dtype.itemsize for x in out_shape)
    return pl.pallas_call(
        body,
        in_specs=in_specs or [VMEM] * len(inputs),
        out_specs=out_specs or [VMEM] * len(out_shape),
        out_shape=out_shape,
        scratch_shapes=list(scratch),
        input_output_aliases=alias or {},
        compiler_params=pltpu.CompilerParams(vmem_limit_bytes=GRANT),
        cost_estimate=pl.CostEstimate(flops=flops, bytes_accessed=nbytes, transcendentals=0),
        name=name,
    )(*inputs)


def joined(mine, other, mine_is_first, reverse):
    out = []
    for (a, ea, ga), (b, eb, gb) in zip(mine, other):
        near = mine_is_first if reverse else jnp.logical_not(mine_is_first)
        wa = jnp.where(near, 1.0, jnp.exp(eb))
        wb = jnp.where(near, jnp.exp(ea), 1.0)
        out.append((a * wa + b * wb, ea + eb, ga + gb))
    return out


def chip_total_body(reverse, hq, *refs):
    if reverse:
        keep, got, own, send = refs
    else:
        keep, got, _, own, send, _ = refs
    first = core() == 0
    here, there = pair(), 1 - pair()
    own_items = joined(read_wide(keep.at[here], hq), read_wide(got.at[here], hq), first, reverse)
    write_wide(own, hq, own_items)
    send_items = joined(read_wide(keep.at[there], hq), read_wide(got.at[there], hq), first, reverse)
    write_narrow(send, hq, send_items)


def group_total_body(reverse, hq, own, got, *refs):
    total, send = refs[-2:]
    items = joined(read_wide(own, hq), read_narrow(got, hq), pair() == 0, reverse)
    write_wide(total, hq, items)
    write_narrow(send, hq, items)


def doubled(reverse, hq, step, groups, before, got):
    there = group() + step < groups if reverse else group() - step >= 0
    out = []
    for old, (term, edge, gain) in zip(before, read_narrow(got, hq)):
        term = jnp.where(there, term, 0.0)
        edge = jnp.where(there, edge, 0.0)
        if old is None:
            out.append((term, edge, gain))
        else:
            out.append((old[0] + jnp.exp(old[1]) * term, old[1] + edge, old[2] + gain))
    return out


def doubling_body(reverse, hq, step, groups, total, *refs):
    so_far, send = refs[-2:]
    if step == 1:
        got = refs[0]
        before = [None] * hq
    else:
        got = refs[1]
        before = read_wide(refs[0], hq)
    items = doubled(reverse, hq, step, groups, before, got)
    write_wide(so_far, hq, items)
    whole = []
    for (t, e, g), (s, es, gs) in zip(read_wide(total, hq), items):
        whole.append((t + jnp.exp(e) * s, e + es, g + gs))
    write_narrow(send, hq, whole)


def into_chips_body(reverse, hq, step, groups, own, got_pair, total, so_far, got, *refs):
    keep, send = refs[-2:]
    before = read_wide(so_far, hq) if step > 1 else [None] * hq
    entering = doubled(reverse, hq, step, groups, before, got)
    mine_near = pair() == (1 if reverse else 0)
    kept, sent = [], []
    for (r, _, gr), (c, ec, _), (o, eo, _), (_, _, gt) in zip(
        entering, read_wide(own, hq), read_narrow(got_pair, hq), read_wide(total, hq)
    ):
        gain = gr + gt
        zero = jnp.zeros_like(ec)
        kept.append((jnp.where(mine_near, r, jnp.exp(eo) * r + o), zero, gain))
        sent.append((jnp.where(mine_near, jnp.exp(ec) * r + c, r), zero, gain))
    write_wide(keep, hq, kept)
    write_narrow(send, hq, sent)


def into_cores_body(reverse, hq, keep, got, own, other, *refs):
    mine, send = refs[-2:]
    mine_near = core() == (1 if reverse else 0)
    for y in range(2):
        a, b = read_wide(own, hq), read_narrow(other, hq)
        here = pair() == y
        items_mine, items_send = [], []
        for p, q, (k, ek, _), (g, eg, _) in zip(a, b, read_wide(keep.at[y], hq), read_wide(got.at[y], hq)):
            r = jnp.where(here, p[0], q[0])
            gain = jnp.where(here, p[2], q[2])
            zero = jnp.zeros_like(ek)
            items_mine.append((jnp.where(mine_near, r, jnp.exp(eg) * r + g), zero, gain))
            items_send.append((jnp.where(mine_near, jnp.exp(ek) * r + k, r), zero, gain))
        write_narrow(mine.at[y], hq, items_mine)
        write_narrow(send.at[y], hq, items_send)


def local_states_body(heads, swaps, k_hbm, v_hbm, ld, *refs):
    hq = heads // TEAM
    w = hq * HEAD
    if swaps:
        grad, keep, give, row, away, own, k, v, sems, grad_sems = refs
        width = heads * HEAD
        mine = lax.axis_index("tp")
        cols = lambda t: pl.ds(pl.multiple_of(t * width, HEAD), width)
        grad_copies = [
            pltpu.make_async_copy(grad.at[:, cols(1 - mine)], away, grad_sems.at[0]),
            pltpu.make_async_copy(grad.at[:, cols(mine)], own, grad_sems.at[1]),
        ]
    else:
        keep, give, row, k, v, sems = refs
        grad_copies = []
    order = [(give, 0, False), (give, 1, False), (keep, 0, True), (keep, 1, True)]
    copies = []
    for slot, (_, y, same) in enumerate(order):
        cols_d = pl.ds(pl.multiple_of(quarter_of(y, same) * w, HEAD), w)
        both = [
            pltpu.make_async_copy(k_hbm.at[:, cols_d], k.at[slot], sems.at[0, slot]),
            pltpu.make_async_copy(v_hbm.at[:, cols_d], v.at[slot], sems.at[1, slot]),
        ]
        for c in both:
            c.start()
        copies.append(both)
    for c in grad_copies:
        c.start()
    at = lax.broadcasted_iota(jnp.int32, (BLOCK, BLOCK), 0)
    other = lax.broadcasted_iota(jnp.int32, (BLOCK, BLOCK), 1)
    tri = (at <= other).astype(BF16)
    x = ld[...]
    if heads < EXTRA:
        x = jnp.concatenate([x, jnp.zeros((EXTRA - heads, BLOCK), F32)], axis=0)
    a, b, c = (nn(term, tri) for term in split_terms(x, 3))
    row[...] = a + (b + c)
    for slot, (out, y, same) in enumerate(order):
        for c in copies[slot]:
            c.wait()
        items = []
        for j in range(hq):
            sums = row[pl.ds(quarter_of(y, same) * hq + j, 1), :]
            edge = sums[:, BLOCK - 1 : BLOCK]
            kd = (transposed(k[slot, :, chunk(j)]) * jnp.exp(edge - sums)).astype(BF16)
            spread = jnp.broadcast_to(edge, (1, HEAD))
            items.append((nn(kd, v[slot, :, chunk(j)]), spread, jnp.zeros((1, HEAD), F32)))
        write_wide(out.at[y], hq, items)
    for c in grad_copies:
        c.wait()


def decays_body(heads, row, _, col, growth, shrink):
    hq = heads // TEAM
    for g in range(TEAM):
        rows = row[g * hq : (g + 1) * hq, :]
        across = jnp.concatenate([rows, jnp.zeros((HEAD - hq, BLOCK), F32)], axis=0).T
        col[g] = across
        growth[g] = jnp.exp(across)
        shrink[g] = jnp.exp(across[BLOCK - 1 : BLOCK, :] - across)


def lower_tiles(i):
    tiles = [(s, WIDE, False) for s in range(0, (i // 2) * WIDE, WIDE)]
    return tiles + [((i // 2) * WIDE, HEAD if i % 2 == 0 else WIDE, True)]


def upper_tiles(i):
    first = i * HEAD
    width = WIDE if i % 2 == 0 else HEAD
    return [(first, width, True)] + [(s, WIDE, False) for s in range(first + width, BLOCK, WIDE)]


def lower_table(left, line, i, start, width, cut):
    table = jnp.exp(left - line[:, start : start + width])
    if cut:
        at = lax.broadcasted_iota(jnp.int32, (HEAD, width), 0) + (i * HEAD - start)
        table = jnp.where(at >= lax.broadcasted_iota(jnp.int32, (HEAD, width), 1), table, 0.0)
    return table


def upper_table(left, line, i, start, width, cut):
    table = jnp.exp(line[:, start : start + width] - left)
    if cut:
        at = lax.broadcasted_iota(jnp.int32, (HEAD, width), 0)
        table = jnp.where(at <= lax.broadcasted_iota(jnp.int32, (HEAD, width), 1), table, 0.0)
    return table


def intra_body(heads, q, k, v, row, col, _, intra):
    hq = heads // TEAM

    def one(g, _):
        for j in range(hq):
            h, c = head_at(g, hq, j)
            line = row[pl.ds(h, 1), :]
            for i in range(BLOCK // HEAD):
                left = col[g, chunk(i), j : j + 1]
                total = None
                for start, width, cut in lower_tiles(i):
                    u = slice(start, start + width)
                    table = lower_table(left, line, i, start, width, cut)
                    probs = (nt(q[chunk(i), c], k[u, c]) * table).astype(BF16)
                    term = nn(probs, v[u, c])
                    total = term if total is None else total + term
                intra[chunk(i), c] = total
        return 0

    lax.fori_loop(0, TEAM, one, 0)


def dscaled_body(heads, swaps, gate, own, got, gain, q, row, dscaled, turned):
    hq = heads // TEAM
    part = own.shape[0]
    mine = lax.axis_index("tp") if swaps else 0

    def one(g, _):
        for j in range(hq):
            h, c = head_at(g, hq, j)
            for where, ref in ((mine, own), (1 - mine, got)):
                rows = pl.ds(pl.multiple_of(where * part, part), part)
                opened = jax.nn.sigmoid(gate[rows, c].astype(F32))
                dscaled[rows, c] = ref[:, c].astype(F32) * opened * gain[:, c]
            turned[h] = (transposed(q[:, c]) * jnp.exp(row[pl.ds(h, 1), :])).astype(BF16)
        return 0

    lax.fori_loop(0, TEAM, one, 0)


def by_quarter(mine, got):
    return [(ref.at[y], quarter_of(y, same)) for ref, same in ((mine, True), (got, False)) for y in range(2)]


def attention_body(heads, q, intra, dscaled, growth, mine, got, att, sums, sq, inn):
    hq = heads // TEAM
    for i in range(BLOCK // HEAD):
        r = chunk(i)
        a_sq = jnp.zeros((HEAD, HEAD), F32)
        a_in = jnp.zeros((HEAD, HEAD), F32)
        for state, g in by_quarter(mine, got):
            grow = growth[g, r, :]
            for j in range(hq):
                _, c = head_at(g, hq, j)
                a = intra[r, c] + nn(q[r, c], state[chunk(j), :]) * grow[:, j : j + 1]
                att[r, c] = a
                a_sq = a_sq + a * a
                a_in = a_in + a * dscaled[r, c]
        sq[r, :] = a_sq
        inn[r, :] = a_in
    ones = jnp.ones((8, HEAD), F32)
    a = nt(ones, sq[...], lax.Precision.HIGHEST)
    b = nt(ones, inn[...], lax.Precision.HIGHEST)
    sums[...] = jnp.where(lax.broadcasted_iota(jnp.int32, (8, BLOCK), 0) == 0, a, b)


def dattn_body(heads, channels, att, dscaled, turned, gain, row, sum_a, sum_b, dattn, scale, keep, give):
    hq = heads // TEAM
    total = sum_a[...] + sum_b[...]
    rs = lax.rsqrt(total[0:1, :] / channels + EPSILON)
    coef = total[1:2, :] * (rs * rs * rs) / channels
    scale[...] = jnp.concatenate([rs, coef, jnp.zeros((HEAD - 2, BLOCK), F32)], axis=0).T
    for out, y, same in ((give, 0, False), (give, 1, False), (keep, 0, True), (keep, 1, True)):
        items = []
        for j in range(hq):
            h, c = head_at(quarter_of(y, same), hq, j)
            gsum = jnp.zeros((8, HEAD), F32)
            for i in range(BLOCK // HEAD):
                r = chunk(i)
                a = att[r, c]
                t = dscaled[r, c] * scale[r, 0:1]
                dattn[r, c] = (t - a * scale[r, 1:2]).astype(BF16)
                gsum = gsum + jnp.sum((t * a).reshape(HEAD // 8, 8, HEAD), axis=0)
            edge = jnp.broadcast_to(row[pl.ds(h, 1), :][:, BLOCK - 1 : BLOCK], (1, HEAD))
            part = jnp.sum(gsum, axis=0, keepdims=True) / gain[:, c]
            items.append((nn(turned[h], dattn[:, c]), edge, part))
        write_wide(out.at[y], hq, items)


def gate_body(heads, gate, att, dscaled, scale, _, gate_grad, token):
    token[...] = jnp.zeros_like(token)

    def one(h, _):
        _, c = head_at(h, 1, 0)
        opened = jax.nn.sigmoid(gate[:, c].astype(F32))
        gate_grad[:, c] = (dscaled[:, c] * att[:, c] * scale[:, 0:1] * (1.0 - opened)).astype(BF16)
        return 0

    lax.fori_loop(0, heads, one, 0)


def query_body(heads, k, v, dattn, row, col, growth, mine, got, _, query_grad, token):
    token[...] = jnp.zeros_like(token)
    hq = heads // TEAM
    for state, g in by_quarter(mine, got):
        for j in range(hq):
            h, c = head_at(g, hq, j)
            line = row[pl.ds(h, 1), :]
            for i in range(BLOCK // HEAD):
                d = dattn[chunk(i), c]
                left = col[g, chunk(i), j : j + 1]
                total = nt(d, state[chunk(j), :]) * growth[g, chunk(i), j : j + 1]
                for start, width, cut in lower_tiles(i):
                    u = slice(start, start + width)
                    table = lower_table(left, line, i, start, width, cut)
                    dscores = (nt(d, v[u, c]) * table).astype(BF16)
                    total = total + nn(dscores, k[u, c])
                query_grad[chunk(i), c] = total.astype(BF16)


def key_value_body(heads, first, q, k, v, dattn, row, col, *refs):
    hq = heads // TEAM
    dk, dv = refs[-2:]

    def one(g, _):
        for j in range(hq):
            h, c = head_at(g, hq, j)
            line = row[pl.ds(h, 1), :]
            for i in range(BLOCK // HEAD):
                left = col[g, chunk(i), j : j + 1]
                dkey = dvalue = None
                for start, width, cut in upper_tiles(i):
                    t = slice(start, start + width)
                    table = upper_table(left, line, i, start, width, cut)
                    probs = (nt(k[chunk(i), c], q[t, c]) * table).astype(BF16)
                    dscores = (nt(v[chunk(i), c], dattn[t, c]) * table).astype(BF16)
                    a = nn(dscores, q[t, c])
                    b = nn(probs, dattn[t, c])
                    dkey, dvalue = (a, b) if dkey is None else (dkey + a, dvalue + b)
                dk[chunk(i), c] = dkey
                dv[chunk(i), c] = dvalue
        return 0

    lax.fori_loop(first, first + TEAM // 2, one, 0)


def final_body(heads, k, v, dk, dv, shrink, mine, got, key_grad, value_grad, gain_grad, key_out, value_out, sems):
    hq = heads // TEAM
    w = hq * HEAD
    copies = []
    for slot, (state, g) in enumerate(by_quarter(mine, got)):
        items = read_narrow(state, hq)
        for j in range(hq):
            _, c = head_at(g, hq, j)
            fade = shrink[g, :, j : j + 1]
            after = state[chunk(j), :]
            key_out[slot, :, chunk(j)] = (dk[:, c] + nt(v[:, c], after) * fade).astype(BF16)
            value_out[slot, :, chunk(j)] = (dv[:, c] + nn(k[:, c], after) * fade).astype(BF16)
            gain_grad[:, c] = items[j][2]
        cols = pl.ds(pl.multiple_of(g * w, HEAD), w)
        for i, (src, dst) in enumerate(((key_out, key_grad), (value_out, value_grad))):
            copy = pltpu.make_async_copy(src.at[slot], dst.at[:, cols], sems.at[i, slot])
            copy.start()
            copies.append(copy)
    for copy in copies:
        copy.wait()


def in_hbm(x):
    return pltpu.with_memory_space_constraint(x, pltpu.HBM)


def swap(x, bit):
    n = lax.axis_size("ctx")
    return lax.ppermute(x, "ctx", [(i, i ^ bit) for i in range(n)])


def across(x, k):
    n = lax.axis_size("ctx")
    return lax.ppermute(x, "ctx", [(i, (i + TEAM * k) % n) for i in range(n)])


def local(queries, keys, values, log_decay, gate, gain, grad_out):
    rows, width = queries.shape
    heads = width // HEAD
    hq = heads // TEAM
    tp = lax.axis_size("tp")
    n = lax.axis_size("ctx")
    groups = n // TEAM
    channels = width * tp
    bf = lambda *shape: jax.ShapeDtypeStruct(shape, BF16)
    f32 = lambda *shape: jax.ShapeDtypeStruct(shape, F32)
    swaps = tp == 2
    part = rows // 2
    small = 2 * heads * rows * HEAD * HEAD
    large = 2 * heads * rows * rows * HEAD
    wide = f32(hq * HEAD + SIDE, HEAD)
    wide2 = f32(2, hq * HEAD + SIDE, HEAD)
    narrow = bf(hq * HEAD + EXTRA, HEAD)
    narrow2 = bf(2, hq * HEAD + EXTRA, HEAD)
    table = f32(TEAM, rows, HEAD)
    gain_row = gain.reshape(1, width)

    def beside(work, after, name):
        return [work[name](after)] if name in work else []

    def step_call(body, reverse, inputs, unread, shapes, name, *sizes):
        return call(
            functools.partial(body, reverse, hq, *sizes),
            [*inputs, *unread],
            shapes,
            name,
            in_specs=[VMEM] * len(inputs) + [ANY] * len(unread),
        )

    def scan(reverse, keep, give, held, work):
        got = swap(give, 1)
        if held is None:
            own, send = step_call(chip_total_body, True, [keep, got], [], [wide, narrow], "chip_total_back")
        else:
            own, send, held = call(
                functools.partial(chip_total_body, False, hq),
                [keep, got, held],
                [wide, narrow, jax.ShapeDtypeStruct(held.shape, held.dtype)],
                "chip_total",
                in_specs=[VMEM, VMEM, ANY],
                out_specs=[VMEM, VMEM, ANY],
                alias={2: 2},
            )
        got_pair = swap(send, 2)
        unread = beside(work, send, "pair")
        total, send = step_call(group_total_body, reverse, [own, got_pair], unread, [wide, narrow], "group_total")
        so_far, step = total, 1
        while 2 * step < groups:
            far = across(send, -step if reverse else step)
            unread = beside(work, send, "one") if step == 1 else []
            before = [] if step == 1 else [so_far]
            so_far, send = step_call(
                doubling_body, reverse, [total, *before, far], unread, [wide, narrow], "doubling", step, groups
            )
            step *= 2
        far = across(send, -step if reverse else step)
        unread = beside(work, send, "last")
        kept, send = step_call(
            into_chips_body,
            reverse,
            [own, got_pair, total, so_far, far],
            unread,
            [wide, narrow],
            "into_chips",
            step,
            groups,
        )
        other = swap(send, 2)
        unread = beside(work, send, "pair_back")
        mine, send = step_call(
            into_cores_body, reverse, [keep, got, kept, other], unread, [narrow2, narrow2], "into_cores"
        )
        return mine, swap(send, 1), held

    outs = call(
        functools.partial(local_states_body, heads, swaps),
        [in_hbm(keys), in_hbm(values), log_decay] + [in_hbm(grad_out)] * swaps,
        [wide2, wide2, f32(EXTRA, rows)] + [bf(part, width)] * 2 * swaps,
        "local_states",
        [pltpu.VMEM((TEAM, rows, hq * HEAD), BF16)] * 2
        + [pltpu.SemaphoreType.DMA((2, TEAM))]
        + [pltpu.SemaphoreType.DMA((2,))] * swaps,
        small,
        [HBM, HBM, VMEM] + [HBM] * swaps,
        [VMEM] * 3 + [HBM, VMEM] * swaps,
    )
    keep, give, row = outs[:3]
    done = {}

    def decays_beside(after):
        done["decays"] = call(
            functools.partial(decays_body, heads),
            [row, after],
            [table] * 3,
            "decays",
            in_specs=[VMEM, ANY],
        )
        return done["decays"][0]

    def intra_beside(after):
        (done["intra"],) = call(
            functools.partial(intra_body, heads),
            [queries, keys, values, row, done["decays"][0], after],
            [f32(rows, width)],
            "intra",
            flops=2 * large,
            in_specs=[VMEM] * 5 + [ANY],
        )
        return done["intra"]

    held = outs[3] if swaps else keep
    mine, got, held = scan(False, keep, give, held, {"one": decays_beside, "last": intra_beside})
    (col, growth, shrink), intra = done["decays"], done["intra"]
    if swaps:
        own = outs[4]
        arrived = lax.ppermute(held, "tp", [(0, 1), (1, 0)])
    else:
        every = lax.all_to_all(grad_out, "tp", split_axis=1, concat_axis=0, tiled=True)
        own, arrived = every[:part], every[part:]
    dscaled, turned = call(
        functools.partial(dscaled_body, heads, swaps),
        [gate, own, arrived, gain_row, queries, row],
        [f32(rows, width), bf(heads, HEAD, rows)],
        "dscaled",
        flops=small,
    )
    att, sums = call(
        functools.partial(attention_body, heads),
        [queries, intra, dscaled, growth, mine, got],
        [f32(rows, width), f32(8, rows)],
        "attention",
        [pltpu.VMEM((rows, HEAD), F32)] * 2,
        small,
    )
    if swaps:
        others = lax.ppermute(sums, "tp", [(0, 1), (1, 0)])
    else:
        others = lax.psum(sums, "tp") - sums
    dattn, scale, keep, give = call(
        functools.partial(dattn_body, heads, channels),
        [att, dscaled, turned, gain_row, row, sums, others],
        [bf(rows, width), f32(rows, HEAD), wide2, wide2],
        "dattn",
        flops=small,
    )
    def gate_beside(after):
        done["gate"], token = call(
            functools.partial(gate_body, heads),
            [gate, att, dscaled, scale, after],
            [bf(rows, width), f32(SIDE, HEAD)],
            "gate",
            flops=small,
            in_specs=[VMEM] * 4 + [ANY],
        )
        return token

    def key_value_first(after):
        done["key_value"] = call(
            functools.partial(key_value_body, heads, 0),
            [queries, keys, values, dattn, row, col, after],
            [f32(rows, width)] * 2,
            "key_value",
            flops=2 * large,
            in_specs=[VMEM] * 6 + [ANY],
        )
        return done["key_value"][0]

    def query_beside(after):
        done["query"], token = call(
            functools.partial(query_body, heads),
            [keys, values, dattn, row, col, growth, mine, got, after],
            [bf(rows, width), f32(SIDE, HEAD)],
            "query",
            flops=2 * large + small,
            in_specs=[VMEM] * 8 + [ANY],
        )
        return token

    def key_value_last(after):
        done["key_value"] = call(
            functools.partial(key_value_body, heads, TEAM // 2),
            [queries, keys, values, dattn, row, col, after, *done["key_value"]],
            [f32(rows, width)] * 2,
            "key_value",
            flops=2 * large,
            in_specs=[VMEM] * 6 + [ANY, VMEM, VMEM],
            alias={7: 0, 8: 1},
        )
        return done["key_value"][0]

    work = {"pair": gate_beside, "one": key_value_first, "last": query_beside, "pair_back": key_value_last}
    back_mine, back_got, _ = scan(True, keep, give, None, work)
    gate_grad, query_grad, (dk, dv) = done["gate"], done["query"], done["key_value"]
    key_grad, value_grad, gain_grad = call(
        functools.partial(final_body, heads),
        [keys, values, dk, dv, shrink, back_mine, back_got],
        [bf(rows, width), bf(rows, width), f32(1, width)],
        "final",
        [pltpu.VMEM((TEAM, rows, hq * HEAD), BF16)] * 2 + [pltpu.SemaphoreType.DMA((2, TEAM))],
        2 * small,
        out_specs=[HBM, HBM, VMEM],
    )
    return query_grad, key_grad, value_grad, gate_grad, gain_grad.reshape(width)


def solution(mesh):
    return jax.shard_map(
        local,
        mesh=mesh,
        in_specs=(
            P("ctx", "tp"),
            P("ctx", "tp"),
            P("ctx", "tp"),
            P("tp", "ctx"),
            P("ctx", "tp"),
            P("tp"),
            P(("ctx", "tp"), None),
        ),
        out_specs=(P("ctx", "tp"), P("ctx", "tp"), P("ctx", "tp"), P("ctx", "tp"), P("tp")),
        check_vma=False,
    )
```

```python
import functools

import jax
import jax.numpy as jnp
from jax import lax
from jax.experimental import pallas as pl
from jax.experimental.pallas import tpu as pltpu
from jax.sharding import PartitionSpec as P

HEAD = 128
BLOCK = 512
HALF = BLOCK // 2
TEAM = 4
SIDE = 8
EXTRA = 16
EPSILON = 1e-06
F32 = jnp.float32
BF16 = jnp.bfloat16
GRANT = 12 * 1024 * 1024
VMEM = pl.BlockSpec(memory_space=pltpu.VMEM)
HBM = pl.BlockSpec(memory_space=pltpu.HBM)
ANY = pl.BlockSpec(memory_space=pl.ANY)


def nt(a, b, precision=None):
    return lax.dot_general(a, b, (((1,), (1,)), ((), ())), preferred_element_type=F32, precision=precision)


def nn(a, b):
    return lax.dot_general(a, b, (((1,), (0,)), ((), ())), preferred_element_type=F32)


def half(i):
    return slice(i * HALF, (i + 1) * HALF)


def chunk(i):
    return slice(i * HEAD, (i + 1) * HEAD)


def split_terms(x, count):
    terms = []
    for _ in range(count):
        term = x.astype(BF16)
        terms.append(term)
        x = x - term.astype(F32)
    return terms


def read_wide(ref, hq):
    base = hq * HEAD
    return [
        (ref[chunk(j), :], ref[base + j : base + j + 1, :], ref[base + TEAM + j : base + TEAM + j + 1, :])
        for j in range(hq)
    ]


def write_wide(ref, hq, items):
    base = hq * HEAD
    at = lax.broadcasted_iota(jnp.int32, (SIDE, HEAD), 0)
    side = jnp.zeros((SIDE, HEAD), F32)
    for j, (term, edge, gain) in enumerate(items):
        ref[chunk(j), :] = term
        side = jnp.where(at == j, edge, side)
        side = jnp.where(at == TEAM + j, gain, side)
    ref[base : base + SIDE, :] = side


def read_narrow(ref, hq):
    base = hq * HEAD
    side = ref[base : base + EXTRA, :].astype(F32)
    row = lambda i: side[i : i + 1, :] + side[i + 1 : i + 2, :]
    return [(ref[chunk(j), :].astype(F32), row(2 * j), row(2 * TEAM + 2 * j)) for j in range(hq)]


def write_narrow(ref, hq, items):
    base = hq * HEAD
    at = lax.broadcasted_iota(jnp.int32, (EXTRA, HEAD), 0)
    side = jnp.zeros((EXTRA, HEAD), F32)
    for j, (term, edge, gain) in enumerate(items):
        ref[chunk(j), :] = term.astype(BF16)
        for first, value in ((2 * j, edge), (2 * TEAM + 2 * j, gain)):
            for i, part in enumerate(split_terms(value, 2)):
                side = jnp.where(at == first + i, part.astype(F32), side)
    ref[base : base + EXTRA, :] = side.astype(BF16)


def core():
    return lax.rem(lax.axis_index("ctx"), 2)


def pair():
    return lax.rem(lax.axis_index("ctx") // 2, 2)


def group():
    return lax.axis_index("ctx") // TEAM


def quarter_of(y, same):
    return 2 * y + (core() if same else 1 - core())


def head_at(quarter, hq, j):
    h = quarter * hq + j
    return h, pl.ds(pl.multiple_of(h * HEAD, HEAD), HEAD)


def transposed(x):
    eye = (
        lax.broadcasted_iota(jnp.int32, (HEAD, HEAD), 0) == lax.broadcasted_iota(jnp.int32, (HEAD, HEAD), 1)
    ).astype(BF16)
    return nt(eye, x)


def call(body, inputs, out_shape, name, scratch=(), flops=0, in_specs=None, out_specs=None, alias=None):
    nbytes = sum(x.size * x.dtype.itemsize for x in inputs)
    nbytes += sum(x.size * x.dtype.itemsize for x in out_shape)
    return pl.pallas_call(
        body,
        in_specs=in_specs or [VMEM] * len(inputs),
        out_specs=out_specs or [VMEM] * len(out_shape),
        out_shape=out_shape,
        scratch_shapes=list(scratch),
        input_output_aliases=alias or {},
        compiler_params=pltpu.CompilerParams(vmem_limit_bytes=GRANT),
        cost_estimate=pl.CostEstimate(flops=flops, bytes_accessed=nbytes, transcendentals=0),
        name=name,
    )(*inputs)


def joined(mine, other, mine_is_first, reverse):
    out = []
    for (a, ea, ga), (b, eb, gb) in zip(mine, other):
        near = mine_is_first if reverse else jnp.logical_not(mine_is_first)
        wa = jnp.where(near, 1.0, jnp.exp(eb))
        wb = jnp.where(near, jnp.exp(ea), 1.0)
        out.append((a * wa + b * wb, ea + eb, ga + gb))
    return out


def chip_total_body(reverse, hq, keep, got, own, send):
    first = core() == 0
    here, there = pair(), 1 - pair()
    own_items = joined(read_wide(keep.at[here], hq), read_wide(got.at[here], hq), first, reverse)
    write_wide(own, hq, own_items)
    send_items = joined(read_wide(keep.at[there], hq), read_wide(got.at[there], hq), first, reverse)
    write_narrow(send, hq, send_items)


def group_total_body(reverse, hq, own, got, *refs):
    total, send = refs[-2:]
    items = joined(read_wide(own, hq), read_narrow(got, hq), pair() == 0, reverse)
    write_wide(total, hq, items)
    write_narrow(send, hq, items)


def doubled(reverse, hq, step, groups, before, got):
    there = group() + step < groups if reverse else group() - step >= 0
    out = []
    for old, (term, edge, gain) in zip(before, read_narrow(got, hq)):
        term = jnp.where(there, term, 0.0)
        edge = jnp.where(there, edge, 0.0)
        if old is None:
            out.append((term, edge, gain))
        else:
            out.append((old[0] + jnp.exp(old[1]) * term, old[1] + edge, old[2] + gain))
    return out


def doubling_body(reverse, hq, step, groups, total, *refs):
    so_far, send = refs[-2:]
    if step == 1:
        got = refs[0]
        before = [None] * hq
    else:
        got = refs[1]
        before = read_wide(refs[0], hq)
    items = doubled(reverse, hq, step, groups, before, got)
    write_wide(so_far, hq, items)
    whole = []
    for (t, e, g), (s, es, gs) in zip(read_wide(total, hq), items):
        whole.append((t + jnp.exp(e) * s, e + es, g + gs))
    write_narrow(send, hq, whole)


def into_chips_body(reverse, hq, step, groups, own, got_pair, total, so_far, got, *refs):
    keep, send = refs[-2:]
    before = read_wide(so_far, hq) if step > 1 else [None] * hq
    entering = doubled(reverse, hq, step, groups, before, got)
    mine_near = pair() == (1 if reverse else 0)
    kept, sent = [], []
    for (r, _, gr), (c, ec, _), (o, eo, _), (_, _, gt) in zip(
        entering, read_wide(own, hq), read_narrow(got_pair, hq), read_wide(total, hq)
    ):
        gain = gr + gt
        zero = jnp.zeros_like(ec)
        kept.append((jnp.where(mine_near, r, jnp.exp(eo) * r + o), zero, gain))
        sent.append((jnp.where(mine_near, jnp.exp(ec) * r + c, r), zero, gain))
    write_wide(keep, hq, kept)
    write_narrow(send, hq, sent)


def into_cores_body(reverse, hq, keep, got, own, other, *refs):
    mine, send = refs[-2:]
    mine_near = core() == (1 if reverse else 0)
    for y in range(2):
        a, b = read_wide(own, hq), read_narrow(other, hq)
        here = pair() == y
        items_mine, items_send = [], []
        for p, q, (k, ek, _), (g, eg, _) in zip(a, b, read_wide(keep.at[y], hq), read_wide(got.at[y], hq)):
            r = jnp.where(here, p[0], q[0])
            gain = jnp.where(here, p[2], q[2])
            zero = jnp.zeros_like(ek)
            items_mine.append((jnp.where(mine_near, r, jnp.exp(eg) * r + g), zero, gain))
            items_send.append((jnp.where(mine_near, jnp.exp(ek) * r + k, r), zero, gain))
        write_narrow(mine.at[y], hq, items_mine)
        write_narrow(send.at[y], hq, items_send)


def local_states_body(heads, swaps, k_hbm, v_hbm, ld_hbm, *refs):
    hq = heads // TEAM
    w = hq * HEAD
    if swaps:
        grad, keep, give, row, k, v, away, own, ld, sems, side_sems = refs
        width = heads * HEAD
        mine = lax.axis_index("tp")
        cols = lambda t: pl.ds(pl.multiple_of(t * width, HEAD), width)
        side_copies = [
            pltpu.make_async_copy(grad.at[:, cols(1 - mine)], away, side_sems.at[1]),
            pltpu.make_async_copy(grad.at[:, cols(mine)], own, side_sems.at[2]),
        ]
    else:
        keep, give, row, k, v, ld, sems, side_sems = refs
        side_copies = []
    first = pltpu.make_async_copy(ld_hbm, ld, side_sems.at[0])
    first.start()
    order = [(give, 0, False), (give, 1, False), (keep, 0, True), (keep, 1, True)]
    copies = []
    for slot, (_, y, same) in enumerate(order):
        cols_d = pl.ds(pl.multiple_of(quarter_of(y, same) * w, HEAD), w)
        both = [
            pltpu.make_async_copy(k_hbm.at[:, cols_d], k.at[:, cols_d], sems.at[0, slot]),
            pltpu.make_async_copy(v_hbm.at[:, cols_d], v.at[:, cols_d], sems.at[1, slot]),
        ]
        for c in both:
            c.start()
        copies.append(both)
    for c in side_copies:
        c.start()
    at = lax.broadcasted_iota(jnp.int32, (BLOCK, BLOCK), 0)
    other = lax.broadcasted_iota(jnp.int32, (BLOCK, BLOCK), 1)
    tri = (at <= other).astype(BF16)
    first.wait()
    x = ld[...]
    if heads < EXTRA:
        x = jnp.concatenate([x, jnp.zeros((EXTRA - heads, BLOCK), F32)], axis=0)
    sums = nn(jnp.concatenate(split_terms(x, 3), axis=0), tri)
    row[...] = sums[0:EXTRA] + (sums[EXTRA : 2 * EXTRA] + sums[2 * EXTRA : 3 * EXTRA])
    for slot, (out, y, same) in enumerate(order):
        for c in copies[slot]:
            c.wait()
        items = []
        for j in range(hq):
            h, c = head_at(quarter_of(y, same), hq, j)
            sums = row[pl.ds(h, 1), :]
            edge = sums[:, BLOCK - 1 : BLOCK]
            kd = (transposed(k[:, c]) * jnp.exp(edge - sums)).astype(BF16)
            spread = jnp.broadcast_to(edge, (1, HEAD))
            items.append((nn(kd, v[:, c]), spread, jnp.zeros((1, HEAD), F32)))
        write_wide(out.at[y], hq, items)
    for c in side_copies:
        c.wait()


def decays_body(heads, row, q_hbm, _, col, growth, shrink, q, sem):
    hq = heads // TEAM
    copy = pltpu.make_async_copy(q_hbm, q, sem)
    copy.start()
    for g in range(TEAM):
        rows = row[g * hq : (g + 1) * hq, :]
        across = jnp.concatenate([rows, jnp.zeros((HEAD - hq, BLOCK), F32)], axis=0).T
        col[g] = across
        growth[g] = jnp.exp(across)
        shrink[g] = jnp.exp(across[BLOCK - 1 : BLOCK, :] - across)
    copy.wait()


def decay_table(high, low, lower):
    table = jnp.exp(high - low)
    at = lax.broadcasted_iota(jnp.int32, (HALF, HALF), 0)
    other = lax.broadcasted_iota(jnp.int32, (HALF, HALF), 1)
    if lower:
        cut = jnp.where(at >= other, table[:, -HALF:], 0.0)
        return cut if table.shape[1] == HALF else jnp.concatenate([table[:, :HALF], cut], axis=1)
    cut = jnp.where(at <= other, table[:, :HALF], 0.0)
    return cut if table.shape[1] == HALF else jnp.concatenate([cut, table[:, HALF:]], axis=1)


def turned_probs_body(heads, first, q, k, row, col, _, *refs):
    hq = heads // TEAM
    tables, probs = refs[-4:-2], refs[-2:]

    def one(g, _):
        for j in range(hq):
            h, c = head_at(g, hq, j)
            line = row[pl.ds(h, 1), :]
            for i in range(2):
                t = slice(i * HALF, BLOCK)
                table = decay_table(line[:, t], col[g, half(i), j : j + 1], False)
                tables[i][h] = table
                probs[i][h] = (nt(k[half(i), c], q[t, c]) * table).astype(BF16)
        return 0

    lax.fori_loop(first, first + TEAM // 2, one, 0)


def intra_body(heads, q, k, v, row, col, _, intra):
    hq = heads // TEAM

    def one(g, _):
        for j in range(hq):
            h, c = head_at(g, hq, j)
            line = row[pl.ds(h, 1), :]
            for i in range(2):
                u = slice(0, (i + 1) * HALF)
                table = decay_table(col[g, half(i), j : j + 1], line[:, u], True)
                probs = (nt(q[half(i), c], k[u, c]) * table).astype(BF16)
                intra[half(i), c] = nn(probs, v[u, c])
        return 0

    lax.fori_loop(0, TEAM, one, 0)


def dscaled_body(heads, swaps, gate, own, got, gain, q, row, _, dscaled, turned):
    hq = heads // TEAM
    part = own.shape[0]
    mine = lax.axis_index("tp") if swaps else 0

    def one(g, _):
        for j in range(hq):
            h, c = head_at(g, hq, j)
            for where, ref in ((mine, own), (1 - mine, got)):
                rows = pl.ds(pl.multiple_of(where * part, part), part)
                opened = jax.nn.sigmoid(gate[rows, c].astype(F32))
                dscaled[rows, c] = ref[:, c].astype(F32) * opened * gain[:, c]
            turned[h] = (transposed(q[:, c]) * jnp.exp(row[pl.ds(h, 1), :])).astype(BF16)
        return 0

    lax.fori_loop(0, TEAM, one, 0)


def by_quarter(mine, got):
    return [(ref.at[y], quarter_of(y, same)) for ref, same in ((mine, True), (got, False)) for y in range(2)]


def diagonal(a, b):
    zero = jnp.zeros((HEAD, HEAD), BF16)
    return jnp.concatenate(
        [jnp.concatenate([a, zero], axis=1), jnp.concatenate([zero, b], axis=1)], axis=0
    )


def attention_body(heads, q, intra, dscaled, growth, mine, got, att, sums, sq, inn, both):
    hq = heads // TEAM
    sides = by_quarter(mine, got)
    step = min(hq, 2)
    for slot, (state, g) in enumerate(sides):
        for j in range(0, hq, step):
            _, c = head_at(g, hq, j)
            if step == 2:
                c = pl.ds(pl.multiple_of((g * hq + j) * HEAD, HEAD), 2 * HEAD)
                both[...] = nn(q[:, c], diagonal(state[chunk(j), :], state[chunk(j + 1), :]))
            else:
                both[:, 0:HEAD] = nn(q[:, c], state[chunk(j), :])
            for i in range(BLOCK // HEAD):
                r = chunk(i)
                a_sq = a_in = 0.0
                for m in range(step):
                    _, c = head_at(g, hq, j + m)
                    a = intra[r, c] + both[r, chunk(m)] * growth[g, r, j + m : j + m + 1]
                    att[r, c] = a
                    a_sq = a_sq + a * a
                    a_in = a_in + a * dscaled[r, c]
                if slot == 0 and j == 0:
                    sq[r, :] = a_sq
                    inn[r, :] = a_in
                else:
                    sq[r, :] += a_sq
                    inn[r, :] += a_in
    ones = jnp.ones((8, HEAD), F32)
    a = nt(ones, sq[...], lax.Precision.HIGHEST)
    b = nt(ones, inn[...], lax.Precision.HIGHEST)
    sums[...] = jnp.where(lax.broadcasted_iota(jnp.int32, (8, BLOCK), 0) == 0, a, b)


def dattn_body(heads, channels, att, dscaled, turned, gain, row, sum_a, sum_b, dattn, scale, keep, give, rsb, coefb):
    hq = heads // TEAM
    total = sum_a[...] + sum_b[...]
    rs = lax.rsqrt(total[0:1, :] / channels + EPSILON)
    coef = total[1:2, :] * (rs * rs * rs) / channels
    down = jnp.concatenate([rs, coef, jnp.zeros((HEAD - 2, BLOCK), F32)], axis=0).T
    rsb[...] = jnp.broadcast_to(down[:, 0:1], (BLOCK, HEAD))
    coefb[...] = jnp.broadcast_to(down[:, 1:2], (BLOCK, HEAD))
    scale[...] = rsb[...]
    for out, y, same in ((give, 0, False), (give, 1, False), (keep, 0, True), (keep, 1, True)):
        items = []
        for j in range(hq):
            h, c = head_at(quarter_of(y, same), hq, j)
            gsum = jnp.zeros((8, HEAD), F32)
            for i in range(BLOCK // HEAD):
                r = chunk(i)
                a = att[r, c]
                t = dscaled[r, c] * rsb[r, :]
                dattn[r, c] = (t - a * coefb[r, :]).astype(BF16)
                gsum = gsum + jnp.sum((t * a).reshape(HEAD // 8, 8, HEAD), axis=0)
            edge = jnp.broadcast_to(row[pl.ds(h, 1), :][:, BLOCK - 1 : BLOCK], (1, HEAD))
            part = jnp.sum(gsum, axis=0, keepdims=True) / gain[:, c]
            items.append((nn(turned[h], dattn[:, c]), edge, part))
        write_wide(out.at[y], hq, items)


def leave(out, ref, sems, g, w):
    cols = pl.ds(pl.multiple_of(g * w, HEAD), w)
    copy = pltpu.make_async_copy(out, ref.at[:, cols], sems)
    copy.start()
    return copy


def gate_body(heads, gate, att, dscaled, scale, _, gate_grad, token, out, sems):
    hq = heads // TEAM
    token[...] = jnp.zeros_like(token)
    copies = []
    for g in range(TEAM):
        for j in range(hq):
            _, c = head_at(g, hq, j)
            opened = jax.nn.sigmoid(gate[:, c].astype(F32))
            out[g, :, chunk(j)] = (dscaled[:, c] * att[:, c] * scale[...] * (1.0 - opened)).astype(BF16)
        copies.append(leave(out.at[g], gate_grad, sems.at[g], g, hq * HEAD))
    for copy in copies:
        copy.wait()


def query_body(heads, k, v, dattn, row, col, growth, mine, got, _, query_grad, token, out, sems):
    hq = heads // TEAM
    token[...] = jnp.zeros_like(token)
    copies = []
    for slot, (state, g) in enumerate(by_quarter(mine, got)):
        for j in range(hq):
            h, c = head_at(g, hq, j)
            line = row[pl.ds(h, 1), :]
            for i in range(2):
                d = dattn[half(i), c]
                u = slice(0, (i + 1) * HALF)
                table = decay_table(col[g, half(i), j : j + 1], line[:, u], True)
                dscores = (nt(d, v[u, c]) * table).astype(BF16)
                inter = nt(d, state[chunk(j), :]) * growth[g, half(i), j : j + 1]
                out[slot, half(i), chunk(j)] = (inter + nn(dscores, k[u, c])).astype(BF16)
        copies.append(leave(out.at[slot], query_grad, sems.at[slot], g, hq * HEAD))
    for copy in copies:
        copy.wait()


def key_value_body(heads, first, q, v, dattn, table0, table1, probs0, probs1, _, *refs):
    hq = heads // TEAM
    dk, dv = refs[-2:]

    def one(g, _):
        for j in range(hq):
            h, c = head_at(g, hq, j)
            for i, (table, probs) in enumerate(((table0, probs0), (table1, probs1))):
                t = slice(i * HALF, BLOCK)
                dscores = (nt(v[half(i), c], dattn[t, c]) * table[h]).astype(BF16)
                dk[half(i), c] = nn(dscores, q[t, c])
                dv[half(i), c] = nn(probs[h], dattn[t, c])
        return 0

    lax.fori_loop(first, first + TEAM // 2, one, 0)


def final_body(heads, k, v, dk, dv, shrink, mine, got, key_grad, value_grad, gain_grad, key_out, value_out, sems):
    hq = heads // TEAM
    w = hq * HEAD
    copies = []
    for slot, (state, g) in enumerate(by_quarter(mine, got)):
        items = read_narrow(state, hq)
        for j in range(hq):
            _, c = head_at(g, hq, j)
            fade = shrink[g, :, j : j + 1]
            after = state[chunk(j), :]
            side = jnp.concatenate([k[:, c], v[:, c]], axis=1)
            back = items[j][0].T.astype(BF16)
            both = nn(side, diagonal(after, back))
            key_out[slot, :, chunk(j)] = (dk[:, c] + both[:, HEAD:] * fade).astype(BF16)
            value_out[slot, :, chunk(j)] = (dv[:, c] + both[:, :HEAD] * fade).astype(BF16)
            gain_grad[:, c] = items[j][2]
        copies.append(leave(key_out.at[slot], key_grad, sems.at[0, slot], g, w))
        copies.append(leave(value_out.at[slot], value_grad, sems.at[1, slot], g, w))
    for copy in copies:
        copy.wait()


def in_hbm(x):
    return pltpu.with_memory_space_constraint(x, pltpu.HBM)


def swap(x, bit):
    n = lax.axis_size("ctx")
    return lax.ppermute(x, "ctx", [(i, i ^ bit) for i in range(n)])


def across(x, k):
    n = lax.axis_size("ctx")
    return lax.ppermute(x, "ctx", [(i, (i + TEAM * k) % n) for i in range(n)])


def local(queries, keys, values, log_decay, gate, gain, grad_out):
    rows, width = queries.shape
    heads = width // HEAD
    hq = heads // TEAM
    tp = lax.axis_size("tp")
    n = lax.axis_size("ctx")
    groups = n // TEAM
    channels = width * tp
    bf = lambda *shape: jax.ShapeDtypeStruct(shape, BF16)
    f32 = lambda *shape: jax.ShapeDtypeStruct(shape, F32)
    swaps = tp == 2
    part = rows // 2
    small = 2 * heads * rows * HEAD * HEAD
    large = 2 * heads * rows * rows * HEAD
    wide = f32(hq * HEAD + SIDE, HEAD)
    wide2 = f32(2, hq * HEAD + SIDE, HEAD)
    narrow = bf(hq * HEAD + EXTRA, HEAD)
    narrow2 = bf(2, hq * HEAD + EXTRA, HEAD)
    table = f32(TEAM, rows, HEAD)
    gain_row = gain.reshape(1, width)

    def beside(work, after, name):
        return [work[name](after)] if name in work else []

    def step_call(body, reverse, inputs, unread, shapes, name, *sizes):
        return call(
            functools.partial(body, reverse, hq, *sizes),
            [*inputs, *unread],
            shapes,
            name,
            in_specs=[VMEM] * len(inputs) + [ANY] * len(unread),
        )

    def scan(reverse, keep, give, work):
        got = swap(give, 1)
        own, send = step_call(chip_total_body, reverse, [keep, got], [], [wide, narrow], "chip_total")
        got_pair = swap(send, 2)
        unread = beside(work, send, "pair")
        total, send = step_call(group_total_body, reverse, [own, got_pair], unread, [wide, narrow], "group_total")
        so_far, step = total, 1
        while 2 * step < groups:
            far = across(send, -step if reverse else step)
            unread = beside(work, send, "one") if step == 1 else []
            before = [] if step == 1 else [so_far]
            so_far, send = step_call(
                doubling_body, reverse, [total, *before, far], unread, [wide, narrow], "doubling", step, groups
            )
            step *= 2
        far = across(send, -step if reverse else step)
        unread = beside(work, send, "last")
        kept, send = step_call(
            into_chips_body,
            reverse,
            [own, got_pair, total, so_far, far],
            unread,
            [wide, narrow],
            "into_chips",
            step,
            groups,
        )
        other = swap(send, 2)
        unread = beside(work, send, "pair_back")
        mine, send = step_call(
            into_cores_body, reverse, [keep, got, kept, other], unread, [narrow2, narrow2], "into_cores"
        )
        return mine, swap(send, 1)

    outs = call(
        functools.partial(local_states_body, heads, swaps),
        [in_hbm(keys), in_hbm(values), in_hbm(log_decay)] + [in_hbm(grad_out)] * swaps,
        [wide2, wide2, f32(EXTRA, rows), bf(rows, width), bf(rows, width)] + [bf(part, width)] * 2 * swaps,
        "local_states",
        [
            pltpu.VMEM(log_decay.shape, F32),
            pltpu.SemaphoreType.DMA((2, TEAM)),
            pltpu.SemaphoreType.DMA((3,)),
        ],
        small,
        [HBM] * (3 + swaps),
        [VMEM] * 5 + [HBM, VMEM] * swaps,
    )
    keep, give, row, keys, values = outs[:5]
    if swaps:
        own = outs[6]
        arrived = lax.ppermute(outs[5], "tp", [(0, 1), (1, 0)])
    else:
        every = lax.all_to_all(grad_out, "tp", split_axis=1, concat_axis=0, tiled=True)
        own, arrived = every[:part], every[part:]
    done = {}

    def probs_beside(after):
        if "decays" not in done:
            *done["decays"], done["queries"] = call(
                functools.partial(decays_body, heads),
                [row, in_hbm(queries), after],
                [table] * 3 + [bf(rows, width)],
                "decays",
                [pltpu.SemaphoreType.DMA(())],
                in_specs=[VMEM, HBM, ANY],
            )
        before = done.get("probs", [])
        done["probs"] = call(
            functools.partial(turned_probs_body, heads, TEAM // 2 if before else 0),
            [done["queries"], keys, row, done["decays"][0], after, *before],
            [f32(heads, HALF, BLOCK), f32(heads, HALF, HALF), bf(heads, HALF, BLOCK), bf(heads, HALF, HALF)],
            "turned_probs",
            flops=large // 2,
            in_specs=[VMEM] * 4 + [ANY] + [VMEM] * len(before),
            alias={5 + i: i for i in range(len(before))},
        )
        return done["probs"][3]

    def intra_beside(after):
        (done["intra"],) = call(
            functools.partial(intra_body, heads),
            [done["queries"], keys, values, row, done["decays"][0], after],
            [f32(rows, width)],
            "intra",
            flops=2 * large,
            in_specs=[VMEM] * 5 + [ANY],
        )
        return done["intra"]

    def dscaled_beside(after):
        done["dscaled"] = call(
            functools.partial(dscaled_body, heads, swaps),
            [gate, own, arrived, gain_row, done["queries"], row, after],
            [f32(rows, width), bf(heads, HEAD, rows)],
            "dscaled",
            flops=small,
            in_specs=[VMEM] * 6 + [ANY],
        )
        return done["dscaled"][0]

    work = {"pair": probs_beside, "one": probs_beside, "last": intra_beside, "pair_back": dscaled_beside}
    mine, got = scan(False, keep, give, work)
    queries = done["queries"]
    (col, growth, shrink), intra, (dscaled, turned) = done["decays"], done["intra"], done["dscaled"]
    att, sums = call(
        functools.partial(attention_body, heads),
        [queries, intra, dscaled, growth, mine, got],
        [f32(rows, width), f32(8, rows)],
        "attention",
        [pltpu.VMEM((rows, HEAD), F32)] * 2 + [pltpu.VMEM((rows, 2 * HEAD), F32)],
        small,
    )
    if swaps:
        others = lax.ppermute(sums, "tp", [(0, 1), (1, 0)])
    else:
        others = lax.psum(sums, "tp") - sums
    dattn, scale, keep, give = call(
        functools.partial(dattn_body, heads, channels),
        [att, dscaled, turned, gain_row, row, sums, others],
        [bf(rows, width), f32(rows, HEAD), wide2, wide2],
        "dattn",
        [pltpu.VMEM((rows, HEAD), F32)] * 2,
        small,
    )
    out_scratch = [pltpu.VMEM((TEAM, rows, hq * HEAD), BF16), pltpu.SemaphoreType.DMA((TEAM,))]

    def gate_beside(after):
        done["gate"], token = call(
            functools.partial(gate_body, heads),
            [gate, att, dscaled, scale, after],
            [bf(rows, width), f32(SIDE, HEAD)],
            "gate",
            out_scratch,
            small,
            [VMEM] * 4 + [ANY],
            [HBM, VMEM],
        )
        return token

    def key_value_first(after):
        done["key_value"] = call(
            functools.partial(key_value_body, heads, 0),
            [queries, values, dattn, *done["probs"], after],
            [f32(rows, width)] * 2,
            "key_value",
            flops=2 * large,
            in_specs=[VMEM] * 7 + [ANY],
        )
        return done["key_value"][0]

    def query_beside(after):
        done["query"], token = call(
            functools.partial(query_body, heads),
            [keys, values, dattn, row, col, growth, mine, got, after],
            [bf(rows, width), f32(SIDE, HEAD)],
            "query",
            out_scratch,
            2 * large + small,
            [VMEM] * 8 + [ANY],
            [HBM, VMEM],
        )
        return token

    def key_value_last(after):
        done["key_value"] = call(
            functools.partial(key_value_body, heads, TEAM // 2),
            [queries, values, dattn, *done["probs"], after, *done["key_value"]],
            [f32(rows, width)] * 2,
            "key_value",
            flops=2 * large,
            in_specs=[VMEM] * 7 + [ANY, VMEM, VMEM],
            alias={8: 0, 9: 1},
        )
        return done["key_value"][0]

    work = {"pair": gate_beside, "one": key_value_first, "last": query_beside, "pair_back": key_value_last}
    back_mine, back_got = scan(True, keep, give, work)
    gate_grad, query_grad, (dk, dv) = done["gate"], done["query"], done["key_value"]
    key_grad, value_grad, gain_grad = call(
        functools.partial(final_body, heads),
        [keys, values, dk, dv, shrink, back_mine, back_got],
        [bf(rows, width), bf(rows, width), f32(1, width)],
        "final",
        [pltpu.VMEM((TEAM, rows, hq * HEAD), BF16)] * 2 + [pltpu.SemaphoreType.DMA((2, TEAM))],
        2 * small,
        out_specs=[HBM, HBM, VMEM],
    )
    return query_grad, key_grad, value_grad, gate_grad, gain_grad.reshape(width)


def solution(mesh):
    return jax.shard_map(
        local,
        mesh=mesh,
        in_specs=(
            P("ctx", "tp"),
            P("ctx", "tp"),
            P("ctx", "tp"),
            P("tp", "ctx"),
            P("ctx", "tp"),
            P("tp"),
            P(("ctx", "tp"), None),
        ),
        out_specs=(P("ctx", "tp"), P("ctx", "tp"), P("ctx", "tp"), P("ctx", "tp"), P("tp")),
        check_vma=False,
    )
```

```python
import functools

import jax
import jax.numpy as jnp
from jax import lax
from jax.experimental import pallas as pl
from jax.experimental.pallas import tpu as pltpu
from jax.sharding import PartitionSpec as P

HEAD = 128
BLOCK = 512
HALF = BLOCK // 2
TEAM = 4
SIDE = 8
EXTRA = 16
EPSILON = 1e-06
F32 = jnp.float32
BF16 = jnp.bfloat16
GRANT = 6 * 1024 * 1024
VMEM = pl.BlockSpec(memory_space=pltpu.VMEM)
HBM = pl.BlockSpec(memory_space=pltpu.HBM)
ANY = pl.BlockSpec(memory_space=pl.ANY)


def nt(a, b, precision=None):
    return lax.dot_general(a, b, (((1,), (1,)), ((), ())), preferred_element_type=F32, precision=precision)


def nn(a, b):
    return lax.dot_general(a, b, (((1,), (0,)), ((), ())), preferred_element_type=F32)


def half(i):
    return slice(i * HALF, (i + 1) * HALF)


def chunk(i):
    return slice(i * HEAD, (i + 1) * HEAD)


def split_terms(x, count):
    terms = []
    for _ in range(count):
        term = x.astype(BF16)
        terms.append(term)
        x = x - term.astype(F32)
    return terms


def read_wide(ref, hq):
    base = hq * HEAD
    return [
        (ref[chunk(j), :], ref[base + j : base + j + 1, :], ref[base + TEAM + j : base + TEAM + j + 1, :])
        for j in range(hq)
    ]


def write_wide(ref, hq, items):
    base = hq * HEAD
    at = lax.broadcasted_iota(jnp.int32, (SIDE, HEAD), 0)
    side = jnp.zeros((SIDE, HEAD), F32)
    for j, (term, edge, gain) in enumerate(items):
        ref[chunk(j), :] = term
        side = jnp.where(at == j, edge, side)
        side = jnp.where(at == TEAM + j, gain, side)
    ref[base : base + SIDE, :] = side


def read_narrow(ref, hq):
    base = hq * HEAD
    side = ref[base : base + EXTRA, :].astype(F32)
    row = lambda i: side[i : i + 1, :] + side[i + 1 : i + 2, :]
    return [(ref[chunk(j), :].astype(F32), row(2 * j), row(2 * TEAM + 2 * j)) for j in range(hq)]


def write_narrow(ref, hq, items):
    base = hq * HEAD
    at = lax.broadcasted_iota(jnp.int32, (EXTRA, HEAD), 0)
    side = jnp.zeros((EXTRA, HEAD), F32)
    for j, (term, edge, gain) in enumerate(items):
        ref[chunk(j), :] = term.astype(BF16)
        for first, value in ((2 * j, edge), (2 * TEAM + 2 * j, gain)):
            for i, part in enumerate(split_terms(value, 2)):
                side = jnp.where(at == first + i, part.astype(F32), side)
    ref[base : base + EXTRA, :] = side.astype(BF16)


def core():
    return lax.rem(lax.axis_index("ctx"), 2)


def pair():
    return lax.rem(lax.axis_index("ctx") // 2, 2)


def group():
    return lax.axis_index("ctx") // TEAM


def quarter_of(y, same):
    return 2 * y + (core() if same else 1 - core())


def head_at(quarter, hq, j):
    h = quarter * hq + j
    return h, pl.ds(pl.multiple_of(h * HEAD, HEAD), HEAD)


def transposed(x):
    shape = (x.shape[1], x.shape[1])
    eye = (lax.broadcasted_iota(jnp.int32, shape, 0) == lax.broadcasted_iota(jnp.int32, shape, 1)).astype(BF16)
    return nt(eye, x)


def several(quarter, hq):
    count = min(hq, 2)
    for j in range(0, hq, count):
        h = quarter * hq + j
        yield j, h, count, pl.ds(pl.multiple_of(h * HEAD, HEAD), count * HEAD)


def call(body, inputs, out_shape, name, scratch=(), flops=0, in_specs=None, out_specs=None, alias=None):
    nbytes = sum(x.size * x.dtype.itemsize for x in inputs)
    nbytes += sum(x.size * x.dtype.itemsize for x in out_shape)
    return pl.pallas_call(
        body,
        in_specs=in_specs or [VMEM] * len(inputs),
        out_specs=out_specs or [VMEM] * len(out_shape),
        out_shape=out_shape,
        scratch_shapes=list(scratch),
        input_output_aliases=alias or {},
        compiler_params=pltpu.CompilerParams(vmem_limit_bytes=GRANT),
        cost_estimate=pl.CostEstimate(flops=flops, bytes_accessed=nbytes, transcendentals=0),
        name=name,
    )(*inputs)


def joined(mine, other, mine_is_first, reverse):
    out = []
    for (a, ea, ga), (b, eb, gb) in zip(mine, other):
        near = mine_is_first if reverse else jnp.logical_not(mine_is_first)
        wa = jnp.where(near, 1.0, jnp.exp(eb))
        wb = jnp.where(near, jnp.exp(ea), 1.0)
        out.append((a * wa + b * wb, ea + eb, ga + gb))
    return out


def chip_total_body(reverse, hq, keep, got, own, send):
    first = core() == 0
    here, there = pair(), 1 - pair()
    own_items = joined(read_wide(keep.at[here], hq), read_wide(got.at[here], hq), first, reverse)
    write_wide(own, hq, own_items)
    send_items = joined(read_wide(keep.at[there], hq), read_wide(got.at[there], hq), first, reverse)
    write_narrow(send, hq, send_items)


def group_total_body(reverse, hq, own, got, *refs):
    total, send = refs[-2:]
    items = joined(read_wide(own, hq), read_narrow(got, hq), pair() == 0, reverse)
    write_wide(total, hq, items)
    write_narrow(send, hq, items)


def doubled(reverse, hq, step, groups, before, got):
    there = group() + step < groups if reverse else group() - step >= 0
    out = []
    for old, (term, edge, gain) in zip(before, read_narrow(got, hq)):
        term = jnp.where(there, term, 0.0)
        edge = jnp.where(there, edge, 0.0)
        if old is None:
            out.append((term, edge, gain))
        else:
            out.append((old[0] + jnp.exp(old[1]) * term, old[1] + edge, old[2] + gain))
    return out


def doubling_body(reverse, hq, step, groups, total, *refs):
    so_far, send = refs[-2:]
    if step == 1:
        got = refs[0]
        before = [None] * hq
    else:
        got = refs[1]
        before = read_wide(refs[0], hq)
    items = doubled(reverse, hq, step, groups, before, got)
    write_wide(so_far, hq, items)
    whole = []
    for (t, e, g), (s, es, gs) in zip(read_wide(total, hq), items):
        whole.append((t + jnp.exp(e) * s, e + es, g + gs))
    write_narrow(send, hq, whole)


def into_chips_body(reverse, hq, step, groups, own, got_pair, total, so_far, got, *refs):
    keep, send = refs[-2:]
    before = read_wide(so_far, hq) if step > 1 else [None] * hq
    entering = doubled(reverse, hq, step, groups, before, got)
    mine_near = pair() == (1 if reverse else 0)
    kept, sent = [], []
    for (r, _, gr), (c, ec, _), (o, eo, _), (_, _, gt) in zip(
        entering, read_wide(own, hq), read_narrow(got_pair, hq), read_wide(total, hq)
    ):
        gain = gr + gt
        zero = jnp.zeros_like(ec)
        kept.append((jnp.where(mine_near, r, jnp.exp(eo) * r + o), zero, gain))
        sent.append((jnp.where(mine_near, jnp.exp(ec) * r + c, r), zero, gain))
    write_wide(keep, hq, kept)
    write_narrow(send, hq, sent)


def into_cores_body(reverse, hq, keep, got, own, other, *refs):
    mine, send = refs[-2:]
    mine_near = core() == (1 if reverse else 0)
    for y in range(2):
        a, b = read_wide(own, hq), read_narrow(other, hq)
        here = pair() == y
        items_mine, items_send = [], []
        for p, q, (k, ek, _), (g, eg, _) in zip(a, b, read_wide(keep.at[y], hq), read_wide(got.at[y], hq)):
            r = jnp.where(here, p[0], q[0])
            gain = jnp.where(here, p[2], q[2])
            zero = jnp.zeros_like(ek)
            items_mine.append((jnp.where(mine_near, r, jnp.exp(eg) * r + g), zero, gain))
            items_send.append((jnp.where(mine_near, jnp.exp(ek) * r + k, r), zero, gain))
        write_narrow(mine.at[y], hq, items_mine)
        write_narrow(send.at[y], hq, items_send)


def block_states(hq, y, same, k, v, row, out):
    items = []
    for j, h, count, c in several(quarter_of(y, same), hq):
        turned = transposed(k[:, c])
        lines = [row[pl.ds(h + m, 1), :] for m in range(count)]
        edges = [line[:, BLOCK - 1 : BLOCK] for line in lines]
        faded = [turned[chunk(m)] * jnp.exp(edges[m] - lines[m]) for m in range(count)]
        both = nn(jnp.concatenate([x.astype(BF16) for x in faded], axis=0), v[:, c])
        for m in range(count):
            items.append((both[chunk(m), chunk(m)], jnp.broadcast_to(edges[m], (1, HEAD)), jnp.zeros((1, HEAD), F32)))
    write_wide(out.at[y], hq, items)


def sent_states_body(heads, swaps, k_hbm, v_hbm, ld_hbm, *refs):
    hq = heads // TEAM
    w = hq * HEAD
    if swaps:
        grad, give, row, k, v, away, ld, sems, side_sems = refs
        width = heads * HEAD
        there = pl.ds(pl.multiple_of((1 - lax.axis_index("tp")) * width, HEAD), width)
        side_copies = [pltpu.make_async_copy(grad.at[:, there], away, side_sems.at[1])]
    else:
        give, row, k, v, ld, sems, side_sems = refs
        side_copies = []
    first = pltpu.make_async_copy(ld_hbm, ld, side_sems.at[0])
    first.start()
    order = [(0, False), (1, False), (0, True), (1, True)]
    copies = []
    for slot, (y, same) in enumerate(order):
        cols_d = pl.ds(pl.multiple_of(quarter_of(y, same) * w, HEAD), w)
        both = [
            pltpu.make_async_copy(k_hbm.at[:, cols_d], k.at[:, cols_d], sems.at[0, slot]),
            pltpu.make_async_copy(v_hbm.at[:, cols_d], v.at[:, cols_d], sems.at[1, slot]),
        ]
        for c in both:
            c.start()
        copies.append(both)
    for c in side_copies:
        c.start()
    at = lax.broadcasted_iota(jnp.int32, (BLOCK, BLOCK), 0)
    other = lax.broadcasted_iota(jnp.int32, (BLOCK, BLOCK), 1)
    tri = (at <= other).astype(BF16)
    first.wait()
    x = ld[...]
    if heads < EXTRA:
        x = jnp.concatenate([x, jnp.zeros((EXTRA - heads, BLOCK), F32)], axis=0)
    sums = nn(jnp.concatenate(split_terms(x, 3), axis=0), tri)
    row[...] = sums[0:EXTRA] + (sums[EXTRA : 2 * EXTRA] + sums[2 * EXTRA : 3 * EXTRA])
    for slot, (y, same) in enumerate(order):
        for c in copies[slot]:
            c.wait()
        if not same:
            block_states(hq, y, same, k, v, row, give)
    for c in side_copies:
        c.wait()


def kept_states_body(heads, k, v, row, keep):
    for y in range(2):
        block_states(heads // TEAM, y, True, k, v, row, keep)


def decays_body(heads, row, q_hbm, _, col, growth, shrink, q, sem):
    hq = heads // TEAM
    copy = pltpu.make_async_copy(q_hbm, q, sem)
    copy.start()
    for g in range(TEAM):
        rows = row[g * hq : (g + 1) * hq, :]
        across = jnp.concatenate([rows, jnp.zeros((HEAD - hq, BLOCK), F32)], axis=0).T
        col[g] = across
        growth[g] = jnp.exp(across)
        shrink[g] = jnp.exp(across[BLOCK - 1 : BLOCK, :] - across)
    copy.wait()


def decay_table(high, low, lower):
    table = jnp.exp(high - low)
    at = lax.broadcasted_iota(jnp.int32, (HALF, HALF), 0)
    other = lax.broadcasted_iota(jnp.int32, (HALF, HALF), 1)
    if lower:
        cut = jnp.where(at >= other, table[:, -HALF:], 0.0)
        return cut if table.shape[1] == HALF else jnp.concatenate([table[:, :HALF], cut], axis=1)
    cut = jnp.where(at <= other, table[:, :HALF], 0.0)
    return cut if table.shape[1] == HALF else jnp.concatenate([cut, table[:, HALF:]], axis=1)


def turned_probs_body(heads, first, q, k, row, col, _, *refs):
    hq = heads // TEAM
    tables, probs = refs[-4:-2], refs[-2:]

    def one(g, _):
        for j in range(hq):
            h, c = head_at(g, hq, j)
            line = row[pl.ds(h, 1), :]
            for i in range(2):
                t = slice(i * HALF, BLOCK)
                table = decay_table(line[:, t], col[g, half(i), j : j + 1], False)
                tables[i][h] = table
                probs[i][h] = (nt(k[half(i), c], q[t, c]) * table).astype(BF16)
        return 0

    lax.fori_loop(first, first + TEAM // 2, one, 0)


def intra_body(heads, q, k, v, row, col, _, intra):
    hq = heads // TEAM

    def one(g, _):
        for j in range(hq):
            h, c = head_at(g, hq, j)
            line = row[pl.ds(h, 1), :]
            for i in range(2):
                u = slice(0, (i + 1) * HALF)
                table = decay_table(col[g, half(i), j : j + 1], line[:, u], True)
                probs = (nt(q[half(i), c], k[u, c]) * table).astype(BF16)
                intra[half(i), c] = nn(probs, v[u, c])
        return 0

    lax.fori_loop(0, TEAM, one, 0)


def dscaled_rows(heads, where, gate, ref, gain, dscaled):
    part = ref.shape[0]
    rows = pl.ds(pl.multiple_of(where * part, part), part)

    def one(g, _):
        for j in range(heads // TEAM):
            _, c = head_at(g, heads // TEAM, j)
            opened = jax.nn.sigmoid(gate[rows, c].astype(F32))
            dscaled[rows, c] = ref[:, c].astype(F32) * opened * gain[:, c]
        return 0

    lax.fori_loop(0, TEAM, one, 0)


def own_dscaled_body(heads, swaps, gate, grad, gain, q, row, _, dscaled, turned, own, sem):
    width = heads * HEAD
    mine = lax.axis_index("tp") if swaps else 0
    here = pl.ds(pl.multiple_of(mine * width, HEAD), width)
    copy = pltpu.make_async_copy(grad.at[:, here], own, sem)
    copy.start()

    def one(g, _):
        for j, h, count, c in several(g, heads // TEAM):
            both = transposed(q[:, c])
            for m in range(count):
                rows = pl.ds(pl.multiple_of((h + m) * HEAD, HEAD), HEAD)
                turned[rows, :] = (both[chunk(m)] * jnp.exp(row[pl.ds(h + m, 1), :])).astype(BF16)
        return 0

    lax.fori_loop(0, TEAM, one, 0)
    copy.wait()
    dscaled_rows(heads, mine, gate, own, gain, dscaled)


def got_dscaled_body(heads, swaps, gate, got, gain, _, dscaled):
    dscaled_rows(heads, 1 - lax.axis_index("tp") if swaps else 1, gate, got, gain, dscaled)


def diagonal(a, b):
    zero = jnp.zeros((HEAD, HEAD), BF16)
    return jnp.concatenate(
        [jnp.concatenate([a, zero], axis=1), jnp.concatenate([zero, b], axis=1)], axis=0
    )


def attention_body(heads, same, q, intra, dscaled, growth, state, *refs):
    hq = heads // TEAM
    if same:
        att, sq, inn, both = refs
    else:
        _, sq_before, inn_before, att, sums, sq, inn, both = refs
        sq[...] = sq_before[...]
        inn[...] = inn_before[...]
    for y in range(2):
        g = quarter_of(y, same)
        for j, h, count, c in several(g, hq):
            if count == 2:
                both[...] = nn(q[:, c], diagonal(state[y, chunk(j), :], state[y, chunk(j + 1), :]))
            else:
                both[:, 0:HEAD] = nn(q[:, c], state[y, chunk(j), :])
            for i in range(BLOCK // HEAD):
                r = chunk(i)
                a_sq = a_in = 0.0
                for m in range(count):
                    _, c = head_at(g, hq, j + m)
                    a = intra[r, c] + both[r, chunk(m)] * growth[g, r, j + m : j + m + 1]
                    att[r, c] = a
                    a_sq = a_sq + a * a
                    a_in = a_in + a * dscaled[r, c]
                if same and y == 0 and j == 0:
                    sq[r, :] = a_sq
                    inn[r, :] = a_in
                else:
                    sq[r, :] += a_sq
                    inn[r, :] += a_in
    if not same:
        ones = jnp.ones((8, HEAD), F32)
        a = nt(ones, sq[...], lax.Precision.HIGHEST)
        b = nt(ones, inn[...], lax.Precision.HIGHEST)
        sums[...] = jnp.where(lax.broadcasted_iota(jnp.int32, (8, BLOCK), 0) == 0, a, b)


def dattn_body(heads, channels, same, att, dscaled, turned, gain, row, *refs):
    hq = heads // TEAM
    if same:
        rsb, coefb, _, dattn, out = refs
    else:
        sum_a, sum_b, dattn, out, rsb, coefb = refs
        total = sum_a[...] + sum_b[...]
        rs = lax.rsqrt(total[0:1, :] / channels + EPSILON)
        coef = total[1:2, :] * (rs * rs * rs) / channels
        down = jnp.concatenate([rs, coef, jnp.zeros((HEAD - 2, BLOCK), F32)], axis=0).T
        rsb[...] = jnp.broadcast_to(down[:, 0:1], (BLOCK, HEAD))
        coefb[...] = jnp.broadcast_to(down[:, 1:2], (BLOCK, HEAD))
    for y in range(2):
        items = []
        for j, h, count, cols in several(quarter_of(y, same), hq):
            parts = []
            for m in range(count):
                _, c = head_at(quarter_of(y, same), hq, j + m)
                gsum = jnp.zeros((8, HEAD), F32)
                for i in range(BLOCK // HEAD):
                    r = chunk(i)
                    a = att[r, c]
                    t = dscaled[r, c] * rsb[r, :]
                    dattn[r, c] = (t - a * coefb[r, :]).astype(BF16)
                    gsum = gsum + jnp.sum((t * a).reshape(HEAD // 8, 8, HEAD), axis=0)
                parts.append(jnp.sum(gsum, axis=0, keepdims=True) / gain[:, c])
            both = nn(turned[pl.ds(pl.multiple_of(h * HEAD, HEAD), count * HEAD), :], dattn[:, cols])
            for m in range(count):
                edge = jnp.broadcast_to(row[pl.ds(h + m, 1), :][:, BLOCK - 1 : BLOCK], (1, HEAD))
                items.append((both[chunk(m), chunk(m)], edge, parts[m]))
        write_wide(out.at[y], hq, items)


def leave(out, ref, sems, g, w):
    cols = pl.ds(pl.multiple_of(g * w, HEAD), w)
    copy = pltpu.make_async_copy(out, ref.at[:, cols], sems)
    copy.start()
    return copy


def gate_body(heads, gate, att, dscaled, scale, _, gate_grad, token, out, sems):
    hq = heads // TEAM
    token[...] = jnp.zeros_like(token)
    copies = []
    for g in range(TEAM):
        for j in range(hq):
            _, c = head_at(g, hq, j)
            opened = jax.nn.sigmoid(gate[:, c].astype(F32))
            out[g, :, chunk(j)] = (dscaled[:, c] * att[:, c] * scale[...] * (1.0 - opened)).astype(BF16)
        copies.append(leave(out.at[g], gate_grad, sems.at[g], g, hq * HEAD))
    for copy in copies:
        copy.wait()


def by_quarter(mine, got):
    return [(ref.at[y], quarter_of(y, same)) for ref, same in ((mine, True), (got, False)) for y in range(2)]


def query_body(heads, k, v, dattn, row, col, growth, mine, got, _, query_grad, token, out, sems):
    hq = heads // TEAM
    token[...] = jnp.zeros_like(token)
    copies = []
    for slot, (state, g) in enumerate(by_quarter(mine, got)):
        for j in range(hq):
            h, c = head_at(g, hq, j)
            line = row[pl.ds(h, 1), :]
            for i in range(2):
                d = dattn[half(i), c]
                u = slice(0, (i + 1) * HALF)
                table = decay_table(col[g, half(i), j : j + 1], line[:, u], True)
                dscores = (nt(d, v[u, c]) * table).astype(BF16)
                inter = nt(d, state[chunk(j), :]) * growth[g, half(i), j : j + 1]
                out[slot, half(i), chunk(j)] = (inter + nn(dscores, k[u, c])).astype(BF16)
        copies.append(leave(out.at[slot], query_grad, sems.at[slot], g, hq * HEAD))
    for copy in copies:
        copy.wait()


def key_value_body(heads, first, q, v, dattn, table0, table1, probs0, probs1, _, *refs):
    hq = heads // TEAM
    dk, dv = refs[-2:]

    def one(g, _):
        for j in range(hq):
            h, c = head_at(g, hq, j)
            for i, (table, probs) in enumerate(((table0, probs0), (table1, probs1))):
                t = slice(i * HALF, BLOCK)
                dscores = (nt(v[half(i), c], dattn[t, c]) * table[h]).astype(BF16)
                dk[half(i), c] = nn(dscores, q[t, c])
                dv[half(i), c] = nn(probs[h], dattn[t, c])
        return 0

    lax.fori_loop(first, first + TEAM // 2, one, 0)


def final_body(heads, same, k, v, dk, dv, shrink, state, *refs):
    hq = heads // TEAM
    w = hq * HEAD
    key_grad, value_grad, gain_grad, key_out, value_out, sems = refs[-6:]
    if not same:
        gain_grad[...] = refs[2][...]
    copies = []
    for y in range(2):
        g = quarter_of(y, same)
        items = read_narrow(state.at[y], hq)
        for j in range(hq):
            _, c = head_at(g, hq, j)
            fade = shrink[g, :, j : j + 1]
            after = state[y, chunk(j), :]
            key_out[y, :, chunk(j)] = (dk[:, c] + nt(v[:, c], after) * fade).astype(BF16)
            value_out[y, :, chunk(j)] = (dv[:, c] + nn(k[:, c], after) * fade).astype(BF16)
            gain_grad[:, c] = items[j][2]
        copies.append(leave(key_out.at[y], key_grad, sems.at[0, y], g, w))
        copies.append(leave(value_out.at[y], value_grad, sems.at[1, y], g, w))
    for copy in copies:
        copy.wait()


def in_hbm(x):
    return pltpu.with_memory_space_constraint(x, pltpu.HBM)


def swap(x, bit):
    n = lax.axis_size("ctx")
    return lax.ppermute(x, "ctx", [(i, i ^ bit) for i in range(n)])


def across(x, k):
    n = lax.axis_size("ctx")
    return lax.ppermute(x, "ctx", [(i, (i + TEAM * k) % n) for i in range(n)])


def local(queries, keys, values, log_decay, gate, gain, grad_out):
    rows, width = queries.shape
    heads = width // HEAD
    hq = heads // TEAM
    tp = lax.axis_size("tp")
    n = lax.axis_size("ctx")
    groups = n // TEAM
    channels = width * tp
    bf = lambda *shape: jax.ShapeDtypeStruct(shape, BF16)
    f32 = lambda *shape: jax.ShapeDtypeStruct(shape, F32)
    swaps = tp == 2
    part = rows // 2
    small = 2 * heads * rows * HEAD * HEAD
    large = 2 * heads * rows * rows * HEAD
    wide = f32(hq * HEAD + SIDE, HEAD)
    wide2 = f32(2, hq * HEAD + SIDE, HEAD)
    narrow = bf(hq * HEAD + EXTRA, HEAD)
    narrow2 = bf(2, hq * HEAD + EXTRA, HEAD)
    table = f32(TEAM, rows, HEAD)
    gain_row = gain.reshape(1, width)

    def beside(work, after, name):
        return [work[name](after)] if name in work else []

    def step_call(body, reverse, inputs, unread, shapes, name, *sizes):
        return call(
            functools.partial(body, reverse, hq, *sizes),
            [*inputs, *unread],
            shapes,
            name,
            in_specs=[VMEM] * len(inputs) + [ANY] * len(unread),
        )

    def scan(reverse, keep, give, work):
        got = swap(give, 1)
        own, send = step_call(chip_total_body, reverse, [keep, got], [], [wide, narrow], "chip_total")
        got_pair = swap(send, 2)
        unread = beside(work, send, "pair")
        total, send = step_call(group_total_body, reverse, [own, got_pair], unread, [wide, narrow], "group_total")
        so_far, step = total, 1
        while 2 * step < groups:
            far = across(send, -step if reverse else step)
            unread = beside(work, send, "one") if step == 1 else []
            before = [] if step == 1 else [so_far]
            so_far, send = step_call(
                doubling_body, reverse, [total, *before, far], unread, [wide, narrow], "doubling", step, groups
            )
            step *= 2
        far = across(send, -step if reverse else step)
        unread = beside(work, send, "last")
        kept, send = step_call(
            into_chips_body,
            reverse,
            [own, got_pair, total, so_far, far],
            unread,
            [wide, narrow],
            "into_chips",
            step,
            groups,
        )
        other = swap(send, 2)
        unread = beside(work, send, "pair_back")
        mine, send = step_call(
            into_cores_body, reverse, [keep, got, kept, other], unread, [narrow2, narrow2], "into_cores"
        )
        return mine, swap(send, 1)

    outs = call(
        functools.partial(sent_states_body, heads, swaps),
        [in_hbm(keys), in_hbm(values), in_hbm(log_decay)] + [in_hbm(grad_out)] * swaps,
        [wide2, f32(EXTRA, rows), bf(rows, width), bf(rows, width)] + [bf(part, width)] * swaps,
        "sent_states",
        [
            pltpu.VMEM(log_decay.shape, F32),
            pltpu.SemaphoreType.DMA((2, TEAM)),
            pltpu.SemaphoreType.DMA((2,)),
        ],
        small // 2,
        [HBM] * (3 + swaps),
        [VMEM] * 4 + [HBM] * swaps,
    )
    give, row, keys, values = outs[:4]
    if swaps:
        arrived = lax.ppermute(outs[4], "tp", [(0, 1), (1, 0)])
        own = grad_out
    else:
        every = lax.all_to_all(grad_out, "tp", split_axis=1, concat_axis=0, tiled=True)
        own, arrived = every[:part], every[part:]
    (keep,) = call(
        functools.partial(kept_states_body, heads), [keys, values, row], [wide2], "kept_states", flops=small // 2
    )
    done = {}

    def probs_beside(after):
        if "decays" not in done:
            *done["decays"], done["queries"] = call(
                functools.partial(decays_body, heads),
                [row, in_hbm(queries), after],
                [table] * 3 + [bf(rows, width)],
                "decays",
                [pltpu.SemaphoreType.DMA(())],
                in_specs=[VMEM, HBM, ANY],
            )
        before = done.get("probs", [])
        done["probs"] = call(
            functools.partial(turned_probs_body, heads, TEAM // 2 if before else 0),
            [done["queries"], keys, row, done["decays"][0], after, *before],
            [f32(heads, HALF, BLOCK), f32(heads, HALF, HALF), bf(heads, HALF, BLOCK), bf(heads, HALF, HALF)],
            "turned_probs",
            flops=large // 2,
            in_specs=[VMEM] * 4 + [ANY] + [VMEM] * len(before),
            alias={5 + i: i for i in range(len(before))},
        )
        return done["probs"][3]

    def intra_beside(after):
        (done["intra"],) = call(
            functools.partial(intra_body, heads),
            [done["queries"], keys, values, row, done["decays"][0], after],
            [f32(rows, width)],
            "intra",
            flops=2 * large,
            in_specs=[VMEM] * 5 + [ANY],
        )
        return done["intra"]

    def dscaled_beside(after):
        done["dscaled"] = call(
            functools.partial(own_dscaled_body, heads, swaps),
            [gate, in_hbm(own), gain_row, done["queries"], row, after],
            [f32(rows, width), bf(width, rows)],
            "own_dscaled",
            [pltpu.VMEM((part, width), BF16), pltpu.SemaphoreType.DMA(())],
            small,
            [VMEM, HBM, VMEM, VMEM, VMEM, ANY],
        )
        return done["dscaled"][1]

    work = {"pair": probs_beside, "one": probs_beside, "last": intra_beside, "pair_back": dscaled_beside}
    mine, got = scan(False, keep, give, work)
    queries = done["queries"]
    (col, growth, shrink), intra, (dscaled, turned) = done["decays"], done["intra"], done["dscaled"]
    (dscaled,) = call(
        functools.partial(got_dscaled_body, heads, swaps),
        [gate, arrived, gain_row, dscaled],
        [f32(rows, width)],
        "got_dscaled",
        alias={3: 0},
    )
    tall = f32(rows, HEAD)
    wide_scratch = pltpu.VMEM((rows, 2 * HEAD), F32)
    att, squares, inner = call(
        functools.partial(attention_body, heads, True),
        [queries, intra, dscaled, growth, mine],
        [f32(rows, width), tall, tall],
        "attention",
        [wide_scratch],
        small // 2,
    )
    att, sums = call(
        functools.partial(attention_body, heads, False),
        [queries, intra, dscaled, growth, got, att, squares, inner],
        [f32(rows, width), f32(8, rows)],
        "attention",
        [pltpu.VMEM((rows, HEAD), F32)] * 2 + [wide_scratch],
        small // 2,
        alias={5: 0},
    )
    if swaps:
        others = lax.ppermute(sums, "tp", [(0, 1), (1, 0)])
    else:
        others = lax.psum(sums, "tp") - sums
    dattn, give, scale, coef = call(
        functools.partial(dattn_body, heads, channels, False),
        [att, dscaled, turned, gain_row, row, sums, others],
        [bf(rows, width), wide2, tall, tall],
        "sent_dattn",
        flops=small // 2,
    )
    dattn, keep = call(
        functools.partial(dattn_body, heads, channels, True),
        [att, dscaled, turned, gain_row, row, scale, coef, dattn],
        [bf(rows, width), wide2],
        "kept_dattn",
        flops=small // 2,
        alias={7: 0},
    )
    out_scratch = [pltpu.VMEM((TEAM, rows, hq * HEAD), BF16), pltpu.SemaphoreType.DMA((TEAM,))]

    def gate_beside(after):
        done["gate"], token = call(
            functools.partial(gate_body, heads),
            [gate, att, dscaled, scale, after],
            [bf(rows, width), f32(SIDE, HEAD)],
            "gate",
            out_scratch,
            small,
            [VMEM] * 4 + [ANY],
            [HBM, VMEM],
        )
        return token

    def key_value_first(after):
        done["key_value"] = call(
            functools.partial(key_value_body, heads, 0),
            [queries, values, dattn, *done["probs"], after],
            [f32(rows, width)] * 2,
            "key_value",
            flops=2 * large,
            in_specs=[VMEM] * 7 + [ANY],
        )
        return done["key_value"][0]

    def query_beside(after):
        done["query"], token = call(
            functools.partial(query_body, heads),
            [keys, values, dattn, row, col, growth, mine, got, after],
            [bf(rows, width), f32(SIDE, HEAD)],
            "query",
            out_scratch,
            2 * large + small,
            [VMEM] * 8 + [ANY],
            [HBM, VMEM],
        )
        return token

    def key_value_last(after):
        done["key_value"] = call(
            functools.partial(key_value_body, heads, TEAM // 2),
            [queries, values, dattn, *done["probs"], after, *done["key_value"]],
            [f32(rows, width)] * 2,
            "key_value",
            flops=2 * large,
            in_specs=[VMEM] * 7 + [ANY, VMEM, VMEM],
            alias={8: 0, 9: 1},
        )
        return done["key_value"][0]

    work = {"pair": gate_beside, "one": key_value_first, "last": query_beside, "pair_back": key_value_last}
    back_mine, back_got = scan(True, keep, give, work)
    gate_grad, query_grad, (dk, dv) = done["gate"], done["query"], done["key_value"]
    final = lambda same, state, *before: call(
        functools.partial(final_body, heads, same),
        [keys, values, dk, dv, shrink, state, *before],
        [bf(rows, width), bf(rows, width), f32(1, width)],
        "final",
        [pltpu.VMEM((2, rows, hq * HEAD), BF16)] * 2 + [pltpu.SemaphoreType.DMA((2, 2))],
        small,
        [VMEM] * 6 + [HBM, HBM, VMEM][: len(before)],
        [HBM, HBM, VMEM],
        {6 + i: i for i in range(len(before))},
    )
    key_grad, value_grad, gain_grad = final(False, back_got, *final(True, back_mine))
    return query_grad, key_grad, value_grad, gate_grad, gain_grad.reshape(width)


def solution(mesh):
    return jax.shard_map(
        local,
        mesh=mesh,
        in_specs=(
            P("ctx", "tp"),
            P("ctx", "tp"),
            P("ctx", "tp"),
            P("tp", "ctx"),
            P("ctx", "tp"),
            P("tp"),
            P(("ctx", "tp"), None),
        ),
        out_specs=(P("ctx", "tp"), P("ctx", "tp"), P("ctx", "tp"), P("ctx", "tp"), P("tp")),
        check_vma=False,
    )
```

```python
import functools

import jax
import jax.numpy as jnp
from jax import lax
from jax.experimental import pallas as pl
from jax.experimental.pallas import tpu as pltpu
from jax.sharding import PartitionSpec as P

HEAD = 128
BLOCK = 512
HALF = BLOCK // 2
TEAM = 4
SIDE = 8
EXTRA = 16
EPSILON = 1e-06
F32 = jnp.float32
BF16 = jnp.bfloat16
GRANT = 6 * 1024 * 1024
VMEM = pl.BlockSpec(memory_space=pltpu.VMEM)
HBM = pl.BlockSpec(memory_space=pltpu.HBM)
ANY = pl.BlockSpec(memory_space=pl.ANY)


def nt(a, b, precision=None):
    return lax.dot_general(a, b, (((1,), (1,)), ((), ())), preferred_element_type=F32, precision=precision)


def nn(a, b):
    return lax.dot_general(a, b, (((1,), (0,)), ((), ())), preferred_element_type=F32)


def half(i):
    return slice(i * HALF, (i + 1) * HALF)


def chunk(i):
    return slice(i * HEAD, (i + 1) * HEAD)


def split_terms(x, count):
    terms = []
    for _ in range(count):
        term = x.astype(BF16)
        terms.append(term)
        x = x - term.astype(F32)
    return terms


def read_wide(ref, hq):
    base = hq * HEAD
    return [
        (ref[chunk(j), :], ref[base + j : base + j + 1, :], ref[base + TEAM + j : base + TEAM + j + 1, :])
        for j in range(hq)
    ]


def write_wide(ref, hq, items):
    base = hq * HEAD
    at = lax.broadcasted_iota(jnp.int32, (SIDE, HEAD), 0)
    side = jnp.zeros((SIDE, HEAD), F32)
    for j, (term, edge, gain) in enumerate(items):
        ref[chunk(j), :] = term
        side = jnp.where(at == j, edge, side)
        side = jnp.where(at == TEAM + j, gain, side)
    ref[base : base + SIDE, :] = side


def read_narrow(ref, hq):
    base = hq * HEAD
    side = ref[base : base + EXTRA, :].astype(F32)
    row = lambda i: side[i : i + 1, :] + side[i + 1 : i + 2, :]
    return [(ref[chunk(j), :].astype(F32), row(2 * j), row(2 * TEAM + 2 * j)) for j in range(hq)]


def write_narrow(ref, hq, items):
    base = hq * HEAD
    at = lax.broadcasted_iota(jnp.int32, (EXTRA, HEAD), 0)
    side = jnp.zeros((EXTRA, HEAD), F32)
    for j, (term, edge, gain) in enumerate(items):
        ref[chunk(j), :] = term.astype(BF16)
        for first, value in ((2 * j, edge), (2 * TEAM + 2 * j, gain)):
            for i, part in enumerate(split_terms(value, 2)):
                side = jnp.where(at == first + i, part.astype(F32), side)
    ref[base : base + EXTRA, :] = side.astype(BF16)


def core():
    return lax.rem(lax.axis_index("ctx"), 2)


def pair():
    return lax.rem(lax.axis_index("ctx") // 2, 2)


def group():
    return lax.axis_index("ctx") // TEAM


def quarter_of(y, same):
    return 2 * y + (core() if same else 1 - core())


def head_at(quarter, hq, j):
    h = quarter * hq + j
    return h, pl.ds(pl.multiple_of(h * HEAD, HEAD), HEAD)


def transposed(x):
    shape = (x.shape[1], x.shape[1])
    eye = (lax.broadcasted_iota(jnp.int32, shape, 0) == lax.broadcasted_iota(jnp.int32, shape, 1)).astype(BF16)
    return nt(eye, x)


def several(quarter, hq):
    count = min(hq, 2)
    for j in range(0, hq, count):
        h = quarter * hq + j
        yield j, h, count, pl.ds(pl.multiple_of(h * HEAD, HEAD), count * HEAD)


def call(body, inputs, out_shape, name, scratch=(), flops=0, in_specs=None, out_specs=None, alias=None):
    nbytes = sum(x.size * x.dtype.itemsize for x in inputs)
    nbytes += sum(x.size * x.dtype.itemsize for x in out_shape)
    return pl.pallas_call(
        body,
        in_specs=in_specs or [VMEM] * len(inputs),
        out_specs=out_specs or [VMEM] * len(out_shape),
        out_shape=out_shape,
        scratch_shapes=list(scratch),
        input_output_aliases=alias or {},
        compiler_params=pltpu.CompilerParams(vmem_limit_bytes=GRANT),
        cost_estimate=pl.CostEstimate(flops=flops, bytes_accessed=nbytes, transcendentals=0),
        name=name,
    )(*inputs)


def joined(mine, other, mine_is_first, reverse):
    out = []
    for (a, ea, ga), (b, eb, gb) in zip(mine, other):
        near = mine_is_first if reverse else jnp.logical_not(mine_is_first)
        wa = jnp.where(near, 1.0, jnp.exp(eb))
        wb = jnp.where(near, jnp.exp(ea), 1.0)
        out.append((a * wa + b * wb, ea + eb, ga + gb))
    return out


def chip_total_body(reverse, hq, keep, got, own, send):
    first = core() == 0
    here, there = pair(), 1 - pair()
    own_items = joined(read_wide(keep.at[here], hq), read_wide(got.at[here], hq), first, reverse)
    write_wide(own, hq, own_items)
    send_items = joined(read_wide(keep.at[there], hq), read_wide(got.at[there], hq), first, reverse)
    write_narrow(send, hq, send_items)


def group_total_body(reverse, hq, own, got, *refs):
    total, send = refs[-2:]
    items = joined(read_wide(own, hq), read_narrow(got, hq), pair() == 0, reverse)
    write_wide(total, hq, items)
    write_narrow(send, hq, items)


def doubled(reverse, hq, step, groups, before, got):
    there = group() + step < groups if reverse else group() - step >= 0
    out = []
    for old, (term, edge, gain) in zip(before, read_narrow(got, hq)):
        term = jnp.where(there, term, 0.0)
        edge = jnp.where(there, edge, 0.0)
        if old is None:
            out.append((term, edge, gain))
        else:
            out.append((old[0] + jnp.exp(old[1]) * term, old[1] + edge, old[2] + gain))
    return out


def doubling_body(reverse, hq, step, groups, total, *refs):
    so_far, send = refs[-2:]
    if step == 1:
        got = refs[0]
        before = [None] * hq
    else:
        got = refs[1]
        before = read_wide(refs[0], hq)
    items = doubled(reverse, hq, step, groups, before, got)
    write_wide(so_far, hq, items)
    whole = []
    for (t, e, g), (s, es, gs) in zip(read_wide(total, hq), items):
        whole.append((t + jnp.exp(e) * s, e + es, g + gs))
    write_narrow(send, hq, whole)


def into_chips_body(reverse, hq, step, groups, own, got_pair, total, so_far, got, *refs):
    keep, send = refs[-2:]
    before = read_wide(so_far, hq) if step > 1 else [None] * hq
    entering = doubled(reverse, hq, step, groups, before, got)
    mine_near = pair() == (1 if reverse else 0)
    kept, sent = [], []
    for (r, _, gr), (c, ec, _), (o, eo, _), (_, _, gt) in zip(
        entering, read_wide(own, hq), read_narrow(got_pair, hq), read_wide(total, hq)
    ):
        gain = gr + gt
        zero = jnp.zeros_like(ec)
        kept.append((jnp.where(mine_near, r, jnp.exp(eo) * r + o), zero, gain))
        sent.append((jnp.where(mine_near, jnp.exp(ec) * r + c, r), zero, gain))
    write_wide(keep, hq, kept)
    write_narrow(send, hq, sent)


def into_cores_body(reverse, hq, keep, got, own, other, *refs):
    mine, send = refs[-2:]
    mine_near = core() == (1 if reverse else 0)
    for y in range(2):
        a, b = read_wide(own, hq), read_narrow(other, hq)
        here = pair() == y
        items_mine, items_send = [], []
        for p, q, (k, ek, _), (g, eg, _) in zip(a, b, read_wide(keep.at[y], hq), read_wide(got.at[y], hq)):
            r = jnp.where(here, p[0], q[0])
            gain = jnp.where(here, p[2], q[2])
            zero = jnp.zeros_like(ek)
            items_mine.append((jnp.where(mine_near, r, jnp.exp(eg) * r + g), zero, gain))
            items_send.append((jnp.where(mine_near, jnp.exp(ek) * r + k, r), zero, gain))
        write_narrow(mine.at[y], hq, items_mine)
        write_narrow(send.at[y], hq, items_send)


def block_states(hq, y, same, k, v, row, out):
    items = []
    for j, h, count, c in several(quarter_of(y, same), hq):
        turned = transposed(k[:, c])
        lines = [row[pl.ds(h + m, 1), :] for m in range(count)]
        edges = [line[:, BLOCK - 1 : BLOCK] for line in lines]
        faded = [turned[chunk(m)] * jnp.exp(edges[m] - lines[m]) for m in range(count)]
        both = nn(jnp.concatenate([x.astype(BF16) for x in faded], axis=0), v[:, c])
        for m in range(count):
            items.append((both[chunk(m), chunk(m)], jnp.broadcast_to(edges[m], (1, HEAD)), jnp.zeros((1, HEAD), F32)))
    write_wide(out.at[y], hq, items)


def sent_states_body(heads, swaps, k_hbm, v_hbm, ld_hbm, *refs):
    hq = heads // TEAM
    w = hq * HEAD
    if swaps:
        grad, give, row, k, v, away, ld, sems, side_sems = refs
        width = heads * HEAD
        there = pl.ds(pl.multiple_of((1 - lax.axis_index("tp")) * width, HEAD), width)
        side_copies = [pltpu.make_async_copy(grad.at[:, there], away, side_sems.at[1])]
    else:
        give, row, k, v, ld, sems, side_sems = refs
        side_copies = []
    first = pltpu.make_async_copy(ld_hbm, ld, side_sems.at[0])
    first.start()
    order = [(0, False), (1, False), (0, True), (1, True)]
    copies = []
    for slot, (y, same) in enumerate(order):
        cols_d = pl.ds(pl.multiple_of(quarter_of(y, same) * w, HEAD), w)
        both = [
            pltpu.make_async_copy(k_hbm.at[:, cols_d], k.at[:, cols_d], sems.at[0, slot]),
            pltpu.make_async_copy(v_hbm.at[:, cols_d], v.at[:, cols_d], sems.at[1, slot]),
        ]
        for c in both:
            c.start()
        copies.append(both)
    for c in side_copies:
        c.start()
    at = lax.broadcasted_iota(jnp.int32, (BLOCK, BLOCK), 0)
    other = lax.broadcasted_iota(jnp.int32, (BLOCK, BLOCK), 1)
    tri = (at <= other).astype(BF16)
    first.wait()
    x = ld[...]
    if heads < EXTRA:
        x = jnp.concatenate([x, jnp.zeros((EXTRA - heads, BLOCK), F32)], axis=0)
    sums = nn(jnp.concatenate(split_terms(x, 3), axis=0), tri)
    row[...] = sums[0:EXTRA] + (sums[EXTRA : 2 * EXTRA] + sums[2 * EXTRA : 3 * EXTRA])
    for slot, (y, same) in enumerate(order):
        for c in copies[slot]:
            c.wait()
        if not same:
            block_states(hq, y, same, k, v, row, give)
    for c in side_copies:
        c.wait()


def kept_states_body(heads, k, v, row, keep):
    for y in range(2):
        block_states(heads // TEAM, y, True, k, v, row, keep)


def decays_body(heads, row, q_hbm, _, col, growth, shrink, q, sem):
    hq = heads // TEAM
    copy = pltpu.make_async_copy(q_hbm, q, sem)
    copy.start()
    for g in range(TEAM):
        rows = row[g * hq : (g + 1) * hq, :]
        across = jnp.concatenate([rows, jnp.zeros((HEAD - hq, BLOCK), F32)], axis=0).T
        col[g] = across
        growth[g] = jnp.exp(across)
        shrink[g] = jnp.exp(across[BLOCK - 1 : BLOCK, :] - across)
    copy.wait()


def decay_table(high, low, lower):
    table = jnp.exp(high - low)
    at = lax.broadcasted_iota(jnp.int32, (HALF, HALF), 0)
    other = lax.broadcasted_iota(jnp.int32, (HALF, HALF), 1)
    if lower:
        cut = jnp.where(at >= other, table[:, -HALF:], 0.0)
        return cut if table.shape[1] == HALF else jnp.concatenate([table[:, :HALF], cut], axis=1)
    cut = jnp.where(at <= other, table[:, :HALF], 0.0)
    return cut if table.shape[1] == HALF else jnp.concatenate([cut, table[:, HALF:]], axis=1)


def turned_probs_body(heads, first, q, k, row, col, _, *refs):
    hq = heads // TEAM
    tables, probs = refs[-4:-2], refs[-2:]

    def one(g, _):
        for j in range(hq):
            h, c = head_at(g, hq, j)
            line = row[pl.ds(h, 1), :]
            for i in range(2):
                t = slice(i * HALF, BLOCK)
                table = decay_table(line[:, t], col[g, half(i), j : j + 1], False)
                tables[i][h] = table
                probs[i][h] = (nt(k[half(i), c], q[t, c]) * table).astype(BF16)
        return 0

    lax.fori_loop(first, first + TEAM // 2, one, 0)


def intra_body(heads, q, k, v, row, col, _, intra):
    hq = heads // TEAM

    def one(g, _):
        for j in range(hq):
            h, c = head_at(g, hq, j)
            line = row[pl.ds(h, 1), :]
            for i in range(2):
                u = slice(0, (i + 1) * HALF)
                table = decay_table(col[g, half(i), j : j + 1], line[:, u], True)
                probs = (nt(q[half(i), c], k[u, c]) * table).astype(BF16)
                intra[half(i), c] = nn(probs, v[u, c])
        return 0

    lax.fori_loop(0, TEAM, one, 0)


def dscaled_rows(heads, where, gate, ref, gain, dscaled):
    part = ref.shape[0]
    rows = pl.ds(pl.multiple_of(where * part, part), part)

    def one(g, _):
        for j in range(heads // TEAM):
            _, c = head_at(g, heads // TEAM, j)
            opened = jax.nn.sigmoid(gate[rows, c].astype(F32))
            dscaled[rows, c] = ref[:, c].astype(F32) * opened * gain[:, c]
        return 0

    lax.fori_loop(0, TEAM, one, 0)


def own_dscaled_body(heads, swaps, gate, grad, gain, q, row, _, dscaled, turned, own, sem):
    width = heads * HEAD
    mine = lax.axis_index("tp") if swaps else 0
    here = pl.ds(pl.multiple_of(mine * width, HEAD), width)
    copy = pltpu.make_async_copy(grad.at[:, here], own, sem)
    copy.start()

    def one(g, _):
        for j, h, count, c in several(g, heads // TEAM):
            both = transposed(q[:, c])
            for m in range(count):
                rows = pl.ds(pl.multiple_of((h + m) * HEAD, HEAD), HEAD)
                turned[rows, :] = (both[chunk(m)] * jnp.exp(row[pl.ds(h + m, 1), :])).astype(BF16)
        return 0

    lax.fori_loop(0, TEAM, one, 0)
    copy.wait()
    dscaled_rows(heads, mine, gate, own, gain, dscaled)


def got_dscaled_body(heads, swaps, gate, got, gain, _, dscaled):
    dscaled_rows(heads, 1 - lax.axis_index("tp") if swaps else 1, gate, got, gain, dscaled)


def diagonal(a, b):
    zero = jnp.zeros((HEAD, HEAD), BF16)
    return jnp.concatenate(
        [jnp.concatenate([a, zero], axis=1), jnp.concatenate([zero, b], axis=1)], axis=0
    )


def attention_body(heads, same, q, intra, dscaled, growth, state, *refs):
    hq = heads // TEAM
    if same:
        att, sq, inn, both = refs
    else:
        sq_before, inn_before, att, sums, sq, inn, both = refs
        sq[...] = sq_before[...]
        inn[...] = inn_before[...]
    for y in range(2):
        g = quarter_of(y, same)
        for j, h, count, c in several(g, hq):
            if count == 2:
                both[...] = nn(q[:, c], diagonal(state[y, chunk(j), :], state[y, chunk(j + 1), :]))
            else:
                both[:, 0:HEAD] = nn(q[:, c], state[y, chunk(j), :])
            for i in range(BLOCK // HEAD):
                r = chunk(i)
                a_sq = a_in = 0.0
                for m in range(count):
                    _, c = head_at(g, hq, j + m)
                    a = intra[r, c] + both[r, chunk(m)] * growth[g, r, j + m : j + m + 1]
                    att[r, c] = a
                    a_sq = a_sq + a * a
                    a_in = a_in + a * dscaled[r, c]
                if same and y == 0 and j == 0:
                    sq[r, :] = a_sq
                    inn[r, :] = a_in
                else:
                    sq[r, :] += a_sq
                    inn[r, :] += a_in
    if not same:
        ones = jnp.ones((8, HEAD), F32)
        a = nt(ones, sq[...], lax.Precision.HIGHEST)
        b = nt(ones, inn[...], lax.Precision.HIGHEST)
        sums[...] = jnp.where(lax.broadcasted_iota(jnp.int32, (8, BLOCK), 0) == 0, a, b)


def dattn_body(heads, channels, same, att, dscaled, turned, gain, row, *refs):
    hq = heads // TEAM
    if same:
        rsb, coefb, _, dattn, out = refs
    else:
        sum_a, sum_b, dattn, out, rsb, coefb = refs
        total = sum_a[...] + sum_b[...]
        rs = lax.rsqrt(total[0:1, :] / channels + EPSILON)
        coef = total[1:2, :] * (rs * rs * rs) / channels
        down = jnp.concatenate([rs, coef, jnp.zeros((HEAD - 2, BLOCK), F32)], axis=0).T
        rsb[...] = jnp.broadcast_to(down[:, 0:1], (BLOCK, HEAD))
        coefb[...] = jnp.broadcast_to(down[:, 1:2], (BLOCK, HEAD))
    for y in range(2):
        items = []
        for j, h, count, cols in several(quarter_of(y, same), hq):
            parts = []
            for m in range(count):
                _, c = head_at(quarter_of(y, same), hq, j + m)
                gsum = jnp.zeros((8, HEAD), F32)
                for i in range(BLOCK // HEAD):
                    r = chunk(i)
                    a = att[r, c]
                    t = dscaled[r, c] * rsb[r, :]
                    dattn[r, c] = (t - a * coefb[r, :]).astype(BF16)
                    gsum = gsum + jnp.sum((t * a).reshape(HEAD // 8, 8, HEAD), axis=0)
                parts.append(jnp.sum(gsum, axis=0, keepdims=True) / gain[:, c])
            both = nn(turned[pl.ds(pl.multiple_of(h * HEAD, HEAD), count * HEAD), :], dattn[:, cols])
            for m in range(count):
                edge = jnp.broadcast_to(row[pl.ds(h + m, 1), :][:, BLOCK - 1 : BLOCK], (1, HEAD))
                items.append((both[chunk(m), chunk(m)], edge, parts[m]))
        write_wide(out.at[y], hq, items)


def leave(out, ref, sems, g, w):
    cols = pl.ds(pl.multiple_of(g * w, HEAD), w)
    copy = pltpu.make_async_copy(out, ref.at[:, cols], sems)
    copy.start()
    return copy


def gate_body(heads, gate, att, dscaled, scale, _, gate_grad, token, out, sems):
    hq = heads // TEAM
    token[...] = jnp.zeros_like(token)
    copies = []
    for g in range(TEAM):
        for j in range(hq):
            _, c = head_at(g, hq, j)
            opened = jax.nn.sigmoid(gate[:, c].astype(F32))
            out[g, :, chunk(j)] = (dscaled[:, c] * att[:, c] * scale[...] * (1.0 - opened)).astype(BF16)
        copies.append(leave(out.at[g], gate_grad, sems.at[g], g, hq * HEAD))
    for copy in copies:
        copy.wait()


def by_quarter(mine, got):
    return [(ref.at[y], quarter_of(y, same)) for ref, same in ((mine, True), (got, False)) for y in range(2)]


def query_body(heads, k, v, dattn, row, col, growth, mine, got, _, query_grad, token, out, sems):
    hq = heads // TEAM
    token[...] = jnp.zeros_like(token)
    copies = []
    for slot, (state, g) in enumerate(by_quarter(mine, got)):
        for j in range(hq):
            h, c = head_at(g, hq, j)
            line = row[pl.ds(h, 1), :]
            for i in range(2):
                d = dattn[half(i), c]
                u = slice(0, (i + 1) * HALF)
                table = decay_table(col[g, half(i), j : j + 1], line[:, u], True)
                dscores = (nt(d, v[u, c]) * table).astype(BF16)
                inter = nt(d, state[chunk(j), :]) * growth[g, half(i), j : j + 1]
                out[slot, half(i), chunk(j)] = (inter + nn(dscores, k[u, c])).astype(BF16)
        copies.append(leave(out.at[slot], query_grad, sems.at[slot], g, hq * HEAD))
    for copy in copies:
        copy.wait()


def key_value_body(heads, first, q, v, dattn, table0, table1, probs0, probs1, _, *refs):
    hq = heads // TEAM
    dk, dv = refs[-2:]

    def one(g, _):
        for j in range(hq):
            h, c = head_at(g, hq, j)
            for i, (table, probs) in enumerate(((table0, probs0), (table1, probs1))):
                t = slice(i * HALF, BLOCK)
                dscores = (nt(v[half(i), c], dattn[t, c]) * table[h]).astype(BF16)
                dk[half(i), c] = nn(dscores, q[t, c])
                dv[half(i), c] = nn(probs[h], dattn[t, c])
        return 0

    lax.fori_loop(first, first + TEAM // 2, one, 0)


def final_rows(hq, y, j, same, k, v, dk, dv, shrink, state, key_out, value_out):
    g = quarter_of(y, same)
    _, c = head_at(g, hq, j)
    fade = shrink[g, :, j : j + 1]
    after = state[y, chunk(j), :]
    key_out[y, :, chunk(j)] = (dk[:, c] + nt(v[:, c], after) * fade).astype(BF16)
    value_out[y, :, chunk(j)] = (dv[:, c] + nn(k[:, c], after) * fade).astype(BF16)


def own_final_body(heads, k, v, dk, dv, shrink, state, key_out, value_out, gain_grad):
    hq = heads // TEAM
    for y in range(2):
        items = read_narrow(state.at[y], hq)
        for j in range(hq):
            final_rows(hq, y, j, True, k, v, dk, dv, shrink, state, key_out, value_out)
            gain_grad[:, head_at(quarter_of(y, True), hq, j)[1]] = items[j][2]


def final_body(heads, k, v, dk, dv, shrink, state, own_key, own_value, own_gain, *refs):
    hq = heads // TEAM
    key_grad, value_grad, gain_grad, key_out, value_out, sems = refs
    copies = []

    def send(src, dst, cols):
        copy = pltpu.make_async_copy(src, dst.at[:, cols], sems.at[len(copies)])
        copy.start()
        copies.append(copy)

    for y in range(2):
        for j, _, count, c in several(quarter_of(y, True), hq):
            place = slice(j * HEAD, (j + count) * HEAD)
            send(own_key.at[y, :, place], key_grad, c)
            send(own_value.at[y, :, place], value_grad, c)
    gain_grad[...] = own_gain[...]
    for y in range(2):
        items = read_narrow(state.at[y], hq)
        for j, _, count, c in several(quarter_of(y, False), hq):
            for m in range(j, j + count):
                final_rows(hq, y, m, False, k, v, dk, dv, shrink, state, key_out, value_out)
                gain_grad[:, head_at(quarter_of(y, False), hq, m)[1]] = items[m][2]
            place = slice(j * HEAD, (j + count) * HEAD)
            send(key_out.at[y, :, place], key_grad, c)
            send(value_out.at[y, :, place], value_grad, c)
    for copy in copies:
        copy.wait()


def in_hbm(x):
    return pltpu.with_memory_space_constraint(x, pltpu.HBM)


def swap(x, bit):
    n = lax.axis_size("ctx")
    return lax.ppermute(x, "ctx", [(i, i ^ bit) for i in range(n)])


def across(x, k):
    n = lax.axis_size("ctx")
    moves = [(i, i + TEAM * k) for i in range(n)]
    return lax.ppermute(x, "ctx", [(i, j % n) for i, j in moves if k < 0 or j < n])


def local(queries, keys, values, log_decay, gate, gain, grad_out):
    rows, width = queries.shape
    heads = width // HEAD
    hq = heads // TEAM
    tp = lax.axis_size("tp")
    n = lax.axis_size("ctx")
    groups = n // TEAM
    channels = width * tp
    bf = lambda *shape: jax.ShapeDtypeStruct(shape, BF16)
    f32 = lambda *shape: jax.ShapeDtypeStruct(shape, F32)
    swaps = tp == 2
    part = rows // 2
    small = 2 * heads * rows * HEAD * HEAD
    large = 2 * heads * rows * rows * HEAD
    wide = f32(hq * HEAD + SIDE, HEAD)
    wide2 = f32(2, hq * HEAD + SIDE, HEAD)
    narrow = bf(hq * HEAD + EXTRA, HEAD)
    narrow2 = bf(2, hq * HEAD + EXTRA, HEAD)
    table = f32(TEAM, rows, HEAD)
    gain_row = gain.reshape(1, width)

    def beside(work, after, name):
        return [work[name](after)] if name in work else []

    def step_call(body, reverse, inputs, unread, shapes, name, *sizes):
        return call(
            functools.partial(body, reverse, hq, *sizes),
            [*inputs, *unread],
            shapes,
            name,
            in_specs=[VMEM] * len(inputs) + [ANY] * len(unread),
        )

    def scan(reverse, keep, give, work):
        got = swap(give, 1)
        own, send = step_call(chip_total_body, reverse, [keep, got], [], [wide, narrow], "chip_total")
        got_pair = swap(send, 2)
        unread = beside(work, send, "pair")
        total, send = step_call(group_total_body, reverse, [own, got_pair], unread, [wide, narrow], "group_total")
        so_far, step = total, 1
        while 2 * step < groups:
            far = across(send, -step if reverse else step)
            unread = beside(work, send, "one") if step == 1 else []
            before = [] if step == 1 else [so_far]
            so_far, send = step_call(
                doubling_body, reverse, [total, *before, far], unread, [wide, narrow], "doubling", step, groups
            )
            step *= 2
        far = across(send, -step if reverse else step)
        unread = beside(work, send, "last")
        kept, send = step_call(
            into_chips_body,
            reverse,
            [own, got_pair, total, so_far, far],
            unread,
            [wide, narrow],
            "into_chips",
            step,
            groups,
        )
        other = swap(send, 2)
        unread = beside(work, send, "pair_back")
        mine, send = step_call(
            into_cores_body, reverse, [keep, got, kept, other], unread, [narrow2, narrow2], "into_cores"
        )
        return mine, swap(send, 1)

    outs = call(
        functools.partial(sent_states_body, heads, swaps),
        [in_hbm(keys), in_hbm(values), in_hbm(log_decay)] + [in_hbm(grad_out)] * swaps,
        [wide2, f32(EXTRA, rows), bf(rows, width), bf(rows, width)] + [bf(part, width)] * swaps,
        "sent_states",
        [
            pltpu.VMEM(log_decay.shape, F32),
            pltpu.SemaphoreType.DMA((2, TEAM)),
            pltpu.SemaphoreType.DMA((2,)),
        ],
        small // 2,
        [HBM] * (3 + swaps),
        [VMEM] * 4 + [HBM] * swaps,
    )
    give, row, keys, values = outs[:4]
    if swaps:
        arrived = lax.ppermute(outs[4], "tp", [(0, 1), (1, 0)])
        own = grad_out
    else:
        every = lax.all_to_all(grad_out, "tp", split_axis=1, concat_axis=0, tiled=True)
        own, arrived = every[:part], every[part:]
    (keep,) = call(
        functools.partial(kept_states_body, heads), [keys, values, row], [wide2], "kept_states", flops=small // 2
    )
    done = {}

    def probs_beside(after):
        if "decays" not in done:
            *done["decays"], done["queries"] = call(
                functools.partial(decays_body, heads),
                [row, in_hbm(queries), after],
                [table] * 3 + [bf(rows, width)],
                "decays",
                [pltpu.SemaphoreType.DMA(())],
                in_specs=[VMEM, HBM, ANY],
            )
        before = done.get("probs", [])
        done["probs"] = call(
            functools.partial(turned_probs_body, heads, TEAM // 2 if before else 0),
            [done["queries"], keys, row, done["decays"][0], after, *before],
            [f32(heads, HALF, BLOCK), f32(heads, HALF, HALF), bf(heads, HALF, BLOCK), bf(heads, HALF, HALF)],
            "turned_probs",
            flops=large // 2,
            in_specs=[VMEM] * 4 + [ANY] + [VMEM] * len(before),
            alias={5 + i: i for i in range(len(before))},
        )
        return done["probs"][3]

    def intra_beside(after):
        (done["intra"],) = call(
            functools.partial(intra_body, heads),
            [done["queries"], keys, values, row, done["decays"][0], after],
            [f32(rows, width)],
            "intra",
            flops=2 * large,
            in_specs=[VMEM] * 5 + [ANY],
        )
        return done["intra"]

    def dscaled_beside(after):
        done["dscaled"] = call(
            functools.partial(own_dscaled_body, heads, swaps),
            [gate, in_hbm(own), gain_row, done["queries"], row, after],
            [f32(rows, width), bf(width, rows)],
            "own_dscaled",
            [pltpu.VMEM((part, width), BF16), pltpu.SemaphoreType.DMA(())],
            small,
            [VMEM, HBM, VMEM, VMEM, VMEM, ANY],
        )
        return done["dscaled"][1]

    work = {"pair": probs_beside, "one": probs_beside, "last": intra_beside, "pair_back": dscaled_beside}
    mine, got = scan(False, keep, give, work)
    queries = done["queries"]
    (col, growth, shrink), intra, (dscaled, turned) = done["decays"], done["intra"], done["dscaled"]
    (dscaled,) = call(
        functools.partial(got_dscaled_body, heads, swaps),
        [gate, arrived, gain_row, dscaled],
        [f32(rows, width)],
        "got_dscaled",
        alias={3: 0},
    )
    tall = f32(rows, HEAD)
    wide_scratch = pltpu.VMEM((rows, 2 * HEAD), F32)
    att, squares, inner = call(
        functools.partial(attention_body, heads, True),
        [queries, intra, dscaled, growth, mine],
        [f32(rows, width), tall, tall],
        "attention",
        [wide_scratch],
        small // 2,
        alias={1: 0},
    )
    att, sums = call(
        functools.partial(attention_body, heads, False),
        [queries, att, dscaled, growth, got, squares, inner],
        [f32(rows, width), f32(8, rows)],
        "attention",
        [pltpu.VMEM((rows, HEAD), F32)] * 2 + [wide_scratch],
        small // 2,
        alias={1: 0},
    )
    if swaps:
        others = lax.ppermute(sums, "tp", [(0, 1), (1, 0)])
    else:
        others = lax.psum(sums, "tp") - sums
    dattn, give, scale, coef = call(
        functools.partial(dattn_body, heads, channels, False),
        [att, dscaled, turned, gain_row, row, sums, others],
        [bf(rows, width), wide2, tall, tall],
        "sent_dattn",
        flops=small // 2,
    )
    dattn, keep = call(
        functools.partial(dattn_body, heads, channels, True),
        [att, dscaled, turned, gain_row, row, scale, coef, dattn],
        [bf(rows, width), wide2],
        "kept_dattn",
        flops=small // 2,
        alias={7: 0},
    )
    out_scratch = [pltpu.VMEM((TEAM, rows, hq * HEAD), BF16), pltpu.SemaphoreType.DMA((TEAM,))]

    def gate_beside(after):
        done["gate"], token = call(
            functools.partial(gate_body, heads),
            [gate, att, dscaled, scale, after],
            [bf(rows, width), f32(SIDE, HEAD)],
            "gate",
            out_scratch,
            small,
            [VMEM] * 4 + [ANY],
            [HBM, VMEM],
        )
        return token

    def key_value_first(after):
        done["key_value"] = call(
            functools.partial(key_value_body, heads, 0),
            [queries, values, dattn, *done["probs"], after],
            [f32(rows, width)] * 2,
            "key_value",
            flops=2 * large,
            in_specs=[VMEM] * 7 + [ANY],
        )
        return done["key_value"][0]

    def query_beside(after):
        done["query"], token = call(
            functools.partial(query_body, heads),
            [keys, values, dattn, row, col, growth, mine, got, after],
            [bf(rows, width), f32(SIDE, HEAD)],
            "query",
            out_scratch,
            2 * large + small,
            [VMEM] * 8 + [ANY],
            [HBM, VMEM],
        )
        return token

    def key_value_last(after):
        done["key_value"] = call(
            functools.partial(key_value_body, heads, TEAM // 2),
            [queries, values, dattn, *done["probs"], after, *done["key_value"]],
            [f32(rows, width)] * 2,
            "key_value",
            flops=2 * large,
            in_specs=[VMEM] * 7 + [ANY, VMEM, VMEM],
            alias={8: 0, 9: 1},
        )
        return done["key_value"][0]

    work = {"pair": gate_beside, "one": key_value_first, "last": query_beside, "pair_back": key_value_last}
    back_mine, back_got = scan(True, keep, give, work)
    gate_grad, query_grad, (dk, dv) = done["gate"], done["query"], done["key_value"]
    both = bf(2, rows, hq * HEAD)
    own_key, own_value, own_gain = call(
        functools.partial(own_final_body, heads),
        [keys, values, dk, dv, shrink, back_mine],
        [both, both, f32(1, width)],
        "own_final",
        flops=small,
    )
    key_grad, value_grad, gain_grad = call(
        functools.partial(final_body, heads),
        [keys, values, dk, dv, shrink, back_got, own_key, own_value, own_gain],
        [bf(rows, width), bf(rows, width), f32(1, width)],
        "final",
        [pltpu.VMEM(both.shape, BF16)] * 2 + [pltpu.SemaphoreType.DMA((8 * hq,))],
        small,
        out_specs=[HBM, HBM, VMEM],
    )
    return query_grad, key_grad, value_grad, gate_grad, gain_grad.reshape(width)


def solution(mesh):
    return jax.shard_map(
        local,
        mesh=mesh,
        in_specs=(
            P("ctx", "tp"),
            P("ctx", "tp"),
            P("ctx", "tp"),
            P("tp", "ctx"),
            P("ctx", "tp"),
            P("tp"),
            P(("ctx", "tp"), None),
        ),
        out_specs=(P("ctx", "tp"), P("ctx", "tp"), P("ctx", "tp"), P("ctx", "tp"), P("tp")),
        check_vma=False,
    )
```

```python
import functools

import jax
import jax.numpy as jnp
from jax import lax
from jax.experimental import pallas as pl
from jax.experimental.pallas import tpu as pltpu
from jax.sharding import PartitionSpec as P

HEAD = 128
BLOCK = 512
HALF = BLOCK // 2
TEAM = 4
SIDE = 8
EXTRA = 16
EPSILON = 1e-06
F32 = jnp.float32
BF16 = jnp.bfloat16
GRANT = 5 * 1024 * 1024
VMEM = pl.BlockSpec(memory_space=pltpu.VMEM)
HBM = pl.BlockSpec(memory_space=pltpu.HBM)
ANY = pl.BlockSpec(memory_space=pl.ANY)


def nt(a, b, precision=None):
    return lax.dot_general(a, b, (((1,), (1,)), ((), ())), preferred_element_type=F32, precision=precision)


def nn(a, b):
    return lax.dot_general(a, b, (((1,), (0,)), ((), ())), preferred_element_type=F32)


def half(i):
    return slice(i * HALF, (i + 1) * HALF)


def chunk(i):
    return slice(i * HEAD, (i + 1) * HEAD)


def split_terms(x, count):
    terms = []
    for _ in range(count):
        term = x.astype(BF16)
        terms.append(term)
        x = x - term.astype(F32)
    return terms


def read_wide(ref, hq):
    base = hq * HEAD
    return [
        (ref[chunk(j), :], ref[base + j : base + j + 1, :], ref[base + TEAM + j : base + TEAM + j + 1, :])
        for j in range(hq)
    ]


def write_wide(ref, hq, items):
    base = hq * HEAD
    at = lax.broadcasted_iota(jnp.int32, (SIDE, HEAD), 0)
    side = jnp.zeros((SIDE, HEAD), F32)
    for j, (term, edge, gain) in enumerate(items):
        ref[chunk(j), :] = term
        side = jnp.where(at == j, edge, side)
        side = jnp.where(at == TEAM + j, gain, side)
    ref[base : base + SIDE, :] = side


def read_narrow(ref, hq):
    base = hq * HEAD
    side = ref[base : base + EXTRA, :].astype(F32)
    row = lambda i: side[i : i + 1, :] + side[i + 1 : i + 2, :]
    return [(ref[chunk(j), :].astype(F32), row(2 * j), row(2 * TEAM + 2 * j)) for j in range(hq)]


def write_narrow(ref, hq, items):
    base = hq * HEAD
    at = lax.broadcasted_iota(jnp.int32, (EXTRA, HEAD), 0)
    side = jnp.zeros((EXTRA, HEAD), F32)
    for j, (term, edge, gain) in enumerate(items):
        ref[chunk(j), :] = term.astype(BF16)
        for first, value in ((2 * j, edge), (2 * TEAM + 2 * j, gain)):
            for i, part in enumerate(split_terms(value, 2)):
                side = jnp.where(at == first + i, part.astype(F32), side)
    ref[base : base + EXTRA, :] = side.astype(BF16)


def core():
    return lax.rem(lax.axis_index("ctx"), 2)


def pair():
    return lax.rem(lax.axis_index("ctx") // 2, 2)


def group():
    return lax.axis_index("ctx") // TEAM


def quarter_of(y, same):
    return 2 * y + (core() if same else 1 - core())


def head_at(quarter, hq, j):
    h = quarter * hq + j
    return h, pl.ds(pl.multiple_of(h * HEAD, HEAD), HEAD)


def transposed(x):
    shape = (x.shape[1], x.shape[1])
    eye = (lax.broadcasted_iota(jnp.int32, shape, 0) == lax.broadcasted_iota(jnp.int32, shape, 1)).astype(BF16)
    return nt(eye, x)


def several(quarter, hq):
    count = min(hq, 2)
    for j in range(0, hq, count):
        h = quarter * hq + j
        yield j, h, count, pl.ds(pl.multiple_of(h * HEAD, HEAD), count * HEAD)


def call(body, inputs, out_shape, name, scratch=(), flops=0, in_specs=None, out_specs=None, alias=None):
    nbytes = sum(x.size * x.dtype.itemsize for x in inputs)
    nbytes += sum(x.size * x.dtype.itemsize for x in out_shape)
    return pl.pallas_call(
        body,
        in_specs=in_specs or [VMEM] * len(inputs),
        out_specs=out_specs or [VMEM] * len(out_shape),
        out_shape=out_shape,
        scratch_shapes=list(scratch),
        input_output_aliases=alias or {},
        compiler_params=pltpu.CompilerParams(vmem_limit_bytes=GRANT),
        cost_estimate=pl.CostEstimate(flops=flops, bytes_accessed=nbytes, transcendentals=0),
        name=name,
    )(*inputs)


def joined(mine, other, mine_is_first, reverse):
    out = []
    for (a, ea, ga), (b, eb, gb) in zip(mine, other):
        near = mine_is_first if reverse else jnp.logical_not(mine_is_first)
        wa = jnp.where(near, 1.0, jnp.exp(eb))
        wb = jnp.where(near, jnp.exp(ea), 1.0)
        out.append((a * wa + b * wb, ea + eb, ga + gb))
    return out


def chip_total_body(reverse, hq, keep, got, own, send):
    first = core() == 0
    here, there = pair(), 1 - pair()
    own_items = joined(read_wide(keep.at[here], hq), read_wide(got.at[here], hq), first, reverse)
    write_wide(own, hq, own_items)
    send_items = joined(read_wide(keep.at[there], hq), read_wide(got.at[there], hq), first, reverse)
    write_narrow(send, hq, send_items)


def group_total_body(reverse, hq, own, got, *refs):
    total, send = refs[-2:]
    items = joined(read_wide(own, hq), read_narrow(got, hq), pair() == 0, reverse)
    write_wide(total, hq, items)
    write_narrow(send, hq, items)


def doubled(reverse, hq, step, groups, before, got):
    there = group() + step < groups if reverse else group() - step >= 0
    out = []
    for old, (term, edge, gain) in zip(before, read_narrow(got, hq)):
        term = jnp.where(there, term, 0.0)
        edge = jnp.where(there, edge, 0.0)
        if old is None:
            out.append((term, edge, gain))
        else:
            out.append((old[0] + jnp.exp(old[1]) * term, old[1] + edge, old[2] + gain))
    return out


def doubling_body(reverse, hq, step, groups, total, *refs):
    so_far, send = refs[-2:]
    if step == 1:
        got = refs[0]
        before = [None] * hq
    else:
        got = refs[1]
        before = read_wide(refs[0], hq)
    items = doubled(reverse, hq, step, groups, before, got)
    write_wide(so_far, hq, items)
    whole = []
    for (t, e, g), (s, es, gs) in zip(read_wide(total, hq), items):
        whole.append((t + jnp.exp(e) * s, e + es, g + gs))
    write_narrow(send, hq, whole)


def into_chips_body(reverse, hq, step, groups, own, got_pair, total, so_far, got, *refs):
    keep, send = refs[-2:]
    before = read_wide(so_far, hq) if step > 1 else [None] * hq
    entering = doubled(reverse, hq, step, groups, before, got)
    mine_near = pair() == (1 if reverse else 0)
    kept, sent = [], []
    for (r, _, gr), (c, ec, _), (o, eo, _), (_, _, gt) in zip(
        entering, read_wide(own, hq), read_narrow(got_pair, hq), read_wide(total, hq)
    ):
        gain = gr + gt
        zero = jnp.zeros_like(ec)
        kept.append((jnp.where(mine_near, r, jnp.exp(eo) * r + o), zero, gain))
        sent.append((jnp.where(mine_near, jnp.exp(ec) * r + c, r), zero, gain))
    write_wide(keep, hq, kept)
    write_narrow(send, hq, sent)


def into_cores_body(reverse, hq, keep, got, own, other, *refs):
    mine, send = refs[-2:]
    mine_near = core() == (1 if reverse else 0)
    for y in range(2):
        a, b = read_wide(own, hq), read_narrow(other, hq)
        here = pair() == y
        items_mine, items_send = [], []
        for p, q, (k, ek, _), (g, eg, _) in zip(a, b, read_wide(keep.at[y], hq), read_wide(got.at[y], hq)):
            r = jnp.where(here, p[0], q[0])
            gain = jnp.where(here, p[2], q[2])
            zero = jnp.zeros_like(ek)
            items_mine.append((jnp.where(mine_near, r, jnp.exp(eg) * r + g), zero, gain))
            items_send.append((jnp.where(mine_near, jnp.exp(ek) * r + k, r), zero, gain))
        write_narrow(mine.at[y], hq, items_mine)
        write_narrow(send.at[y], hq, items_send)


def block_states(hq, y, same, k, v, row, out):
    items = []
    for j, h, count, c in several(quarter_of(y, same), hq):
        turned = transposed(k[:, c])
        lines = [row[pl.ds(h + m, 1), :] for m in range(count)]
        edges = [line[:, BLOCK - 1 : BLOCK] for line in lines]
        faded = [turned[chunk(m)] * jnp.exp(edges[m] - lines[m]) for m in range(count)]
        both = nn(jnp.concatenate([x.astype(BF16) for x in faded], axis=0), v[:, c])
        for m in range(count):
            items.append((both[chunk(m), chunk(m)], jnp.broadcast_to(edges[m], (1, HEAD)), jnp.zeros((1, HEAD), F32)))
    write_wide(out.at[y], hq, items)


def sent_states_body(heads, swaps, k_hbm, v_hbm, ld_hbm, *refs):
    hq = heads // TEAM
    w = hq * HEAD
    if swaps:
        grad, give, row, k, v, away, ld, sems, side_sems = refs
        width = heads * HEAD
        there = pl.ds(pl.multiple_of((1 - lax.axis_index("tp")) * width, HEAD), width)
        side_copies = [pltpu.make_async_copy(grad.at[:, there], away, side_sems.at[1])]
    else:
        give, row, k, v, ld, sems, side_sems = refs
        side_copies = []
    first = pltpu.make_async_copy(ld_hbm, ld, side_sems.at[0])
    first.start()
    order = [(0, False), (1, False), (0, True), (1, True)]
    copies = []
    for slot, (y, same) in enumerate(order):
        cols_d = pl.ds(pl.multiple_of(quarter_of(y, same) * w, HEAD), w)
        both = [
            pltpu.make_async_copy(k_hbm.at[:, cols_d], k.at[:, cols_d], sems.at[0, slot]),
            pltpu.make_async_copy(v_hbm.at[:, cols_d], v.at[:, cols_d], sems.at[1, slot]),
        ]
        for c in both:
            c.start()
        copies.append(both)
    for c in side_copies:
        c.start()
    at = lax.broadcasted_iota(jnp.int32, (BLOCK, BLOCK), 0)
    other = lax.broadcasted_iota(jnp.int32, (BLOCK, BLOCK), 1)
    tri = (at <= other).astype(BF16)
    first.wait()
    x = ld[...]
    if heads < EXTRA:
        x = jnp.concatenate([x, jnp.zeros((EXTRA - heads, BLOCK), F32)], axis=0)
    sums = nn(jnp.concatenate(split_terms(x, 3), axis=0), tri)
    row[...] = sums[0:EXTRA] + (sums[EXTRA : 2 * EXTRA] + sums[2 * EXTRA : 3 * EXTRA])
    for slot, (y, same) in enumerate(order):
        for c in copies[slot]:
            c.wait()
        if not same:
            block_states(hq, y, same, k, v, row, give)
    for c in side_copies:
        c.wait()


def kept_states_body(heads, k, v, row, keep):
    for y in range(2):
        block_states(heads // TEAM, y, True, k, v, row, keep)


def decays_body(heads, row, q_hbm, _, col, growth, shrink, q, sem):
    hq = heads // TEAM
    copy = pltpu.make_async_copy(q_hbm, q, sem)
    copy.start()
    for g in range(TEAM):
        rows = row[g * hq : (g + 1) * hq, :]
        across = jnp.concatenate([rows, jnp.zeros((HEAD - hq, BLOCK), F32)], axis=0).T
        col[g] = across
        growth[g] = jnp.exp(across)
        shrink[g] = jnp.exp(across[BLOCK - 1 : BLOCK, :] - across)
    copy.wait()


def decay_table(high, low, lower):
    table = jnp.exp(high - low)
    at = lax.broadcasted_iota(jnp.int32, (HALF, HALF), 0)
    other = lax.broadcasted_iota(jnp.int32, (HALF, HALF), 1)
    if lower:
        cut = jnp.where(at >= other, table[:, -HALF:], 0.0)
        return cut if table.shape[1] == HALF else jnp.concatenate([table[:, :HALF], cut], axis=1)
    cut = jnp.where(at <= other, table[:, :HALF], 0.0)
    return cut if table.shape[1] == HALF else jnp.concatenate([cut, table[:, HALF:]], axis=1)


def turned_probs_body(heads, first, q, k, row, col, _, *refs):
    hq = heads // TEAM
    tables, probs = refs[-4:-2], refs[-2:]

    def one(g, _):
        for j in range(hq):
            h, c = head_at(g, hq, j)
            line = row[pl.ds(h, 1), :]
            for i in range(2):
                t = slice(i * HALF, BLOCK)
                table = decay_table(line[:, t], col[g, half(i), j : j + 1], False)
                tables[i][h] = table
                probs[i][h] = (nt(k[half(i), c], q[t, c]) * table).astype(BF16)
        return 0

    lax.fori_loop(first, first + TEAM // 2, one, 0)


def intra_body(heads, q, k, v, row, col, _, intra):
    hq = heads // TEAM

    def one(g, _):
        for j in range(hq):
            h, c = head_at(g, hq, j)
            line = row[pl.ds(h, 1), :]
            for i in range(2):
                u = slice(0, (i + 1) * HALF)
                table = decay_table(col[g, half(i), j : j + 1], line[:, u], True)
                probs = (nt(q[half(i), c], k[u, c]) * table).astype(BF16)
                intra[half(i), c] = nn(probs, v[u, c])
        return 0

    lax.fori_loop(0, TEAM, one, 0)


def dscaled_rows(heads, where, gate, ref, gain, dscaled):
    part = ref.shape[0]
    rows = pl.ds(pl.multiple_of(where * part, part), part)

    def one(g, _):
        for j in range(heads // TEAM):
            _, c = head_at(g, heads // TEAM, j)
            opened = jax.nn.sigmoid(gate[rows, c].astype(F32))
            dscaled[rows, c] = ref[:, c].astype(F32) * opened * gain[:, c]
        return 0

    lax.fori_loop(0, TEAM, one, 0)


def own_dscaled_body(heads, swaps, gate, grad, gain, q, row, _, dscaled, turned, own, sem):
    width = heads * HEAD
    mine = lax.axis_index("tp") if swaps else 0
    here = pl.ds(pl.multiple_of(mine * width, HEAD), width)
    copy = pltpu.make_async_copy(grad.at[:, here], own, sem)
    copy.start()

    def one(g, _):
        for j, h, count, c in several(g, heads // TEAM):
            both = transposed(q[:, c])
            for m in range(count):
                rows = pl.ds(pl.multiple_of((h + m) * HEAD, HEAD), HEAD)
                turned[rows, :] = (both[chunk(m)] * jnp.exp(row[pl.ds(h + m, 1), :])).astype(BF16)
        return 0

    lax.fori_loop(0, TEAM, one, 0)
    copy.wait()
    dscaled_rows(heads, mine, gate, own, gain, dscaled)


def got_dscaled_body(heads, swaps, gate, got, gain, _, dscaled):
    dscaled_rows(heads, 1 - lax.axis_index("tp") if swaps else 1, gate, got, gain, dscaled)


def diagonal(a, b):
    zero = jnp.zeros((HEAD, HEAD), BF16)
    return jnp.concatenate(
        [jnp.concatenate([a, zero], axis=1), jnp.concatenate([zero, b], axis=1)], axis=0
    )


def attention_body(heads, same, q, intra, dscaled, growth, state, *refs):
    hq = heads // TEAM
    if same:
        att, sq, inn, both = refs
    else:
        _, sq_before, inn_before, att, sums, sq, inn, both = refs
        sq[...] = sq_before[...]
        inn[...] = inn_before[...]
    for y in range(2):
        g = quarter_of(y, same)
        for j, h, count, c in several(g, hq):
            if count == 2:
                both[...] = nn(q[:, c], diagonal(state[y, chunk(j), :], state[y, chunk(j + 1), :]))
            else:
                both[:, 0:HEAD] = nn(q[:, c], state[y, chunk(j), :])
            for i in range(BLOCK // HEAD):
                r = chunk(i)
                a_sq = a_in = 0.0
                for m in range(count):
                    _, c = head_at(g, hq, j + m)
                    a = intra[r, c] + both[r, chunk(m)] * growth[g, r, j + m : j + m + 1]
                    att[r, c] = a
                    a_sq = a_sq + a * a
                    a_in = a_in + a * dscaled[r, c]
                if same and y == 0 and j == 0:
                    sq[r, :] = a_sq
                    inn[r, :] = a_in
                else:
                    sq[r, :] += a_sq
                    inn[r, :] += a_in
    if not same:
        ones = jnp.ones((8, HEAD), F32)
        a = nt(ones, sq[...], lax.Precision.HIGHEST)
        b = nt(ones, inn[...], lax.Precision.HIGHEST)
        sums[...] = jnp.where(lax.broadcasted_iota(jnp.int32, (8, BLOCK), 0) == 0, a, b)


def dattn_body(heads, channels, same, att, dscaled, turned, gain, row, *refs):
    hq = heads // TEAM
    if same:
        rsb, coefb, _, dattn, out = refs
    else:
        sum_a, sum_b, dattn, out, rsb, coefb = refs
        total = sum_a[...] + sum_b[...]
        rs = lax.rsqrt(total[0:1, :] / channels + EPSILON)
        coef = total[1:2, :] * (rs * rs * rs) / channels
        down = jnp.concatenate([rs, coef, jnp.zeros((HEAD - 2, BLOCK), F32)], axis=0).T
        rsb[...] = jnp.broadcast_to(down[:, 0:1], (BLOCK, HEAD))
        coefb[...] = jnp.broadcast_to(down[:, 1:2], (BLOCK, HEAD))
    for y in range(2):
        items = []
        for j, h, count, cols in several(quarter_of(y, same), hq):
            parts = []
            for m in range(count):
                _, c = head_at(quarter_of(y, same), hq, j + m)
                gsum = jnp.zeros((8, HEAD), F32)
                for i in range(BLOCK // HEAD):
                    r = chunk(i)
                    a = att[r, c]
                    t = dscaled[r, c] * rsb[r, :]
                    dattn[r, c] = (t - a * coefb[r, :]).astype(BF16)
                    gsum = gsum + jnp.sum((t * a).reshape(HEAD // 8, 8, HEAD), axis=0)
                parts.append(jnp.sum(gsum, axis=0, keepdims=True) / gain[:, c])
            both = nn(turned[pl.ds(pl.multiple_of(h * HEAD, HEAD), count * HEAD), :], dattn[:, cols])
            for m in range(count):
                edge = jnp.broadcast_to(row[pl.ds(h + m, 1), :][:, BLOCK - 1 : BLOCK], (1, HEAD))
                items.append((both[chunk(m), chunk(m)], edge, parts[m]))
        write_wide(out.at[y], hq, items)


def leave(out, ref, sems, g, w):
    cols = pl.ds(pl.multiple_of(g * w, HEAD), w)
    copy = pltpu.make_async_copy(out, ref.at[:, cols], sems)
    copy.start()
    return copy


def gate_body(heads, gate, att, dscaled, scale, _, gate_grad, token, out, sems):
    hq = heads // TEAM
    token[...] = jnp.zeros_like(token)
    copies = []
    for g in range(TEAM):
        for j in range(hq):
            _, c = head_at(g, hq, j)
            opened = jax.nn.sigmoid(gate[:, c].astype(F32))
            out[g, :, chunk(j)] = (dscaled[:, c] * att[:, c] * scale[...] * (1.0 - opened)).astype(BF16)
        copies.append(leave(out.at[g], gate_grad, sems.at[g], g, hq * HEAD))
    for copy in copies:
        copy.wait()


def by_quarter(mine, got):
    return [(ref.at[y], quarter_of(y, same)) for ref, same in ((mine, True), (got, False)) for y in range(2)]


def query_body(heads, k, v, dattn, row, col, growth, mine, got, _, query_grad, token, out, sems):
    hq = heads // TEAM
    token[...] = jnp.zeros_like(token)
    copies = []
    for slot, (state, g) in enumerate(by_quarter(mine, got)):
        for j in range(hq):
            h, c = head_at(g, hq, j)
            line = row[pl.ds(h, 1), :]
            for i in range(2):
                d = dattn[half(i), c]
                u = slice(0, (i + 1) * HALF)
                table = decay_table(col[g, half(i), j : j + 1], line[:, u], True)
                dscores = (nt(d, v[u, c]) * table).astype(BF16)
                inter = nt(d, state[chunk(j), :]) * growth[g, half(i), j : j + 1]
                out[slot, half(i), chunk(j)] = (inter + nn(dscores, k[u, c])).astype(BF16)
        copies.append(leave(out.at[slot], query_grad, sems.at[slot], g, hq * HEAD))
    for copy in copies:
        copy.wait()


def key_value_body(heads, first, last, q, v, dattn, table0, table1, probs0, probs1, _, *refs):
    hq = heads // TEAM
    count = min(hq, 2)
    dk, dv = refs[-2:]

    def one(step, _):
        for m in range(count):
            h = step * count + m
            _, c = head_at(h, 1, 0)
            for i, (table, probs) in enumerate(((table0, probs0), (table1, probs1))):
                t = slice(i * HALF, BLOCK)
                dscores = (nt(v[half(i), c], dattn[t, c]) * table[h]).astype(BF16)
                dk[half(i), c] = nn(dscores, q[t, c])
                dv[half(i), c] = nn(probs[h], dattn[t, c])
        return 0

    lax.fori_loop(first, last, one, 0)


def final_rows(hq, y, j, same, k, v, dk, dv, shrink, state, key_out, value_out):
    g = quarter_of(y, same)
    _, c = head_at(g, hq, j)
    fade = shrink[g, :, j : j + 1]
    after = state[y, chunk(j), :]
    key_out[y, :, chunk(j)] = (dk[:, c] + nt(v[:, c], after) * fade).astype(BF16)
    value_out[y, :, chunk(j)] = (dv[:, c] + nn(k[:, c], after) * fade).astype(BF16)


def own_final_body(heads, k, v, dk, dv, shrink, state, key_out, value_out, gain_grad):
    hq = heads // TEAM
    for y in range(2):
        items = read_narrow(state.at[y], hq)
        for j in range(hq):
            final_rows(hq, y, j, True, k, v, dk, dv, shrink, state, key_out, value_out)
            gain_grad[:, head_at(quarter_of(y, True), hq, j)[1]] = items[j][2]


def final_body(heads, k, v, dk, dv, shrink, state, own_key, own_value, own_gain, *refs):
    hq = heads // TEAM
    key_grad, value_grad, gain_grad, key_out, value_out, sems = refs
    copies = []

    def send(src, dst, cols):
        copy = pltpu.make_async_copy(src, dst.at[:, cols], sems.at[len(copies)])
        copy.start()
        copies.append(copy)

    for y in range(2):
        for j, _, count, c in several(quarter_of(y, True), hq):
            place = slice(j * HEAD, (j + count) * HEAD)
            send(own_key.at[y, :, place], key_grad, c)
            send(own_value.at[y, :, place], value_grad, c)
    gain_grad[...] = own_gain[...]
    for y in range(2):
        items = read_narrow(state.at[y], hq)
        for j, _, count, c in several(quarter_of(y, False), hq):
            for m in range(j, j + count):
                final_rows(hq, y, m, False, k, v, dk, dv, shrink, state, key_out, value_out)
                gain_grad[:, head_at(quarter_of(y, False), hq, m)[1]] = items[m][2]
            place = slice(j * HEAD, (j + count) * HEAD)
            send(key_out.at[y, :, place], key_grad, c)
            send(value_out.at[y, :, place], value_grad, c)
    for copy in copies:
        copy.wait()


def in_hbm(x):
    return pltpu.with_memory_space_constraint(x, pltpu.HBM)


def swap(x, bit):
    n = lax.axis_size("ctx")
    return lax.ppermute(x, "ctx", [(i, i ^ bit) for i in range(n)])


def across(x, k):
    n = lax.axis_size("ctx")
    return lax.ppermute(x, "ctx", [(i, (i + TEAM * k) % n) for i in range(n)])


def local(queries, keys, values, log_decay, gate, gain, grad_out):
    rows, width = queries.shape
    heads = width // HEAD
    hq = heads // TEAM
    tp = lax.axis_size("tp")
    n = lax.axis_size("ctx")
    groups = n // TEAM
    channels = width * tp
    bf = lambda *shape: jax.ShapeDtypeStruct(shape, BF16)
    f32 = lambda *shape: jax.ShapeDtypeStruct(shape, F32)
    swaps = tp == 2
    part = rows // 2
    small = 2 * heads * rows * HEAD * HEAD
    large = 2 * heads * rows * rows * HEAD
    wide = f32(hq * HEAD + SIDE, HEAD)
    wide2 = f32(2, hq * HEAD + SIDE, HEAD)
    narrow = bf(hq * HEAD + EXTRA, HEAD)
    narrow2 = bf(2, hq * HEAD + EXTRA, HEAD)
    table = f32(TEAM, rows, HEAD)
    gain_row = gain.reshape(1, width)

    def beside(work, after, name):
        return [work[name](after)] if name in work else []

    def step_call(body, reverse, inputs, unread, shapes, name, *sizes):
        return call(
            functools.partial(body, reverse, hq, *sizes),
            [*inputs, *unread],
            shapes,
            name,
            in_specs=[VMEM] * len(inputs) + [ANY] * len(unread),
        )

    def scan(reverse, keep, give, work):
        got = swap(give, 1)
        own, send = step_call(chip_total_body, reverse, [keep, got], [], [wide, narrow], "chip_total")
        got_pair = swap(send, 2)
        unread = beside(work, send, "pair")
        total, send = step_call(group_total_body, reverse, [own, got_pair], unread, [wide, narrow], "group_total")
        so_far, step = total, 1
        while 2 * step < groups:
            far = across(send, -step if reverse else step)
            unread = beside(work, send, "one") if step == 1 else []
            before = [] if step == 1 else [so_far]
            so_far, send = step_call(
                doubling_body, reverse, [total, *before, far], unread, [wide, narrow], "doubling", step, groups
            )
            step *= 2
        far = across(send, -step if reverse else step)
        unread = beside(work, send, "last")
        kept, send = step_call(
            into_chips_body,
            reverse,
            [own, got_pair, total, so_far, far],
            unread,
            [wide, narrow],
            "into_chips",
            step,
            groups,
        )
        other = swap(send, 2)
        unread = beside(work, send, "pair_back")
        mine, send = step_call(
            into_cores_body, reverse, [keep, got, kept, other], unread, [narrow2, narrow2], "into_cores"
        )
        return mine, swap(send, 1)

    outs = call(
        functools.partial(sent_states_body, heads, swaps),
        [in_hbm(keys), in_hbm(values), in_hbm(log_decay)] + [in_hbm(grad_out)] * swaps,
        [wide2, f32(EXTRA, rows), bf(rows, width), bf(rows, width)] + [bf(part, width)] * swaps,
        "sent_states",
        [
            pltpu.VMEM(log_decay.shape, F32),
            pltpu.SemaphoreType.DMA((2, TEAM)),
            pltpu.SemaphoreType.DMA((2,)),
        ],
        small // 2,
        [HBM] * (3 + swaps),
        [VMEM] * 4 + [HBM] * swaps,
    )
    give, row, keys, values = outs[:4]
    if swaps:
        arrived = lax.ppermute(outs[4], "tp", [(0, 1), (1, 0)])
        own = grad_out
    else:
        every = lax.all_to_all(grad_out, "tp", split_axis=1, concat_axis=0, tiled=True)
        own, arrived = every[:part], every[part:]
    (keep,) = call(
        functools.partial(kept_states_body, heads), [keys, values, row], [wide2], "kept_states", flops=small // 2
    )
    done = {}

    def probs_beside(after):
        if "decays" not in done:
            *done["decays"], done["queries"] = call(
                functools.partial(decays_body, heads),
                [row, in_hbm(queries), after],
                [table] * 3 + [bf(rows, width)],
                "decays",
                [pltpu.SemaphoreType.DMA(())],
                in_specs=[VMEM, HBM, ANY],
            )
        before = done.get("probs", [])
        done["probs"] = call(
            functools.partial(turned_probs_body, heads, TEAM // 2 if before else 0),
            [done["queries"], keys, row, done["decays"][0], after, *before],
            [f32(heads, HALF, BLOCK), f32(heads, HALF, HALF), bf(heads, HALF, BLOCK), bf(heads, HALF, HALF)],
            "turned_probs",
            flops=large // 2,
            in_specs=[VMEM] * 4 + [ANY] + [VMEM] * len(before),
            alias={5 + i: i for i in range(len(before))},
        )
        return done["probs"][3]

    def intra_beside(after):
        (done["intra"],) = call(
            functools.partial(intra_body, heads),
            [done["queries"], keys, values, row, done["decays"][0], after],
            [f32(rows, width)],
            "intra",
            flops=2 * large,
            in_specs=[VMEM] * 5 + [ANY],
        )
        return done["intra"]

    def dscaled_beside(after):
        done["dscaled"] = call(
            functools.partial(own_dscaled_body, heads, swaps),
            [gate, in_hbm(own), gain_row, done["queries"], row, after],
            [f32(rows, width), bf(width, rows)],
            "own_dscaled",
            [pltpu.VMEM((part, width), BF16), pltpu.SemaphoreType.DMA(())],
            small,
            [VMEM, HBM, VMEM, VMEM, VMEM, ANY],
        )
        return done["dscaled"][1]

    work = {"pair": probs_beside, "one": probs_beside, "last": intra_beside, "pair_back": dscaled_beside}
    mine, got = scan(False, keep, give, work)
    queries = done["queries"]
    (col, growth, shrink), intra, (dscaled, turned) = done["decays"], done["intra"], done["dscaled"]
    (dscaled,) = call(
        functools.partial(got_dscaled_body, heads, swaps),
        [gate, arrived, gain_row, dscaled],
        [f32(rows, width)],
        "got_dscaled",
        alias={3: 0},
    )
    tall = f32(rows, HEAD)
    wide_scratch = pltpu.VMEM((rows, 2 * HEAD), F32)
    att, squares, inner = call(
        functools.partial(attention_body, heads, True),
        [queries, intra, dscaled, growth, mine],
        [f32(rows, width), tall, tall],
        "attention",
        [wide_scratch],
        small // 2,
    )
    att, sums = call(
        functools.partial(attention_body, heads, False),
        [queries, intra, dscaled, growth, got, att, squares, inner],
        [f32(rows, width), f32(8, rows)],
        "attention",
        [pltpu.VMEM((rows, HEAD), F32)] * 2 + [wide_scratch],
        small // 2,
        alias={5: 0},
    )
    if swaps:
        others = lax.ppermute(sums, "tp", [(0, 1), (1, 0)])
    else:
        others = lax.psum(sums, "tp") - sums
    dattn, give, scale, coef = call(
        functools.partial(dattn_body, heads, channels, False),
        [att, dscaled, turned, gain_row, row, sums, others],
        [bf(rows, width), wide2, tall, tall],
        "sent_dattn",
        flops=small // 2,
    )
    dattn, keep = call(
        functools.partial(dattn_body, heads, channels, True),
        [att, dscaled, turned, gain_row, row, scale, coef, dattn],
        [bf(rows, width), wide2],
        "kept_dattn",
        flops=small // 2,
        alias={7: 0},
    )
    out_scratch = [pltpu.VMEM((TEAM, rows, hq * HEAD), BF16), pltpu.SemaphoreType.DMA((TEAM,))]

    def gate_beside(after):
        done["gate"], token = call(
            functools.partial(gate_body, heads),
            [gate, att, dscaled, scale, after],
            [bf(rows, width), f32(SIDE, HEAD)],
            "gate",
            out_scratch,
            small,
            [VMEM] * 4 + [ANY],
            [HBM, VMEM],
        )
        return token

    units = heads // min(hq, 2)
    cuts = [0, units // 8, units // 8 + units // 2, units]

    def key_value_beside(after):
        before = done.get("key_value", [])
        piece = done.get("piece", 0)
        done["piece"] = piece + 1
        done["key_value"] = call(
            functools.partial(key_value_body, heads, cuts[piece], cuts[piece + 1]),
            [queries, values, dattn, *done["probs"], after, *before],
            [f32(rows, width)] * 2,
            "key_value",
            flops=4 * large * (cuts[piece + 1] - cuts[piece]) // units,
            in_specs=[VMEM] * 7 + [ANY] + [VMEM] * len(before),
            alias={8 + i: i for i in range(len(before))},
        )
        return done["key_value"][0]

    def gate_and_key_value(after):
        return key_value_beside(gate_beside(after))

    def query_beside(after):
        done["query"], token = call(
            functools.partial(query_body, heads),
            [keys, values, dattn, row, col, growth, mine, got, after],
            [bf(rows, width), f32(SIDE, HEAD)],
            "query",
            out_scratch,
            2 * large + small,
            [VMEM] * 8 + [ANY],
            [HBM, VMEM],
        )
        return token

    work = {"pair": gate_and_key_value, "one": key_value_beside, "last": query_beside, "pair_back": key_value_beside}
    back_mine, back_got = scan(True, keep, give, work)
    gate_grad, query_grad, (dk, dv) = done["gate"], done["query"], done["key_value"]
    both = bf(2, rows, hq * HEAD)
    own_key, own_value, own_gain = call(
        functools.partial(own_final_body, heads),
        [keys, values, dk, dv, shrink, back_mine],
        [both, both, f32(1, width)],
        "own_final",
        flops=small,
    )
    key_grad, value_grad, gain_grad = call(
        functools.partial(final_body, heads),
        [keys, values, dk, dv, shrink, back_got, own_key, own_value, own_gain],
        [bf(rows, width), bf(rows, width), f32(1, width)],
        "final",
        [pltpu.VMEM(both.shape, BF16)] * 2 + [pltpu.SemaphoreType.DMA((8 * hq,))],
        small,
        out_specs=[HBM, HBM, VMEM],
    )
    return query_grad, key_grad, value_grad, gate_grad, gain_grad.reshape(width)


def solution(mesh):
    return jax.shard_map(
        local,
        mesh=mesh,
        in_specs=(
            P("ctx", "tp"),
            P("ctx", "tp"),
            P("ctx", "tp"),
            P("tp", "ctx"),
            P("ctx", "tp"),
            P("tp"),
            P(("ctx", "tp"), None),
        ),
        out_specs=(P("ctx", "tp"), P("ctx", "tp"), P("ctx", "tp"), P("ctx", "tp"), P("tp")),
        check_vma=False,
    )
```

```python
import functools

import jax
import jax.numpy as jnp
from jax import lax
from jax.experimental import pallas as pl
from jax.experimental.pallas import tpu as pltpu
from jax.sharding import PartitionSpec as P

HEAD = 128
BLOCK = 512
HALF = BLOCK // 2
TEAM = 4
SIDE = 8
EXTRA = 16
EPSILON = 1e-06
F32 = jnp.float32
BF16 = jnp.bfloat16
GRANT = 5 * 1024 * 1024
VMEM = pl.BlockSpec(memory_space=pltpu.VMEM)
HBM = pl.BlockSpec(memory_space=pltpu.HBM)
ANY = pl.BlockSpec(memory_space=pl.ANY)


def nt(a, b, precision=None):
    return lax.dot_general(a, b, (((1,), (1,)), ((), ())), preferred_element_type=F32, precision=precision)


def nn(a, b):
    return lax.dot_general(a, b, (((1,), (0,)), ((), ())), preferred_element_type=F32)


def half(i):
    return slice(i * HALF, (i + 1) * HALF)


def chunk(i):
    return slice(i * HEAD, (i + 1) * HEAD)


def split_terms(x, count):
    terms = []
    for _ in range(count):
        term = x.astype(BF16)
        terms.append(term)
        x = x - term.astype(F32)
    return terms


def read_wide(ref, hq):
    base = hq * HEAD
    return [
        (ref[chunk(j), :], ref[base + j : base + j + 1, :], ref[base + TEAM + j : base + TEAM + j + 1, :])
        for j in range(hq)
    ]


def write_wide(ref, hq, items):
    base = hq * HEAD
    at = lax.broadcasted_iota(jnp.int32, (SIDE, HEAD), 0)
    side = jnp.zeros((SIDE, HEAD), F32)
    for j, (term, edge, gain) in enumerate(items):
        ref[chunk(j), :] = term
        side = jnp.where(at == j, edge, side)
        side = jnp.where(at == TEAM + j, gain, side)
    ref[base : base + SIDE, :] = side


def read_narrow(ref, hq):
    base = hq * HEAD
    side = ref[base : base + EXTRA, :].astype(F32)
    row = lambda i: side[i : i + 1, :] + side[i + 1 : i + 2, :]
    return [(ref[chunk(j), :].astype(F32), row(2 * j), row(2 * TEAM + 2 * j)) for j in range(hq)]


def write_narrow(ref, hq, items):
    base = hq * HEAD
    at = lax.broadcasted_iota(jnp.int32, (EXTRA, HEAD), 0)
    side = jnp.zeros((EXTRA, HEAD), F32)
    for j, (term, edge, gain) in enumerate(items):
        ref[chunk(j), :] = term.astype(BF16)
        for first, value in ((2 * j, edge), (2 * TEAM + 2 * j, gain)):
            for i, part in enumerate(split_terms(value, 2)):
                side = jnp.where(at == first + i, part.astype(F32), side)
    ref[base : base + EXTRA, :] = side.astype(BF16)


def core():
    return lax.rem(lax.axis_index("ctx"), 2)


def pair():
    return lax.rem(lax.axis_index("ctx") // 2, 2)


def group():
    return lax.axis_index("ctx") // TEAM


def quarter_of(y, same):
    return 2 * y + (core() if same else 1 - core())


def head_at(quarter, hq, j):
    h = quarter * hq + j
    return h, pl.ds(pl.multiple_of(h * HEAD, HEAD), HEAD)


def transposed(x):
    shape = (x.shape[1], x.shape[1])
    eye = (lax.broadcasted_iota(jnp.int32, shape, 0) == lax.broadcasted_iota(jnp.int32, shape, 1)).astype(BF16)
    return nt(eye, x)


def several(quarter, hq):
    count = min(hq, 2)
    for j in range(0, hq, count):
        h = quarter * hq + j
        yield j, h, count, pl.ds(pl.multiple_of(h * HEAD, HEAD), count * HEAD)


def call(body, inputs, out_shape, name, scratch=(), flops=0, in_specs=None, out_specs=None, alias=None):
    nbytes = sum(x.size * x.dtype.itemsize for x in inputs)
    nbytes += sum(x.size * x.dtype.itemsize for x in out_shape)
    return pl.pallas_call(
        body,
        in_specs=in_specs or [VMEM] * len(inputs),
        out_specs=out_specs or [VMEM] * len(out_shape),
        out_shape=out_shape,
        scratch_shapes=list(scratch),
        input_output_aliases=alias or {},
        compiler_params=pltpu.CompilerParams(vmem_limit_bytes=GRANT),
        cost_estimate=pl.CostEstimate(flops=flops, bytes_accessed=nbytes, transcendentals=0),
        name=name,
    )(*inputs)


def joined(mine, other, mine_is_first, reverse):
    out = []
    for (a, ea, ga), (b, eb, gb) in zip(mine, other):
        near = mine_is_first if reverse else jnp.logical_not(mine_is_first)
        wa = jnp.where(near, 1.0, jnp.exp(eb))
        wb = jnp.where(near, jnp.exp(ea), 1.0)
        out.append((a * wa + b * wb, ea + eb, ga + gb))
    return out


def chip_total_body(reverse, hq, keep, got, own, send):
    first = core() == 0
    here, there = pair(), 1 - pair()
    own_items = joined(read_wide(keep.at[here], hq), read_wide(got.at[here], hq), first, reverse)
    write_wide(own, hq, own_items)
    send_items = joined(read_wide(keep.at[there], hq), read_wide(got.at[there], hq), first, reverse)
    write_narrow(send, hq, send_items)


def group_total_body(reverse, hq, own, got, *refs):
    total, send = refs[-2:]
    items = joined(read_wide(own, hq), read_narrow(got, hq), pair() == 0, reverse)
    write_wide(total, hq, items)
    write_narrow(send, hq, items)


def met(reverse, step, before, other):
    near = lax.rem(group() // step, 2) == (0 if reverse else 1)
    out = []
    for old, (term, edge, gain) in zip(before, other):
        term = jnp.where(near, term, 0.0)
        edge = jnp.where(near, edge, 0.0)
        if old is None:
            out.append((term, edge, gain))
        else:
            out.append((old[0] + jnp.exp(old[1]) * term, old[1] + edge, gain))
    return out


def window_body(reverse, hq, step, total, *refs):
    so_far, whole, send = refs[-3:]
    if step == 1:
        got = refs[0]
        before = [None] * hq
    else:
        got = refs[1]
        before = read_wide(refs[0], hq)
    other = read_narrow(got, hq)
    write_wide(so_far, hq, met(reverse, step, before, other))
    items = joined(read_wide(total, hq), other, lax.rem(group() // step, 2) == 0, reverse)
    write_wide(whole, hq, items)
    write_narrow(send, hq, items)


def into_chips_body(reverse, hq, step, own, got_pair, total, so_far, got, *refs):
    keep, send = refs[-2:]
    before = read_wide(so_far, hq) if step > 1 else [None] * hq
    entering = met(reverse, step, before, read_narrow(got, hq))
    mine_near = pair() == (1 if reverse else 0)
    kept, sent = [], []
    for (r, _, gr), (c, ec, _), (o, eo, _), (_, _, gt) in zip(
        entering, read_wide(own, hq), read_narrow(got_pair, hq), read_wide(total, hq)
    ):
        gain = gr + gt
        zero = jnp.zeros_like(ec)
        kept.append((jnp.where(mine_near, r, jnp.exp(eo) * r + o), zero, gain))
        sent.append((jnp.where(mine_near, jnp.exp(ec) * r + c, r), zero, gain))
    write_wide(keep, hq, kept)
    write_narrow(send, hq, sent)


def into_cores_body(reverse, hq, keep, got, own, other, *refs):
    mine, send = refs[-2:]
    mine_near = core() == (1 if reverse else 0)
    for y in range(2):
        a, b = read_wide(own, hq), read_narrow(other, hq)
        here = pair() == y
        items_mine, items_send = [], []
        for p, q, (k, ek, _), (g, eg, _) in zip(a, b, read_wide(keep.at[y], hq), read_wide(got.at[y], hq)):
            r = jnp.where(here, p[0], q[0])
            gain = jnp.where(here, p[2], q[2])
            zero = jnp.zeros_like(ek)
            items_mine.append((jnp.where(mine_near, r, jnp.exp(eg) * r + g), zero, gain))
            items_send.append((jnp.where(mine_near, jnp.exp(ek) * r + k, r), zero, gain))
        write_narrow(mine.at[y], hq, items_mine)
        write_narrow(send.at[y], hq, items_send)


def block_states(hq, y, same, k, v, row, out):
    items = []
    for j, h, count, c in several(quarter_of(y, same), hq):
        turned = transposed(k[:, c])
        lines = [row[pl.ds(h + m, 1), :] for m in range(count)]
        edges = [line[:, BLOCK - 1 : BLOCK] for line in lines]
        faded = [turned[chunk(m)] * jnp.exp(edges[m] - lines[m]) for m in range(count)]
        both = nn(jnp.concatenate([x.astype(BF16) for x in faded], axis=0), v[:, c])
        for m in range(count):
            items.append((both[chunk(m), chunk(m)], jnp.broadcast_to(edges[m], (1, HEAD)), jnp.zeros((1, HEAD), F32)))
    write_wide(out.at[y], hq, items)


def sent_states_body(heads, swaps, k_hbm, v_hbm, ld_hbm, *refs):
    hq = heads // TEAM
    w = hq * HEAD
    if swaps:
        grad, give, row, k, v, away, ld, sems, side_sems = refs
        width = heads * HEAD
        there = pl.ds(pl.multiple_of((1 - lax.axis_index("tp")) * width, HEAD), width)
        side_copies = [pltpu.make_async_copy(grad.at[:, there], away, side_sems.at[1])]
    else:
        give, row, k, v, ld, sems, side_sems = refs
        side_copies = []
    first = pltpu.make_async_copy(ld_hbm, ld, side_sems.at[0])
    first.start()
    order = [(0, False), (1, False), (0, True), (1, True)]
    copies = []
    for slot, (y, same) in enumerate(order):
        cols_d = pl.ds(pl.multiple_of(quarter_of(y, same) * w, HEAD), w)
        both = [
            pltpu.make_async_copy(k_hbm.at[:, cols_d], k.at[:, cols_d], sems.at[0, slot]),
            pltpu.make_async_copy(v_hbm.at[:, cols_d], v.at[:, cols_d], sems.at[1, slot]),
        ]
        for c in both:
            c.start()
        copies.append(both)
    for c in side_copies:
        c.start()
    at = lax.broadcasted_iota(jnp.int32, (BLOCK, BLOCK), 0)
    other = lax.broadcasted_iota(jnp.int32, (BLOCK, BLOCK), 1)
    tri = (at <= other).astype(BF16)
    first.wait()
    x = ld[...]
    if heads < EXTRA:
        x = jnp.concatenate([x, jnp.zeros((EXTRA - heads, BLOCK), F32)], axis=0)
    sums = nn(jnp.concatenate(split_terms(x, 3), axis=0), tri)
    row[...] = sums[0:EXTRA] + (sums[EXTRA : 2 * EXTRA] + sums[2 * EXTRA : 3 * EXTRA])
    for slot, (y, same) in enumerate(order):
        for c in copies[slot]:
            c.wait()
        if not same:
            block_states(hq, y, same, k, v, row, give)
    for c in side_copies:
        c.wait()


def kept_states_body(heads, k, v, row, keep):
    for y in range(2):
        block_states(heads // TEAM, y, True, k, v, row, keep)


def decays_body(heads, row, q_hbm, _, col, growth, q, sem):
    hq = heads // TEAM
    copy = pltpu.make_async_copy(q_hbm, q, sem)
    copy.start()
    for g in range(TEAM):
        rows = row[g * hq : (g + 1) * hq, :]
        across = jnp.concatenate([rows, jnp.zeros((HEAD - hq, BLOCK), F32)], axis=0).T
        col[g] = across
        growth[g] = jnp.exp(across)
    copy.wait()


def decay_table(high, low, lower):
    table = jnp.exp(high - low)
    at = lax.broadcasted_iota(jnp.int32, (HALF, HALF), 0)
    other = lax.broadcasted_iota(jnp.int32, (HALF, HALF), 1)
    if lower:
        cut = jnp.where(at >= other, table[:, -HALF:], 0.0)
        return cut if table.shape[1] == HALF else jnp.concatenate([table[:, :HALF], cut], axis=1)
    cut = jnp.where(at <= other, table[:, :HALF], 0.0)
    return cut if table.shape[1] == HALF else jnp.concatenate([cut, table[:, HALF:]], axis=1)


def turned_probs_body(heads, first, q, k, row, col, _, *refs):
    hq = heads // TEAM
    tables, probs = refs[-4:-2], refs[-2:]

    def one(g, _):
        for j in range(hq):
            h, c = head_at(g, hq, j)
            line = row[pl.ds(h, 1), :]
            for i in range(2):
                t = slice(i * HALF, BLOCK)
                table = decay_table(line[:, t], col[g, half(i), j : j + 1], False)
                tables[i][h] = table
                probs[i][h] = (nt(k[half(i), c], q[t, c]) * table).astype(BF16)
        return 0

    lax.fori_loop(first, first + TEAM // 2, one, 0)


def intra_body(heads, q, k, v, row, col, _, intra):
    hq = heads // TEAM

    def one(g, _):
        for j in range(hq):
            h, c = head_at(g, hq, j)
            line = row[pl.ds(h, 1), :]
            for i in range(2):
                u = slice(0, (i + 1) * HALF)
                table = decay_table(col[g, half(i), j : j + 1], line[:, u], True)
                probs = (nt(q[half(i), c], k[u, c]) * table).astype(BF16)
                intra[half(i), c] = nn(probs, v[u, c])
        return 0

    lax.fori_loop(0, TEAM, one, 0)


def dscaled_rows(heads, where, gate, ref, gain, dscaled):
    part = ref.shape[0]
    rows = pl.ds(pl.multiple_of(where * part, part), part)

    def one(g, _):
        for j in range(heads // TEAM):
            _, c = head_at(g, heads // TEAM, j)
            opened = jax.nn.sigmoid(gate[rows, c].astype(F32))
            dscaled[rows, c] = ref[:, c].astype(F32) * opened * gain[:, c]
        return 0

    lax.fori_loop(0, TEAM, one, 0)


def own_dscaled_body(heads, swaps, gate, grad, gain, q, row, _, dscaled, turned, own, sem):
    width = heads * HEAD
    mine = lax.axis_index("tp") if swaps else 0
    here = pl.ds(pl.multiple_of(mine * width, HEAD), width)
    copy = pltpu.make_async_copy(grad.at[:, here], own, sem)
    copy.start()

    def one(g, _):
        for j, h, count, c in several(g, heads // TEAM):
            both = transposed(q[:, c])
            for m in range(count):
                rows = pl.ds(pl.multiple_of((h + m) * HEAD, HEAD), HEAD)
                turned[rows, :] = (both[chunk(m)] * jnp.exp(row[pl.ds(h + m, 1), :])).astype(BF16)
        return 0

    lax.fori_loop(0, TEAM, one, 0)
    copy.wait()
    dscaled_rows(heads, mine, gate, own, gain, dscaled)


def got_dscaled_body(heads, swaps, gate, got, gain, _, dscaled):
    dscaled_rows(heads, 1 - lax.axis_index("tp") if swaps else 1, gate, got, gain, dscaled)


def diagonal(a, b):
    zero = jnp.zeros((HEAD, HEAD), BF16)
    return jnp.concatenate(
        [jnp.concatenate([a, zero], axis=1), jnp.concatenate([zero, b], axis=1)], axis=0
    )


def attention_body(heads, same, q, intra, dscaled, growth, state, *refs):
    hq = heads // TEAM
    if same:
        att, sq, inn, both = refs
    else:
        _, sq_before, inn_before, att, sums, sq, inn, both = refs
        sq[...] = sq_before[...]
        inn[...] = inn_before[...]
    for y in range(2):
        g = quarter_of(y, same)
        for j, h, count, c in several(g, hq):
            if count == 2:
                both[...] = nn(q[:, c], diagonal(state[y, chunk(j), :], state[y, chunk(j + 1), :]))
            else:
                both[:, 0:HEAD] = nn(q[:, c], state[y, chunk(j), :])
            for i in range(BLOCK // HEAD):
                r = chunk(i)
                a_sq = a_in = 0.0
                for m in range(count):
                    _, c = head_at(g, hq, j + m)
                    a = intra[r, c] + both[r, chunk(m)] * growth[g, r, j + m : j + m + 1]
                    att[r, c] = a
                    a_sq = a_sq + a * a
                    a_in = a_in + a * dscaled[r, c]
                if same and y == 0 and j == 0:
                    sq[r, :] = a_sq
                    inn[r, :] = a_in
                else:
                    sq[r, :] += a_sq
                    inn[r, :] += a_in
    if not same:
        ones = jnp.ones((8, HEAD), F32)
        a = nt(ones, sq[...], lax.Precision.HIGHEST)
        b = nt(ones, inn[...], lax.Precision.HIGHEST)
        sums[...] = jnp.where(lax.broadcasted_iota(jnp.int32, (8, BLOCK), 0) == 0, a, b)


def dattn_body(heads, channels, same, att, dscaled, turned, gain, row, *refs):
    hq = heads // TEAM
    if same:
        rsb, coefb, _, dattn, out = refs
    else:
        sum_a, sum_b, dattn, out, rsb, coefb = refs
        total = sum_a[...] + sum_b[...]
        rs = lax.rsqrt(total[0:1, :] / channels + EPSILON)
        coef = total[1:2, :] * (rs * rs * rs) / channels
        down = jnp.concatenate([rs, coef, jnp.zeros((HEAD - 2, BLOCK), F32)], axis=0).T
        rsb[...] = jnp.broadcast_to(down[:, 0:1], (BLOCK, HEAD))
        coefb[...] = jnp.broadcast_to(down[:, 1:2], (BLOCK, HEAD))
    for y in range(2):
        items = []
        for j, h, count, cols in several(quarter_of(y, same), hq):
            parts = []
            for m in range(count):
                _, c = head_at(quarter_of(y, same), hq, j + m)
                gsum = jnp.zeros((8, HEAD), F32)
                for i in range(BLOCK // HEAD):
                    r = chunk(i)
                    a = att[r, c]
                    t = dscaled[r, c] * rsb[r, :]
                    dattn[r, c] = (t - a * coefb[r, :]).astype(BF16)
                    gsum = gsum + jnp.sum((t * a).reshape(HEAD // 8, 8, HEAD), axis=0)
                parts.append(jnp.sum(gsum, axis=0, keepdims=True) / gain[:, c])
            both = nn(turned[pl.ds(pl.multiple_of(h * HEAD, HEAD), count * HEAD), :], dattn[:, cols])
            for m in range(count):
                edge = jnp.broadcast_to(row[pl.ds(h + m, 1), :][:, BLOCK - 1 : BLOCK], (1, HEAD))
                items.append((both[chunk(m), chunk(m)], edge, parts[m]))
        write_wide(out.at[y], hq, items)


def leave(out, ref, sems, g, w):
    cols = pl.ds(pl.multiple_of(g * w, HEAD), w)
    copy = pltpu.make_async_copy(out, ref.at[:, cols], sems)
    copy.start()
    return copy


def gate_body(heads, gate, att, dscaled, scale, _, gate_grad, token, out, sems):
    hq = heads // TEAM
    token[...] = jnp.zeros_like(token)
    copies = []
    for g in range(TEAM):
        for j in range(hq):
            _, c = head_at(g, hq, j)
            opened = jax.nn.sigmoid(gate[:, c].astype(F32))
            out[g, :, chunk(j)] = (dscaled[:, c] * att[:, c] * scale[...] * (1.0 - opened)).astype(BF16)
        copies.append(leave(out.at[g], gate_grad, sems.at[g], g, hq * HEAD))
    for copy in copies:
        copy.wait()


def by_quarter(mine, got):
    return [(ref.at[y], quarter_of(y, same)) for ref, same in ((mine, True), (got, False)) for y in range(2)]


def query_body(heads, k, v, dattn, row, col, growth, mine, got, _, query_grad, token, out, sems):
    hq = heads // TEAM
    token[...] = jnp.zeros_like(token)
    copies = []
    for slot, (state, g) in enumerate(by_quarter(mine, got)):
        for j in range(hq):
            h, c = head_at(g, hq, j)
            line = row[pl.ds(h, 1), :]
            for i in range(2):
                d = dattn[half(i), c]
                u = slice(0, (i + 1) * HALF)
                table = decay_table(col[g, half(i), j : j + 1], line[:, u], True)
                dscores = (nt(d, v[u, c]) * table).astype(BF16)
                inter = nt(d, state[chunk(j), :]) * growth[g, half(i), j : j + 1]
                out[slot, half(i), chunk(j)] = (inter + nn(dscores, k[u, c])).astype(BF16)
        copies.append(leave(out.at[slot], query_grad, sems.at[slot], g, hq * HEAD))
    for copy in copies:
        copy.wait()


def key_value_body(heads, first, last, q, v, dattn, table0, table1, probs0, probs1, _, *refs):
    hq = heads // TEAM
    count = min(hq, 2)
    dk, dv = refs[-2:]

    def one(step, _):
        for m in range(count):
            h = step * count + m
            _, c = head_at(h, 1, 0)
            for i, (table, probs) in enumerate(((table0, probs0), (table1, probs1))):
                t = slice(i * HALF, BLOCK)
                dscores = (nt(v[half(i), c], dattn[t, c]) * table[h]).astype(BF16)
                dk[half(i), c] = nn(dscores, q[t, c])
                dv[half(i), c] = nn(probs[h], dattn[t, c])
        return 0

    lax.fori_loop(first, last, one, 0)


def fades(col, y, same):
    sums = col[quarter_of(y, same)]
    return jnp.exp(sums[BLOCK - 1 : BLOCK, :] - sums)


def final_rows(hq, y, j, same, k, v, dk, dv, shrink, state, key_out, value_out):
    g = quarter_of(y, same)
    _, c = head_at(g, hq, j)
    fade = shrink[:, j : j + 1]
    after = state[y, chunk(j), :]
    key_out[y, :, chunk(j)] = (dk[:, c] + nt(v[:, c], after) * fade).astype(BF16)
    value_out[y, :, chunk(j)] = (dv[:, c] + nn(k[:, c], after) * fade).astype(BF16)


def own_final_body(heads, k, v, dk, dv, col, state, key_out, value_out, gain_grad):
    hq = heads // TEAM
    for y in range(2):
        items = read_narrow(state.at[y], hq)
        shrink = fades(col, y, True)
        for j in range(hq):
            final_rows(hq, y, j, True, k, v, dk, dv, shrink, state, key_out, value_out)
            gain_grad[:, head_at(quarter_of(y, True), hq, j)[1]] = items[j][2]


def final_body(heads, k, v, dk, dv, col, state, own_key, own_value, own_gain, *refs):
    hq = heads // TEAM
    key_grad, value_grad, gain_grad, key_out, value_out, sems = refs
    copies = []

    def send(src, dst, cols):
        copy = pltpu.make_async_copy(src, dst.at[:, cols], sems.at[len(copies)])
        copy.start()
        copies.append(copy)

    for y in range(2):
        for j, _, count, c in several(quarter_of(y, True), hq):
            place = slice(j * HEAD, (j + count) * HEAD)
            send(own_key.at[y, :, place], key_grad, c)
            send(own_value.at[y, :, place], value_grad, c)
    gain_grad[...] = own_gain[...]
    for y in range(2):
        items = read_narrow(state.at[y], hq)
        shrink = fades(col, y, False)
        for j, _, count, c in several(quarter_of(y, False), hq):
            for m in range(j, j + count):
                final_rows(hq, y, m, False, k, v, dk, dv, shrink, state, key_out, value_out)
                gain_grad[:, head_at(quarter_of(y, False), hq, m)[1]] = items[m][2]
            place = slice(j * HEAD, (j + count) * HEAD)
            send(key_out.at[y, :, place], key_grad, c)
            send(value_out.at[y, :, place], value_grad, c)
    for copy in copies:
        copy.wait()


def in_hbm(x):
    return pltpu.with_memory_space_constraint(x, pltpu.HBM)


def swap(x, bit):
    n = lax.axis_size("ctx")
    return lax.ppermute(x, "ctx", [(i, i ^ bit) for i in range(n)])


def local(queries, keys, values, log_decay, gate, gain, grad_out):
    rows, width = queries.shape
    heads = width // HEAD
    hq = heads // TEAM
    tp = lax.axis_size("tp")
    n = lax.axis_size("ctx")
    groups = n // TEAM
    channels = width * tp
    bf = lambda *shape: jax.ShapeDtypeStruct(shape, BF16)
    f32 = lambda *shape: jax.ShapeDtypeStruct(shape, F32)
    swaps = tp == 2
    part = rows // 2
    small = 2 * heads * rows * HEAD * HEAD
    large = 2 * heads * rows * rows * HEAD
    wide = f32(hq * HEAD + SIDE, HEAD)
    wide2 = f32(2, hq * HEAD + SIDE, HEAD)
    narrow = bf(hq * HEAD + EXTRA, HEAD)
    narrow2 = bf(2, hq * HEAD + EXTRA, HEAD)
    table = f32(TEAM, rows, HEAD)
    gain_row = gain.reshape(1, width)

    def beside(work, after, name):
        return [work[name](after)] if name in work else []

    def step_call(body, reverse, inputs, unread, shapes, name, *sizes):
        return call(
            functools.partial(body, reverse, hq, *sizes),
            [*inputs, *unread],
            shapes,
            name,
            in_specs=[VMEM] * len(inputs) + [ANY] * len(unread),
        )

    def scan(reverse, keep, give, work):
        got = swap(give, 1)
        own, send = step_call(chip_total_body, reverse, [keep, got], [], [wide, narrow], "chip_total")
        got_pair = swap(send, 2)
        unread = beside(work, send, "pair")
        total, send = step_call(group_total_body, reverse, [own, got_pair], unread, [wide, narrow], "group_total")
        so_far, step = total, 1
        while 2 * step < groups:
            far = swap(send, TEAM * step)
            unread = beside(work, send, "one") if step == 1 else []
            before = [] if step == 1 else [so_far]
            so_far, total, send = step_call(
                window_body, reverse, [total, *before, far], unread, [wide, wide, narrow], "window", step
            )
            step *= 2
        far = swap(send, TEAM * step)
        unread = beside(work, send, "last")
        kept, send = step_call(
            into_chips_body, reverse, [own, got_pair, total, so_far, far], unread, [wide, narrow], "into_chips", step
        )
        other = swap(send, 2)
        unread = beside(work, send, "pair_back")
        mine, send = step_call(
            into_cores_body, reverse, [keep, got, kept, other], unread, [narrow2, narrow2], "into_cores"
        )
        return mine, swap(send, 1)

    outs = call(
        functools.partial(sent_states_body, heads, swaps),
        [in_hbm(keys), in_hbm(values), in_hbm(log_decay)] + [in_hbm(grad_out)] * swaps,
        [wide2, f32(EXTRA, rows), bf(rows, width), bf(rows, width)] + [bf(part, width)] * swaps,
        "sent_states",
        [
            pltpu.VMEM(log_decay.shape, F32),
            pltpu.SemaphoreType.DMA((2, TEAM)),
            pltpu.SemaphoreType.DMA((2,)),
        ],
        small // 2,
        [HBM] * (3 + swaps),
        [VMEM] * 4 + [HBM] * swaps,
    )
    give, row, keys, values = outs[:4]
    if swaps:
        arrived = lax.ppermute(outs[4], "tp", [(0, 1), (1, 0)])
        own = grad_out
    else:
        every = lax.all_to_all(grad_out, "tp", split_axis=1, concat_axis=0, tiled=True)
        own, arrived = every[:part], every[part:]
    (keep,) = call(
        functools.partial(kept_states_body, heads), [keys, values, row], [wide2], "kept_states", flops=small // 2
    )
    done = {}

    def probs_beside(after):
        if "decays" not in done:
            *done["decays"], done["queries"] = call(
                functools.partial(decays_body, heads),
                [row, in_hbm(queries), after],
                [table] * 2 + [bf(rows, width)],
                "decays",
                [pltpu.SemaphoreType.DMA(())],
                in_specs=[VMEM, HBM, ANY],
            )
        before = done.get("probs", [])
        done["probs"] = call(
            functools.partial(turned_probs_body, heads, TEAM // 2 if before else 0),
            [done["queries"], keys, row, done["decays"][0], after, *before],
            [f32(heads, HALF, BLOCK), f32(heads, HALF, HALF), bf(heads, HALF, BLOCK), bf(heads, HALF, HALF)],
            "turned_probs",
            flops=large // 2,
            in_specs=[VMEM] * 4 + [ANY] + [VMEM] * len(before),
            alias={5 + i: i for i in range(len(before))},
        )
        return done["probs"][3]

    def intra_beside(after):
        (done["intra"],) = call(
            functools.partial(intra_body, heads),
            [done["queries"], keys, values, row, done["decays"][0], after],
            [f32(rows, width)],
            "intra",
            flops=2 * large,
            in_specs=[VMEM] * 5 + [ANY],
        )
        return done["intra"]

    def dscaled_beside(after):
        done["dscaled"] = call(
            functools.partial(own_dscaled_body, heads, swaps),
            [gate, in_hbm(own), gain_row, done["queries"], row, after],
            [f32(rows, width), bf(width, rows)],
            "own_dscaled",
            [pltpu.VMEM((part, width), BF16), pltpu.SemaphoreType.DMA(())],
            small,
            [VMEM, HBM, VMEM, VMEM, VMEM, ANY],
        )
        return done["dscaled"][1]

    work = {"pair": probs_beside, "one": probs_beside, "last": intra_beside, "pair_back": dscaled_beside}
    mine, got = scan(False, keep, give, work)
    queries = done["queries"]
    (col, growth), intra, (dscaled, turned) = done["decays"], done["intra"], done["dscaled"]
    (dscaled,) = call(
        functools.partial(got_dscaled_body, heads, swaps),
        [gate, arrived, gain_row, dscaled],
        [f32(rows, width)],
        "got_dscaled",
        alias={3: 0},
    )
    tall = f32(rows, HEAD)
    wide_scratch = pltpu.VMEM((rows, 2 * HEAD), F32)
    att, squares, inner = call(
        functools.partial(attention_body, heads, True),
        [queries, intra, dscaled, growth, mine],
        [f32(rows, width), tall, tall],
        "attention",
        [wide_scratch],
        small // 2,
    )
    att, sums = call(
        functools.partial(attention_body, heads, False),
        [queries, intra, dscaled, growth, got, att, squares, inner],
        [f32(rows, width), f32(8, rows)],
        "attention",
        [pltpu.VMEM((rows, HEAD), F32)] * 2 + [wide_scratch],
        small // 2,
        alias={5: 0},
    )
    if swaps:
        others = lax.ppermute(sums, "tp", [(0, 1), (1, 0)])
    else:
        others = lax.psum(sums, "tp") - sums
    dattn, give, scale, coef = call(
        functools.partial(dattn_body, heads, channels, False),
        [att, dscaled, turned, gain_row, row, sums, others],
        [bf(rows, width), wide2, tall, tall],
        "sent_dattn",
        flops=small // 2,
    )
    dattn, keep = call(
        functools.partial(dattn_body, heads, channels, True),
        [att, dscaled, turned, gain_row, row, scale, coef, dattn],
        [bf(rows, width), wide2],
        "kept_dattn",
        flops=small // 2,
        alias={7: 0},
    )
    out_scratch = [pltpu.VMEM((TEAM, rows, hq * HEAD), BF16), pltpu.SemaphoreType.DMA((TEAM,))]

    def gate_beside(after):
        done["gate"], token = call(
            functools.partial(gate_body, heads),
            [gate, att, dscaled, scale, after],
            [bf(rows, width), f32(SIDE, HEAD)],
            "gate",
            out_scratch,
            small,
            [VMEM] * 4 + [ANY],
            [HBM, VMEM],
        )
        return token

    units = heads // min(hq, 2)
    cuts = [0, units // 4, (5 * units) // 8, units]

    def key_value_beside(after):
        before = done.get("key_value", [])
        piece = done.get("piece", 0)
        done["piece"] = piece + 1
        done["key_value"] = call(
            functools.partial(key_value_body, heads, cuts[piece], cuts[piece + 1]),
            [queries, values, dattn, *done["probs"], after, *before],
            [f32(rows, width)] * 2,
            "key_value",
            flops=4 * large * (cuts[piece + 1] - cuts[piece]) // units,
            in_specs=[VMEM] * 7 + [ANY] + [VMEM] * len(before),
            alias={8 + i: i for i in range(len(before))},
        )
        return done["key_value"][0]

    def gate_and_key_value(after):
        return key_value_beside(gate_beside(after))

    def query_beside(after):
        done["query"], token = call(
            functools.partial(query_body, heads),
            [keys, values, dattn, row, col, growth, mine, got, after],
            [bf(rows, width), f32(SIDE, HEAD)],
            "query",
            out_scratch,
            2 * large + small,
            [VMEM] * 8 + [ANY],
            [HBM, VMEM],
        )
        return token

    work = {"pair": gate_and_key_value, "one": key_value_beside, "last": query_beside, "pair_back": key_value_beside}
    back_mine, back_got = scan(True, keep, give, work)
    gate_grad, query_grad, (dk, dv) = done["gate"], done["query"], done["key_value"]
    both = bf(2, rows, hq * HEAD)
    own_key, own_value, own_gain = call(
        functools.partial(own_final_body, heads),
        [keys, values, dk, dv, col, back_mine],
        [both, both, f32(1, width)],
        "own_final",
        flops=small,
    )
    key_grad, value_grad, gain_grad = call(
        functools.partial(final_body, heads),
        [keys, values, dk, dv, col, back_got, own_key, own_value, own_gain],
        [bf(rows, width), bf(rows, width), f32(1, width)],
        "final",
        [pltpu.VMEM(both.shape, BF16)] * 2 + [pltpu.SemaphoreType.DMA((8 * hq,))],
        small,
        out_specs=[HBM, HBM, VMEM],
    )
    return query_grad, key_grad, value_grad, gate_grad, gain_grad.reshape(width)


def solution(mesh):
    return jax.shard_map(
        local,
        mesh=mesh,
        in_specs=(
            P("ctx", "tp"),
            P("ctx", "tp"),
            P("ctx", "tp"),
            P("tp", "ctx"),
            P("ctx", "tp"),
            P("tp"),
            P(("ctx", "tp"), None),
        ),
        out_specs=(P("ctx", "tp"), P("ctx", "tp"), P("ctx", "tp"), P("ctx", "tp"), P("tp")),
        check_vma=False,
    )
```

```python
import functools

import jax
import jax.numpy as jnp
from jax import lax
from jax.experimental import pallas as pl
from jax.experimental.pallas import tpu as pltpu
from jax.sharding import PartitionSpec as P

HEAD = 128
BLOCK = 512
HALF = BLOCK // 2
TEAM = 4
SIDE = 8
EXTRA = 16
EPSILON = 1e-06
F32 = jnp.float32
BF16 = jnp.bfloat16
GRANT = 5 * 1024 * 1024
VMEM = pl.BlockSpec(memory_space=pltpu.VMEM)
HBM = pl.BlockSpec(memory_space=pltpu.HBM)
ANY = pl.BlockSpec(memory_space=pl.ANY)


def nt(a, b, precision=None):
    return lax.dot_general(a, b, (((1,), (1,)), ((), ())), preferred_element_type=F32, precision=precision)


def nn(a, b):
    return lax.dot_general(a, b, (((1,), (0,)), ((), ())), preferred_element_type=F32)


def half(i):
    return slice(i * HALF, (i + 1) * HALF)


def chunk(i):
    return slice(i * HEAD, (i + 1) * HEAD)


def split_terms(x, count):
    terms = []
    for _ in range(count):
        term = x.astype(BF16)
        terms.append(term)
        x = x - term.astype(F32)
    return terms


def read_wide(ref, hq):
    base = hq * HEAD
    return [
        (ref[chunk(j), :], ref[base + j : base + j + 1, :], ref[base + TEAM + j : base + TEAM + j + 1, :])
        for j in range(hq)
    ]


def write_wide(ref, hq, items):
    base = hq * HEAD
    at = lax.broadcasted_iota(jnp.int32, (SIDE, HEAD), 0)
    side = jnp.zeros((SIDE, HEAD), F32)
    for j, (term, edge, gain) in enumerate(items):
        ref[chunk(j), :] = term
        side = jnp.where(at == j, edge, side)
        side = jnp.where(at == TEAM + j, gain, side)
    ref[base : base + SIDE, :] = side


def read_narrow(ref, hq):
    base = hq * HEAD
    side = ref[base : base + EXTRA, :].astype(F32)
    row = lambda i: side[i : i + 1, :] + side[i + 1 : i + 2, :]
    return [(ref[chunk(j), :].astype(F32), row(2 * j), row(2 * TEAM + 2 * j)) for j in range(hq)]


def write_narrow(ref, hq, items):
    base = hq * HEAD
    at = lax.broadcasted_iota(jnp.int32, (EXTRA, HEAD), 0)
    side = jnp.zeros((EXTRA, HEAD), F32)
    for j, (term, edge, gain) in enumerate(items):
        ref[chunk(j), :] = term.astype(BF16)
        for first, value in ((2 * j, edge), (2 * TEAM + 2 * j, gain)):
            for i, part in enumerate(split_terms(value, 2)):
                side = jnp.where(at == first + i, part.astype(F32), side)
    ref[base : base + EXTRA, :] = side.astype(BF16)


def core():
    return lax.rem(lax.axis_index("ctx"), 2)


def pair():
    return lax.rem(lax.axis_index("ctx") // 2, 2)


def group():
    return lax.axis_index("ctx") // TEAM


def quarter_of(y, same):
    return 2 * y + (core() if same else 1 - core())


def head_at(quarter, hq, j):
    h = quarter * hq + j
    return h, pl.ds(pl.multiple_of(h * HEAD, HEAD), HEAD)


def transposed(x):
    shape = (x.shape[1], x.shape[1])
    eye = (lax.broadcasted_iota(jnp.int32, shape, 0) == lax.broadcasted_iota(jnp.int32, shape, 1)).astype(BF16)
    return nt(eye, x)


def several(quarter, hq):
    count = min(hq, 2)
    for j in range(0, hq, count):
        h = quarter * hq + j
        yield j, h, count, pl.ds(pl.multiple_of(h * HEAD, HEAD), count * HEAD)


def call(body, inputs, out_shape, name, scratch=(), flops=0, in_specs=None, out_specs=None, alias=None):
    nbytes = sum(x.size * x.dtype.itemsize for x in inputs)
    nbytes += sum(x.size * x.dtype.itemsize for x in out_shape)
    return pl.pallas_call(
        body,
        in_specs=in_specs or [VMEM] * len(inputs),
        out_specs=out_specs or [VMEM] * len(out_shape),
        out_shape=out_shape,
        scratch_shapes=list(scratch),
        input_output_aliases=alias or {},
        compiler_params=pltpu.CompilerParams(vmem_limit_bytes=GRANT),
        cost_estimate=pl.CostEstimate(flops=flops, bytes_accessed=nbytes, transcendentals=0),
        name=name,
    )(*inputs)


def joined(mine, other, mine_is_first, reverse):
    out = []
    for (a, ea, ga), (b, eb, gb) in zip(mine, other):
        near = mine_is_first if reverse else jnp.logical_not(mine_is_first)
        wa = jnp.where(near, 1.0, jnp.exp(eb))
        wb = jnp.where(near, jnp.exp(ea), 1.0)
        out.append((a * wa + b * wb, ea + eb, ga + gb))
    return out


def chip_total_body(reverse, hq, keep, got, own, send):
    first = core() == 0
    read_got = read_narrow if reverse else read_wide
    here, there = pair(), 1 - pair()
    own_items = joined(read_wide(keep.at[here], hq), read_got(got.at[here], hq), first, reverse)
    write_wide(own, hq, own_items)
    send_items = joined(read_wide(keep.at[there], hq), read_got(got.at[there], hq), first, reverse)
    write_narrow(send, hq, send_items)


def group_total_body(reverse, hq, own, got, *refs):
    total, send = refs[-2:]
    items = joined(read_wide(own, hq), read_narrow(got, hq), pair() == 0, reverse)
    write_wide(total, hq, items)
    write_narrow(send, hq, items)


def met(reverse, step, before, other):
    near = lax.rem(group() // step, 2) == (0 if reverse else 1)
    out = []
    for old, (term, edge, gain) in zip(before, other):
        term = jnp.where(near, term, 0.0)
        edge = jnp.where(near, edge, 0.0)
        if old is None:
            out.append((term, edge, gain))
        else:
            out.append((old[0] + jnp.exp(old[1]) * term, old[1] + edge, gain))
    return out


def window_body(reverse, hq, step, total, *refs):
    so_far, whole, send = refs[-3:]
    if step == 1:
        got = refs[0]
        before = [None] * hq
    else:
        got = refs[1]
        before = read_wide(refs[0], hq)
    other = read_narrow(got, hq)
    write_wide(so_far, hq, met(reverse, step, before, other))
    items = joined(read_wide(total, hq), other, lax.rem(group() // step, 2) == 0, reverse)
    write_wide(whole, hq, items)
    write_narrow(send, hq, items)


def into_chips_body(reverse, hq, step, own, got_pair, total, so_far, got, *refs):
    keep, send = refs[-2:]
    before = read_wide(so_far, hq) if step > 1 else [None] * hq
    entering = met(reverse, step, before, read_narrow(got, hq))
    mine_near = pair() == (1 if reverse else 0)
    kept, sent = [], []
    for (r, _, gr), (c, ec, _), (o, eo, _), (_, _, gt) in zip(
        entering, read_wide(own, hq), read_narrow(got_pair, hq), read_wide(total, hq)
    ):
        gain = gr + gt
        zero = jnp.zeros_like(ec)
        kept.append((jnp.where(mine_near, r, jnp.exp(eo) * r + o), zero, gain))
        sent.append((jnp.where(mine_near, jnp.exp(ec) * r + c, r), zero, gain))
    write_wide(keep, hq, kept)
    write_narrow(send, hq, sent)


def into_cores_body(reverse, hq, keep, got, own, other, *refs):
    mine, send = refs[-2:]
    mine_near = core() == (1 if reverse else 0)
    read_got = read_narrow if reverse else read_wide
    for y in range(2):
        a, b = read_wide(own, hq), read_narrow(other, hq)
        here = pair() == y
        items_mine, items_send = [], []
        for p, q, (k, ek, _), (g, eg, _) in zip(a, b, read_wide(keep.at[y], hq), read_got(got.at[y], hq)):
            r = jnp.where(here, p[0], q[0])
            gain = jnp.where(here, p[2], q[2])
            zero = jnp.zeros_like(ek)
            items_mine.append((jnp.where(mine_near, r, jnp.exp(eg) * r + g), zero, gain))
            items_send.append((jnp.where(mine_near, jnp.exp(ek) * r + k, r), zero, gain))
        write_narrow(mine.at[y], hq, items_mine)
        write_narrow(send.at[y], hq, items_send)


def block_states(hq, y, same, k, v, row, out):
    items = []
    for j, h, count, c in several(quarter_of(y, same), hq):
        turned = transposed(k[:, c])
        lines = [row[pl.ds(h + m, 1), :] for m in range(count)]
        edges = [line[:, BLOCK - 1 : BLOCK] for line in lines]
        faded = [turned[chunk(m)] * jnp.exp(edges[m] - lines[m]) for m in range(count)]
        both = nn(jnp.concatenate([x.astype(BF16) for x in faded], axis=0), v[:, c])
        for m in range(count):
            items.append((both[chunk(m), chunk(m)], jnp.broadcast_to(edges[m], (1, HEAD)), jnp.zeros((1, HEAD), F32)))
    write_wide(out.at[y], hq, items)


def sent_states_body(heads, swaps, k_hbm, v_hbm, ld_hbm, *refs):
    hq = heads // TEAM
    w = hq * HEAD
    if swaps:
        grad, give, row, k, v, away, ld, sems, side_sems = refs
        width = heads * HEAD
        there = pl.ds(pl.multiple_of((1 - lax.axis_index("tp")) * width, HEAD), width)
        side_copies = [pltpu.make_async_copy(grad.at[:, there], away, side_sems.at[1])]
    else:
        give, row, k, v, ld, sems, side_sems = refs
        side_copies = []
    first = pltpu.make_async_copy(ld_hbm, ld, side_sems.at[0])
    first.start()
    order = [(0, False), (1, False), (0, True), (1, True)]
    copies = []
    for slot, (y, same) in enumerate(order):
        cols_d = pl.ds(pl.multiple_of(quarter_of(y, same) * w, HEAD), w)
        both = [
            pltpu.make_async_copy(k_hbm.at[:, cols_d], k.at[:, cols_d], sems.at[0, slot]),
            pltpu.make_async_copy(v_hbm.at[:, cols_d], v.at[:, cols_d], sems.at[1, slot]),
        ]
        for c in both:
            c.start()
        copies.append(both)
    for c in side_copies:
        c.start()
    at = lax.broadcasted_iota(jnp.int32, (BLOCK, BLOCK), 0)
    other = lax.broadcasted_iota(jnp.int32, (BLOCK, BLOCK), 1)
    tri = (at <= other).astype(BF16)
    first.wait()
    x = ld[...]
    if heads < EXTRA:
        x = jnp.concatenate([x, jnp.zeros((EXTRA - heads, BLOCK), F32)], axis=0)
    sums = nn(jnp.concatenate(split_terms(x, 3), axis=0), tri)
    row[...] = sums[0:EXTRA] + (sums[EXTRA : 2 * EXTRA] + sums[2 * EXTRA : 3 * EXTRA])
    for slot, (y, same) in enumerate(order):
        for c in copies[slot]:
            c.wait()
        if not same:
            block_states(hq, y, same, k, v, row, give)
    for c in side_copies:
        c.wait()


def kept_states_body(heads, k, v, row, keep):
    for y in range(2):
        block_states(heads // TEAM, y, True, k, v, row, keep)


def decays_body(heads, row, q_hbm, _, col, growth, q, sem):
    hq = heads // TEAM
    copy = pltpu.make_async_copy(q_hbm, q, sem)
    copy.start()
    for g in range(TEAM):
        rows = row[g * hq : (g + 1) * hq, :]
        across = jnp.concatenate([rows, jnp.zeros((HEAD - hq, BLOCK), F32)], axis=0).T
        col[g] = across
        growth[g] = jnp.exp(across)
    copy.wait()


def decay_table(high, low, lower):
    table = jnp.exp(high - low)
    at = lax.broadcasted_iota(jnp.int32, (HALF, HALF), 0)
    other = lax.broadcasted_iota(jnp.int32, (HALF, HALF), 1)
    if lower:
        cut = jnp.where(at >= other, table[:, -HALF:], 0.0)
        return cut if table.shape[1] == HALF else jnp.concatenate([table[:, :HALF], cut], axis=1)
    cut = jnp.where(at <= other, table[:, :HALF], 0.0)
    return cut if table.shape[1] == HALF else jnp.concatenate([cut, table[:, HALF:]], axis=1)


def turned_probs_body(heads, first, q, k, row, col, _, *refs):
    hq = heads // TEAM
    tables, probs = refs[-4:-2], refs[-2:]

    def one(g, _):
        for j in range(hq):
            h, c = head_at(g, hq, j)
            line = row[pl.ds(h, 1), :]
            for i in range(2):
                t = slice(i * HALF, BLOCK)
                table = decay_table(line[:, t], col[g, half(i), j : j + 1], False)
                tables[i][h] = table
                probs[i][h] = (nt(k[half(i), c], q[t, c]) * table).astype(BF16)
        return 0

    lax.fori_loop(first, first + TEAM // 2, one, 0)


def intra_body(heads, first, last, q, k, v, row, col, *refs):
    hq = heads // TEAM
    intra = refs[-1]

    def one(g, _):
        for j in range(hq):
            h, c = head_at(g, hq, j)
            line = row[pl.ds(h, 1), :]
            for i in range(2):
                u = slice(0, (i + 1) * HALF)
                table = decay_table(col[g, half(i), j : j + 1], line[:, u], True)
                probs = (nt(q[half(i), c], k[u, c]) * table).astype(BF16)
                intra[half(i), c] = nn(probs, v[u, c])
        return 0

    lax.fori_loop(first, last, one, 0)


def dscaled_rows(heads, where, gate, ref, gain, dscaled):
    part = ref.shape[0]
    rows = pl.ds(pl.multiple_of(where * part, part), part)

    def one(g, _):
        for j in range(heads // TEAM):
            _, c = head_at(g, heads // TEAM, j)
            opened = jax.nn.sigmoid(gate[rows, c].astype(F32))
            dscaled[rows, c] = ref[:, c].astype(F32) * opened * gain[:, c]
        return 0

    lax.fori_loop(0, TEAM, one, 0)


def own_dscaled_body(heads, swaps, gate, grad, gain, q, row, _, dscaled, turned, own, sem):
    width = heads * HEAD
    mine = lax.axis_index("tp") if swaps else 0
    here = pl.ds(pl.multiple_of(mine * width, HEAD), width)
    copy = pltpu.make_async_copy(grad.at[:, here], own, sem)
    copy.start()

    def one(g, _):
        for j, h, count, c in several(g, heads // TEAM):
            both = transposed(q[:, c])
            for m in range(count):
                rows = pl.ds(pl.multiple_of((h + m) * HEAD, HEAD), HEAD)
                turned[rows, :] = (both[chunk(m)] * jnp.exp(row[pl.ds(h + m, 1), :])).astype(BF16)
        return 0

    lax.fori_loop(0, TEAM, one, 0)
    copy.wait()
    dscaled_rows(heads, mine, gate, own, gain, dscaled)


def got_dscaled_body(heads, swaps, gate, got, gain, _, dscaled):
    dscaled_rows(heads, 1 - lax.axis_index("tp") if swaps else 1, gate, got, gain, dscaled)


def diagonal(a, b):
    zero = jnp.zeros((HEAD, HEAD), BF16)
    return jnp.concatenate(
        [jnp.concatenate([a, zero], axis=1), jnp.concatenate([zero, b], axis=1)], axis=0
    )


def attention_body(heads, same, q, intra, dscaled, growth, state, *refs):
    hq = heads // TEAM
    if same:
        att, sq, inn, both = refs
    else:
        _, sq_before, inn_before, att, sums, sq, inn, both = refs
        sq[...] = sq_before[...]
        inn[...] = inn_before[...]
    for y in range(2):
        g = quarter_of(y, same)
        for j, h, count, c in several(g, hq):
            if count == 2:
                both[...] = nn(q[:, c], diagonal(state[y, chunk(j), :], state[y, chunk(j + 1), :]))
            else:
                both[:, 0:HEAD] = nn(q[:, c], state[y, chunk(j), :])
            for i in range(BLOCK // HEAD):
                r = chunk(i)
                a_sq = a_in = 0.0
                for m in range(count):
                    _, c = head_at(g, hq, j + m)
                    a = intra[r, c] + both[r, chunk(m)] * growth[g, r, j + m : j + m + 1]
                    att[r, c] = a
                    a_sq = a_sq + a * a
                    a_in = a_in + a * dscaled[r, c]
                if same and y == 0 and j == 0:
                    sq[r, :] = a_sq
                    inn[r, :] = a_in
                else:
                    sq[r, :] += a_sq
                    inn[r, :] += a_in
    if not same:
        ones = jnp.ones((8, HEAD), F32)
        a = nt(ones, sq[...], lax.Precision.HIGHEST)
        b = nt(ones, inn[...], lax.Precision.HIGHEST)
        sums[...] = jnp.where(lax.broadcasted_iota(jnp.int32, (8, BLOCK), 0) == 0, a, b)


def dattn_body(heads, channels, same, att, dscaled, turned, gain, row, *refs):
    hq = heads // TEAM
    if same:
        rsb, coefb, _, dattn, out = refs
    else:
        sum_a, sum_b, dattn, out, rsb, coefb = refs
        total = sum_a[...] + sum_b[...]
        rs = lax.rsqrt(total[0:1, :] / channels + EPSILON)
        coef = total[1:2, :] * (rs * rs * rs) / channels
        down = jnp.concatenate([rs, coef, jnp.zeros((HEAD - 2, BLOCK), F32)], axis=0).T
        rsb[...] = jnp.broadcast_to(down[:, 0:1], (BLOCK, HEAD))
        coefb[...] = jnp.broadcast_to(down[:, 1:2], (BLOCK, HEAD))
    for y in range(2):
        items = []
        for j, h, count, cols in several(quarter_of(y, same), hq):
            parts = []
            for m in range(count):
                _, c = head_at(quarter_of(y, same), hq, j + m)
                gsum = jnp.zeros((8, HEAD), F32)
                for i in range(BLOCK // HEAD):
                    r = chunk(i)
                    a = att[r, c]
                    t = dscaled[r, c] * rsb[r, :]
                    dattn[r, c] = (t - a * coefb[r, :]).astype(BF16)
                    gsum = gsum + jnp.sum((t * a).reshape(HEAD // 8, 8, HEAD), axis=0)
                parts.append(jnp.sum(gsum, axis=0, keepdims=True) / gain[:, c])
            both = nn(turned[pl.ds(pl.multiple_of(h * HEAD, HEAD), count * HEAD), :], dattn[:, cols])
            for m in range(count):
                edge = jnp.broadcast_to(row[pl.ds(h + m, 1), :][:, BLOCK - 1 : BLOCK], (1, HEAD))
                items.append((both[chunk(m), chunk(m)], edge, parts[m]))
        (write_wide if same else write_narrow)(out.at[y], hq, items)


def leave(out, ref, sems, g, w):
    cols = pl.ds(pl.multiple_of(g * w, HEAD), w)
    copy = pltpu.make_async_copy(out, ref.at[:, cols], sems)
    copy.start()
    return copy


def gate_body(heads, gate, att, dscaled, scale, _, gate_grad, token, out, sems):
    hq = heads // TEAM
    token[...] = jnp.zeros_like(token)
    copies = []
    for g in range(TEAM):
        for j in range(hq):
            _, c = head_at(g, hq, j)
            opened = jax.nn.sigmoid(gate[:, c].astype(F32))
            out[g, :, chunk(j)] = (dscaled[:, c] * att[:, c] * scale[...] * (1.0 - opened)).astype(BF16)
        copies.append(leave(out.at[g], gate_grad, sems.at[g], g, hq * HEAD))
    for copy in copies:
        copy.wait()


def by_quarter(mine, got):
    return [(ref.at[y], quarter_of(y, same)) for ref, same in ((mine, True), (got, False)) for y in range(2)]


def query_body(heads, k, v, dattn, row, col, growth, mine, got, _, query_grad, token, out, sems):
    hq = heads // TEAM
    token[...] = jnp.zeros_like(token)
    copies = []
    for slot, (state, g) in enumerate(by_quarter(mine, got)):
        for j in range(hq):
            h, c = head_at(g, hq, j)
            line = row[pl.ds(h, 1), :]
            for i in range(2):
                d = dattn[half(i), c]
                u = slice(0, (i + 1) * HALF)
                table = decay_table(col[g, half(i), j : j + 1], line[:, u], True)
                dscores = (nt(d, v[u, c]) * table).astype(BF16)
                inter = nt(d, state[chunk(j), :]) * growth[g, half(i), j : j + 1]
                out[slot, half(i), chunk(j)] = (inter + nn(dscores, k[u, c])).astype(BF16)
        copies.append(leave(out.at[slot], query_grad, sems.at[slot], g, hq * HEAD))
    for copy in copies:
        copy.wait()


def key_value_body(heads, first, last, q, v, dattn, table0, table1, probs0, probs1, _, *refs):
    hq = heads // TEAM
    count = min(hq, 2)
    dk, dv = refs[-2:]

    def one(step, _):
        for m in range(count):
            h = step * count + m
            _, c = head_at(h, 1, 0)
            for i, (table, probs) in enumerate(((table0, probs0), (table1, probs1))):
                t = slice(i * HALF, BLOCK)
                dscores = (nt(v[half(i), c], dattn[t, c]) * table[h]).astype(BF16)
                dk[half(i), c] = nn(dscores, q[t, c])
                dv[half(i), c] = nn(probs[h], dattn[t, c])
        return 0

    lax.fori_loop(first, last, one, 0)


def fades(col, y, same):
    sums = col[quarter_of(y, same)]
    return jnp.exp(sums[BLOCK - 1 : BLOCK, :] - sums)


def final_rows(hq, y, j, same, k, v, dk, dv, shrink, state, key_out, value_out):
    g = quarter_of(y, same)
    _, c = head_at(g, hq, j)
    fade = shrink[:, j : j + 1]
    after = state[y, chunk(j), :]
    key_out[y, :, chunk(j)] = (dk[:, c] + nt(v[:, c], after) * fade).astype(BF16)
    value_out[y, :, chunk(j)] = (dv[:, c] + nn(k[:, c], after) * fade).astype(BF16)


def own_final_body(heads, k, v, dk, dv, col, state, key_out, value_out, gain_grad):
    hq = heads // TEAM
    for y in range(2):
        items = read_narrow(state.at[y], hq)
        shrink = fades(col, y, True)
        for j in range(hq):
            final_rows(hq, y, j, True, k, v, dk, dv, shrink, state, key_out, value_out)
            gain_grad[:, head_at(quarter_of(y, True), hq, j)[1]] = items[j][2]


def final_body(heads, k, v, dk, dv, col, state, own_key, own_value, own_gain, *refs):
    hq = heads // TEAM
    key_grad, value_grad, gain_grad, key_out, value_out, sems = refs
    copies = []

    def send(src, dst, cols):
        copy = pltpu.make_async_copy(src, dst.at[:, cols], sems.at[len(copies)])
        copy.start()
        copies.append(copy)

    for y in range(2):
        for j, _, count, c in several(quarter_of(y, True), hq):
            place = slice(j * HEAD, (j + count) * HEAD)
            send(own_key.at[y, :, place], key_grad, c)
            send(own_value.at[y, :, place], value_grad, c)
    gain_grad[...] = own_gain[...]
    for y in range(2):
        items = read_narrow(state.at[y], hq)
        shrink = fades(col, y, False)
        for j, _, count, c in several(quarter_of(y, False), hq):
            for m in range(j, j + count):
                final_rows(hq, y, m, False, k, v, dk, dv, shrink, state, key_out, value_out)
                gain_grad[:, head_at(quarter_of(y, False), hq, m)[1]] = items[m][2]
            place = slice(j * HEAD, (j + count) * HEAD)
            send(key_out.at[y, :, place], key_grad, c)
            send(value_out.at[y, :, place], value_grad, c)
    for copy in copies:
        copy.wait()


def in_hbm(x):
    return pltpu.with_memory_space_constraint(x, pltpu.HBM)


def swap(x, bit):
    n = lax.axis_size("ctx")
    return lax.ppermute(x, "ctx", [(i, i ^ bit) for i in range(n)])


def local(queries, keys, values, log_decay, gate, gain, grad_out):
    rows, width = queries.shape
    heads = width // HEAD
    hq = heads // TEAM
    tp = lax.axis_size("tp")
    n = lax.axis_size("ctx")
    groups = n // TEAM
    channels = width * tp
    bf = lambda *shape: jax.ShapeDtypeStruct(shape, BF16)
    f32 = lambda *shape: jax.ShapeDtypeStruct(shape, F32)
    swaps = tp == 2
    part = rows // 2
    small = 2 * heads * rows * HEAD * HEAD
    large = 2 * heads * rows * rows * HEAD
    wide = f32(hq * HEAD + SIDE, HEAD)
    wide2 = f32(2, hq * HEAD + SIDE, HEAD)
    narrow = bf(hq * HEAD + EXTRA, HEAD)
    narrow2 = bf(2, hq * HEAD + EXTRA, HEAD)
    table = f32(TEAM, rows, HEAD)
    gain_row = gain.reshape(1, width)

    def beside(work, after, name):
        return [work[name](after)] if name in work else []

    def step_call(body, reverse, inputs, unread, shapes, name, *sizes):
        return call(
            functools.partial(body, reverse, hq, *sizes),
            [*inputs, *unread],
            shapes,
            name,
            in_specs=[VMEM] * len(inputs) + [ANY] * len(unread),
        )

    def scan(reverse, keep, give, work):
        got = swap(give, 1)
        own, send = step_call(chip_total_body, reverse, [keep, got], [], [wide, narrow], "chip_total")
        got_pair = swap(send, 2)
        unread = beside(work, send, "pair")
        total, send = step_call(group_total_body, reverse, [own, got_pair], unread, [wide, narrow], "group_total")
        so_far, step = total, 1
        while 2 * step < groups:
            far = swap(send, TEAM * step)
            unread = beside(work, send, "one") if step == 1 else []
            before = [] if step == 1 else [so_far]
            so_far, total, send = step_call(
                window_body, reverse, [total, *before, far], unread, [wide, wide, narrow], "window", step
            )
            step *= 2
        far = swap(send, TEAM * step)
        unread = beside(work, send, "last")
        kept, send = step_call(
            into_chips_body, reverse, [own, got_pair, total, so_far, far], unread, [wide, narrow], "into_chips", step
        )
        other = swap(send, 2)
        unread = beside(work, send, "pair_back")
        mine, send = step_call(
            into_cores_body, reverse, [keep, got, kept, other], unread, [narrow2, narrow2], "into_cores"
        )
        return mine, swap(send, 1)

    outs = call(
        functools.partial(sent_states_body, heads, swaps),
        [in_hbm(keys), in_hbm(values), in_hbm(log_decay)] + [in_hbm(grad_out)] * swaps,
        [wide2, f32(EXTRA, rows), bf(rows, width), bf(rows, width)] + [bf(part, width)] * swaps,
        "sent_states",
        [
            pltpu.VMEM(log_decay.shape, F32),
            pltpu.SemaphoreType.DMA((2, TEAM)),
            pltpu.SemaphoreType.DMA((2,)),
        ],
        small // 2,
        [HBM] * (3 + swaps),
        [VMEM] * 4 + [HBM] * swaps,
    )
    give, row, keys, values = outs[:4]
    if swaps:
        arrived = lax.ppermute(outs[4], "tp", [(0, 1), (1, 0)])
        own = grad_out
    else:
        every = lax.all_to_all(grad_out, "tp", split_axis=1, concat_axis=0, tiled=True)
        own, arrived = every[:part], every[part:]
    (keep,) = call(
        functools.partial(kept_states_body, heads), [keys, values, row], [wide2], "kept_states", flops=small // 2
    )
    done = {}

    def probs_beside(after):
        if "decays" not in done:
            *done["decays"], done["queries"] = call(
                functools.partial(decays_body, heads),
                [row, in_hbm(queries), after],
                [table] * 2 + [bf(rows, width)],
                "decays",
                [pltpu.SemaphoreType.DMA(())],
                in_specs=[VMEM, HBM, ANY],
            )
        before = done.get("probs", [])
        done["probs"] = call(
            functools.partial(turned_probs_body, heads, TEAM // 2 if before else 0),
            [done["queries"], keys, row, done["decays"][0], after, *before],
            [f32(heads, HALF, BLOCK), f32(heads, HALF, HALF), bf(heads, HALF, BLOCK), bf(heads, HALF, HALF)],
            "turned_probs",
            flops=large // 2,
            in_specs=[VMEM] * 4 + [ANY] + [VMEM] * len(before),
            alias={5 + i: i for i in range(len(before))},
        )
        return done["probs"][3]

    def intra_beside(after):
        before = [done["intra"]] if "intra" in done else []
        first, last = (1, TEAM) if before else (0, 1)
        (done["intra"],) = call(
            functools.partial(intra_body, heads, first, last),
            [done["queries"], keys, values, row, done["decays"][0], after, *before],
            [f32(rows, width)],
            "intra",
            flops=2 * large * (last - first) // TEAM,
            in_specs=[VMEM] * 5 + [ANY] + [VMEM] * len(before),
            alias={6: 0} if before else None,
        )
        return done["intra"]

    def probs_and_intra(after):
        return intra_beside(probs_beside(after))

    def dscaled_beside(after):
        done["dscaled"] = call(
            functools.partial(own_dscaled_body, heads, swaps),
            [gate, in_hbm(own), gain_row, done["queries"], row, after],
            [f32(rows, width), bf(width, rows)],
            "own_dscaled",
            [pltpu.VMEM((part, width), BF16), pltpu.SemaphoreType.DMA(())],
            small,
            [VMEM, HBM, VMEM, VMEM, VMEM, ANY],
        )
        (dscaled,) = call(
            functools.partial(got_dscaled_body, heads, swaps),
            [gate, arrived, gain_row, done["dscaled"][0]],
            [f32(rows, width)],
            "got_dscaled",
            alias={3: 0},
        )
        done["dscaled"] = dscaled, done["dscaled"][1]
        return dscaled

    work = {"pair": probs_beside, "one": probs_and_intra, "last": intra_beside, "pair_back": dscaled_beside}
    mine, got = scan(False, keep, give, work)
    queries = done["queries"]
    (col, growth), intra, (dscaled, turned) = done["decays"], done["intra"], done["dscaled"]
    tall = f32(rows, HEAD)
    wide_scratch = pltpu.VMEM((rows, 2 * HEAD), F32)
    att, squares, inner = call(
        functools.partial(attention_body, heads, True),
        [queries, intra, dscaled, growth, mine],
        [f32(rows, width), tall, tall],
        "attention",
        [wide_scratch],
        small // 2,
    )
    att, sums = call(
        functools.partial(attention_body, heads, False),
        [queries, intra, dscaled, growth, got, att, squares, inner],
        [f32(rows, width), f32(8, rows)],
        "attention",
        [pltpu.VMEM((rows, HEAD), F32)] * 2 + [wide_scratch],
        small // 2,
        alias={5: 0},
    )
    if swaps:
        others = lax.ppermute(sums, "tp", [(0, 1), (1, 0)])
    else:
        others = lax.psum(sums, "tp") - sums
    dattn, give, scale, coef = call(
        functools.partial(dattn_body, heads, channels, False),
        [att, dscaled, turned, gain_row, row, sums, others],
        [bf(rows, width), narrow2, tall, tall],
        "sent_dattn",
        flops=small // 2,
    )
    dattn, keep = call(
        functools.partial(dattn_body, heads, channels, True),
        [att, dscaled, turned, gain_row, row, scale, coef, dattn],
        [bf(rows, width), wide2],
        "kept_dattn",
        flops=small // 2,
        alias={7: 0},
    )
    out_scratch = [pltpu.VMEM((TEAM, rows, hq * HEAD), BF16), pltpu.SemaphoreType.DMA((TEAM,))]

    def gate_beside(after):
        done["gate"], token = call(
            functools.partial(gate_body, heads),
            [gate, att, dscaled, scale, after],
            [bf(rows, width), f32(SIDE, HEAD)],
            "gate",
            out_scratch,
            small,
            [VMEM] * 4 + [ANY],
            [HBM, VMEM],
        )
        return token

    units = heads // min(hq, 2)
    cuts = [0, units // 8, units // 2, units]

    def key_value_beside(after):
        before = done.get("key_value", [])
        piece = done.get("piece", 0)
        done["piece"] = piece + 1
        done["key_value"] = call(
            functools.partial(key_value_body, heads, cuts[piece], cuts[piece + 1]),
            [queries, values, dattn, *done["probs"], after, *before],
            [f32(rows, width)] * 2,
            "key_value",
            flops=4 * large * (cuts[piece + 1] - cuts[piece]) // units,
            in_specs=[VMEM] * 7 + [ANY] + [VMEM] * len(before),
            alias={8 + i: i for i in range(len(before))},
        )
        return done["key_value"][0]

    def gate_and_key_value(after):
        return key_value_beside(gate_beside(after))

    def query_beside(after):
        done["query"], token = call(
            functools.partial(query_body, heads),
            [keys, values, dattn, row, col, growth, mine, got, after],
            [bf(rows, width), f32(SIDE, HEAD)],
            "query",
            out_scratch,
            2 * large + small,
            [VMEM] * 8 + [ANY],
            [HBM, VMEM],
        )
        return token

    work = {"pair": gate_and_key_value, "one": key_value_beside, "last": query_beside, "pair_back": key_value_beside}
    back_mine, back_got = scan(True, keep, give, work)
    gate_grad, query_grad, (dk, dv) = done["gate"], done["query"], done["key_value"]
    both = bf(2, rows, hq * HEAD)
    own_key, own_value, own_gain = call(
        functools.partial(own_final_body, heads),
        [keys, values, dk, dv, col, back_mine],
        [both, both, f32(1, width)],
        "own_final",
        flops=small,
    )
    key_grad, value_grad, gain_grad = call(
        functools.partial(final_body, heads),
        [keys, values, dk, dv, col, back_got, own_key, own_value, own_gain],
        [bf(rows, width), bf(rows, width), f32(1, width)],
        "final",
        [pltpu.VMEM(both.shape, BF16)] * 2 + [pltpu.SemaphoreType.DMA((8 * hq,))],
        small,
        out_specs=[HBM, HBM, VMEM],
    )
    return query_grad, key_grad, value_grad, gate_grad, gain_grad.reshape(width)


def solution(mesh):
    return jax.shard_map(
        local,
        mesh=mesh,
        in_specs=(
            P("ctx", "tp"),
            P("ctx", "tp"),
            P("ctx", "tp"),
            P("tp", "ctx"),
            P("ctx", "tp"),
            P("tp"),
            P(("ctx", "tp"), None),
        ),
        out_specs=(P("ctx", "tp"), P("ctx", "tp"), P("ctx", "tp"), P("ctx", "tp"), P("tp")),
        check_vma=False,
    )
```

```python
import functools

import jax
import jax.numpy as jnp
from jax import lax
from jax.experimental import pallas as pl
from jax.experimental.pallas import tpu as pltpu
from jax.sharding import PartitionSpec as P

HEAD = 128
BLOCK = 512
HALF = BLOCK // 2
TEAM = 4
SIDE = 8
EXTRA = 16
EPSILON = 1e-06
F32 = jnp.float32
BF16 = jnp.bfloat16
GRANT = 5 * 1024 * 1024
VMEM = pl.BlockSpec(memory_space=pltpu.VMEM)
HBM = pl.BlockSpec(memory_space=pltpu.HBM)
ANY = pl.BlockSpec(memory_space=pl.ANY)


def nt(a, b, precision=None):
    return lax.dot_general(a, b, (((1,), (1,)), ((), ())), preferred_element_type=F32, precision=precision)


def nn(a, b):
    return lax.dot_general(a, b, (((1,), (0,)), ((), ())), preferred_element_type=F32)


def half(i):
    return slice(i * HALF, (i + 1) * HALF)


def chunk(i):
    return slice(i * HEAD, (i + 1) * HEAD)


def split_terms(x, count):
    terms = []
    for _ in range(count):
        term = x.astype(BF16)
        terms.append(term)
        x = x - term.astype(F32)
    return terms


def read_wide(ref, hq):
    base = hq * HEAD
    return [
        (ref[chunk(j), :], ref[base + j : base + j + 1, :], ref[base + TEAM + j : base + TEAM + j + 1, :])
        for j in range(hq)
    ]


def write_wide(ref, hq, items):
    base = hq * HEAD
    at = lax.broadcasted_iota(jnp.int32, (SIDE, HEAD), 0)
    side = jnp.zeros((SIDE, HEAD), F32)
    for j, (term, edge, gain) in enumerate(items):
        ref[chunk(j), :] = term
        side = jnp.where(at == j, edge, side)
        side = jnp.where(at == TEAM + j, gain, side)
    ref[base : base + SIDE, :] = side


def read_narrow(ref, hq):
    base = hq * HEAD
    side = ref[base : base + EXTRA, :].astype(F32)
    row = lambda i: side[i : i + 1, :] + side[i + 1 : i + 2, :]
    return [(ref[chunk(j), :].astype(F32), row(2 * j), row(2 * TEAM + 2 * j)) for j in range(hq)]


def write_narrow(ref, hq, items):
    base = hq * HEAD
    at = lax.broadcasted_iota(jnp.int32, (EXTRA, HEAD), 0)
    side = jnp.zeros((EXTRA, HEAD), F32)
    for j, (term, edge, gain) in enumerate(items):
        ref[chunk(j), :] = term.astype(BF16)
        for first, value in ((2 * j, edge), (2 * TEAM + 2 * j, gain)):
            for i, part in enumerate(split_terms(value, 2)):
                side = jnp.where(at == first + i, part.astype(F32), side)
    ref[base : base + EXTRA, :] = side.astype(BF16)


def core():
    return lax.rem(lax.axis_index("ctx"), 2)


def pair():
    return lax.rem(lax.axis_index("ctx") // 2, 2)


def group():
    return lax.axis_index("ctx") // TEAM


def quarter_of(y, same):
    return 2 * y + (core() if same else 1 - core())


def head_at(quarter, hq, j):
    h = quarter * hq + j
    return h, pl.ds(pl.multiple_of(h * HEAD, HEAD), HEAD)


def transposed(x):
    shape = (x.shape[1], x.shape[1])
    eye = (lax.broadcasted_iota(jnp.int32, shape, 0) == lax.broadcasted_iota(jnp.int32, shape, 1)).astype(BF16)
    return nt(eye, x)


def several(quarter, hq):
    count = min(hq, 2)
    for j in range(0, hq, count):
        h = quarter * hq + j
        yield j, h, count, pl.ds(pl.multiple_of(h * HEAD, HEAD), count * HEAD)


def call(body, inputs, out_shape, name, scratch=(), flops=0, in_specs=None, out_specs=None, alias=None):
    nbytes = sum(x.size * x.dtype.itemsize for x in inputs)
    nbytes += sum(x.size * x.dtype.itemsize for x in out_shape)
    return pl.pallas_call(
        body,
        in_specs=in_specs or [VMEM] * len(inputs),
        out_specs=out_specs or [VMEM] * len(out_shape),
        out_shape=out_shape,
        scratch_shapes=list(scratch),
        input_output_aliases=alias or {},
        compiler_params=pltpu.CompilerParams(vmem_limit_bytes=GRANT),
        cost_estimate=pl.CostEstimate(flops=flops, bytes_accessed=nbytes, transcendentals=0),
        name=name,
    )(*inputs)


def joined(mine, other, mine_is_first, reverse):
    out = []
    for (a, ea, ga), (b, eb, gb) in zip(mine, other):
        near = mine_is_first if reverse else jnp.logical_not(mine_is_first)
        wa = jnp.where(near, 1.0, jnp.exp(eb))
        wb = jnp.where(near, jnp.exp(ea), 1.0)
        out.append((a * wa + b * wb, ea + eb, ga + gb))
    return out


def chip_total_body(reverse, hq, keep, got, own, send):
    first = core() == 0
    read_got = read_narrow if reverse else read_wide
    here, there = pair(), 1 - pair()
    own_items = joined(read_wide(keep.at[here], hq), read_got(got.at[here], hq), first, reverse)
    write_wide(own, hq, own_items)
    send_items = joined(read_wide(keep.at[there], hq), read_got(got.at[there], hq), first, reverse)
    write_narrow(send, hq, send_items)


def group_total_body(reverse, hq, own, got, *refs):
    total, send = refs[-2:]
    items = joined(read_wide(own, hq), read_narrow(got, hq), pair() == 0, reverse)
    write_wide(total, hq, items)
    write_narrow(send, hq, items)


def met(reverse, step, before, other):
    near = lax.rem(group() // step, 2) == (0 if reverse else 1)
    out = []
    for old, (term, edge, gain) in zip(before, other):
        term = jnp.where(near, term, 0.0)
        edge = jnp.where(near, edge, 0.0)
        if old is None:
            out.append((term, edge, gain))
        else:
            out.append((old[0] + jnp.exp(old[1]) * term, old[1] + edge, gain))
    return out


def window_body(reverse, hq, step, total, *refs):
    so_far, whole, send = refs[-3:]
    if step == 1:
        got = refs[0]
        before = [None] * hq
    else:
        got = refs[1]
        before = read_wide(refs[0], hq)
    other = read_narrow(got, hq)
    write_wide(so_far, hq, met(reverse, step, before, other))
    items = joined(read_wide(total, hq), other, lax.rem(group() // step, 2) == 0, reverse)
    write_wide(whole, hq, items)
    write_narrow(send, hq, items)


def into_chips_body(reverse, hq, step, own, got_pair, total, so_far, got, *refs):
    keep, send = refs[-2:]
    before = read_wide(so_far, hq) if step > 1 else [None] * hq
    entering = met(reverse, step, before, read_narrow(got, hq))
    mine_near = pair() == (1 if reverse else 0)
    kept, sent = [], []
    for (r, _, gr), (c, ec, _), (o, eo, _), (_, _, gt) in zip(
        entering, read_wide(own, hq), read_narrow(got_pair, hq), read_wide(total, hq)
    ):
        gain = gr + gt
        zero = jnp.zeros_like(ec)
        kept.append((jnp.where(mine_near, r, jnp.exp(eo) * r + o), zero, gain))
        sent.append((jnp.where(mine_near, jnp.exp(ec) * r + c, r), zero, gain))
    write_wide(keep, hq, kept)
    write_narrow(send, hq, sent)


def into_cores_body(reverse, hq, keep, got, own, other, *refs):
    mine, send = refs[-2:]
    mine_near = core() == (1 if reverse else 0)
    read_got = read_narrow if reverse else read_wide
    for y in range(2):
        a, b = read_wide(own, hq), read_narrow(other, hq)
        here = pair() == y
        items_mine, items_send = [], []
        for p, q, (k, ek, _), (g, eg, _) in zip(a, b, read_wide(keep.at[y], hq), read_got(got.at[y], hq)):
            r = jnp.where(here, p[0], q[0])
            gain = jnp.where(here, p[2], q[2])
            zero = jnp.zeros_like(ek)
            items_mine.append((jnp.where(mine_near, r, jnp.exp(eg) * r + g), zero, gain))
            items_send.append((jnp.where(mine_near, jnp.exp(ek) * r + k, r), zero, gain))
        write_narrow(mine.at[y], hq, items_mine)
        write_narrow(send.at[y], hq, items_send)


def block_states(hq, y, same, k, v, row, out):
    items = []
    for j, h, count, c in several(quarter_of(y, same), hq):
        turned = transposed(k[:, c])
        lines = [row[pl.ds(h + m, 1), :] for m in range(count)]
        edges = [line[:, BLOCK - 1 : BLOCK] for line in lines]
        faded = [turned[chunk(m)] * jnp.exp(edges[m] - lines[m]) for m in range(count)]
        both = nn(jnp.concatenate([x.astype(BF16) for x in faded], axis=0), v[:, c])
        for m in range(count):
            items.append((both[chunk(m), chunk(m)], jnp.broadcast_to(edges[m], (1, HEAD)), jnp.zeros((1, HEAD), F32)))
    write_wide(out.at[y], hq, items)


def sent_states_body(heads, swaps, k_hbm, v_hbm, ld_hbm, *refs):
    hq = heads // TEAM
    w = hq * HEAD
    if swaps:
        grad, give, row, k, v, away, ld, sems, side_sems = refs
        width = heads * HEAD
        there = pl.ds(pl.multiple_of((1 - lax.axis_index("tp")) * width, HEAD), width)
        side_copies = [pltpu.make_async_copy(grad.at[:, there], away, side_sems.at[1])]
    else:
        give, row, k, v, ld, sems, side_sems = refs
        side_copies = []
    first = pltpu.make_async_copy(ld_hbm, ld, side_sems.at[0])
    first.start()
    order = [(0, False), (1, False), (0, True), (1, True)]
    copies = []
    for slot, (y, same) in enumerate(order):
        cols_d = pl.ds(pl.multiple_of(quarter_of(y, same) * w, HEAD), w)
        both = [
            pltpu.make_async_copy(k_hbm.at[:, cols_d], k.at[:, cols_d], sems.at[0, slot]),
            pltpu.make_async_copy(v_hbm.at[:, cols_d], v.at[:, cols_d], sems.at[1, slot]),
        ]
        for c in both:
            c.start()
        copies.append(both)
    for c in side_copies:
        c.start()
    at = lax.broadcasted_iota(jnp.int32, (BLOCK, BLOCK), 0)
    other = lax.broadcasted_iota(jnp.int32, (BLOCK, BLOCK), 1)
    tri = (at <= other).astype(BF16)
    first.wait()
    x = ld[...]
    if heads < EXTRA:
        x = jnp.concatenate([x, jnp.zeros((EXTRA - heads, BLOCK), F32)], axis=0)
    sums = nn(jnp.concatenate(split_terms(x, 3), axis=0), tri)
    row[...] = sums[0:EXTRA] + (sums[EXTRA : 2 * EXTRA] + sums[2 * EXTRA : 3 * EXTRA])
    for slot, (y, same) in enumerate(order):
        for c in copies[slot]:
            c.wait()
        if not same:
            block_states(hq, y, same, k, v, row, give)
    for c in side_copies:
        c.wait()


def kept_states_body(heads, k, v, row, keep):
    for y in range(2):
        block_states(heads // TEAM, y, True, k, v, row, keep)


def decays_body(heads, row, q_hbm, _, col, growth, q, sem):
    hq = heads // TEAM
    copy = pltpu.make_async_copy(q_hbm, q, sem)
    copy.start()
    for g in range(TEAM):
        rows = row[g * hq : (g + 1) * hq, :]
        across = jnp.concatenate([rows, jnp.zeros((HEAD - hq, BLOCK), F32)], axis=0).T
        col[g] = across
        growth[g] = jnp.exp(across)
    copy.wait()


def decay_table(high, low, lower):
    table = jnp.exp(high - low)
    at = lax.broadcasted_iota(jnp.int32, (HALF, HALF), 0)
    other = lax.broadcasted_iota(jnp.int32, (HALF, HALF), 1)
    if lower:
        cut = jnp.where(at >= other, table[:, -HALF:], 0.0)
        return cut if table.shape[1] == HALF else jnp.concatenate([table[:, :HALF], cut], axis=1)
    cut = jnp.where(at <= other, table[:, :HALF], 0.0)
    return cut if table.shape[1] == HALF else jnp.concatenate([cut, table[:, HALF:]], axis=1)


def turned_probs_body(heads, first, q, k, row, col, _, *refs):
    hq = heads // TEAM
    tables, probs = refs[-4:-2], refs[-2:]

    def one(g, _):
        for j in range(hq):
            h, c = head_at(g, hq, j)
            line = row[pl.ds(h, 1), :]
            for i in range(2):
                t = slice(i * HALF, BLOCK)
                table = decay_table(line[:, t], col[g, half(i), j : j + 1], False)
                tables[i][h] = table
                probs[i][h] = (nt(k[half(i), c], q[t, c]) * table).astype(BF16)
        return 0

    lax.fori_loop(first, first + TEAM // 2, one, 0)


def intra_body(heads, first, last, q, k, v, row, col, *refs):
    hq = heads // TEAM
    intra = refs[-1]

    def one(g, _):
        for j in range(hq):
            h, c = head_at(g, hq, j)
            line = row[pl.ds(h, 1), :]
            for i in range(2):
                u = slice(0, (i + 1) * HALF)
                table = decay_table(col[g, half(i), j : j + 1], line[:, u], True)
                probs = (nt(q[half(i), c], k[u, c]) * table).astype(BF16)
                intra[half(i), c] = nn(probs, v[u, c])
        return 0

    lax.fori_loop(first, last, one, 0)


def dscaled_rows(heads, where, gate, ref, gain, dscaled):
    part = ref.shape[0]
    rows = pl.ds(pl.multiple_of(where * part, part), part)

    def one(g, _):
        for j in range(heads // TEAM):
            _, c = head_at(g, heads // TEAM, j)
            opened = jax.nn.sigmoid(gate[rows, c].astype(F32))
            dscaled[rows, c] = ref[:, c].astype(F32) * opened * gain[:, c]
        return 0

    lax.fori_loop(0, TEAM, one, 0)


def own_dscaled_body(heads, swaps, gate, grad, gain, q, row, _, dscaled, turned, own, sem):
    width = heads * HEAD
    mine = lax.axis_index("tp") if swaps else 0
    here = pl.ds(pl.multiple_of(mine * width, HEAD), width)
    copy = pltpu.make_async_copy(grad.at[:, here], own, sem)
    copy.start()

    def one(g, _):
        for j, h, count, c in several(g, heads // TEAM):
            both = transposed(q[:, c])
            for m in range(count):
                rows = pl.ds(pl.multiple_of((h + m) * HEAD, HEAD), HEAD)
                turned[rows, :] = (both[chunk(m)] * jnp.exp(row[pl.ds(h + m, 1), :])).astype(BF16)
        return 0

    lax.fori_loop(0, TEAM, one, 0)
    copy.wait()
    dscaled_rows(heads, mine, gate, own, gain, dscaled)


def got_dscaled_body(heads, swaps, gate, got, gain, _, dscaled):
    dscaled_rows(heads, 1 - lax.axis_index("tp") if swaps else 1, gate, got, gain, dscaled)


def states_of(state, j, count):
    if count == 1:
        return state[chunk(j), :]
    zero = jnp.zeros((HEAD, HEAD), BF16)
    upper = jnp.concatenate([state[chunk(j), :], zero], axis=1)
    lower = jnp.concatenate([zero, state[chunk(j + 1), :]], axis=1)
    return jnp.concatenate([upper, lower], axis=0)


def attention_body(heads, same, q, intra, dscaled, growth, state, *refs):
    hq = heads // TEAM
    if same:
        att, sq, inn, both = refs
    else:
        _, sq_before, inn_before, att, sums, sq, inn, both = refs
        sq[...] = sq_before[...]
        inn[...] = inn_before[...]
    for y in range(2):
        g = quarter_of(y, same)
        for j, h, count, c in several(g, hq):
            both[:, 0 : count * HEAD] = nn(q[:, c], states_of(state.at[y], j, count))
            for i in range(BLOCK // HEAD):
                r = chunk(i)
                a_sq = a_in = 0.0
                for m in range(count):
                    _, c = head_at(g, hq, j + m)
                    a = intra[r, c] + both[r, chunk(m)] * growth[g, r, j + m : j + m + 1]
                    att[r, c] = a
                    a_sq = a_sq + a * a
                    a_in = a_in + a * dscaled[r, c]
                if same and y == 0 and j == 0:
                    sq[r, :] = a_sq
                    inn[r, :] = a_in
                else:
                    sq[r, :] += a_sq
                    inn[r, :] += a_in
    if not same:
        ones = jnp.ones((8, HEAD), F32)
        a = nt(ones, sq[...], lax.Precision.HIGHEST)
        b = nt(ones, inn[...], lax.Precision.HIGHEST)
        sums[...] = jnp.where(lax.broadcasted_iota(jnp.int32, (8, BLOCK), 0) == 0, a, b)


def dattn_body(heads, channels, same, att, dscaled, turned, gain, row, *refs):
    hq = heads // TEAM
    if same:
        rsb, coefb, _, dattn, out = refs
    else:
        sum_a, sum_b, _, dattn, out, rsb, coefb = refs
        total = sum_a[...] + sum_b[...]
        rs = lax.rsqrt(total[0:1, :] / channels + EPSILON)
        coef = total[1:2, :] * (rs * rs * rs) / channels
        down = jnp.concatenate([rs, coef, jnp.zeros((HEAD - 2, BLOCK), F32)], axis=0).T
        rsb[...] = jnp.broadcast_to(down[:, 0:1], (BLOCK, HEAD))
        coefb[...] = jnp.broadcast_to(down[:, 1:2], (BLOCK, HEAD))
    for y in range(2):
        items = []
        for j, h, count, cols in several(quarter_of(y, same), hq):
            parts = []
            for m in range(count):
                _, c = head_at(quarter_of(y, same), hq, j + m)
                gsum = jnp.zeros((8, HEAD), F32)
                for i in range(BLOCK // HEAD):
                    r = chunk(i)
                    a = att[r, c]
                    t = dscaled[r, c] * rsb[r, :]
                    dattn[r, c] = (t - a * coefb[r, :]).astype(BF16)
                    gsum = gsum + jnp.sum((t * a).reshape(HEAD // 8, 8, HEAD), axis=0)
                parts.append(jnp.sum(gsum, axis=0, keepdims=True) / gain[:, c])
            both = nn(turned[pl.ds(pl.multiple_of(h * HEAD, HEAD), count * HEAD), :], dattn[:, cols])
            for m in range(count):
                edge = jnp.broadcast_to(row[pl.ds(h + m, 1), :][:, BLOCK - 1 : BLOCK], (1, HEAD))
                items.append((both[chunk(m), chunk(m)], edge, parts[m]))
        (write_wide if same else write_narrow)(out.at[y], hq, items)


def leave(out, ref, sems, g, w):
    cols = pl.ds(pl.multiple_of(g * w, HEAD), w)
    copy = pltpu.make_async_copy(out, ref.at[:, cols], sems)
    copy.start()
    return copy


def unscaled_gate_body(heads, gate, att, dscaled, out):
    hq = heads // TEAM
    for g in range(TEAM):
        for j in range(hq):
            _, c = head_at(g, hq, j)
            closed = jax.nn.sigmoid(-gate[:, c].astype(F32))
            out[:, c] = dscaled[:, c] * att[:, c] * closed


def gate_body(heads, unscaled, scale, _, gate_grad, token, out, sems):
    hq = heads // TEAM
    token[...] = jnp.zeros_like(token)
    copies = []
    for g in range(TEAM):
        for j in range(hq):
            _, c = head_at(g, hq, j)
            out[g, :, chunk(j)] = (unscaled[:, c] * scale[...]).astype(BF16)
        copies.append(leave(out.at[g], gate_grad, sems.at[g], g, hq * HEAD))
    for copy in copies:
        copy.wait()


def by_quarter(mine, got):
    return [(ref.at[y], quarter_of(y, same)) for ref, same in ((mine, True), (got, False)) for y in range(2)]


def query_body(heads, k, v, dattn, row, col, growth, mine, got, _, query_grad, token, out, sems):
    hq = heads // TEAM
    token[...] = jnp.zeros_like(token)
    copies = []
    for slot, (state, g) in enumerate(by_quarter(mine, got)):
        for j, first, count, cols in several(g, hq):
            both = nt(dattn[:, cols], states_of(state, j, count))
            for m in range(count):
                h, c = head_at(g, hq, j + m)
                line = row[pl.ds(h, 1), :]
                for i in range(2):
                    d = dattn[half(i), c]
                    u = slice(0, (i + 1) * HALF)
                    table = decay_table(col[g, half(i), j + m : j + m + 1], line[:, u], True)
                    dscores = (nt(d, v[u, c]) * table).astype(BF16)
                    inter = both[half(i), chunk(m)] * growth[g, half(i), j + m : j + m + 1]
                    out[slot, half(i), chunk(j + m)] = (inter + nn(dscores, k[u, c])).astype(BF16)
        copies.append(leave(out.at[slot], query_grad, sems.at[slot], g, hq * HEAD))
    for copy in copies:
        copy.wait()


def key_value_body(heads, first, last, q, v, dattn, table0, table1, probs0, probs1, _, *refs):
    hq = heads // TEAM
    count = min(hq, 2)
    dk, dv = refs[-2:]

    def one(step, _):
        for m in range(count):
            h = step * count + m
            _, c = head_at(h, 1, 0)
            for i, (table, probs) in enumerate(((table0, probs0), (table1, probs1))):
                t = slice(i * HALF, BLOCK)
                dscores = (nt(v[half(i), c], dattn[t, c]) * table[h]).astype(BF16)
                dk[half(i), c] = nn(dscores, q[t, c])
                dv[half(i), c] = nn(probs[h], dattn[t, c])
        return 0

    lax.fori_loop(first, last, one, 0)


def fades(col, y, same):
    sums = col[quarter_of(y, same)]
    return jnp.exp(sums[BLOCK - 1 : BLOCK, :] - sums)


def final_rows(hq, y, j, count, c, k, v, dk, dv, shrink, state, key_out, value_out):
    after = states_of(state.at[y], j, count)
    key_side, value_side = nt(v[:, c], after), nn(k[:, c], after)
    for m in range(count):
        fade = shrink[:, j + m : j + m + 1]
        own = pl.ds(pl.multiple_of(c.start + m * HEAD, HEAD), HEAD)
        key_out[y, :, chunk(j + m)] = (dk[:, own] + key_side[:, chunk(m)] * fade).astype(BF16)
        value_out[y, :, chunk(j + m)] = (dv[:, own] + value_side[:, chunk(m)] * fade).astype(BF16)


def own_final_body(heads, k, v, dk, dv, col, state, key_out, value_out, gain_grad):
    hq = heads // TEAM
    for y in range(2):
        items = read_narrow(state.at[y], hq)
        shrink = fades(col, y, True)
        for j, _, count, c in several(quarter_of(y, True), hq):
            final_rows(hq, y, j, count, c, k, v, dk, dv, shrink, state, key_out, value_out)
            for m in range(j, j + count):
                gain_grad[:, head_at(quarter_of(y, True), hq, m)[1]] = items[m][2]


def final_body(heads, k, v, dk, dv, col, state, own_key, own_value, own_gain, *refs):
    hq = heads // TEAM
    key_grad, value_grad, gain_grad, key_out, value_out, sems = refs
    copies = []

    def send(src, dst, cols):
        copy = pltpu.make_async_copy(src, dst.at[:, cols], sems.at[len(copies)])
        copy.start()
        copies.append(copy)

    for y in range(2):
        for j, _, count, c in several(quarter_of(y, True), hq):
            place = slice(j * HEAD, (j + count) * HEAD)
            send(own_key.at[y, :, place], key_grad, c)
            send(own_value.at[y, :, place], value_grad, c)
    gain_grad[...] = own_gain[...]
    for y in range(2):
        items = read_narrow(state.at[y], hq)
        shrink = fades(col, y, False)
        for j, _, count, c in several(quarter_of(y, False), hq):
            final_rows(hq, y, j, count, c, k, v, dk, dv, shrink, state, key_out, value_out)
            for m in range(j, j + count):
                gain_grad[:, head_at(quarter_of(y, False), hq, m)[1]] = items[m][2]
            place = slice(j * HEAD, (j + count) * HEAD)
            send(key_out.at[y, :, place], key_grad, c)
            send(value_out.at[y, :, place], value_grad, c)
    for copy in copies:
        copy.wait()


def in_hbm(x):
    return pltpu.with_memory_space_constraint(x, pltpu.HBM)


def swap(x, bit):
    n = lax.axis_size("ctx")
    return lax.ppermute(x, "ctx", [(i, i ^ bit) for i in range(n)])


def local(queries, keys, values, log_decay, gate, gain, grad_out):
    rows, width = queries.shape
    heads = width // HEAD
    hq = heads // TEAM
    tp = lax.axis_size("tp")
    n = lax.axis_size("ctx")
    groups = n // TEAM
    channels = width * tp
    bf = lambda *shape: jax.ShapeDtypeStruct(shape, BF16)
    f32 = lambda *shape: jax.ShapeDtypeStruct(shape, F32)
    swaps = tp == 2
    part = rows // 2
    small = 2 * heads * rows * HEAD * HEAD
    large = 2 * heads * rows * rows * HEAD
    wide = f32(hq * HEAD + SIDE, HEAD)
    wide2 = f32(2, hq * HEAD + SIDE, HEAD)
    narrow = bf(hq * HEAD + EXTRA, HEAD)
    narrow2 = bf(2, hq * HEAD + EXTRA, HEAD)
    table = f32(TEAM, rows, HEAD)
    gain_row = gain.reshape(1, width)

    def beside(work, after, name):
        return [work[name](after)] if name in work else []

    def step_call(body, reverse, inputs, unread, shapes, name, *sizes):
        return call(
            functools.partial(body, reverse, hq, *sizes),
            [*inputs, *unread],
            shapes,
            name,
            in_specs=[VMEM] * len(inputs) + [ANY] * len(unread),
        )

    def scan(reverse, keep, give, work):
        got = swap(give, 1)
        own, send = step_call(chip_total_body, reverse, [keep, got], [], [wide, narrow], "chip_total")
        got_pair = swap(send, 2)
        unread = beside(work, send, "pair")
        total, send = step_call(group_total_body, reverse, [own, got_pair], unread, [wide, narrow], "group_total")
        so_far, step = total, 1
        while 2 * step < groups:
            far = swap(send, TEAM * step)
            unread = beside(work, send, "one") if step == 1 else []
            before = [] if step == 1 else [so_far]
            so_far, total, send = step_call(
                window_body, reverse, [total, *before, far], unread, [wide, wide, narrow], "window", step
            )
            step *= 2
        far = swap(send, TEAM * step)
        unread = beside(work, send, "last")
        kept, send = step_call(
            into_chips_body, reverse, [own, got_pair, total, so_far, far], unread, [wide, narrow], "into_chips", step
        )
        other = swap(send, 2)
        unread = beside(work, send, "pair_back")
        mine, send = step_call(
            into_cores_body, reverse, [keep, got, kept, other], unread, [narrow2, narrow2], "into_cores"
        )
        return mine, swap(send, 1)

    outs = call(
        functools.partial(sent_states_body, heads, swaps),
        [in_hbm(keys), in_hbm(values), in_hbm(log_decay)] + [in_hbm(grad_out)] * swaps,
        [wide2, f32(EXTRA, rows), bf(rows, width), bf(rows, width)] + [bf(part, width)] * swaps,
        "sent_states",
        [
            pltpu.VMEM(log_decay.shape, F32),
            pltpu.SemaphoreType.DMA((2, TEAM)),
            pltpu.SemaphoreType.DMA((2,)),
        ],
        small // 2,
        [HBM] * (3 + swaps),
        [VMEM] * 4 + [HBM] * swaps,
    )
    give, row, keys, values = outs[:4]
    if swaps:
        arrived = lax.ppermute(outs[4], "tp", [(0, 1), (1, 0)])
        own = grad_out
    else:
        every = lax.all_to_all(grad_out, "tp", split_axis=1, concat_axis=0, tiled=True)
        own, arrived = every[:part], every[part:]
    (keep,) = call(
        functools.partial(kept_states_body, heads), [keys, values, row], [wide2], "kept_states", flops=small // 2
    )
    done = {}

    def probs_beside(after):
        if "decays" not in done:
            *done["decays"], done["queries"] = call(
                functools.partial(decays_body, heads),
                [row, in_hbm(queries), after],
                [table] * 2 + [bf(rows, width)],
                "decays",
                [pltpu.SemaphoreType.DMA(())],
                in_specs=[VMEM, HBM, ANY],
            )
        before = done.get("probs", [])
        done["probs"] = call(
            functools.partial(turned_probs_body, heads, TEAM // 2 if before else 0),
            [done["queries"], keys, row, done["decays"][0], after, *before],
            [f32(heads, HALF, BLOCK), f32(heads, HALF, HALF), bf(heads, HALF, BLOCK), bf(heads, HALF, HALF)],
            "turned_probs",
            flops=large // 2,
            in_specs=[VMEM] * 4 + [ANY] + [VMEM] * len(before),
            alias={5 + i: i for i in range(len(before))},
        )
        return done["probs"][3]

    def intra_beside(after):
        before = [done["intra"]] if "intra" in done else []
        first, last = (1, TEAM) if before else (0, 1)
        (done["intra"],) = call(
            functools.partial(intra_body, heads, first, last),
            [done["queries"], keys, values, row, done["decays"][0], after, *before],
            [f32(rows, width)],
            "intra",
            flops=2 * large * (last - first) // TEAM,
            in_specs=[VMEM] * 5 + [ANY] + [VMEM] * len(before),
            alias={6: 0} if before else None,
        )
        return done["intra"]

    def probs_and_intra(after):
        return intra_beside(probs_beside(after))

    def dscaled_beside(after):
        done["dscaled"] = call(
            functools.partial(own_dscaled_body, heads, swaps),
            [gate, in_hbm(own), gain_row, done["queries"], row, after],
            [f32(rows, width), bf(width, rows)],
            "own_dscaled",
            [pltpu.VMEM((part, width), BF16), pltpu.SemaphoreType.DMA(())],
            small,
            [VMEM, HBM, VMEM, VMEM, VMEM, ANY],
        )
        (dscaled,) = call(
            functools.partial(got_dscaled_body, heads, swaps),
            [gate, arrived, gain_row, done["dscaled"][0]],
            [f32(rows, width)],
            "got_dscaled",
            alias={3: 0},
        )
        done["dscaled"] = dscaled, done["dscaled"][1]
        return dscaled

    work = {"pair": probs_beside, "one": probs_and_intra, "last": intra_beside, "pair_back": dscaled_beside}
    mine, got = scan(False, keep, give, work)
    queries = done["queries"]
    (col, growth), intra, (dscaled, turned) = done["decays"], done["intra"], done["dscaled"]
    tall = f32(rows, HEAD)
    wide_scratch = pltpu.VMEM((rows, 2 * HEAD), F32)
    att, squares, inner = call(
        functools.partial(attention_body, heads, True),
        [queries, intra, dscaled, growth, mine],
        [f32(rows, width), tall, tall],
        "attention",
        [wide_scratch],
        small // 2,
    )
    att, sums = call(
        functools.partial(attention_body, heads, False),
        [queries, intra, dscaled, growth, got, att, squares, inner],
        [f32(rows, width), f32(8, rows)],
        "attention",
        [pltpu.VMEM((rows, HEAD), F32)] * 2 + [wide_scratch],
        small // 2,
        alias={5: 0},
    )
    (unscaled_gate,) = call(
        functools.partial(unscaled_gate_body, heads), [gate, att, dscaled], [f32(rows, width)], "unscaled_gate"
    )
    if swaps:
        others = lax.ppermute(sums, "tp", [(0, 1), (1, 0)])
    else:
        others = lax.psum(sums, "tp") - sums
    dattn, give, scale, coef = call(
        functools.partial(dattn_body, heads, channels, False),
        [att, dscaled, turned, gain_row, row, sums, others, unscaled_gate],
        [bf(rows, width), narrow2, tall, tall],
        "sent_dattn",
        flops=small // 2,
        in_specs=[VMEM] * 7 + [ANY],
    )
    dattn, keep = call(
        functools.partial(dattn_body, heads, channels, True),
        [att, dscaled, turned, gain_row, row, scale, coef, dattn],
        [bf(rows, width), wide2],
        "kept_dattn",
        flops=small // 2,
        alias={7: 0},
    )
    out_scratch = [pltpu.VMEM((TEAM, rows, hq * HEAD), BF16), pltpu.SemaphoreType.DMA((TEAM,))]

    def gate_beside(after):
        done["gate"], token = call(
            functools.partial(gate_body, heads),
            [unscaled_gate, scale, after],
            [bf(rows, width), f32(SIDE, HEAD)],
            "gate",
            out_scratch,
            small,
            [VMEM] * 2 + [ANY],
            [HBM, VMEM],
        )
        return token

    units = heads // min(hq, 2)
    cuts = [0, units // 4, (5 * units) // 8, units]

    def key_value_beside(after):
        before = done.get("key_value", [])
        piece = done.get("piece", 0)
        done["piece"] = piece + 1
        done["key_value"] = call(
            functools.partial(key_value_body, heads, cuts[piece], cuts[piece + 1]),
            [queries, values, dattn, *done["probs"], after, *before],
            [f32(rows, width)] * 2,
            "key_value",
            flops=4 * large * (cuts[piece + 1] - cuts[piece]) // units,
            in_specs=[VMEM] * 7 + [ANY] + [VMEM] * len(before),
            alias={8 + i: i for i in range(len(before))},
        )
        return done["key_value"][0]

    def gate_and_key_value(after):
        return key_value_beside(gate_beside(after))

    def query_beside(after):
        done["query"], token = call(
            functools.partial(query_body, heads),
            [keys, values, dattn, row, col, growth, mine, got, after],
            [bf(rows, width), f32(SIDE, HEAD)],
            "query",
            out_scratch,
            2 * large + small,
            [VMEM] * 8 + [ANY],
            [HBM, VMEM],
        )
        return token

    work = {"pair": gate_and_key_value, "one": key_value_beside, "last": query_beside, "pair_back": key_value_beside}
    back_mine, back_got = scan(True, keep, give, work)
    gate_grad, query_grad, (dk, dv) = done["gate"], done["query"], done["key_value"]
    both = bf(2, rows, hq * HEAD)
    own_key, own_value, own_gain = call(
        functools.partial(own_final_body, heads),
        [keys, values, dk, dv, col, back_mine],
        [both, both, f32(1, width)],
        "own_final",
        flops=small,
    )
    key_grad, value_grad, gain_grad = call(
        functools.partial(final_body, heads),
        [keys, values, dk, dv, col, back_got, own_key, own_value, own_gain],
        [bf(rows, width), bf(rows, width), f32(1, width)],
        "final",
        [pltpu.VMEM(both.shape, BF16)] * 2 + [pltpu.SemaphoreType.DMA((8 * hq,))],
        small,
        out_specs=[HBM, HBM, VMEM],
    )
    return query_grad, key_grad, value_grad, gate_grad, gain_grad.reshape(width)


def solution(mesh):
    return jax.shard_map(
        local,
        mesh=mesh,
        in_specs=(
            P("ctx", "tp"),
            P("ctx", "tp"),
            P("ctx", "tp"),
            P("tp", "ctx"),
            P("ctx", "tp"),
            P("tp"),
            P(("ctx", "tp"), None),
        ),
        out_specs=(P("ctx", "tp"), P("ctx", "tp"), P("ctx", "tp"), P("ctx", "tp"), P("tp")),
        check_vma=False,
    )
```

```python
import functools

import jax
import jax.numpy as jnp
from jax import lax
from jax.experimental import pallas as pl
from jax.experimental.pallas import tpu as pltpu
from jax.sharding import PartitionSpec as P

HEAD = 128
BLOCK = 512
HALF = BLOCK // 2
TEAM = 4
SIDE = 8
EXTRA = 16
EPSILON = 1e-06
F32 = jnp.float32
BF16 = jnp.bfloat16
GRANT = 5 * 1024 * 1024
VMEM = pl.BlockSpec(memory_space=pltpu.VMEM)
HBM = pl.BlockSpec(memory_space=pltpu.HBM)
ANY = pl.BlockSpec(memory_space=pl.ANY)


def nt(a, b, precision=None):
    return lax.dot_general(a, b, (((1,), (1,)), ((), ())), preferred_element_type=F32, precision=precision)


def nn(a, b):
    return lax.dot_general(a, b, (((1,), (0,)), ((), ())), preferred_element_type=F32)


def half(i):
    return slice(i * HALF, (i + 1) * HALF)


def chunk(i):
    return slice(i * HEAD, (i + 1) * HEAD)


def split_terms(x, count):
    terms = []
    for _ in range(count):
        term = x.astype(BF16)
        terms.append(term)
        x = x - term.astype(F32)
    return terms


def read_wide(ref, hq):
    base = hq * HEAD
    return [
        (ref[chunk(j), :], ref[base + j : base + j + 1, :], ref[base + TEAM + j : base + TEAM + j + 1, :])
        for j in range(hq)
    ]


def write_wide(ref, hq, items):
    base = hq * HEAD
    at = lax.broadcasted_iota(jnp.int32, (SIDE, HEAD), 0)
    side = jnp.zeros((SIDE, HEAD), F32)
    for j, (term, edge, gain) in enumerate(items):
        ref[chunk(j), :] = term
        side = jnp.where(at == j, edge, side)
        side = jnp.where(at == TEAM + j, gain, side)
    ref[base : base + SIDE, :] = side


def read_narrow(ref, hq):
    base = hq * HEAD
    side = ref[base : base + EXTRA, :].astype(F32)
    row = lambda i: side[i : i + 1, :] + side[i + 1 : i + 2, :]
    return [(ref[chunk(j), :].astype(F32), row(2 * j), row(2 * TEAM + 2 * j)) for j in range(hq)]


def write_narrow(ref, hq, items):
    base = hq * HEAD
    at = lax.broadcasted_iota(jnp.int32, (EXTRA, HEAD), 0)
    side = jnp.zeros((EXTRA, HEAD), F32)
    for j, (term, edge, gain) in enumerate(items):
        ref[chunk(j), :] = term.astype(BF16)
        for first, value in ((2 * j, edge), (2 * TEAM + 2 * j, gain)):
            for i, part in enumerate(split_terms(value, 2)):
                side = jnp.where(at == first + i, part.astype(F32), side)
    ref[base : base + EXTRA, :] = side.astype(BF16)


def core():
    return lax.rem(lax.axis_index("ctx"), 2)


def pair():
    return lax.rem(lax.axis_index("ctx") // 2, 2)


def group():
    return lax.axis_index("ctx") // TEAM


def quarter_of(y, same):
    return 2 * y + (core() if same else 1 - core())


def head_at(quarter, hq, j):
    h = quarter * hq + j
    return h, pl.ds(pl.multiple_of(h * HEAD, HEAD), HEAD)


def transposed(x):
    shape = (x.shape[1], x.shape[1])
    eye = (lax.broadcasted_iota(jnp.int32, shape, 0) == lax.broadcasted_iota(jnp.int32, shape, 1)).astype(BF16)
    return nt(eye, x)


def several(quarter, hq):
    count = min(hq, 2)
    for j in range(0, hq, count):
        h = quarter * hq + j
        yield j, h, count, pl.ds(pl.multiple_of(h * HEAD, HEAD), count * HEAD)


def call(body, inputs, out_shape, name, scratch=(), flops=0, in_specs=None, out_specs=None, alias=None):
    nbytes = sum(x.size * x.dtype.itemsize for x in inputs)
    nbytes += sum(x.size * x.dtype.itemsize for x in out_shape)
    return pl.pallas_call(
        body,
        in_specs=in_specs or [VMEM] * len(inputs),
        out_specs=out_specs or [VMEM] * len(out_shape),
        out_shape=out_shape,
        scratch_shapes=list(scratch),
        input_output_aliases=alias or {},
        compiler_params=pltpu.CompilerParams(vmem_limit_bytes=GRANT),
        cost_estimate=pl.CostEstimate(flops=flops, bytes_accessed=nbytes, transcendentals=0),
        name=name,
    )(*inputs)


def joined(mine, other, mine_is_first, reverse):
    out = []
    for (a, ea, ga), (b, eb, gb) in zip(mine, other):
        near = mine_is_first if reverse else jnp.logical_not(mine_is_first)
        wa = jnp.where(near, 1.0, jnp.exp(eb))
        wb = jnp.where(near, jnp.exp(ea), 1.0)
        out.append((a * wa + b * wb, ea + eb, ga + gb))
    return out


def chip_total_body(reverse, hq, keep, got, own, send):
    first = core() == 0
    read_got = read_narrow if reverse else read_wide
    here, there = pair(), 1 - pair()
    own_items = joined(read_wide(keep.at[here], hq), read_got(got.at[here], hq), first, reverse)
    write_wide(own, hq, own_items)
    send_items = joined(read_wide(keep.at[there], hq), read_got(got.at[there], hq), first, reverse)
    write_narrow(send, hq, send_items)


def group_total_body(reverse, hq, own, got, *refs):
    total, send = refs[-2:]
    items = joined(read_wide(own, hq), read_narrow(got, hq), pair() == 0, reverse)
    write_wide(total, hq, items)
    write_narrow(send, hq, items)


def met(reverse, step, before, other):
    near = lax.rem(group() // step, 2) == (0 if reverse else 1)
    out = []
    for old, (term, edge, gain) in zip(before, other):
        term = jnp.where(near, term, 0.0)
        edge = jnp.where(near, edge, 0.0)
        if old is None:
            out.append((term, edge, gain))
        else:
            out.append((old[0] + jnp.exp(old[1]) * term, old[1] + edge, gain))
    return out


def window_body(reverse, hq, step, total, *refs):
    so_far, whole, send = refs[-3:]
    if step == 1:
        got = refs[0]
        before = [None] * hq
    else:
        got = refs[1]
        before = read_wide(refs[0], hq)
    other = read_narrow(got, hq)
    write_wide(so_far, hq, met(reverse, step, before, other))
    items = joined(read_wide(total, hq), other, lax.rem(group() // step, 2) == 0, reverse)
    write_wide(whole, hq, items)
    write_narrow(send, hq, items)


def into_chips_body(reverse, hq, step, own, got_pair, total, so_far, got, *refs):
    keep, send = refs[-2:]
    before = read_wide(so_far, hq) if step > 1 else [None] * hq
    entering = met(reverse, step, before, read_narrow(got, hq))
    mine_near = pair() == (1 if reverse else 0)
    kept, sent = [], []
    for (r, _, gr), (c, ec, _), (o, eo, _), (_, _, gt) in zip(
        entering, read_wide(own, hq), read_narrow(got_pair, hq), read_wide(total, hq)
    ):
        gain = gr + gt
        zero = jnp.zeros_like(ec)
        kept.append((jnp.where(mine_near, r, jnp.exp(eo) * r + o), zero, gain))
        sent.append((jnp.where(mine_near, jnp.exp(ec) * r + c, r), zero, gain))
    write_wide(keep, hq, kept)
    write_narrow(send, hq, sent)


def into_cores_body(reverse, hq, keep, got, own, other, *refs):
    mine, send = refs[-2:]
    mine_near = core() == (1 if reverse else 0)
    read_got = read_narrow if reverse else read_wide
    for y in range(2):
        a, b = read_wide(own, hq), read_narrow(other, hq)
        here = pair() == y
        items_mine, items_send = [], []
        for p, q, (k, ek, _), (g, eg, _) in zip(a, b, read_wide(keep.at[y], hq), read_got(got.at[y], hq)):
            r = jnp.where(here, p[0], q[0])
            gain = jnp.where(here, p[2], q[2])
            zero = jnp.zeros_like(ek)
            items_mine.append((jnp.where(mine_near, r, jnp.exp(eg) * r + g), zero, gain))
            items_send.append((jnp.where(mine_near, jnp.exp(ek) * r + k, r), zero, gain))
        write_narrow(mine.at[y], hq, items_mine)
        write_narrow(send.at[y], hq, items_send)


def block_states(hq, y, same, k, v, row, out):
    items = []
    for j, h, count, c in several(quarter_of(y, same), hq):
        turned = transposed(k[:, c])
        lines = [row[pl.ds(h + m, 1), :] for m in range(count)]
        edges = [line[:, BLOCK - 1 : BLOCK] for line in lines]
        faded = [turned[chunk(m)] * jnp.exp(edges[m] - lines[m]) for m in range(count)]
        both = nn(jnp.concatenate([x.astype(BF16) for x in faded], axis=0), v[:, c])
        for m in range(count):
            items.append((both[chunk(m), chunk(m)], jnp.broadcast_to(edges[m], (1, HEAD)), jnp.zeros((1, HEAD), F32)))
    write_wide(out.at[y], hq, items)


def sent_states_body(heads, swaps, k_hbm, v_hbm, ld_hbm, *refs):
    hq = heads // TEAM
    w = hq * HEAD
    if swaps:
        grad, give, row, k, v, away, ld, sems, side_sems = refs
        width = heads * HEAD
        there = pl.ds(pl.multiple_of((1 - lax.axis_index("tp")) * width, HEAD), width)
        side_copies = [pltpu.make_async_copy(grad.at[:, there], away, side_sems.at[1])]
    else:
        give, row, k, v, ld, sems, side_sems = refs
        side_copies = []
    first = pltpu.make_async_copy(ld_hbm, ld, side_sems.at[0])
    first.start()
    order = [(0, False), (1, False), (0, True), (1, True)]
    copies = []
    for slot, (y, same) in enumerate(order):
        cols_d = pl.ds(pl.multiple_of(quarter_of(y, same) * w, HEAD), w)
        both = [
            pltpu.make_async_copy(k_hbm.at[:, cols_d], k.at[:, cols_d], sems.at[0, slot]),
            pltpu.make_async_copy(v_hbm.at[:, cols_d], v.at[:, cols_d], sems.at[1, slot]),
        ]
        for c in both:
            c.start()
        copies.append(both)
    for c in side_copies:
        c.start()
    at = lax.broadcasted_iota(jnp.int32, (BLOCK, BLOCK), 0)
    other = lax.broadcasted_iota(jnp.int32, (BLOCK, BLOCK), 1)
    tri = (at <= other).astype(BF16)
    first.wait()
    x = ld[...]
    if heads < EXTRA:
        x = jnp.concatenate([x, jnp.zeros((EXTRA - heads, BLOCK), F32)], axis=0)
    sums = nn(jnp.concatenate(split_terms(x, 3), axis=0), tri)
    row[...] = sums[0:EXTRA] + (sums[EXTRA : 2 * EXTRA] + sums[2 * EXTRA : 3 * EXTRA])
    for slot, (y, same) in enumerate(order):
        for c in copies[slot]:
            c.wait()
        if not same:
            block_states(hq, y, same, k, v, row, give)
    for c in side_copies:
        c.wait()


def kept_states_body(heads, k, v, row, keep):
    for y in range(2):
        block_states(heads // TEAM, y, True, k, v, row, keep)


def decays_body(heads, row, q_hbm, _, col, growth, q, sem):
    hq = heads // TEAM
    copy = pltpu.make_async_copy(q_hbm, q, sem)
    copy.start()
    for g in range(TEAM):
        rows = row[g * hq : (g + 1) * hq, :]
        across = jnp.concatenate([rows, jnp.zeros((HEAD - hq, BLOCK), F32)], axis=0).T
        col[g] = across
        growth[g] = jnp.exp(across)
    copy.wait()


def decay_table(high, low, lower):
    table = jnp.exp(high - low)
    at = lax.broadcasted_iota(jnp.int32, (HALF, HALF), 0)
    other = lax.broadcasted_iota(jnp.int32, (HALF, HALF), 1)
    if lower:
        cut = jnp.where(at >= other, table[:, -HALF:], 0.0)
        return cut if table.shape[1] == HALF else jnp.concatenate([table[:, :HALF], cut], axis=1)
    cut = jnp.where(at <= other, table[:, :HALF], 0.0)
    return cut if table.shape[1] == HALF else jnp.concatenate([cut, table[:, HALF:]], axis=1)


def turned_probs_body(heads, first, q, k, row, col, _, *refs):
    hq = heads // TEAM
    tables, probs = refs[-4:-2], refs[-2:]

    def one(g, _):
        for j in range(hq):
            h, c = head_at(g, hq, j)
            line = row[pl.ds(h, 1), :]
            for i in range(2):
                t = slice(i * HALF, BLOCK)
                table = decay_table(line[:, t], col[g, half(i), j : j + 1], False)
                tables[i][h] = table
                probs[i][h] = (nt(k[half(i), c], q[t, c]) * table).astype(BF16)
        return 0

    lax.fori_loop(first, first + TEAM // 2, one, 0)


def intra_body(heads, first, last, q, k, v, row, col, *refs):
    hq = heads // TEAM
    intra = refs[-1]

    def one(g, _):
        for j in range(hq):
            h, c = head_at(g, hq, j)
            line = row[pl.ds(h, 1), :]
            for i in range(2):
                u = slice(0, (i + 1) * HALF)
                table = decay_table(col[g, half(i), j : j + 1], line[:, u], True)
                probs = (nt(q[half(i), c], k[u, c]) * table).astype(BF16)
                intra[half(i), c] = nn(probs, v[u, c])
        return 0

    lax.fori_loop(first, last, one, 0)


def dscaled_rows(heads, where, gate, ref, gain, dscaled):
    part = ref.shape[0]
    rows = pl.ds(pl.multiple_of(where * part, part), part)

    def one(g, _):
        for j in range(heads // TEAM):
            _, c = head_at(g, heads // TEAM, j)
            opened = jax.nn.sigmoid(gate[rows, c].astype(F32))
            dscaled[rows, c] = ref[:, c].astype(F32) * opened * gain[:, c]
        return 0

    lax.fori_loop(0, TEAM, one, 0)


def own_dscaled_body(heads, swaps, gate, grad, gain, q, row, _, dscaled, turned, own, sem):
    width = heads * HEAD
    mine = lax.axis_index("tp") if swaps else 0
    here = pl.ds(pl.multiple_of(mine * width, HEAD), width)
    copy = pltpu.make_async_copy(grad.at[:, here], own, sem)
    copy.start()

    def one(g, _):
        for j, h, count, c in several(g, heads // TEAM):
            both = transposed(q[:, c])
            for m in range(count):
                rows = pl.ds(pl.multiple_of((h + m) * HEAD, HEAD), HEAD)
                turned[rows, :] = (both[chunk(m)] * jnp.exp(row[pl.ds(h + m, 1), :])).astype(BF16)
        return 0

    lax.fori_loop(0, TEAM, one, 0)
    copy.wait()
    dscaled_rows(heads, mine, gate, own, gain, dscaled)


def got_dscaled_body(heads, swaps, gate, got, gain, _, dscaled):
    dscaled_rows(heads, 1 - lax.axis_index("tp") if swaps else 1, gate, got, gain, dscaled)


def states_of(state, j, count):
    if count == 1:
        return state[chunk(j), :]
    zero = jnp.zeros((HEAD, HEAD), BF16)
    upper = jnp.concatenate([state[chunk(j), :], zero], axis=1)
    lower = jnp.concatenate([zero, state[chunk(j + 1), :]], axis=1)
    return jnp.concatenate([upper, lower], axis=0)


def attention_body(heads, same, q, intra, dscaled, growth, state, *refs):
    hq = heads // TEAM
    if same:
        att, sq, inn, both = refs
    else:
        _, sq_before, inn_before, att, sums, sq, inn, both = refs
        sq[...] = sq_before[...]
        inn[...] = inn_before[...]
    for y in range(2):
        g = quarter_of(y, same)
        for j, h, count, c in several(g, hq):
            both[:, 0 : count * HEAD] = nn(q[:, c], states_of(state.at[y], j, count))
            for i in range(BLOCK // HEAD):
                r = chunk(i)
                a_sq = a_in = 0.0
                for m in range(count):
                    _, c = head_at(g, hq, j + m)
                    a = intra[r, c] + both[r, chunk(m)] * growth[g, r, j + m : j + m + 1]
                    att[r, c] = a
                    a_sq = a_sq + a * a
                    a_in = a_in + a * dscaled[r, c]
                if same and y == 0 and j == 0:
                    sq[r, :] = a_sq
                    inn[r, :] = a_in
                else:
                    sq[r, :] += a_sq
                    inn[r, :] += a_in
    if not same:
        ones = jnp.ones((8, HEAD), F32)
        a = nt(ones, sq[...], lax.Precision.HIGHEST)
        b = nt(ones, inn[...], lax.Precision.HIGHEST)
        sums[...] = jnp.where(lax.broadcasted_iota(jnp.int32, (8, BLOCK), 0) == 0, a, b)


def dattn_body(heads, channels, same, att, dscaled, turned, gain, row, *refs):
    hq = heads // TEAM
    if same:
        rsb, coefb, _, dattn, out = refs
    else:
        sum_a, sum_b, _, dattn, out, rsb, coefb = refs
        total = sum_a[...] + sum_b[...]
        rs = lax.rsqrt(total[0:1, :] / channels + EPSILON)
        coef = total[1:2, :] * (rs * rs * rs) / channels
        down = jnp.concatenate([rs, coef, jnp.zeros((HEAD - 2, BLOCK), F32)], axis=0).T
        rsb[...] = jnp.broadcast_to(down[:, 0:1], (BLOCK, HEAD))
        coefb[...] = jnp.broadcast_to(down[:, 1:2], (BLOCK, HEAD))
    for y in range(2):
        items = []
        for j, h, count, cols in several(quarter_of(y, same), hq):
            parts = []
            for m in range(count):
                _, c = head_at(quarter_of(y, same), hq, j + m)
                gsum = jnp.zeros((8, HEAD), F32)
                for i in range(BLOCK // HEAD):
                    r = chunk(i)
                    a = att[r, c]
                    t = dscaled[r, c] * rsb[r, :]
                    dattn[r, c] = (t - a * coefb[r, :]).astype(BF16)
                    gsum = gsum + jnp.sum((t * a).reshape(HEAD // 8, 8, HEAD), axis=0)
                parts.append(jnp.sum(gsum, axis=0, keepdims=True) / gain[:, c])
            both = nn(turned[pl.ds(pl.multiple_of(h * HEAD, HEAD), count * HEAD), :], dattn[:, cols])
            for m in range(count):
                edge = jnp.broadcast_to(row[pl.ds(h + m, 1), :][:, BLOCK - 1 : BLOCK], (1, HEAD))
                items.append((both[chunk(m), chunk(m)], edge, parts[m]))
        (write_wide if same else write_narrow)(out.at[y], hq, items)


def leave(out, ref, sems, g, w):
    cols = pl.ds(pl.multiple_of(g * w, HEAD), w)
    copy = pltpu.make_async_copy(out, ref.at[:, cols], sems)
    copy.start()
    return copy


def unscaled_gate_body(heads, gate, att, dscaled, _, out):
    hq = heads // TEAM
    for g in range(TEAM):
        for j in range(hq):
            _, c = head_at(g, hq, j)
            closed = jax.nn.sigmoid(-gate[:, c].astype(F32))
            out[:, c] = dscaled[:, c] * att[:, c] * closed


def gate_body(heads, unscaled, scale, _, gate_grad, token, out, sems):
    hq = heads // TEAM
    token[...] = jnp.zeros_like(token)
    copies = []
    for g in range(TEAM):
        for j in range(hq):
            _, c = head_at(g, hq, j)
            out[g, :, chunk(j)] = (unscaled[:, c] * scale[...]).astype(BF16)
        copies.append(leave(out.at[g], gate_grad, sems.at[g], g, hq * HEAD))
    for copy in copies:
        copy.wait()


def by_quarter(mine, got):
    return [(ref.at[y], quarter_of(y, same)) for ref, same in ((mine, True), (got, False)) for y in range(2)]


def query_body(heads, first, last, k, v, dattn, row, col, growth, mine, got, _, *refs):
    hq = heads // TEAM
    query_grad, token, out, sems = refs[-4:]
    token[...] = jnp.zeros_like(token)
    pairs = [(state, g, *pair) for state, g in by_quarter(mine, got) for pair in several(g, hq)]
    copies = []
    for n, (state, g, j, _, count, cols) in enumerate(pairs[first:last]):
        for m in range(count):
            h, c = head_at(g, hq, j + m)
            line = row[pl.ds(h, 1), :]
            for i in range(2):
                d = dattn[half(i), c]
                u = slice(0, (i + 1) * HALF)
                table = decay_table(col[g, half(i), j + m : j + m + 1], line[:, u], True)
                dscores = (nt(d, v[u, c]) * table).astype(BF16)
                inter = nt(d, state[chunk(j + m), :]) * growth[g, half(i), j + m : j + m + 1]
                out[n, half(i), chunk(m)] = (inter + nn(dscores, k[u, c])).astype(BF16)
        copy = pltpu.make_async_copy(out.at[n, :, 0 : count * HEAD], query_grad.at[:, cols], sems.at[n])
        copy.start()
        copies.append(copy)
    for copy in copies:
        copy.wait()


def key_value_body(heads, first, last, q, v, dattn, table0, table1, probs0, probs1, _, *refs):
    hq = heads // TEAM
    count = min(hq, 2)
    dk, dv = refs[-2:]

    def one(step, _):
        for m in range(count):
            h = step * count + m
            _, c = head_at(h, 1, 0)
            for i, (table, probs) in enumerate(((table0, probs0), (table1, probs1))):
                t = slice(i * HALF, BLOCK)
                dscores = (nt(v[half(i), c], dattn[t, c]) * table[h]).astype(BF16)
                dk[half(i), c] = nn(dscores, q[t, c])
                dv[half(i), c] = nn(probs[h], dattn[t, c])
        return 0

    lax.fori_loop(first, last, one, 0)


def fades(col, y, same):
    sums = col[quarter_of(y, same)]
    return jnp.exp(sums[BLOCK - 1 : BLOCK, :] - sums)


def final_rows(hq, y, j, count, c, k, v, dk, dv, shrink, state, key_out, value_out):
    after = states_of(state.at[y], j, count)
    key_side, value_side = nt(v[:, c], after), nn(k[:, c], after)
    for m in range(count):
        fade = shrink[:, j + m : j + m + 1]
        own = pl.ds(pl.multiple_of(c.start + m * HEAD, HEAD), HEAD)
        key_out[:, chunk(j + m)] = (dk[:, own] + key_side[:, chunk(m)] * fade).astype(BF16)
        value_out[:, chunk(j + m)] = (dv[:, own] + value_side[:, chunk(m)] * fade).astype(BF16)


def own_final_body(heads, k, v, dk, dv, col, state, key_grad, value_grad, own_key, own_value, gain_grad, key_out, value_out, sems):
    hq = heads // TEAM
    copies = []
    for y in range(2):
        items = read_narrow(state.at[y], hq)
        shrink = fades(col, y, True)
        for j, _, count, c in several(quarter_of(y, True), hq):
            outs = (key_out, value_out) if y == 0 else (own_key, own_value)
            final_rows(hq, y, j, count, c, k, v, dk, dv, shrink, state, *outs)
            for m in range(j, j + count):
                gain_grad[:, head_at(quarter_of(y, True), hq, m)[1]] = items[m][2]
            if y == 0:
                place = slice(j * HEAD, (j + count) * HEAD)
                for out, dst in ((key_out, key_grad), (value_out, value_grad)):
                    copy = pltpu.make_async_copy(out.at[:, place], dst.at[:, c], sems.at[len(copies)])
                    copy.start()
                    copies.append(copy)
    for copy in copies:
        copy.wait()


def final_body(heads, k, v, dk, dv, col, state, own_key, own_value, own_gain, _key, _value, *refs):
    hq = heads // TEAM
    key_grad, value_grad, gain_grad, key_out, value_out, sems = refs
    copies = []

    def send(src, dst, cols):
        copy = pltpu.make_async_copy(src, dst.at[:, cols], sems.at[len(copies)])
        copy.start()
        copies.append(copy)

    for j, _, count, c in several(quarter_of(1, True), hq):
        place = slice(j * HEAD, (j + count) * HEAD)
        send(own_key.at[:, place], key_grad, c)
        send(own_value.at[:, place], value_grad, c)
    gain_grad[...] = own_gain[...]
    for y in range(2):
        items = read_narrow(state.at[y], hq)
        shrink = fades(col, y, False)
        for j, _, count, c in several(quarter_of(y, False), hq):
            final_rows(hq, y, j, count, c, k, v, dk, dv, shrink, state, key_out.at[y], value_out.at[y])
            for m in range(j, j + count):
                gain_grad[:, head_at(quarter_of(y, False), hq, m)[1]] = items[m][2]
            place = slice(j * HEAD, (j + count) * HEAD)
            send(key_out.at[y, :, place], key_grad, c)
            send(value_out.at[y, :, place], value_grad, c)
    for copy in copies:
        copy.wait()


def in_hbm(x):
    return pltpu.with_memory_space_constraint(x, pltpu.HBM)


def swap(x, bit):
    n = lax.axis_size("ctx")
    return lax.ppermute(x, "ctx", [(i, i ^ bit) for i in range(n)])


def local(queries, keys, values, log_decay, gate, gain, grad_out):
    rows, width = queries.shape
    heads = width // HEAD
    hq = heads // TEAM
    tp = lax.axis_size("tp")
    n = lax.axis_size("ctx")
    groups = n // TEAM
    channels = width * tp
    bf = lambda *shape: jax.ShapeDtypeStruct(shape, BF16)
    f32 = lambda *shape: jax.ShapeDtypeStruct(shape, F32)
    swaps = tp == 2
    part = rows // 2
    small = 2 * heads * rows * HEAD * HEAD
    large = 2 * heads * rows * rows * HEAD
    wide = f32(hq * HEAD + SIDE, HEAD)
    wide2 = f32(2, hq * HEAD + SIDE, HEAD)
    narrow = bf(hq * HEAD + EXTRA, HEAD)
    narrow2 = bf(2, hq * HEAD + EXTRA, HEAD)
    table = f32(TEAM, rows, HEAD)
    gain_row = gain.reshape(1, width)

    def beside(work, after, name):
        return [work[name](after)] if name in work else []

    def step_call(body, reverse, inputs, unread, shapes, name, *sizes):
        return call(
            functools.partial(body, reverse, hq, *sizes),
            [*inputs, *unread],
            shapes,
            name,
            in_specs=[VMEM] * len(inputs) + [ANY] * len(unread),
        )

    def scan(reverse, keep, give, work):
        got = swap(give, 1)
        own, send = step_call(chip_total_body, reverse, [keep, got], [], [wide, narrow], "chip_total")
        got_pair = swap(send, 2)
        unread = beside(work, send, "pair")
        total, send = step_call(group_total_body, reverse, [own, got_pair], unread, [wide, narrow], "group_total")
        so_far, step = total, 1
        while 2 * step < groups:
            far = swap(send, TEAM * step)
            unread = beside(work, send, "one") if step == 1 else []
            before = [] if step == 1 else [so_far]
            so_far, total, send = step_call(
                window_body, reverse, [total, *before, far], unread, [wide, wide, narrow], "window", step
            )
            step *= 2
        far = swap(send, TEAM * step)
        unread = beside(work, send, "last")
        kept, send = step_call(
            into_chips_body, reverse, [own, got_pair, total, so_far, far], unread, [wide, narrow], "into_chips", step
        )
        other = swap(send, 2)
        unread = beside(work, send, "pair_back")
        mine, send = step_call(
            into_cores_body, reverse, [keep, got, kept, other], unread, [narrow2, narrow2], "into_cores"
        )
        return mine, swap(send, 1)

    outs = call(
        functools.partial(sent_states_body, heads, swaps),
        [in_hbm(keys), in_hbm(values), in_hbm(log_decay)] + [in_hbm(grad_out)] * swaps,
        [wide2, f32(EXTRA, rows), bf(rows, width), bf(rows, width)] + [bf(part, width)] * swaps,
        "sent_states",
        [
            pltpu.VMEM(log_decay.shape, F32),
            pltpu.SemaphoreType.DMA((2, TEAM)),
            pltpu.SemaphoreType.DMA((2,)),
        ],
        small // 2,
        [HBM] * (3 + swaps),
        [VMEM] * 4 + [HBM] * swaps,
    )
    give, row, keys, values = outs[:4]
    if swaps:
        arrived = lax.ppermute(outs[4], "tp", [(0, 1), (1, 0)])
        own = grad_out
    else:
        every = lax.all_to_all(grad_out, "tp", split_axis=1, concat_axis=0, tiled=True)
        own, arrived = every[:part], every[part:]
    (keep,) = call(
        functools.partial(kept_states_body, heads), [keys, values, row], [wide2], "kept_states", flops=small // 2
    )
    done = {}

    def probs_beside(after):
        if "decays" not in done:
            *done["decays"], done["queries"] = call(
                functools.partial(decays_body, heads),
                [row, in_hbm(queries), after],
                [table] * 2 + [bf(rows, width)],
                "decays",
                [pltpu.SemaphoreType.DMA(())],
                in_specs=[VMEM, HBM, ANY],
            )
        before = done.get("probs", [])
        done["probs"] = call(
            functools.partial(turned_probs_body, heads, TEAM // 2 if before else 0),
            [done["queries"], keys, row, done["decays"][0], after, *before],
            [f32(heads, HALF, BLOCK), f32(heads, HALF, HALF), bf(heads, HALF, BLOCK), bf(heads, HALF, HALF)],
            "turned_probs",
            flops=large // 2,
            in_specs=[VMEM] * 4 + [ANY] + [VMEM] * len(before),
            alias={5 + i: i for i in range(len(before))},
        )
        return done["probs"][3]

    def intra_beside(after):
        before = [done["intra"]] if "intra" in done else []
        first, last = (1, TEAM) if before else (0, 1)
        (done["intra"],) = call(
            functools.partial(intra_body, heads, first, last),
            [done["queries"], keys, values, row, done["decays"][0], after, *before],
            [f32(rows, width)],
            "intra",
            flops=2 * large * (last - first) // TEAM,
            in_specs=[VMEM] * 5 + [ANY] + [VMEM] * len(before),
            alias={6: 0} if before else None,
        )
        return done["intra"]

    def probs_and_intra(after):
        return intra_beside(probs_beside(after))

    def dscaled_beside(after):
        done["dscaled"] = call(
            functools.partial(own_dscaled_body, heads, swaps),
            [gate, in_hbm(own), gain_row, done["queries"], row, after],
            [f32(rows, width), bf(width, rows)],
            "own_dscaled",
            [pltpu.VMEM((part, width), BF16), pltpu.SemaphoreType.DMA(())],
            small,
            [VMEM, HBM, VMEM, VMEM, VMEM, ANY],
        )
        (dscaled,) = call(
            functools.partial(got_dscaled_body, heads, swaps),
            [gate, arrived, gain_row, done["dscaled"][0]],
            [f32(rows, width)],
            "got_dscaled",
            alias={3: 0},
        )
        done["dscaled"] = dscaled, done["dscaled"][1]
        return dscaled

    work = {"pair": probs_beside, "one": probs_and_intra, "last": intra_beside, "pair_back": dscaled_beside}
    mine, got = scan(False, keep, give, work)
    queries = done["queries"]
    (col, growth), intra, (dscaled, turned) = done["decays"], done["intra"], done["dscaled"]
    tall = f32(rows, HEAD)
    wide_scratch = pltpu.VMEM((rows, 2 * HEAD), F32)
    att, squares, inner = call(
        functools.partial(attention_body, heads, True),
        [queries, intra, dscaled, growth, mine],
        [f32(rows, width), tall, tall],
        "attention",
        [wide_scratch],
        small // 2,
    )
    att, sums = call(
        functools.partial(attention_body, heads, False),
        [queries, intra, dscaled, growth, got, att, squares, inner],
        [f32(rows, width), f32(8, rows)],
        "attention",
        [pltpu.VMEM((rows, HEAD), F32)] * 2 + [wide_scratch],
        small // 2,
        alias={5: 0},
    )
    (unscaled_gate,) = call(
        functools.partial(unscaled_gate_body, heads),
        [gate, att, dscaled, intra],
        [f32(rows, width)],
        "unscaled_gate",
        in_specs=[VMEM] * 3 + [ANY],
        alias={3: 0},
    )
    if swaps:
        others = lax.ppermute(sums, "tp", [(0, 1), (1, 0)])
    else:
        others = lax.psum(sums, "tp") - sums
    dattn, give, scale, coef = call(
        functools.partial(dattn_body, heads, channels, False),
        [att, dscaled, turned, gain_row, row, sums, others, unscaled_gate],
        [bf(rows, width), narrow2, tall, tall],
        "sent_dattn",
        flops=small // 2,
        in_specs=[VMEM] * 7 + [ANY],
    )
    dattn, keep = call(
        functools.partial(dattn_body, heads, channels, True),
        [att, dscaled, turned, gain_row, row, scale, coef, dattn],
        [bf(rows, width), wide2],
        "kept_dattn",
        flops=small // 2,
        alias={7: 0},
    )
    out_scratch = [pltpu.VMEM((TEAM, rows, hq * HEAD), BF16), pltpu.SemaphoreType.DMA((TEAM,))]

    def gate_beside(after):
        done["gate"], token = call(
            functools.partial(gate_body, heads),
            [unscaled_gate, scale, after],
            [bf(rows, width), f32(SIDE, HEAD)],
            "gate",
            out_scratch,
            small,
            [VMEM] * 2 + [ANY],
            [HBM, VMEM],
        )
        return token

    units = heads // min(hq, 2)
    cuts = [0, units // 4, (5 * units) // 8, units]

    def key_value_beside(after):
        before = done.get("key_value", [])
        piece = done.get("piece", 0)
        done["piece"] = piece + 1
        done["key_value"] = call(
            functools.partial(key_value_body, heads, cuts[piece], cuts[piece + 1]),
            [queries, values, dattn, *done["probs"], after, *before],
            [f32(rows, width)] * 2,
            "key_value",
            flops=4 * large * (cuts[piece + 1] - cuts[piece]) // units,
            in_specs=[VMEM] * 7 + [ANY] + [VMEM] * len(before),
            alias={8 + i: i for i in range(len(before))},
        )
        return done["key_value"][0]

    def gate_and_key_value(after):
        return key_value_beside(gate_beside(after))

    pairs = TEAM * hq // min(hq, 2)

    def query_beside(after):
        before = [done["query"]] if "query" in done else []
        first, last = (pairs // 8, pairs) if before else (0, pairs // 8)
        done["query"], token = call(
            functools.partial(query_body, heads, first, last),
            [keys, values, dattn, row, col, growth, mine, got, after, *before],
            [bf(rows, width), f32(SIDE, HEAD)],
            "query",
            [pltpu.VMEM((pairs, rows, 2 * HEAD), BF16), pltpu.SemaphoreType.DMA((pairs,))],
            (2 * large + small) * (last - first) // pairs,
            [VMEM] * 8 + [ANY] + [HBM] * len(before),
            [HBM, VMEM],
            {9: 0} if before else None,
        )
        return token

    def key_value_and_query(after):
        return query_beside(key_value_beside(after))

    work = {"pair": gate_and_key_value, "one": key_value_and_query, "last": query_beside, "pair_back": key_value_beside}
    back_mine, back_got = scan(True, keep, give, work)
    gate_grad, query_grad, (dk, dv) = done["gate"], done["query"], done["key_value"]
    quarter = bf(rows, hq * HEAD)
    scratch = pltpu.VMEM(quarter.shape, BF16)
    key_grad, value_grad, own_key, own_value, own_gain = call(
        functools.partial(own_final_body, heads),
        [keys, values, dk, dv, col, back_mine],
        [bf(rows, width), bf(rows, width), quarter, quarter, f32(1, width)],
        "own_final",
        [scratch, scratch, pltpu.SemaphoreType.DMA((2 * hq,))],
        small,
        out_specs=[HBM, HBM, VMEM, VMEM, VMEM],
    )
    scratch = pltpu.VMEM((2, *quarter.shape), BF16)
    key_grad, value_grad, gain_grad = call(
        functools.partial(final_body, heads),
        [keys, values, dk, dv, col, back_got, own_key, own_value, own_gain, key_grad, value_grad],
        [bf(rows, width), bf(rows, width), f32(1, width)],
        "final",
        [scratch, scratch, pltpu.SemaphoreType.DMA((8 * hq,))],
        small,
        [VMEM] * 9 + [HBM] * 2,
        [HBM, HBM, VMEM],
        {9: 0, 10: 1},
    )
    return query_grad, key_grad, value_grad, gate_grad, gain_grad.reshape(width)


def solution(mesh):
    return jax.shard_map(
        local,
        mesh=mesh,
        in_specs=(
            P("ctx", "tp"),
            P("ctx", "tp"),
            P("ctx", "tp"),
            P("tp", "ctx"),
            P("ctx", "tp"),
            P("tp"),
            P(("ctx", "tp"), None),
        ),
        out_specs=(P("ctx", "tp"), P("ctx", "tp"), P("ctx", "tp"), P("ctx", "tp"), P("tp")),
        check_vma=False,
    )
```

```python
import functools

import jax
import jax.numpy as jnp
from jax import lax
from jax.experimental import pallas as pl
from jax.experimental.pallas import tpu as pltpu
from jax.sharding import PartitionSpec as P

HEAD = 128
BLOCK = 512
HALF = BLOCK // 2
TEAM = 4
SIDE = 8
EXTRA = 16
EPSILON = 1e-06
F32 = jnp.float32
BF16 = jnp.bfloat16
GRANT = 5 * 1024 * 1024
VMEM = pl.BlockSpec(memory_space=pltpu.VMEM)
HBM = pl.BlockSpec(memory_space=pltpu.HBM)
ANY = pl.BlockSpec(memory_space=pl.ANY)


def nt(a, b, precision=None):
    return lax.dot_general(a, b, (((1,), (1,)), ((), ())), preferred_element_type=F32, precision=precision)


def nn(a, b):
    return lax.dot_general(a, b, (((1,), (0,)), ((), ())), preferred_element_type=F32)


def half(i):
    return slice(i * HALF, (i + 1) * HALF)


def chunk(i):
    return slice(i * HEAD, (i + 1) * HEAD)


def split_terms(x, count):
    terms = []
    for _ in range(count):
        term = x.astype(BF16)
        terms.append(term)
        x = x - term.astype(F32)
    return terms


def read_wide(ref, hq):
    base = hq * HEAD
    return [
        (ref[chunk(j), :], ref[base + j : base + j + 1, :], ref[base + TEAM + j : base + TEAM + j + 1, :])
        for j in range(hq)
    ]


def write_wide(ref, hq, items):
    base = hq * HEAD
    at = lax.broadcasted_iota(jnp.int32, (SIDE, HEAD), 0)
    side = jnp.zeros((SIDE, HEAD), F32)
    for j, (term, edge, gain) in enumerate(items):
        ref[chunk(j), :] = term
        side = jnp.where(at == j, edge, side)
        side = jnp.where(at == TEAM + j, gain, side)
    ref[base : base + SIDE, :] = side


def read_narrow(ref, hq):
    base = hq * HEAD
    side = ref[base : base + EXTRA, :].astype(F32)
    row = lambda i: side[i : i + 1, :] + side[i + 1 : i + 2, :]
    return [(ref[chunk(j), :].astype(F32), row(2 * j), row(2 * TEAM + 2 * j)) for j in range(hq)]


def write_narrow(ref, hq, items):
    base = hq * HEAD
    at = lax.broadcasted_iota(jnp.int32, (EXTRA, HEAD), 0)
    side = jnp.zeros((EXTRA, HEAD), F32)
    for j, (term, edge, gain) in enumerate(items):
        ref[chunk(j), :] = term.astype(BF16)
        for first, value in ((2 * j, edge), (2 * TEAM + 2 * j, gain)):
            for i, part in enumerate(split_terms(value, 2)):
                side = jnp.where(at == first + i, part.astype(F32), side)
    ref[base : base + EXTRA, :] = side.astype(BF16)


def core():
    return lax.rem(lax.axis_index("ctx"), 2)


def pair():
    return lax.rem(lax.axis_index("ctx") // 2, 2)


def group():
    return lax.axis_index("ctx") // TEAM


def quarter_of(y, same):
    return 2 * y + (core() if same else 1 - core())


def head_at(quarter, hq, j):
    h = quarter * hq + j
    return h, pl.ds(pl.multiple_of(h * HEAD, HEAD), HEAD)


def transposed(x):
    shape = (x.shape[1], x.shape[1])
    eye = (lax.broadcasted_iota(jnp.int32, shape, 0) == lax.broadcasted_iota(jnp.int32, shape, 1)).astype(BF16)
    return nt(eye, x)


def several(quarter, hq):
    count = min(hq, 2)
    for j in range(0, hq, count):
        h = quarter * hq + j
        yield j, h, count, pl.ds(pl.multiple_of(h * HEAD, HEAD), count * HEAD)


def call(body, inputs, out_shape, name, scratch=(), flops=0, in_specs=None, out_specs=None, alias=None):
    nbytes = sum(x.size * x.dtype.itemsize for x in inputs)
    nbytes += sum(x.size * x.dtype.itemsize for x in out_shape)
    return pl.pallas_call(
        body,
        in_specs=in_specs or [VMEM] * len(inputs),
        out_specs=out_specs or [VMEM] * len(out_shape),
        out_shape=out_shape,
        scratch_shapes=list(scratch),
        input_output_aliases=alias or {},
        compiler_params=pltpu.CompilerParams(vmem_limit_bytes=GRANT),
        cost_estimate=pl.CostEstimate(flops=flops, bytes_accessed=nbytes, transcendentals=0),
        name=name,
    )(*inputs)


def joined(mine, other, mine_is_first, reverse):
    out = []
    for (a, ea, ga), (b, eb, gb) in zip(mine, other):
        near = mine_is_first if reverse else jnp.logical_not(mine_is_first)
        wa = jnp.where(near, 1.0, jnp.exp(eb))
        wb = jnp.where(near, jnp.exp(ea), 1.0)
        out.append((a * wa + b * wb, ea + eb, ga + gb))
    return out


def chip_total_body(reverse, hq, keep, got, own, send):
    first = core() == 0
    read_got = read_narrow if reverse else read_wide
    here, there = pair(), 1 - pair()
    own_items = joined(read_wide(keep.at[here], hq), read_got(got.at[here], hq), first, reverse)
    write_wide(own, hq, own_items)
    send_items = joined(read_wide(keep.at[there], hq), read_got(got.at[there], hq), first, reverse)
    write_narrow(send, hq, send_items)


def group_total_body(reverse, hq, own, got, *refs):
    total, send = refs[-2:]
    items = joined(read_wide(own, hq), read_narrow(got, hq), pair() == 0, reverse)
    write_wide(total, hq, items)
    write_narrow(send, hq, items)


def met(reverse, step, before, other):
    near = lax.rem(group() // step, 2) == (0 if reverse else 1)
    out = []
    for old, (term, edge, gain) in zip(before, other):
        term = jnp.where(near, term, 0.0)
        edge = jnp.where(near, edge, 0.0)
        if old is None:
            out.append((term, edge, gain))
        else:
            out.append((old[0] + jnp.exp(old[1]) * term, old[1] + edge, gain))
    return out


def window_body(reverse, hq, step, total, *refs):
    so_far, whole, send = refs[-3:]
    if step == 1:
        got = refs[0]
        before = [None] * hq
    else:
        got = refs[1]
        before = read_wide(refs[0], hq)
    other = read_narrow(got, hq)
    write_wide(so_far, hq, met(reverse, step, before, other))
    items = joined(read_wide(total, hq), other, lax.rem(group() // step, 2) == 0, reverse)
    write_wide(whole, hq, items)
    write_narrow(send, hq, items)


def into_chips_body(reverse, hq, step, own, got_pair, total, so_far, got, *refs):
    keep, send = refs[-2:]
    before = read_wide(so_far, hq) if step > 1 else [None] * hq
    entering = met(reverse, step, before, read_narrow(got, hq))
    mine_near = pair() == (1 if reverse else 0)
    kept, sent = [], []
    for (r, _, gr), (c, ec, _), (o, eo, _), (_, _, gt) in zip(
        entering, read_wide(own, hq), read_narrow(got_pair, hq), read_wide(total, hq)
    ):
        gain = gr + gt
        zero = jnp.zeros_like(ec)
        kept.append((jnp.where(mine_near, r, jnp.exp(eo) * r + o), zero, gain))
        sent.append((jnp.where(mine_near, jnp.exp(ec) * r + c, r), zero, gain))
    write_wide(keep, hq, kept)
    write_narrow(send, hq, sent)


def into_cores_body(reverse, hq, keep, got, own, other, *refs):
    mine, send = refs[-2:]
    mine_near = core() == (1 if reverse else 0)
    read_got = read_narrow if reverse else read_wide
    for y in range(2):
        a, b = read_wide(own, hq), read_narrow(other, hq)
        here = pair() == y
        items_mine, items_send = [], []
        for p, q, (k, ek, _), (g, eg, _) in zip(a, b, read_wide(keep.at[y], hq), read_got(got.at[y], hq)):
            r = jnp.where(here, p[0], q[0])
            gain = jnp.where(here, p[2], q[2])
            zero = jnp.zeros_like(ek)
            items_mine.append((jnp.where(mine_near, r, jnp.exp(eg) * r + g), zero, gain))
            items_send.append((jnp.where(mine_near, jnp.exp(ek) * r + k, r), zero, gain))
        write_narrow(mine.at[y], hq, items_mine)
        write_narrow(send.at[y], hq, items_send)


def block_states(hq, y, same, k, v, row, out):
    items = []
    for j, h, count, c in several(quarter_of(y, same), hq):
        turned = transposed(k[:, c])
        lines = [row[pl.ds(h + m, 1), :] for m in range(count)]
        edges = [line[:, BLOCK - 1 : BLOCK] for line in lines]
        faded = [turned[chunk(m)] * jnp.exp(edges[m] - lines[m]) for m in range(count)]
        both = nn(jnp.concatenate([x.astype(BF16) for x in faded], axis=0), v[:, c])
        for m in range(count):
            items.append((both[chunk(m), chunk(m)], jnp.broadcast_to(edges[m], (1, HEAD)), jnp.zeros((1, HEAD), F32)))
    write_wide(out.at[y], hq, items)


def sent_states_body(heads, swaps, k_hbm, v_hbm, ld_hbm, *refs):
    hq = heads // TEAM
    w = hq * HEAD
    if swaps:
        grad, give, row, k, v, away, ld, sems, side_sems = refs
        width = heads * HEAD
        there = pl.ds(pl.multiple_of((1 - lax.axis_index("tp")) * width, HEAD), width)
        side_copies = [pltpu.make_async_copy(grad.at[:, there], away, side_sems.at[1])]
    else:
        give, row, k, v, ld, sems, side_sems = refs
        side_copies = []
    first = pltpu.make_async_copy(ld_hbm, ld, side_sems.at[0])
    first.start()
    order = [(0, False), (1, False), (0, True), (1, True)]
    copies = []
    for slot, (y, same) in enumerate(order):
        cols_d = pl.ds(pl.multiple_of(quarter_of(y, same) * w, HEAD), w)
        both = [
            pltpu.make_async_copy(k_hbm.at[:, cols_d], k.at[:, cols_d], sems.at[0, slot]),
            pltpu.make_async_copy(v_hbm.at[:, cols_d], v.at[:, cols_d], sems.at[1, slot]),
        ]
        for c in both:
            c.start()
        copies.append(both)
    for c in side_copies:
        c.start()
    at = lax.broadcasted_iota(jnp.int32, (BLOCK, BLOCK), 0)
    other = lax.broadcasted_iota(jnp.int32, (BLOCK, BLOCK), 1)
    tri = (at <= other).astype(BF16)
    first.wait()
    x = ld[...]
    if heads < EXTRA:
        x = jnp.concatenate([x, jnp.zeros((EXTRA - heads, BLOCK), F32)], axis=0)
    sums = nn(jnp.concatenate(split_terms(x, 3), axis=0), tri)
    row[...] = sums[0:EXTRA] + (sums[EXTRA : 2 * EXTRA] + sums[2 * EXTRA : 3 * EXTRA])
    for slot, (y, same) in enumerate(order):
        for c in copies[slot]:
            c.wait()
        if not same:
            block_states(hq, y, same, k, v, row, give)
    for c in side_copies:
        c.wait()


def kept_states_body(heads, k, v, row, keep):
    for y in range(2):
        block_states(heads // TEAM, y, True, k, v, row, keep)


def decays_body(heads, row, q_hbm, _, col, growth, q, sem):
    hq = heads // TEAM
    copy = pltpu.make_async_copy(q_hbm, q, sem)
    copy.start()
    for g in range(TEAM):
        rows = row[g * hq : (g + 1) * hq, :]
        across = jnp.concatenate([rows, jnp.zeros((HEAD - hq, BLOCK), F32)], axis=0).T
        col[g] = across
        growth[g] = jnp.exp(across)
    copy.wait()


def decay_table(high, low, lower):
    table = jnp.exp(high - low)
    at = lax.broadcasted_iota(jnp.int32, (HALF, HALF), 0)
    other = lax.broadcasted_iota(jnp.int32, (HALF, HALF), 1)
    if lower:
        cut = jnp.where(at >= other, table[:, -HALF:], 0.0)
        return cut if table.shape[1] == HALF else jnp.concatenate([table[:, :HALF], cut], axis=1)
    cut = jnp.where(at <= other, table[:, :HALF], 0.0)
    return cut if table.shape[1] == HALF else jnp.concatenate([cut, table[:, HALF:]], axis=1)


def turned_probs_body(heads, first, q, k, row, col, _, *refs):
    hq = heads // TEAM
    tables, probs = refs[-4:-2], refs[-2:]

    def one(g, _):
        for j in range(hq):
            h, c = head_at(g, hq, j)
            line = row[pl.ds(h, 1), :]
            for i in range(2):
                t = slice(i * HALF, BLOCK)
                table = decay_table(line[:, t], col[g, half(i), j : j + 1], False)
                tables[i][h] = table
                probs[i][h] = (nt(k[half(i), c], q[t, c]) * table).astype(BF16)
        return 0

    lax.fori_loop(first, first + TEAM // 2, one, 0)


def intra_body(heads, first, last, q, k, v, row, col, *refs):
    hq = heads // TEAM
    intra = refs[-1]

    def one(g, _):
        for j in range(hq):
            h, c = head_at(g, hq, j)
            line = row[pl.ds(h, 1), :]
            for i in range(2):
                u = slice(0, (i + 1) * HALF)
                table = decay_table(col[g, half(i), j : j + 1], line[:, u], True)
                probs = (nt(q[half(i), c], k[u, c]) * table).astype(BF16)
                intra[half(i), c] = nn(probs, v[u, c])
        return 0

    lax.fori_loop(first, last, one, 0)


def dscaled_rows(heads, where, gate, ref, gain, dscaled):
    part = ref.shape[0]
    rows = pl.ds(pl.multiple_of(where * part, part), part)

    def one(g, _):
        for j in range(heads // TEAM):
            _, c = head_at(g, heads // TEAM, j)
            opened = jax.nn.sigmoid(gate[rows, c].astype(F32))
            dscaled[rows, c] = ref[:, c].astype(F32) * opened * gain[:, c]
        return 0

    lax.fori_loop(0, TEAM, one, 0)


def own_dscaled_body(heads, swaps, gate, grad, gain, q, row, _, dscaled, turned, own, sem):
    width = heads * HEAD
    mine = lax.axis_index("tp") if swaps else 0
    here = pl.ds(pl.multiple_of(mine * width, HEAD), width)
    copy = pltpu.make_async_copy(grad.at[:, here], own, sem)
    copy.start()

    def one(g, _):
        for j, h, count, c in several(g, heads // TEAM):
            both = transposed(q[:, c])
            for m in range(count):
                rows = pl.ds(pl.multiple_of((h + m) * HEAD, HEAD), HEAD)
                turned[rows, :] = (both[chunk(m)] * jnp.exp(row[pl.ds(h + m, 1), :])).astype(BF16)
        return 0

    lax.fori_loop(0, TEAM, one, 0)
    copy.wait()
    dscaled_rows(heads, mine, gate, own, gain, dscaled)


def got_dscaled_body(heads, swaps, gate, got, gain, _, dscaled):
    dscaled_rows(heads, 1 - lax.axis_index("tp") if swaps else 1, gate, got, gain, dscaled)


def states_of(state, j, count):
    if count == 1:
        return state[chunk(j), :]
    zero = jnp.zeros((HEAD, HEAD), BF16)
    upper = jnp.concatenate([state[chunk(j), :], zero], axis=1)
    lower = jnp.concatenate([zero, state[chunk(j + 1), :]], axis=1)
    return jnp.concatenate([upper, lower], axis=0)


def attention_body(heads, same, q, intra, dscaled, growth, state, *refs):
    hq = heads // TEAM
    if same:
        att, sq, inn, both = refs
    else:
        _, sq_before, inn_before, att, sums, sq, inn, both = refs
        sq[...] = sq_before[...]
        inn[...] = inn_before[...]
    for y in range(2):
        g = quarter_of(y, same)
        for j, h, count, c in several(g, hq):
            both[:, 0 : count * HEAD] = nn(q[:, c], states_of(state.at[y], j, count))
            for i in range(BLOCK // HEAD):
                r = chunk(i)
                a_sq = a_in = 0.0
                for m in range(count):
                    _, c = head_at(g, hq, j + m)
                    a = intra[r, c] + both[r, chunk(m)] * growth[g, r, j + m : j + m + 1]
                    att[r, c] = a
                    a_sq = a_sq + a * a
                    a_in = a_in + a * dscaled[r, c]
                if same and y == 0 and j == 0:
                    sq[r, :] = a_sq
                    inn[r, :] = a_in
                else:
                    sq[r, :] += a_sq
                    inn[r, :] += a_in
    if not same:
        ones = jnp.ones((8, HEAD), F32)
        a = nt(ones, sq[...], lax.Precision.HIGHEST)
        b = nt(ones, inn[...], lax.Precision.HIGHEST)
        sums[...] = jnp.where(lax.broadcasted_iota(jnp.int32, (8, BLOCK), 0) == 0, a, b)


def dattn_body(heads, channels, same, att, dscaled, turned, gain, row, *refs):
    hq = heads // TEAM
    if same:
        rsb, coefb, _, dattn, out = refs
    else:
        sum_a, sum_b, _, dattn, out, rsb, coefb = refs
        total = sum_a[...] + sum_b[...]
        rs = lax.rsqrt(total[0:1, :] / channels + EPSILON)
        coef = total[1:2, :] * (rs * rs * rs) / channels
        down = jnp.concatenate([rs, coef, jnp.zeros((HEAD - 2, BLOCK), F32)], axis=0).T
        rsb[...] = jnp.broadcast_to(down[:, 0:1], (BLOCK, HEAD))
        coefb[...] = jnp.broadcast_to(down[:, 1:2], (BLOCK, HEAD))
    for y in range(2):
        items = []
        for j, h, count, cols in several(quarter_of(y, same), hq):
            parts = []
            for m in range(count):
                _, c = head_at(quarter_of(y, same), hq, j + m)
                gsum = jnp.zeros((8, HEAD), F32)
                for i in range(BLOCK // HEAD):
                    r = chunk(i)
                    a = att[r, c]
                    t = dscaled[r, c] * rsb[r, :]
                    dattn[r, c] = (t - a * coefb[r, :]).astype(BF16)
                    gsum = gsum + jnp.sum((t * a).reshape(HEAD // 8, 8, HEAD), axis=0)
                parts.append(jnp.sum(gsum, axis=0, keepdims=True) / gain[:, c])
            both = nn(turned[pl.ds(pl.multiple_of(h * HEAD, HEAD), count * HEAD), :], dattn[:, cols])
            for m in range(count):
                edge = jnp.broadcast_to(row[pl.ds(h + m, 1), :][:, BLOCK - 1 : BLOCK], (1, HEAD))
                items.append((both[chunk(m), chunk(m)], edge, parts[m]))
        (write_wide if same else write_narrow)(out.at[y], hq, items)


def leave(out, ref, sems, g, w):
    cols = pl.ds(pl.multiple_of(g * w, HEAD), w)
    copy = pltpu.make_async_copy(out, ref.at[:, cols], sems)
    copy.start()
    return copy


def unscaled_gate_body(heads, gate, att, dscaled, _, out):
    hq = heads // TEAM
    for g in range(TEAM):
        for j in range(hq):
            _, c = head_at(g, hq, j)
            closed = jax.nn.sigmoid(-gate[:, c].astype(F32))
            out[:, c] = dscaled[:, c] * att[:, c] * closed


def gate_body(heads, unscaled, scale, _, gate_grad, token, out, sems):
    hq = heads // TEAM
    token[...] = jnp.zeros_like(token)
    copies = []
    for g in range(TEAM):
        for j in range(hq):
            _, c = head_at(g, hq, j)
            out[g, :, chunk(j)] = (unscaled[:, c] * scale[...]).astype(BF16)
        copies.append(leave(out.at[g], gate_grad, sems.at[g], g, hq * HEAD))
    for copy in copies:
        copy.wait()


def by_quarter(mine, got):
    return [(ref.at[y], quarter_of(y, same)) for ref, same in ((mine, True), (got, False)) for y in range(2)]


def query_body(heads, k, v, dattn, row, col, growth, mine, got, _, *refs):
    hq = heads // TEAM
    query_grad, token, out, sems = refs[-4:]
    token[...] = jnp.zeros_like(token)
    pairs = [(state, g, *pair) for state, g in by_quarter(mine, got) for pair in several(g, hq)]
    copies = []
    for n, (state, g, j, _, count, cols) in enumerate(pairs):
        for m in range(count):
            h, c = head_at(g, hq, j + m)
            line = row[pl.ds(h, 1), :]
            for i in range(2):
                d = dattn[half(i), c]
                u = slice(0, (i + 1) * HALF)
                table = decay_table(col[g, half(i), j + m : j + m + 1], line[:, u], True)
                dscores = (nt(d, v[u, c]) * table).astype(BF16)
                inter = nt(d, state[chunk(j + m), :]) * growth[g, half(i), j + m : j + m + 1]
                out[n, half(i), chunk(m)] = (inter + nn(dscores, k[u, c])).astype(BF16)
        copy = pltpu.make_async_copy(out.at[n, :, 0 : count * HEAD], query_grad.at[:, cols], sems.at[n])
        copy.start()
        copies.append(copy)
    for copy in copies:
        copy.wait()


def key_value_body(heads, first, last, q, v, dattn, table0, table1, probs0, probs1, _, *refs):
    hq = heads // TEAM
    count = min(hq, 2)
    dk, dv = refs[-2:]

    def one(step, _):
        for m in range(count):
            h = step * count + m
            _, c = head_at(h, 1, 0)
            for i, (table, probs) in enumerate(((table0, probs0), (table1, probs1))):
                t = slice(i * HALF, BLOCK)
                dscores = (nt(v[half(i), c], dattn[t, c]) * table[h]).astype(BF16)
                dk[half(i), c] = nn(dscores, q[t, c])
                dv[half(i), c] = nn(probs[h], dattn[t, c])
        return 0

    lax.fori_loop(first, last, one, 0)


def fades(col, y, same):
    sums = col[quarter_of(y, same)]
    return jnp.exp(sums[BLOCK - 1 : BLOCK, :] - sums)


def final_rows(hq, y, j, count, c, k, v, dk, dv, shrink, state, key_out, value_out):
    after = states_of(state.at[y], j, count)
    key_side, value_side = nt(v[:, c], after), nn(k[:, c], after)
    for m in range(count):
        fade = shrink[:, j + m : j + m + 1]
        own = pl.ds(pl.multiple_of(c.start + m * HEAD, HEAD), HEAD)
        key_out[y, :, chunk(j + m)] = (dk[:, own] + key_side[:, chunk(m)] * fade).astype(BF16)
        value_out[y, :, chunk(j + m)] = (dv[:, own] + value_side[:, chunk(m)] * fade).astype(BF16)


def own_final_body(heads, k, v, dk, dv, col, state, key_out, value_out, gain_grad):
    hq = heads // TEAM
    for y in range(2):
        items = read_narrow(state.at[y], hq)
        shrink = fades(col, y, True)
        for j, _, count, c in several(quarter_of(y, True), hq):
            final_rows(hq, y, j, count, c, k, v, dk, dv, shrink, state, key_out, value_out)
            for m in range(j, j + count):
                gain_grad[:, head_at(quarter_of(y, True), hq, m)[1]] = items[m][2]


def final_body(heads, k, v, dk, dv, col, state, own_key, own_value, own_gain, *refs):
    hq = heads // TEAM
    key_grad, value_grad, gain_grad, gains, key_out, value_out, sems = refs
    copies = []

    def send(src, dst, cols):
        copy = pltpu.make_async_copy(src, dst.at[:, cols], sems.at[len(copies)])
        copy.start()
        copies.append(copy)

    gains[...] = own_gain[...]
    for y in range(2):
        for j, (_, _, total) in enumerate(read_narrow(state.at[y], hq)):
            gains[:, head_at(quarter_of(y, False), hq, j)[1]] = total
    send(gains, gain_grad, slice(None))
    for y in range(2):
        for j, _, count, c in several(quarter_of(y, True), hq):
            place = slice(j * HEAD, (j + count) * HEAD)
            send(own_key.at[y, :, place], key_grad, c)
            send(own_value.at[y, :, place], value_grad, c)
    for y in range(2):
        shrink = fades(col, y, False)
        for j, _, count, c in several(quarter_of(y, False), hq):
            final_rows(hq, y, j, count, c, k, v, dk, dv, shrink, state, key_out, value_out)
            place = slice(j * HEAD, (j + count) * HEAD)
            send(key_out.at[y, :, place], key_grad, c)
            send(value_out.at[y, :, place], value_grad, c)
    for copy in copies:
        copy.wait()


def in_hbm(x):
    return pltpu.with_memory_space_constraint(x, pltpu.HBM)


def swap(x, bit):
    n = lax.axis_size("ctx")
    return lax.ppermute(x, "ctx", [(i, i ^ bit) for i in range(n)])


def local(queries, keys, values, log_decay, gate, gain, grad_out):
    rows, width = queries.shape
    heads = width // HEAD
    hq = heads // TEAM
    tp = lax.axis_size("tp")
    n = lax.axis_size("ctx")
    groups = n // TEAM
    channels = width * tp
    bf = lambda *shape: jax.ShapeDtypeStruct(shape, BF16)
    f32 = lambda *shape: jax.ShapeDtypeStruct(shape, F32)
    swaps = tp == 2
    part = rows // 2
    small = 2 * heads * rows * HEAD * HEAD
    large = 2 * heads * rows * rows * HEAD
    wide = f32(hq * HEAD + SIDE, HEAD)
    wide2 = f32(2, hq * HEAD + SIDE, HEAD)
    narrow = bf(hq * HEAD + EXTRA, HEAD)
    narrow2 = bf(2, hq * HEAD + EXTRA, HEAD)
    table = f32(TEAM, rows, HEAD)
    gain_row = gain.reshape(1, width)

    def beside(work, after, name):
        return [work[name](after)] if name in work else []

    def step_call(body, reverse, inputs, unread, shapes, name, *sizes):
        return call(
            functools.partial(body, reverse, hq, *sizes),
            [*inputs, *unread],
            shapes,
            name,
            in_specs=[VMEM] * len(inputs) + [ANY] * len(unread),
        )

    def scan(reverse, keep, give, work):
        got = swap(give, 1)
        own, send = step_call(chip_total_body, reverse, [keep, got], [], [wide, narrow], "chip_total")
        got_pair = swap(send, 2)
        unread = beside(work, send, "pair")
        total, send = step_call(group_total_body, reverse, [own, got_pair], unread, [wide, narrow], "group_total")
        so_far, step = total, 1
        while 2 * step < groups:
            far = swap(send, TEAM * step)
            unread = beside(work, send, "one") if step == 1 else []
            before = [] if step == 1 else [so_far]
            so_far, total, send = step_call(
                window_body, reverse, [total, *before, far], unread, [wide, wide, narrow], "window", step
            )
            step *= 2
        far = swap(send, TEAM * step)
        unread = beside(work, send, "last")
        kept, send = step_call(
            into_chips_body, reverse, [own, got_pair, total, so_far, far], unread, [wide, narrow], "into_chips", step
        )
        other = swap(send, 2)
        unread = beside(work, send, "pair_back")
        mine, send = step_call(
            into_cores_body, reverse, [keep, got, kept, other], unread, [narrow2, narrow2], "into_cores"
        )
        return mine, swap(send, 1)

    outs = call(
        functools.partial(sent_states_body, heads, swaps),
        [in_hbm(keys), in_hbm(values), in_hbm(log_decay)] + [in_hbm(grad_out)] * swaps,
        [wide2, f32(EXTRA, rows), bf(rows, width), bf(rows, width)] + [bf(part, width)] * swaps,
        "sent_states",
        [
            pltpu.VMEM(log_decay.shape, F32),
            pltpu.SemaphoreType.DMA((2, TEAM)),
            pltpu.SemaphoreType.DMA((2,)),
        ],
        small // 2,
        [HBM] * (3 + swaps),
        [VMEM] * 4 + [HBM] * swaps,
    )
    give, row, keys, values = outs[:4]
    if swaps:
        arrived = lax.ppermute(outs[4], "tp", [(0, 1), (1, 0)])
        own = grad_out
    else:
        every = lax.all_to_all(grad_out, "tp", split_axis=1, concat_axis=0, tiled=True)
        own, arrived = every[:part], every[part:]
    (keep,) = call(
        functools.partial(kept_states_body, heads), [keys, values, row], [wide2], "kept_states", flops=small // 2
    )
    done = {}

    def probs_beside(after):
        if "decays" not in done:
            *done["decays"], done["queries"] = call(
                functools.partial(decays_body, heads),
                [row, in_hbm(queries), after],
                [table] * 2 + [bf(rows, width)],
                "decays",
                [pltpu.SemaphoreType.DMA(())],
                in_specs=[VMEM, HBM, ANY],
            )
        before = done.get("probs", [])
        done["probs"] = call(
            functools.partial(turned_probs_body, heads, TEAM // 2 if before else 0),
            [done["queries"], keys, row, done["decays"][0], after, *before],
            [f32(heads, HALF, BLOCK), f32(heads, HALF, HALF), bf(heads, HALF, BLOCK), bf(heads, HALF, HALF)],
            "turned_probs",
            flops=large // 2,
            in_specs=[VMEM] * 4 + [ANY] + [VMEM] * len(before),
            alias={5 + i: i for i in range(len(before))},
        )
        return done["probs"][3]

    def intra_beside(after):
        before = [done["intra"]] if "intra" in done else []
        first, last = (1, TEAM) if before else (0, 1)
        (done["intra"],) = call(
            functools.partial(intra_body, heads, first, last),
            [done["queries"], keys, values, row, done["decays"][0], after, *before],
            [f32(rows, width)],
            "intra",
            flops=2 * large * (last - first) // TEAM,
            in_specs=[VMEM] * 5 + [ANY] + [VMEM] * len(before),
            alias={6: 0} if before else None,
        )
        return done["intra"]

    def probs_and_intra(after):
        return intra_beside(probs_beside(after))

    def dscaled_beside(after):
        done["dscaled"] = call(
            functools.partial(own_dscaled_body, heads, swaps),
            [gate, in_hbm(own), gain_row, done["queries"], row, after],
            [f32(rows, width), bf(width, rows)],
            "own_dscaled",
            [pltpu.VMEM((part, width), BF16), pltpu.SemaphoreType.DMA(())],
            small,
            [VMEM, HBM, VMEM, VMEM, VMEM, ANY],
        )
        (dscaled,) = call(
            functools.partial(got_dscaled_body, heads, swaps),
            [gate, arrived, gain_row, done["dscaled"][0]],
            [f32(rows, width)],
            "got_dscaled",
            alias={3: 0},
        )
        done["dscaled"] = dscaled, done["dscaled"][1]
        return dscaled

    work = {"pair": probs_beside, "one": probs_and_intra, "last": intra_beside, "pair_back": dscaled_beside}
    mine, got = scan(False, keep, give, work)
    queries = done["queries"]
    (col, growth), intra, (dscaled, turned) = done["decays"], done["intra"], done["dscaled"]
    tall = f32(rows, HEAD)
    wide_scratch = pltpu.VMEM((rows, 2 * HEAD), F32)
    att, squares, inner = call(
        functools.partial(attention_body, heads, True),
        [queries, intra, dscaled, growth, mine],
        [f32(rows, width), tall, tall],
        "attention",
        [wide_scratch],
        small // 2,
    )
    att, sums = call(
        functools.partial(attention_body, heads, False),
        [queries, intra, dscaled, growth, got, att, squares, inner],
        [f32(rows, width), f32(8, rows)],
        "attention",
        [pltpu.VMEM((rows, HEAD), F32)] * 2 + [wide_scratch],
        small // 2,
        alias={5: 0},
    )
    (unscaled_gate,) = call(
        functools.partial(unscaled_gate_body, heads),
        [gate, att, dscaled, intra],
        [f32(rows, width)],
        "unscaled_gate",
        in_specs=[VMEM] * 3 + [ANY],
        alias={3: 0},
    )
    if swaps:
        others = lax.ppermute(sums, "tp", [(0, 1), (1, 0)])
    else:
        others = lax.psum(sums, "tp") - sums
    dattn, give, scale, coef = call(
        functools.partial(dattn_body, heads, channels, False),
        [att, dscaled, turned, gain_row, row, sums, others, unscaled_gate],
        [bf(rows, width), narrow2, tall, tall],
        "sent_dattn",
        flops=small // 2,
        in_specs=[VMEM] * 7 + [ANY],
    )
    dattn, keep = call(
        functools.partial(dattn_body, heads, channels, True),
        [att, dscaled, turned, gain_row, row, scale, coef, dattn],
        [bf(rows, width), wide2],
        "kept_dattn",
        flops=small // 2,
        alias={7: 0},
    )
    out_scratch = [pltpu.VMEM((TEAM, rows, hq * HEAD), BF16), pltpu.SemaphoreType.DMA((TEAM,))]

    def gate_beside(after):
        done["gate"], token = call(
            functools.partial(gate_body, heads),
            [unscaled_gate, scale, after],
            [bf(rows, width), f32(SIDE, HEAD)],
            "gate",
            out_scratch,
            small,
            [VMEM] * 2 + [ANY],
            [HBM, VMEM],
        )
        return token

    units = heads // min(hq, 2)
    cuts = [0, units // 4, (5 * units) // 8, units]

    def key_value_beside(after):
        before = done.get("key_value", [])
        piece = done.get("piece", 0)
        done["piece"] = piece + 1
        done["key_value"] = call(
            functools.partial(key_value_body, heads, cuts[piece], cuts[piece + 1]),
            [queries, values, dattn, *done["probs"], after, *before],
            [f32(rows, width)] * 2,
            "key_value",
            flops=4 * large * (cuts[piece + 1] - cuts[piece]) // units,
            in_specs=[VMEM] * 7 + [ANY] + [VMEM] * len(before),
            alias={8 + i: i for i in range(len(before))},
        )
        return done["key_value"][0]

    def gate_and_key_value(after):
        return key_value_beside(gate_beside(after))

    pairs = TEAM * hq // min(hq, 2)

    def query_beside(after):
        done["query"], token = call(
            functools.partial(query_body, heads),
            [keys, values, dattn, row, col, growth, mine, got, after],
            [bf(rows, width), f32(SIDE, HEAD)],
            "query",
            [pltpu.VMEM((pairs, rows, 2 * HEAD), BF16), pltpu.SemaphoreType.DMA((pairs,))],
            2 * large + small,
            [VMEM] * 8 + [ANY],
            [HBM, VMEM],
        )
        return token

    work = {"pair": gate_and_key_value, "one": key_value_beside, "last": query_beside, "pair_back": key_value_beside}
    back_mine, back_got = scan(True, keep, give, work)
    gate_grad, query_grad, (dk, dv) = done["gate"], done["query"], done["key_value"]
    both = bf(2, rows, hq * HEAD)
    own_key, own_value, own_gain = call(
        functools.partial(own_final_body, heads),
        [keys, values, dk, dv, col, back_mine],
        [both, both, f32(1, width)],
        "own_final",
        flops=small,
    )
    key_grad, value_grad, gain_grad = call(
        functools.partial(final_body, heads),
        [keys, values, dk, dv, col, back_got, own_key, own_value, own_gain],
        [bf(rows, width), bf(rows, width), f32(1, width)],
        "final",
        [pltpu.VMEM((1, width), F32)]
        + [pltpu.VMEM(both.shape, BF16)] * 2
        + [pltpu.SemaphoreType.DMA((8 * hq + 1,))],
        small,
        out_specs=[HBM, HBM, HBM],
    )
    return query_grad, key_grad, value_grad, gate_grad, gain_grad.reshape(width)


def solution(mesh):
    return jax.shard_map(
        local,
        mesh=mesh,
        in_specs=(
            P("ctx", "tp"),
            P("ctx", "tp"),
            P("ctx", "tp"),
            P("tp", "ctx"),
            P("ctx", "tp"),
            P("tp"),
            P(("ctx", "tp"), None),
        ),
        out_specs=(P("ctx", "tp"), P("ctx", "tp"), P("ctx", "tp"), P("ctx", "tp"), P("tp")),
        check_vma=False,
    )
```

```python
import functools

import jax
import jax.numpy as jnp
from jax import lax
from jax.experimental import pallas as pl
from jax.experimental.pallas import tpu as pltpu
from jax.sharding import PartitionSpec as P

HEAD = 128
BLOCK = 512
HALF = BLOCK // 2
TEAM = 4
SIDE = 8
EXTRA = 16
EPSILON = 1e-06
F32 = jnp.float32
BF16 = jnp.bfloat16
GRANT = 5 * 1024 * 1024
VMEM = pl.BlockSpec(memory_space=pltpu.VMEM)
HBM = pl.BlockSpec(memory_space=pltpu.HBM)
ANY = pl.BlockSpec(memory_space=pl.ANY)


def nt(a, b, precision=None):
    return lax.dot_general(a, b, (((1,), (1,)), ((), ())), preferred_element_type=F32, precision=precision)


def nn(a, b):
    return lax.dot_general(a, b, (((1,), (0,)), ((), ())), preferred_element_type=F32)


def half(i):
    return slice(i * HALF, (i + 1) * HALF)


def chunk(i):
    return slice(i * HEAD, (i + 1) * HEAD)


def split_terms(x, count):
    terms = []
    for _ in range(count):
        term = x.astype(BF16)
        terms.append(term)
        x = x - term.astype(F32)
    return terms


def read_wide(ref, hq):
    base = hq * HEAD
    return [
        (ref[chunk(j), :], ref[base + j : base + j + 1, :], ref[base + TEAM + j : base + TEAM + j + 1, :])
        for j in range(hq)
    ]


def write_wide(ref, hq, items):
    base = hq * HEAD
    at = lax.broadcasted_iota(jnp.int32, (SIDE, HEAD), 0)
    side = jnp.zeros((SIDE, HEAD), F32)
    for j, (term, edge, gain) in enumerate(items):
        ref[chunk(j), :] = term
        side = jnp.where(at == j, edge, side)
        side = jnp.where(at == TEAM + j, gain, side)
    ref[base : base + SIDE, :] = side


def read_narrow(ref, hq):
    base = hq * HEAD
    side = ref[base : base + EXTRA, :].astype(F32)
    row = lambda i: side[i : i + 1, :] + side[i + 1 : i + 2, :]
    return [(ref[chunk(j), :].astype(F32), row(2 * j), row(2 * TEAM + 2 * j)) for j in range(hq)]


def write_narrow(ref, hq, items):
    base = hq * HEAD
    at = lax.broadcasted_iota(jnp.int32, (EXTRA, HEAD), 0)
    side = jnp.zeros((EXTRA, HEAD), F32)
    for j, (term, edge, gain) in enumerate(items):
        ref[chunk(j), :] = term.astype(BF16)
        for first, value in ((2 * j, edge), (2 * TEAM + 2 * j, gain)):
            for i, part in enumerate(split_terms(value, 2)):
                side = jnp.where(at == first + i, part.astype(F32), side)
    ref[base : base + EXTRA, :] = side.astype(BF16)


def core():
    return lax.rem(lax.axis_index("ctx"), 2)


def pair():
    return lax.rem(lax.axis_index("ctx") // 2, 2)


def group():
    return lax.axis_index("ctx") // TEAM


def quarter_of(y, same):
    return 2 * y + (core() if same else 1 - core())


def head_at(quarter, hq, j):
    h = quarter * hq + j
    return h, pl.ds(pl.multiple_of(h * HEAD, HEAD), HEAD)


def transposed(x):
    shape = (x.shape[1], x.shape[1])
    eye = (lax.broadcasted_iota(jnp.int32, shape, 0) == lax.broadcasted_iota(jnp.int32, shape, 1)).astype(BF16)
    return nt(eye, x)


def several(quarter, hq):
    count = min(hq, 2)
    for j in range(0, hq, count):
        h = quarter * hq + j
        yield j, h, count, pl.ds(pl.multiple_of(h * HEAD, HEAD), count * HEAD)


def call(body, inputs, out_shape, name, scratch=(), flops=0, in_specs=None, out_specs=None, alias=None):
    nbytes = sum(x.size * x.dtype.itemsize for x in inputs)
    nbytes += sum(x.size * x.dtype.itemsize for x in out_shape)
    out_shape = list(out_shape)
    for o in (alias or {}).values():
        out_shape[o] = pltpu.VMEM(out_shape[o].shape, out_shape[o].dtype)
    return pl.pallas_call(
        body,
        in_specs=in_specs or [VMEM] * len(inputs),
        out_specs=out_specs or [VMEM] * len(out_shape),
        out_shape=out_shape,
        scratch_shapes=list(scratch),
        input_output_aliases=alias or {},
        compiler_params=pltpu.CompilerParams(vmem_limit_bytes=GRANT),
        cost_estimate=pl.CostEstimate(flops=flops, bytes_accessed=nbytes, transcendentals=0),
        name=name,
    )(*inputs)


def joined(mine, other, mine_is_first, reverse):
    out = []
    for (a, ea, ga), (b, eb, gb) in zip(mine, other):
        near = mine_is_first if reverse else jnp.logical_not(mine_is_first)
        wa = jnp.where(near, 1.0, jnp.exp(eb))
        wb = jnp.where(near, jnp.exp(ea), 1.0)
        out.append((a * wa + b * wb, ea + eb, ga + gb))
    return out


def chip_total_body(reverse, hq, keep, got, own, send):
    first = core() == 0
    read_got = read_narrow if reverse else read_wide
    here, there = pair(), 1 - pair()
    own_items = joined(read_wide(keep.at[here], hq), read_got(got.at[here], hq), first, reverse)
    write_wide(own, hq, own_items)
    send_items = joined(read_wide(keep.at[there], hq), read_got(got.at[there], hq), first, reverse)
    write_narrow(send, hq, send_items)


def group_total_body(reverse, hq, own, got, *refs):
    total, send = refs[-2:]
    items = joined(read_wide(own, hq), read_narrow(got, hq), pair() == 0, reverse)
    write_wide(total, hq, items)
    write_narrow(send, hq, items)


def met(reverse, step, before, other):
    near = lax.rem(group() // step, 2) == (0 if reverse else 1)
    out = []
    for old, (term, edge, gain) in zip(before, other):
        term = jnp.where(near, term, 0.0)
        edge = jnp.where(near, edge, 0.0)
        if old is None:
            out.append((term, edge, gain))
        else:
            out.append((old[0] + jnp.exp(old[1]) * term, old[1] + edge, gain))
    return out


def window_body(reverse, hq, step, total, *refs):
    so_far, whole, send = refs[-3:]
    if step == 1:
        got = refs[0]
        before = [None] * hq
    else:
        got = refs[1]
        before = read_wide(refs[0], hq)
    other = read_narrow(got, hq)
    write_wide(so_far, hq, met(reverse, step, before, other))
    items = joined(read_wide(total, hq), other, lax.rem(group() // step, 2) == 0, reverse)
    write_wide(whole, hq, items)
    write_narrow(send, hq, items)


def into_chips_body(reverse, hq, step, own, got_pair, total, so_far, got, *refs):
    keep, send = refs[-2:]
    before = read_wide(so_far, hq) if step > 1 else [None] * hq
    entering = met(reverse, step, before, read_narrow(got, hq))
    mine_near = pair() == (1 if reverse else 0)
    kept, sent = [], []
    for (r, _, gr), (c, ec, _), (o, eo, _), (_, _, gt) in zip(
        entering, read_wide(own, hq), read_narrow(got_pair, hq), read_wide(total, hq)
    ):
        gain = gr + gt
        zero = jnp.zeros_like(ec)
        kept.append((jnp.where(mine_near, r, jnp.exp(eo) * r + o), zero, gain))
        sent.append((jnp.where(mine_near, jnp.exp(ec) * r + c, r), zero, gain))
    write_wide(keep, hq, kept)
    write_narrow(send, hq, sent)


def into_cores_body(reverse, hq, keep, got, own, other, *refs):
    mine, send = refs[-2:]
    mine_near = core() == (1 if reverse else 0)
    read_got = read_narrow if reverse else read_wide
    for y in range(2):
        a, b = read_wide(own, hq), read_narrow(other, hq)
        here = pair() == y
        items_mine, items_send = [], []
        for p, q, (k, ek, _), (g, eg, _) in zip(a, b, read_wide(keep.at[y], hq), read_got(got.at[y], hq)):
            r = jnp.where(here, p[0], q[0])
            gain = jnp.where(here, p[2], q[2])
            zero = jnp.zeros_like(ek)
            items_mine.append((jnp.where(mine_near, r, jnp.exp(eg) * r + g), zero, gain))
            items_send.append((jnp.where(mine_near, jnp.exp(ek) * r + k, r), zero, gain))
        write_narrow(mine.at[y], hq, items_mine)
        write_narrow(send.at[y], hq, items_send)


def block_states(hq, y, same, k, v, row, out):
    items = []
    for j, h, count, c in several(quarter_of(y, same), hq):
        turned = transposed(k[:, c])
        lines = [row[pl.ds(h + m, 1), :] for m in range(count)]
        edges = [line[:, BLOCK - 1 : BLOCK] for line in lines]
        faded = [turned[chunk(m)] * jnp.exp(edges[m] - lines[m]) for m in range(count)]
        both = nn(jnp.concatenate([x.astype(BF16) for x in faded], axis=0), v[:, c])
        for m in range(count):
            items.append((both[chunk(m), chunk(m)], jnp.broadcast_to(edges[m], (1, HEAD)), jnp.zeros((1, HEAD), F32)))
    write_wide(out.at[y], hq, items)


def sent_states_body(heads, swaps, k_hbm, v_hbm, ld_hbm, *refs):
    hq = heads // TEAM
    w = hq * HEAD
    if swaps:
        grad, give, row, k, v, away, ld, sems, side_sems = refs
        width = heads * HEAD
        there = pl.ds(pl.multiple_of((1 - lax.axis_index("tp")) * width, HEAD), width)
        side_copies = [pltpu.make_async_copy(grad.at[:, there], away, side_sems.at[1])]
    else:
        give, row, k, v, ld, sems, side_sems = refs
        side_copies = []
    first = pltpu.make_async_copy(ld_hbm, ld, side_sems.at[0])
    first.start()
    order = [(0, False), (1, False), (0, True), (1, True)]
    copies = []
    for slot, (y, same) in enumerate(order):
        cols_d = pl.ds(pl.multiple_of(quarter_of(y, same) * w, HEAD), w)
        both = [
            pltpu.make_async_copy(k_hbm.at[:, cols_d], k.at[:, cols_d], sems.at[0, slot]),
            pltpu.make_async_copy(v_hbm.at[:, cols_d], v.at[:, cols_d], sems.at[1, slot]),
        ]
        for c in both:
            c.start()
        copies.append(both)
    for c in side_copies:
        c.start()
    at = lax.broadcasted_iota(jnp.int32, (BLOCK, BLOCK), 0)
    other = lax.broadcasted_iota(jnp.int32, (BLOCK, BLOCK), 1)
    tri = (at <= other).astype(BF16)
    first.wait()
    x = ld[...]
    if heads < EXTRA:
        x = jnp.concatenate([x, jnp.zeros((EXTRA - heads, BLOCK), F32)], axis=0)
    sums = nn(jnp.concatenate(split_terms(x, 3), axis=0), tri)
    row[...] = sums[0:EXTRA] + (sums[EXTRA : 2 * EXTRA] + sums[2 * EXTRA : 3 * EXTRA])
    for slot, (y, same) in enumerate(order):
        for c in copies[slot]:
            c.wait()
        if not same:
            block_states(hq, y, same, k, v, row, give)
    for c in side_copies:
        c.wait()


def kept_states_body(heads, k, v, row, keep):
    for y in range(2):
        block_states(heads // TEAM, y, True, k, v, row, keep)


def decays_body(heads, row, q_hbm, _, col, growth, q, sem):
    hq = heads // TEAM
    copy = pltpu.make_async_copy(q_hbm, q, sem)
    copy.start()
    for g in range(TEAM):
        rows = row[g * hq : (g + 1) * hq, :]
        across = jnp.concatenate([rows, jnp.zeros((HEAD - hq, BLOCK), F32)], axis=0).T
        col[g] = across
        growth[g] = jnp.exp(across)
    copy.wait()


def decay_table(high, low, lower):
    table = jnp.exp(high - low)
    at = lax.broadcasted_iota(jnp.int32, (HALF, HALF), 0)
    other = lax.broadcasted_iota(jnp.int32, (HALF, HALF), 1)
    if lower:
        cut = jnp.where(at >= other, table[:, -HALF:], 0.0)
        return cut if table.shape[1] == HALF else jnp.concatenate([table[:, :HALF], cut], axis=1)
    cut = jnp.where(at <= other, table[:, :HALF], 0.0)
    return cut if table.shape[1] == HALF else jnp.concatenate([cut, table[:, HALF:]], axis=1)


def turned_probs_body(heads, first, q, k, row, col, _, *refs):
    hq = heads // TEAM
    tables, probs = refs[-4:-2], refs[-2:]

    def one(g, _):
        for j in range(hq):
            h, c = head_at(g, hq, j)
            line = row[pl.ds(h, 1), :]
            for i in range(2):
                t = slice(i * HALF, BLOCK)
                table = decay_table(line[:, t], col[g, half(i), j : j + 1], False)
                tables[i][h] = table
                probs[i][h] = (nt(k[half(i), c], q[t, c]) * table).astype(BF16)
        return 0

    lax.fori_loop(first, first + TEAM // 2, one, 0)


def intra_body(heads, first, last, q, k, v, row, col, *refs):
    hq = heads // TEAM
    intra = refs[-1]

    def one(g, _):
        for j in range(hq):
            h, c = head_at(g, hq, j)
            line = row[pl.ds(h, 1), :]
            for i in range(2):
                u = slice(0, (i + 1) * HALF)
                table = decay_table(col[g, half(i), j : j + 1], line[:, u], True)
                probs = (nt(q[half(i), c], k[u, c]) * table).astype(BF16)
                intra[half(i), c] = nn(probs, v[u, c])
        return 0

    lax.fori_loop(first, last, one, 0)


def dscaled_rows(heads, where, gate, ref, gain, dscaled):
    part = ref.shape[0]
    rows = pl.ds(pl.multiple_of(where * part, part), part)

    def one(g, _):
        for j in range(heads // TEAM):
            _, c = head_at(g, heads // TEAM, j)
            opened = jax.nn.sigmoid(gate[rows, c].astype(F32))
            dscaled[rows, c] = ref[:, c].astype(F32) * opened * gain[:, c]
        return 0

    lax.fori_loop(0, TEAM, one, 0)


def own_dscaled_body(heads, swaps, gate, grad, gain, q, row, _, dscaled, turned, own, sem):
    width = heads * HEAD
    mine = lax.axis_index("tp") if swaps else 0
    here = pl.ds(pl.multiple_of(mine * width, HEAD), width)
    copy = pltpu.make_async_copy(grad.at[:, here], own, sem)
    copy.start()

    def one(g, _):
        for j, h, count, c in several(g, heads // TEAM):
            both = transposed(q[:, c])
            for m in range(count):
                rows = pl.ds(pl.multiple_of((h + m) * HEAD, HEAD), HEAD)
                turned[rows, :] = (both[chunk(m)] * jnp.exp(row[pl.ds(h + m, 1), :])).astype(BF16)
        return 0

    lax.fori_loop(0, TEAM, one, 0)
    copy.wait()
    dscaled_rows(heads, mine, gate, own, gain, dscaled)


def got_dscaled_body(heads, swaps, gate, got, gain, _, dscaled):
    dscaled_rows(heads, 1 - lax.axis_index("tp") if swaps else 1, gate, got, gain, dscaled)


def states_of(state, j, count):
    if count == 1:
        return state[chunk(j), :]
    zero = jnp.zeros((HEAD, HEAD), BF16)
    upper = jnp.concatenate([state[chunk(j), :], zero], axis=1)
    lower = jnp.concatenate([zero, state[chunk(j + 1), :]], axis=1)
    return jnp.concatenate([upper, lower], axis=0)


def attention_body(heads, same, q, intra, dscaled, growth, state, *refs):
    hq = heads // TEAM
    if same:
        att, sq, inn, both = refs
    else:
        _, sq_before, inn_before, att, sums, sq, inn, both = refs
        sq[...] = sq_before[...]
        inn[...] = inn_before[...]
    for y in range(2):
        g = quarter_of(y, same)
        for j, h, count, c in several(g, hq):
            both[:, 0 : count * HEAD] = nn(q[:, c], states_of(state.at[y], j, count))
            for i in range(BLOCK // HEAD):
                r = chunk(i)
                a_sq = a_in = 0.0
                for m in range(count):
                    _, c = head_at(g, hq, j + m)
                    a = intra[r, c] + both[r, chunk(m)] * growth[g, r, j + m : j + m + 1]
                    att[r, c] = a
                    a_sq = a_sq + a * a
                    a_in = a_in + a * dscaled[r, c]
                if same and y == 0 and j == 0:
                    sq[r, :] = a_sq
                    inn[r, :] = a_in
                else:
                    sq[r, :] += a_sq
                    inn[r, :] += a_in
    if not same:
        ones = jnp.ones((8, HEAD), F32)
        a = nt(ones, sq[...], lax.Precision.HIGHEST)
        b = nt(ones, inn[...], lax.Precision.HIGHEST)
        sums[...] = jnp.where(lax.broadcasted_iota(jnp.int32, (8, BLOCK), 0) == 0, a, b)


def dattn_body(heads, channels, same, att, dscaled, turned, gain, row, *refs):
    hq = heads // TEAM
    if same:
        rsb, coefb, _, dattn, out = refs
    else:
        sum_a, sum_b, _, dattn, out, rsb, coefb = refs
        total = sum_a[...] + sum_b[...]
        rs = lax.rsqrt(total[0:1, :] / channels + EPSILON)
        coef = total[1:2, :] * (rs * rs * rs) / channels
        down = jnp.concatenate([rs, coef, jnp.zeros((HEAD - 2, BLOCK), F32)], axis=0).T
        rsb[...] = jnp.broadcast_to(down[:, 0:1], (BLOCK, HEAD))
        coefb[...] = jnp.broadcast_to(down[:, 1:2], (BLOCK, HEAD))
    for y in range(2):
        items = []
        for j, h, count, cols in several(quarter_of(y, same), hq):
            parts = []
            for m in range(count):
                _, c = head_at(quarter_of(y, same), hq, j + m)
                gsum = jnp.zeros((8, HEAD), F32)
                for i in range(BLOCK // HEAD):
                    r = chunk(i)
                    a = att[r, c]
                    t = dscaled[r, c] * rsb[r, :]
                    dattn[r, c] = (t - a * coefb[r, :]).astype(BF16)
                    gsum = gsum + jnp.sum((t * a).reshape(HEAD // 8, 8, HEAD), axis=0)
                parts.append(jnp.sum(gsum, axis=0, keepdims=True) / gain[:, c])
            both = nn(turned[pl.ds(pl.multiple_of(h * HEAD, HEAD), count * HEAD), :], dattn[:, cols])
            for m in range(count):
                edge = jnp.broadcast_to(row[pl.ds(h + m, 1), :][:, BLOCK - 1 : BLOCK], (1, HEAD))
                items.append((both[chunk(m), chunk(m)], edge, parts[m]))
        (write_wide if same else write_narrow)(out.at[y], hq, items)


def unscaled_gate_body(heads, gate, att, dscaled, _, out):
    hq = heads // TEAM
    for g in range(TEAM):
        for j in range(hq):
            _, c = head_at(g, hq, j)
            closed = jax.nn.sigmoid(-gate[:, c].astype(F32))
            out[:, c] = dscaled[:, c] * att[:, c] * closed


def leave(out, ref, sems, g, w):
    cols = pl.ds(pl.multiple_of(g * w, HEAD), w)
    copy = pltpu.make_async_copy(out, ref.at[:, cols], sems)
    copy.start()
    return copy


def gate_body(heads, unscaled, scale, _, gate_grad, token, out, sems):
    hq = heads // TEAM
    token[...] = jnp.zeros_like(token)
    copies = []
    for g in range(TEAM):
        for j in range(hq):
            _, c = head_at(g, hq, j)
            out[g, :, chunk(j)] = (unscaled[:, c] * scale[...]).astype(BF16)
        copies.append(leave(out.at[g], gate_grad, sems.at[g], g, hq * HEAD))
    for copy in copies:
        copy.wait()


def by_quarter(mine, got):
    return [(ref.at[y], quarter_of(y, same)) for ref, same in ((mine, True), (got, False)) for y in range(2)]


def query_body(heads, first, last, k, v, dattn, row, col, growth, mine, got, _, *refs):
    hq = heads // TEAM
    query_grad = refs[-1]
    pairs = [(state, g, *pair) for state, g in by_quarter(mine, got) for pair in several(g, hq)]
    for state, g, j, _, count, _ in pairs[first:last]:
        for m in range(count):
            h, c = head_at(g, hq, j + m)
            line = row[pl.ds(h, 1), :]
            for i in range(2):
                d = dattn[half(i), c]
                u = slice(0, (i + 1) * HALF)
                table = decay_table(col[g, half(i), j + m : j + m + 1], line[:, u], True)
                dscores = (nt(d, v[u, c]) * table).astype(BF16)
                inter = nt(d, state[chunk(j + m), :]) * growth[g, half(i), j + m : j + m + 1]
                query_grad[half(i), c] = (inter + nn(dscores, k[u, c])).astype(BF16)


def key_value_body(heads, first, last, carries, q, v, dattn, table0, table1, probs0, probs1, _, *refs):
    hq = heads // TEAM
    count = min(hq, 2)
    if carries:
        dk, dv, outside, sems = refs[-4:]
        rows = [slice(i * HEAD, (i + 1) * HEAD) for i in range(BLOCK // HEAD)]
        copies = [pltpu.make_async_copy(refs[0].at[r], outside.at[r], sems.at[i]) for i, r in enumerate(rows)]
    else:
        dk, dv = refs[-2:]
        copies = []
    for copy in copies:
        copy.start()

    def one(step, _):
        for m in range(count):
            h = step * count + m
            _, c = head_at(h, 1, 0)
            for i, (table, probs) in enumerate(((table0, probs0), (table1, probs1))):
                t = slice(i * HALF, BLOCK)
                dscores = (nt(v[half(i), c], dattn[t, c]) * table[h]).astype(BF16)
                dk[half(i), c] = nn(dscores, q[t, c])
                dv[half(i), c] = nn(probs[h], dattn[t, c])
        return 0

    lax.fori_loop(first, last, one, 0)
    for copy in copies:
        copy.wait()


def fades(col, y, same):
    sums = col[quarter_of(y, same)]
    return jnp.exp(sums[BLOCK - 1 : BLOCK, :] - sums)


def final_rows(hq, y, j, count, c, k, v, dk, dv, shrink, state, key_out, value_out):
    after = states_of(state.at[y], j, count)
    key_side, value_side = nt(v[:, c], after), nn(k[:, c], after)
    for m in range(count):
        fade = shrink[:, j + m : j + m + 1]
        own = pl.ds(pl.multiple_of(c.start + m * HEAD, HEAD), HEAD)
        key_out[y, :, chunk(j + m)] = (dk[:, own] + key_side[:, chunk(m)] * fade).astype(BF16)
        value_out[y, :, chunk(j + m)] = (dv[:, own] + value_side[:, chunk(m)] * fade).astype(BF16)


def own_final_body(heads, k, v, dk, dv, col, state, key_out, value_out, gain_grad):
    hq = heads // TEAM
    for y in range(2):
        items = read_narrow(state.at[y], hq)
        shrink = fades(col, y, True)
        for j, _, count, c in several(quarter_of(y, True), hq):
            final_rows(hq, y, j, count, c, k, v, dk, dv, shrink, state, key_out, value_out)
            for m in range(j, j + count):
                gain_grad[:, head_at(quarter_of(y, True), hq, m)[1]] = items[m][2]


def final_body(heads, k, v, dk, dv, col, state, own_key, own_value, own_gain, *refs):
    hq = heads // TEAM
    key_grad, value_grad, gain_grad, gains, key_out, value_out, sems = refs
    copies = []

    def send(src, dst, cols):
        copy = pltpu.make_async_copy(src, dst.at[:, cols], sems.at[len(copies)])
        copy.start()
        copies.append(copy)

    gains[...] = own_gain[...]
    for y in range(2):
        for j, (_, _, total) in enumerate(read_narrow(state.at[y], hq)):
            gains[:, head_at(quarter_of(y, False), hq, j)[1]] = total
    send(gains, gain_grad, slice(None))
    for y in range(2):
        for j, _, count, c in several(quarter_of(y, True), hq):
            place = slice(j * HEAD, (j + count) * HEAD)
            send(own_key.at[y, :, place], key_grad, c)
            send(own_value.at[y, :, place], value_grad, c)
    for y in range(2):
        shrink = fades(col, y, False)
        for j, _, count, c in several(quarter_of(y, False), hq):
            final_rows(hq, y, j, count, c, k, v, dk, dv, shrink, state, key_out, value_out)
            place = slice(j * HEAD, (j + count) * HEAD)
            send(key_out.at[y, :, place], key_grad, c)
            send(value_out.at[y, :, place], value_grad, c)
    for copy in copies:
        copy.wait()


def in_hbm(x):
    return pltpu.with_memory_space_constraint(x, pltpu.HBM)


def swap(x, bit):
    n = lax.axis_size("ctx")
    return lax.ppermute(x, "ctx", [(i, i ^ bit) for i in range(n)])


def local(queries, keys, values, log_decay, gate, gain, grad_out):
    rows, width = queries.shape
    heads = width // HEAD
    hq = heads // TEAM
    tp = lax.axis_size("tp")
    n = lax.axis_size("ctx")
    groups = n // TEAM
    channels = width * tp
    bf = lambda *shape: jax.ShapeDtypeStruct(shape, BF16)
    f32 = lambda *shape: jax.ShapeDtypeStruct(shape, F32)
    swaps = tp == 2
    part = rows // 2
    small = 2 * heads * rows * HEAD * HEAD
    large = 2 * heads * rows * rows * HEAD
    wide = f32(hq * HEAD + SIDE, HEAD)
    wide2 = f32(2, hq * HEAD + SIDE, HEAD)
    narrow = bf(hq * HEAD + EXTRA, HEAD)
    narrow2 = bf(2, hq * HEAD + EXTRA, HEAD)
    table = f32(TEAM, rows, HEAD)
    gain_row = gain.reshape(1, width)

    def beside(work, after, name):
        return [work[name](after)] if name in work else []

    def step_call(body, reverse, inputs, unread, shapes, name, *sizes):
        return call(
            functools.partial(body, reverse, hq, *sizes),
            [*inputs, *unread],
            shapes,
            name,
            in_specs=[VMEM] * len(inputs) + [ANY] * len(unread),
        )

    def scan(reverse, keep, give, work):
        got = swap(give, 1)
        own, send = step_call(chip_total_body, reverse, [keep, got], [], [wide, narrow], "chip_total")
        got_pair = swap(send, 2)
        unread = beside(work, send, "pair")
        total, send = step_call(group_total_body, reverse, [own, got_pair], unread, [wide, narrow], "group_total")
        so_far, step = total, 1
        while 2 * step < groups:
            far = swap(send, TEAM * step)
            unread = beside(work, send, "one") if step == 1 else []
            before = [] if step == 1 else [so_far]
            so_far, total, send = step_call(
                window_body, reverse, [total, *before, far], unread, [wide, wide, narrow], "window", step
            )
            step *= 2
        far = swap(send, TEAM * step)
        unread = beside(work, send, "last")
        kept, send = step_call(
            into_chips_body, reverse, [own, got_pair, total, so_far, far], unread, [wide, narrow], "into_chips", step
        )
        other = swap(send, 2)
        unread = beside(work, send, "pair_back")
        mine, send = step_call(
            into_cores_body, reverse, [keep, got, kept, other], unread, [narrow2, narrow2], "into_cores"
        )
        return mine, swap(send, 1)

    outs = call(
        functools.partial(sent_states_body, heads, swaps),
        [in_hbm(keys), in_hbm(values), in_hbm(log_decay)] + [in_hbm(grad_out)] * swaps,
        [wide2, f32(EXTRA, rows), bf(rows, width), bf(rows, width)] + [bf(part, width)] * swaps,
        "sent_states",
        [
            pltpu.VMEM(log_decay.shape, F32),
            pltpu.SemaphoreType.DMA((2, TEAM)),
            pltpu.SemaphoreType.DMA((2,)),
        ],
        small // 2,
        [HBM] * (3 + swaps),
        [VMEM] * 4 + [HBM] * swaps,
    )
    give, row, keys, values = outs[:4]
    if swaps:
        arrived = lax.ppermute(outs[4], "tp", [(0, 1), (1, 0)])
        own = grad_out
    else:
        every = lax.all_to_all(grad_out, "tp", split_axis=1, concat_axis=0, tiled=True)
        own, arrived = every[:part], every[part:]
    (keep,) = call(
        functools.partial(kept_states_body, heads), [keys, values, row], [wide2], "kept_states", flops=small // 2
    )
    done = {}

    def probs_beside(after):
        if "decays" not in done:
            *done["decays"], done["queries"] = call(
                functools.partial(decays_body, heads),
                [row, in_hbm(queries), after],
                [table] * 2 + [bf(rows, width)],
                "decays",
                [pltpu.SemaphoreType.DMA(())],
                in_specs=[VMEM, HBM, ANY],
            )
        before = done.get("probs", [])
        done["probs"] = call(
            functools.partial(turned_probs_body, heads, TEAM // 2 if before else 0),
            [done["queries"], keys, row, done["decays"][0], after, *before],
            [f32(heads, HALF, BLOCK), f32(heads, HALF, HALF), bf(heads, HALF, BLOCK), bf(heads, HALF, HALF)],
            "turned_probs",
            flops=large // 2,
            in_specs=[VMEM] * 4 + [ANY] + [VMEM] * len(before),
            alias={5 + i: i for i in range(len(before))},
        )
        return done["probs"][3]

    def intra_beside(after):
        before = [done["intra"]] if "intra" in done else []
        first, last = (1, TEAM) if before else (0, 1)
        (done["intra"],) = call(
            functools.partial(intra_body, heads, first, last),
            [done["queries"], keys, values, row, done["decays"][0], after, *before],
            [f32(rows, width)],
            "intra",
            flops=2 * large * (last - first) // TEAM,
            in_specs=[VMEM] * 5 + [ANY] + [VMEM] * len(before),
            alias={6: 0} if before else None,
        )
        return done["intra"]

    def probs_and_intra(after):
        return intra_beside(probs_beside(after))

    def dscaled_beside(after):
        done["dscaled"] = call(
            functools.partial(own_dscaled_body, heads, swaps),
            [gate, in_hbm(own), gain_row, done["queries"], row, after],
            [f32(rows, width), bf(width, rows)],
            "own_dscaled",
            [pltpu.VMEM((part, width), BF16), pltpu.SemaphoreType.DMA(())],
            small,
            [VMEM, HBM, VMEM, VMEM, VMEM, ANY],
        )
        (dscaled,) = call(
            functools.partial(got_dscaled_body, heads, swaps),
            [gate, arrived, gain_row, done["dscaled"][0]],
            [f32(rows, width)],
            "got_dscaled",
            alias={3: 0},
        )
        done["dscaled"] = dscaled, done["dscaled"][1]
        return dscaled

    work = {"pair": probs_beside, "one": probs_and_intra, "last": intra_beside, "pair_back": dscaled_beside}
    mine, got = scan(False, keep, give, work)
    queries = done["queries"]
    (col, growth), intra, (dscaled, turned) = done["decays"], done["intra"], done["dscaled"]
    tall = f32(rows, HEAD)
    wide_scratch = pltpu.VMEM((rows, 2 * HEAD), F32)
    att, squares, inner = call(
        functools.partial(attention_body, heads, True),
        [queries, intra, dscaled, growth, mine],
        [f32(rows, width), tall, tall],
        "attention",
        [wide_scratch],
        small // 2,
    )
    att, sums = call(
        functools.partial(attention_body, heads, False),
        [queries, intra, dscaled, growth, got, att, squares, inner],
        [f32(rows, width), f32(8, rows)],
        "attention",
        [pltpu.VMEM((rows, HEAD), F32)] * 2 + [wide_scratch],
        small // 2,
        alias={5: 0},
    )
    (unscaled_gate,) = call(
        functools.partial(unscaled_gate_body, heads),
        [gate, att, dscaled, intra],
        [f32(rows, width)],
        "unscaled_gate",
        in_specs=[VMEM] * 3 + [ANY],
        alias={3: 0},
    )
    if swaps:
        others = lax.ppermute(sums, "tp", [(0, 1), (1, 0)])
    else:
        others = lax.psum(sums, "tp") - sums
    dattn, give, scale, coef = call(
        functools.partial(dattn_body, heads, channels, False),
        [att, dscaled, turned, gain_row, row, sums, others, unscaled_gate],
        [bf(rows, width), narrow2, tall, tall],
        "sent_dattn",
        flops=small // 2,
        in_specs=[VMEM] * 7 + [ANY],
    )
    dattn, keep = call(
        functools.partial(dattn_body, heads, channels, True),
        [att, dscaled, turned, gain_row, row, scale, coef, dattn],
        [bf(rows, width), wide2],
        "kept_dattn",
        flops=small // 2,
        alias={7: 0},
    )
    out_scratch = [pltpu.VMEM((TEAM, rows, hq * HEAD), BF16), pltpu.SemaphoreType.DMA((TEAM,))]

    def gate_beside(after):
        done["gate"], token = call(
            functools.partial(gate_body, heads),
            [unscaled_gate, scale, after],
            [bf(rows, width), f32(SIDE, HEAD)],
            "gate",
            out_scratch,
            small,
            [VMEM] * 2 + [ANY],
            [HBM, VMEM],
        )
        return token

    units = heads // min(hq, 2)
    cuts = [0, units // 4, 5 * units // 8, units]

    def key_value_beside(after, carried=()):
        before = done.get("key_value", [])
        piece = done.get("piece", 0)
        done["piece"] = piece + 1
        inputs = [queries, values, dattn, *done["probs"], after, *carried, *before]
        results = call(
            functools.partial(key_value_body, heads, cuts[piece], cuts[piece + 1], len(carried)),
            inputs,
            [f32(rows, width)] * 2 + [bf(rows, width)] * len(carried),
            "key_value",
            [pltpu.SemaphoreType.DMA((rows // HEAD,))] * len(carried),
            4 * large * (cuts[piece + 1] - cuts[piece]) // units,
            [VMEM] * 7 + [ANY] + [VMEM] * (len(carried) + len(before)),
            [VMEM] * 2 + [HBM] * len(carried),
            {8 + len(carried) + i: i for i in range(len(before))},
        )
        done["key_value"] = results[:2]
        return results[0], results[-1]

    def gate_and_key_value(after):
        return key_value_beside(gate_beside(after))[0]

    pairs = TEAM * hq // min(hq, 2)

    def query_beside(after):
        before = [done["query"]] if "query" in done else []
        first, last = (pairs - pairs // 8, pairs) if before else (0, pairs - pairs // 8)
        (done["query"],) = call(
            functools.partial(query_body, heads, first, last),
            [keys, values, dattn, row, col, growth, mine, got, after, *before],
            [bf(rows, width)],
            "query",
            flops=(2 * large + small) * (last - first) // pairs,
            in_specs=[VMEM] * 8 + [ANY] + [VMEM] * len(before),
            alias={9: 0} if before else None,
        )
        return done["query"]

    def query_and_key_value(after):
        dk, done["query"] = key_value_beside(after, [query_beside(after)])
        return dk

    work = {"pair": gate_and_key_value, "one": lambda after: key_value_beside(after)[0], "last": query_beside, "pair_back": query_and_key_value}
    back_mine, back_got = scan(True, keep, give, work)
    gate_grad, query_grad, (dk, dv) = done["gate"], done["query"], done["key_value"]
    both = bf(2, rows, hq * HEAD)
    own_key, own_value, own_gain = call(
        functools.partial(own_final_body, heads),
        [keys, values, dk, dv, col, back_mine],
        [both, both, f32(1, width)],
        "own_final",
        flops=small,
    )
    key_grad, value_grad, gain_grad = call(
        functools.partial(final_body, heads),
        [keys, values, dk, dv, col, back_got, own_key, own_value, own_gain],
        [bf(rows, width), bf(rows, width), f32(1, width)],
        "final",
        [pltpu.VMEM((1, width), F32)]
        + [pltpu.VMEM(both.shape, BF16)] * 2
        + [pltpu.SemaphoreType.DMA((8 * hq + 1,))],
        small,
        out_specs=[HBM, HBM, HBM],
    )
    return query_grad, key_grad, value_grad, gate_grad, gain_grad.reshape(width)


def solution(mesh):
    return jax.shard_map(
        local,
        mesh=mesh,
        in_specs=(
            P("ctx", "tp"),
            P("ctx", "tp"),
            P("ctx", "tp"),
            P("tp", "ctx"),
            P("ctx", "tp"),
            P("tp"),
            P(("ctx", "tp"), None),
        ),
        out_specs=(P("ctx", "tp"), P("ctx", "tp"), P("ctx", "tp"), P("ctx", "tp"), P("tp")),
        check_vma=False,
    )
```

```python
import functools

import jax
import jax.numpy as jnp
from jax import lax
from jax.experimental import pallas as pl
from jax.experimental.pallas import tpu as pltpu
from jax.sharding import PartitionSpec as P

HEAD = 128
BLOCK = 512
HALF = BLOCK // 2
TEAM = 4
SIDE = 8
EXTRA = 16
EPSILON = 1e-06
F32 = jnp.float32
BF16 = jnp.bfloat16
GRANT = 5 * 1024 * 1024
VMEM = pl.BlockSpec(memory_space=pltpu.VMEM)
HBM = pl.BlockSpec(memory_space=pltpu.HBM)
ANY = pl.BlockSpec(memory_space=pl.ANY)


def nt(a, b, precision=None):
    return lax.dot_general(a, b, (((1,), (1,)), ((), ())), preferred_element_type=F32, precision=precision)


def nn(a, b):
    return lax.dot_general(a, b, (((1,), (0,)), ((), ())), preferred_element_type=F32)


def half(i):
    return slice(i * HALF, (i + 1) * HALF)


def chunk(i):
    return slice(i * HEAD, (i + 1) * HEAD)


def split_terms(x, count):
    terms = []
    for _ in range(count):
        term = x.astype(BF16)
        terms.append(term)
        x = x - term.astype(F32)
    return terms


def read_wide(ref, hq):
    base = hq * HEAD
    return [
        (ref[chunk(j), :], ref[base + j : base + j + 1, :], ref[base + TEAM + j : base + TEAM + j + 1, :])
        for j in range(hq)
    ]


def write_wide(ref, hq, items):
    base = hq * HEAD
    at = lax.broadcasted_iota(jnp.int32, (SIDE, HEAD), 0)
    side = jnp.zeros((SIDE, HEAD), F32)
    for j, (term, edge, gain) in enumerate(items):
        ref[chunk(j), :] = term
        side = jnp.where(at == j, edge, side)
        side = jnp.where(at == TEAM + j, gain, side)
    ref[base : base + SIDE, :] = side


def read_narrow(ref, hq):
    base = hq * HEAD
    side = ref[base : base + EXTRA, :].astype(F32)
    row = lambda i: side[i : i + 1, :] + side[i + 1 : i + 2, :]
    return [(ref[chunk(j), :].astype(F32), row(2 * j), row(2 * TEAM + 2 * j)) for j in range(hq)]


def write_narrow(ref, hq, items):
    base = hq * HEAD
    at = lax.broadcasted_iota(jnp.int32, (EXTRA, HEAD), 0)
    side = jnp.zeros((EXTRA, HEAD), F32)
    for j, (term, edge, gain) in enumerate(items):
        ref[chunk(j), :] = term.astype(BF16)
        for first, value in ((2 * j, edge), (2 * TEAM + 2 * j, gain)):
            for i, part in enumerate(split_terms(value, 2)):
                side = jnp.where(at == first + i, part.astype(F32), side)
    ref[base : base + EXTRA, :] = side.astype(BF16)


def core():
    return lax.rem(lax.axis_index("ctx"), 2)


def pair():
    return lax.rem(lax.axis_index("ctx") // 2, 2)


def group():
    return lax.axis_index("ctx") // TEAM


def quarter_of(y, same):
    return 2 * y + (core() if same else 1 - core())


def head_at(quarter, hq, j):
    h = quarter * hq + j
    return h, pl.ds(pl.multiple_of(h * HEAD, HEAD), HEAD)


def transposed(x):
    shape = (x.shape[1], x.shape[1])
    eye = (lax.broadcasted_iota(jnp.int32, shape, 0) == lax.broadcasted_iota(jnp.int32, shape, 1)).astype(BF16)
    return nt(eye, x)


def several(quarter, hq):
    count = min(hq, 2)
    for j in range(0, hq, count):
        h = quarter * hq + j
        yield j, h, count, pl.ds(pl.multiple_of(h * HEAD, HEAD), count * HEAD)


def call(body, inputs, out_shape, name, scratch=(), flops=0, in_specs=None, out_specs=None, alias=None):
    nbytes = sum(x.size * x.dtype.itemsize for x in inputs)
    nbytes += sum(x.size * x.dtype.itemsize for x in out_shape)
    out_shape = list(out_shape)
    for o in (alias or {}).values():
        out_shape[o] = pltpu.VMEM(out_shape[o].shape, out_shape[o].dtype)
    return pl.pallas_call(
        body,
        in_specs=in_specs or [VMEM] * len(inputs),
        out_specs=out_specs or [VMEM] * len(out_shape),
        out_shape=out_shape,
        scratch_shapes=list(scratch),
        input_output_aliases=alias or {},
        compiler_params=pltpu.CompilerParams(vmem_limit_bytes=GRANT),
        cost_estimate=pl.CostEstimate(flops=flops, bytes_accessed=nbytes, transcendentals=0),
        name=name,
    )(*inputs)


def joined(mine, other, mine_is_first, reverse):
    out = []
    for (a, ea, ga), (b, eb, gb) in zip(mine, other):
        near = mine_is_first if reverse else jnp.logical_not(mine_is_first)
        wa = jnp.where(near, 1.0, jnp.exp(eb))
        wb = jnp.where(near, jnp.exp(ea), 1.0)
        out.append((a * wa + b * wb, ea + eb, ga + gb))
    return out


def chip_total_body(reverse, hq, keep, got, own, send):
    first = core() == 0
    read_got = read_narrow if reverse else read_wide
    here, there = pair(), 1 - pair()
    own_items = joined(read_wide(keep.at[here], hq), read_got(got.at[here], hq), first, reverse)
    write_wide(own, hq, own_items)
    send_items = joined(read_wide(keep.at[there], hq), read_got(got.at[there], hq), first, reverse)
    write_narrow(send, hq, send_items)


def group_total_body(reverse, hq, own, got, *refs):
    total, send = refs[-2:]
    items = joined(read_wide(own, hq), read_narrow(got, hq), pair() == 0, reverse)
    write_wide(total, hq, items)
    write_narrow(send, hq, items)


def met(reverse, step, before, other):
    near = lax.rem(group() // step, 2) == (0 if reverse else 1)
    out = []
    for old, (term, edge, gain) in zip(before, other):
        term = jnp.where(near, term, 0.0)
        edge = jnp.where(near, edge, 0.0)
        if old is None:
            out.append((term, edge, gain))
        else:
            out.append((old[0] + jnp.exp(old[1]) * term, old[1] + edge, gain))
    return out


def window_body(reverse, hq, step, total, *refs):
    so_far, whole, send = refs[-3:]
    if step == 1:
        got = refs[0]
        before = [None] * hq
    else:
        got = refs[1]
        before = read_wide(refs[0], hq)
    other = read_narrow(got, hq)
    write_wide(so_far, hq, met(reverse, step, before, other))
    items = joined(read_wide(total, hq), other, lax.rem(group() // step, 2) == 0, reverse)
    write_wide(whole, hq, items)
    write_narrow(send, hq, items)


def into_chips_body(reverse, hq, step, own, got_pair, total, so_far, got, *refs):
    keep, send = refs[-2:]
    before = read_wide(so_far, hq) if step > 1 else [None] * hq
    entering = met(reverse, step, before, read_narrow(got, hq))
    mine_near = pair() == (1 if reverse else 0)
    kept, sent = [], []
    for (r, _, gr), (c, ec, _), (o, eo, _), (_, _, gt) in zip(
        entering, read_wide(own, hq), read_narrow(got_pair, hq), read_wide(total, hq)
    ):
        gain = gr + gt
        zero = jnp.zeros_like(ec)
        kept.append((jnp.where(mine_near, r, jnp.exp(eo) * r + o), zero, gain))
        sent.append((jnp.where(mine_near, jnp.exp(ec) * r + c, r), zero, gain))
    write_wide(keep, hq, kept)
    write_narrow(send, hq, sent)


def into_cores_body(reverse, hq, keep, got, own, other, *refs):
    mine, send = refs[-2:]
    mine_near = core() == (1 if reverse else 0)
    read_got = read_narrow if reverse else read_wide
    for y in range(2):
        a, b = read_wide(own, hq), read_narrow(other, hq)
        here = pair() == y
        items_mine, items_send = [], []
        for p, q, (k, ek, _), (g, eg, _) in zip(a, b, read_wide(keep.at[y], hq), read_got(got.at[y], hq)):
            r = jnp.where(here, p[0], q[0])
            gain = jnp.where(here, p[2], q[2])
            zero = jnp.zeros_like(ek)
            items_mine.append((jnp.where(mine_near, r, jnp.exp(eg) * r + g), zero, gain))
            items_send.append((jnp.where(mine_near, jnp.exp(ek) * r + k, r), zero, gain))
        write_narrow(mine.at[y], hq, items_mine)
        write_narrow(send.at[y], hq, items_send)


def block_states(hq, y, same, k, v, row, out):
    items = []
    for j, h, count, c in several(quarter_of(y, same), hq):
        turned = transposed(k[:, c])
        lines = [row[pl.ds(h + m, 1), :] for m in range(count)]
        edges = [line[:, BLOCK - 1 : BLOCK] for line in lines]
        faded = [turned[chunk(m)] * jnp.exp(edges[m] - lines[m]) for m in range(count)]
        both = nn(jnp.concatenate([x.astype(BF16) for x in faded], axis=0), v[:, c])
        for m in range(count):
            items.append((both[chunk(m), chunk(m)], jnp.broadcast_to(edges[m], (1, HEAD)), jnp.zeros((1, HEAD), F32)))
    write_wide(out.at[y], hq, items)


def sent_states_body(heads, swaps, k_hbm, v_hbm, ld_hbm, *refs):
    hq = heads // TEAM
    w = hq * HEAD
    if swaps:
        grad, give, row, k, v, away, ld, sems, side_sems = refs
        width = heads * HEAD
        there = pl.ds(pl.multiple_of((1 - lax.axis_index("tp")) * width, HEAD), width)
        side_copies = [pltpu.make_async_copy(grad.at[:, there], away, side_sems.at[1])]
    else:
        give, row, k, v, ld, sems, side_sems = refs
        side_copies = []
    first = pltpu.make_async_copy(ld_hbm, ld, side_sems.at[0])
    first.start()
    order = [(0, False), (1, False), (0, True), (1, True)]
    copies = []
    for slot, (y, same) in enumerate(order):
        cols_d = pl.ds(pl.multiple_of(quarter_of(y, same) * w, HEAD), w)
        both = [
            pltpu.make_async_copy(k_hbm.at[:, cols_d], k.at[:, cols_d], sems.at[0, slot]),
            pltpu.make_async_copy(v_hbm.at[:, cols_d], v.at[:, cols_d], sems.at[1, slot]),
        ]
        for c in both:
            c.start()
        copies.append(both)
    for c in side_copies:
        c.start()
    at = lax.broadcasted_iota(jnp.int32, (BLOCK, BLOCK), 0)
    other = lax.broadcasted_iota(jnp.int32, (BLOCK, BLOCK), 1)
    tri = (at <= other).astype(BF16)
    first.wait()
    x = ld[...]
    if heads < EXTRA:
        x = jnp.concatenate([x, jnp.zeros((EXTRA - heads, BLOCK), F32)], axis=0)
    sums = nn(jnp.concatenate(split_terms(x, 3), axis=0), tri)
    row[...] = sums[0:EXTRA] + (sums[EXTRA : 2 * EXTRA] + sums[2 * EXTRA : 3 * EXTRA])
    for slot, (y, same) in enumerate(order):
        for c in copies[slot]:
            c.wait()
        if not same:
            block_states(hq, y, same, k, v, row, give)
    for c in side_copies:
        c.wait()


def kept_states_body(heads, k, v, row, keep):
    for y in range(2):
        block_states(heads // TEAM, y, True, k, v, row, keep)


def decays_body(heads, row, q_hbm, _, col, growth, q, sem):
    hq = heads // TEAM
    copy = pltpu.make_async_copy(q_hbm, q, sem)
    copy.start()
    for g in range(TEAM):
        rows = row[g * hq : (g + 1) * hq, :]
        across = jnp.concatenate([rows, jnp.zeros((HEAD - hq, BLOCK), F32)], axis=0).T
        col[g] = across
        growth[g] = jnp.exp(across)
    copy.wait()


def decay_table(high, low, lower):
    table = jnp.exp(high - low)
    at = lax.broadcasted_iota(jnp.int32, (HALF, HALF), 0)
    other = lax.broadcasted_iota(jnp.int32, (HALF, HALF), 1)
    if lower:
        cut = jnp.where(at >= other, table[:, -HALF:], 0.0)
        return cut if table.shape[1] == HALF else jnp.concatenate([table[:, :HALF], cut], axis=1)
    cut = jnp.where(at <= other, table[:, :HALF], 0.0)
    return cut if table.shape[1] == HALF else jnp.concatenate([cut, table[:, HALF:]], axis=1)


def turned_probs_body(heads, first, q, k, row, col, _, *refs):
    hq = heads // TEAM
    tables, probs = refs[-4:-2], refs[-2:]

    def one(g, _):
        for j in range(hq):
            h, c = head_at(g, hq, j)
            line = row[pl.ds(h, 1), :]
            for i in range(2):
                t = slice(i * HALF, BLOCK)
                table = decay_table(line[:, t], col[g, half(i), j : j + 1], False)
                tables[i][h] = table
                probs[i][h] = (nt(k[half(i), c], q[t, c]) * table).astype(BF16)
        return 0

    lax.fori_loop(first, first + TEAM // 2, one, 0)


def intra_body(heads, first, last, q, k, v, row, col, *refs):
    hq = heads // TEAM
    intra = refs[-1]

    def one(g, _):
        for j in range(hq):
            h, c = head_at(g, hq, j)
            line = row[pl.ds(h, 1), :]
            for i in range(2):
                u = slice(0, (i + 1) * HALF)
                table = decay_table(col[g, half(i), j : j + 1], line[:, u], True)
                probs = (nt(q[half(i), c], k[u, c]) * table).astype(BF16)
                intra[half(i), c] = nn(probs, v[u, c])
        return 0

    lax.fori_loop(first, last, one, 0)


def dscaled_rows(heads, where, gate, ref, gain, dscaled):
    part = ref.shape[0]
    rows = pl.ds(pl.multiple_of(where * part, part), part)

    def one(g, _):
        for j in range(heads // TEAM):
            _, c = head_at(g, heads // TEAM, j)
            opened = jax.nn.sigmoid(gate[rows, c].astype(F32))
            dscaled[rows, c] = ref[:, c].astype(F32) * opened * gain[:, c]
        return 0

    lax.fori_loop(0, TEAM, one, 0)


def own_dscaled_body(heads, swaps, gate, grad, gain, q, row, _, dscaled, turned, own, sem):
    width = heads * HEAD
    mine = lax.axis_index("tp") if swaps else 0
    here = pl.ds(pl.multiple_of(mine * width, HEAD), width)
    copy = pltpu.make_async_copy(grad.at[:, here], own, sem)
    copy.start()

    def one(g, _):
        for j, h, count, c in several(g, heads // TEAM):
            both = transposed(q[:, c])
            for m in range(count):
                rows = pl.ds(pl.multiple_of((h + m) * HEAD, HEAD), HEAD)
                turned[rows, :] = (both[chunk(m)] * jnp.exp(row[pl.ds(h + m, 1), :])).astype(BF16)
        return 0

    lax.fori_loop(0, TEAM, one, 0)
    copy.wait()
    dscaled_rows(heads, mine, gate, own, gain, dscaled)


def got_dscaled_body(heads, swaps, gate, got, gain, _, dscaled):
    dscaled_rows(heads, 1 - lax.axis_index("tp") if swaps else 1, gate, got, gain, dscaled)


def states_of(state, j, count):
    if count == 1:
        return state[chunk(j), :]
    zero = jnp.zeros((HEAD, HEAD), BF16)
    upper = jnp.concatenate([state[chunk(j), :], zero], axis=1)
    lower = jnp.concatenate([zero, state[chunk(j + 1), :]], axis=1)
    return jnp.concatenate([upper, lower], axis=0)


def attention_body(heads, same, q, intra, dscaled, growth, state, *refs):
    hq = heads // TEAM
    if same:
        att, sq, inn, both = refs
    else:
        _, sq_before, inn_before, att, sums, sq, inn, both = refs
        sq[...] = sq_before[...]
        inn[...] = inn_before[...]
    for y in range(2):
        g = quarter_of(y, same)
        for j, h, count, c in several(g, hq):
            both[:, 0 : count * HEAD] = nn(q[:, c], states_of(state.at[y], j, count))
            for i in range(BLOCK // HEAD):
                r = chunk(i)
                a_sq = a_in = 0.0
                for m in range(count):
                    _, c = head_at(g, hq, j + m)
                    a = intra[r, c] + both[r, chunk(m)] * growth[g, r, j + m : j + m + 1]
                    att[r, c] = a
                    a_sq = a_sq + a * a
                    a_in = a_in + a * dscaled[r, c]
                if same and y == 0 and j == 0:
                    sq[r, :] = a_sq
                    inn[r, :] = a_in
                else:
                    sq[r, :] += a_sq
                    inn[r, :] += a_in
    if not same:
        ones = jnp.ones((8, HEAD), F32)
        a = nt(ones, sq[...], lax.Precision.HIGHEST)
        b = nt(ones, inn[...], lax.Precision.HIGHEST)
        sums[...] = jnp.where(lax.broadcasted_iota(jnp.int32, (8, BLOCK), 0) == 0, a, b)


def dattn_body(heads, channels, same, att, dscaled, turned, gain, row, *refs):
    hq = heads // TEAM
    if same:
        rsb, coefb, _, dattn, out = refs
    else:
        sum_a, sum_b, _, dattn, out, rsb, coefb = refs
        total = sum_a[...] + sum_b[...]
        rs = lax.rsqrt(total[0:1, :] / channels + EPSILON)
        coef = total[1:2, :] * (rs * rs * rs) / channels
        down = jnp.concatenate([rs, coef, jnp.zeros((HEAD - 2, BLOCK), F32)], axis=0).T
        rsb[...] = jnp.broadcast_to(down[:, 0:1], (BLOCK, HEAD))
        coefb[...] = jnp.broadcast_to(down[:, 1:2], (BLOCK, HEAD))
    for y in range(2):
        items = []
        for j, h, count, cols in several(quarter_of(y, same), hq):
            parts = []
            for m in range(count):
                _, c = head_at(quarter_of(y, same), hq, j + m)
                gsum = jnp.zeros((8, HEAD), F32)
                for i in range(BLOCK // HEAD):
                    r = chunk(i)
                    a = att[r, c]
                    t = dscaled[r, c] * rsb[r, :]
                    dattn[r, c] = (t - a * coefb[r, :]).astype(BF16)
                    gsum = gsum + jnp.sum((t * a).reshape(HEAD // 8, 8, HEAD), axis=0)
                parts.append(jnp.sum(gsum, axis=0, keepdims=True) / gain[:, c])
            both = nn(turned[pl.ds(pl.multiple_of(h * HEAD, HEAD), count * HEAD), :], dattn[:, cols])
            for m in range(count):
                edge = jnp.broadcast_to(row[pl.ds(h + m, 1), :][:, BLOCK - 1 : BLOCK], (1, HEAD))
                items.append((both[chunk(m), chunk(m)], edge, parts[m]))
        (write_wide if same else write_narrow)(out.at[y], hq, items)


def unscaled_gate_body(heads, gate, att, dscaled, _, out):
    hq = heads // TEAM
    for g in range(TEAM):
        for j in range(hq):
            _, c = head_at(g, hq, j)
            closed = jax.nn.sigmoid(-gate[:, c].astype(F32))
            out[:, c] = dscaled[:, c] * att[:, c] * closed


def leave(out, ref, sems, g, w):
    cols = pl.ds(pl.multiple_of(g * w, HEAD), w)
    copy = pltpu.make_async_copy(out, ref.at[:, cols], sems)
    copy.start()
    return copy


def gate_body(heads, unscaled, scale, _, gate_grad, token, out, sems):
    hq = heads // TEAM
    token[...] = jnp.zeros_like(token)
    copies = []
    for g in range(TEAM):
        for j in range(hq):
            _, c = head_at(g, hq, j)
            out[g, :, chunk(j)] = (unscaled[:, c] * scale[...]).astype(BF16)
        copies.append(leave(out.at[g], gate_grad, sems.at[g], g, hq * HEAD))
    for copy in copies:
        copy.wait()


def by_quarter(mine, got):
    return [(ref.at[y], quarter_of(y, same)) for ref, same in ((mine, True), (got, False)) for y in range(2)]


def query_body(heads, k, v, dattn, row, col, growth, mine, got, _, query_grad):
    hq = heads // TEAM
    for state, g in by_quarter(mine, got):
        for j in range(hq):
            h, c = head_at(g, hq, j)
            line = row[pl.ds(h, 1), :]
            for i in range(2):
                d = dattn[half(i), c]
                u = slice(0, (i + 1) * HALF)
                table = decay_table(col[g, half(i), j : j + 1], line[:, u], True)
                dscores = (nt(d, v[u, c]) * table).astype(BF16)
                inter = nt(d, state[chunk(j), :]) * growth[g, half(i), j : j + 1]
                query_grad[half(i), c] = (inter + nn(dscores, k[u, c])).astype(BF16)


def key_value_body(heads, first, last, carries, q, v, dattn, table0, table1, probs0, probs1, _, *refs):
    hq = heads // TEAM
    count = min(hq, 2)
    if carries:
        dk, dv, outside, sems = refs[-4:]
        rows = [slice(i * HEAD, (i + 1) * HEAD) for i in range(BLOCK // HEAD)]
        copies = [pltpu.make_async_copy(refs[0].at[r], outside.at[r], sems.at[i]) for i, r in enumerate(rows)]
    else:
        dk, dv = refs[-2:]
        copies = []
    for copy in copies:
        copy.start()

    def one(step, _):
        for m in range(count):
            h = step * count + m
            _, c = head_at(h, 1, 0)
            for i, (table, probs) in enumerate(((table0, probs0), (table1, probs1))):
                t = slice(i * HALF, BLOCK)
                dscores = (nt(v[half(i), c], dattn[t, c]) * table[h]).astype(BF16)
                dk[half(i), c] = nn(dscores, q[t, c])
                dv[half(i), c] = nn(probs[h], dattn[t, c])
        return 0

    lax.fori_loop(first, last, one, 0)
    for copy in copies:
        copy.wait()


def fades(col, y, same):
    sums = col[quarter_of(y, same)]
    return jnp.exp(sums[BLOCK - 1 : BLOCK, :] - sums)


def final_rows(hq, y, j, count, c, k, v, dk, dv, shrink, state, key_out, value_out):
    after = states_of(state.at[y], j, count)
    key_side, value_side = nt(v[:, c], after), nn(k[:, c], after)
    for m in range(count):
        fade = shrink[:, j + m : j + m + 1]
        own = pl.ds(pl.multiple_of(c.start + m * HEAD, HEAD), HEAD)
        key_out[y, :, chunk(j + m)] = (dk[:, own] + key_side[:, chunk(m)] * fade).astype(BF16)
        value_out[y, :, chunk(j + m)] = (dv[:, own] + value_side[:, chunk(m)] * fade).astype(BF16)


def own_final_body(heads, k, v, dk, dv, col, state, key_out, value_out, gain_grad):
    hq = heads // TEAM
    for y in range(2):
        items = read_narrow(state.at[y], hq)
        shrink = fades(col, y, True)
        for j, _, count, c in several(quarter_of(y, True), hq):
            final_rows(hq, y, j, count, c, k, v, dk, dv, shrink, state, key_out, value_out)
            for m in range(j, j + count):
                gain_grad[:, head_at(quarter_of(y, True), hq, m)[1]] = items[m][2]


def final_body(heads, k, v, dk, dv, col, state, own_key, own_value, own_gain, *refs):
    hq = heads // TEAM
    key_grad, value_grad, gain_grad, gains, key_out, value_out, sems = refs
    copies = []

    def send(src, dst, cols):
        copy = pltpu.make_async_copy(src, dst.at[:, cols], sems.at[len(copies)])
        copy.start()
        copies.append(copy)

    gains[...] = own_gain[...]
    for y in range(2):
        for j, (_, _, total) in enumerate(read_narrow(state.at[y], hq)):
            gains[:, head_at(quarter_of(y, False), hq, j)[1]] = total
    send(gains, gain_grad, slice(None))
    for y in range(2):
        for j, _, count, c in several(quarter_of(y, True), hq):
            place = slice(j * HEAD, (j + count) * HEAD)
            send(own_key.at[y, :, place], key_grad, c)
            send(own_value.at[y, :, place], value_grad, c)
    for y in range(2):
        shrink = fades(col, y, False)
        for j, _, count, c in several(quarter_of(y, False), hq):
            final_rows(hq, y, j, count, c, k, v, dk, dv, shrink, state, key_out, value_out)
            place = slice(j * HEAD, (j + count) * HEAD)
            send(key_out.at[y, :, place], key_grad, c)
            send(value_out.at[y, :, place], value_grad, c)
    for copy in copies:
        copy.wait()


def in_hbm(x):
    return pltpu.with_memory_space_constraint(x, pltpu.HBM)


def swap(x, bit):
    n = lax.axis_size("ctx")
    return lax.ppermute(x, "ctx", [(i, i ^ bit) for i in range(n)])


def local(queries, keys, values, log_decay, gate, gain, grad_out):
    rows, width = queries.shape
    heads = width // HEAD
    hq = heads // TEAM
    tp = lax.axis_size("tp")
    n = lax.axis_size("ctx")
    groups = n // TEAM
    channels = width * tp
    bf = lambda *shape: jax.ShapeDtypeStruct(shape, BF16)
    f32 = lambda *shape: jax.ShapeDtypeStruct(shape, F32)
    swaps = tp == 2
    part = rows // 2
    small = 2 * heads * rows * HEAD * HEAD
    large = 2 * heads * rows * rows * HEAD
    wide = f32(hq * HEAD + SIDE, HEAD)
    wide2 = f32(2, hq * HEAD + SIDE, HEAD)
    narrow = bf(hq * HEAD + EXTRA, HEAD)
    narrow2 = bf(2, hq * HEAD + EXTRA, HEAD)
    table = f32(TEAM, rows, HEAD)
    gain_row = gain.reshape(1, width)

    def beside(work, after, name):
        return [work[name](after)] if name in work else []

    def step_call(body, reverse, inputs, unread, shapes, name, *sizes):
        return call(
            functools.partial(body, reverse, hq, *sizes),
            [*inputs, *unread],
            shapes,
            name,
            in_specs=[VMEM] * len(inputs) + [ANY] * len(unread),
        )

    def scan(reverse, keep, give, work):
        got = swap(give, 1)
        own, send = step_call(chip_total_body, reverse, [keep, got], [], [wide, narrow], "chip_total")
        got_pair = swap(send, 2)
        unread = beside(work, send, "pair")
        total, send = step_call(group_total_body, reverse, [own, got_pair], unread, [wide, narrow], "group_total")
        so_far, step = total, 1
        while 2 * step < groups:
            far = swap(send, TEAM * step)
            unread = beside(work, send, "one") if step == 1 else []
            before = [] if step == 1 else [so_far]
            so_far, total, send = step_call(
                window_body, reverse, [total, *before, far], unread, [wide, wide, narrow], "window", step
            )
            step *= 2
        far = swap(send, TEAM * step)
        unread = beside(work, send, "last")
        kept, send = step_call(
            into_chips_body, reverse, [own, got_pair, total, so_far, far], unread, [wide, narrow], "into_chips", step
        )
        other = swap(send, 2)
        unread = beside(work, send, "pair_back")
        mine, send = step_call(
            into_cores_body, reverse, [keep, got, kept, other], unread, [narrow2, narrow2], "into_cores"
        )
        return mine, swap(send, 1)

    outs = call(
        functools.partial(sent_states_body, heads, swaps),
        [in_hbm(keys), in_hbm(values), in_hbm(log_decay)] + [in_hbm(grad_out)] * swaps,
        [wide2, f32(EXTRA, rows), bf(rows, width), bf(rows, width)] + [bf(part, width)] * swaps,
        "sent_states",
        [
            pltpu.VMEM(log_decay.shape, F32),
            pltpu.SemaphoreType.DMA((2, TEAM)),
            pltpu.SemaphoreType.DMA((2,)),
        ],
        small // 2,
        [HBM] * (3 + swaps),
        [VMEM] * 4 + [HBM] * swaps,
    )
    give, row, keys, values = outs[:4]
    if swaps:
        arrived = lax.ppermute(outs[4], "tp", [(0, 1), (1, 0)])
        own = grad_out
    else:
        every = lax.all_to_all(grad_out, "tp", split_axis=1, concat_axis=0, tiled=True)
        own, arrived = every[:part], every[part:]
    (keep,) = call(
        functools.partial(kept_states_body, heads), [keys, values, row], [wide2], "kept_states", flops=small // 2
    )
    done = {}

    def probs_beside(after):
        if "decays" not in done:
            *done["decays"], done["queries"] = call(
                functools.partial(decays_body, heads),
                [row, in_hbm(queries), after],
                [table] * 2 + [bf(rows, width)],
                "decays",
                [pltpu.SemaphoreType.DMA(())],
                in_specs=[VMEM, HBM, ANY],
            )
        before = done.get("probs", [])
        done["probs"] = call(
            functools.partial(turned_probs_body, heads, TEAM // 2 if before else 0),
            [done["queries"], keys, row, done["decays"][0], after, *before],
            [f32(heads, HALF, BLOCK), f32(heads, HALF, HALF), bf(heads, HALF, BLOCK), bf(heads, HALF, HALF)],
            "turned_probs",
            flops=large // 2,
            in_specs=[VMEM] * 4 + [ANY] + [VMEM] * len(before),
            alias={5 + i: i for i in range(len(before))},
        )
        return done["probs"][3]

    def intra_beside(after):
        before = [done["intra"]] if "intra" in done else []
        first, last = (1, TEAM) if before else (0, 1)
        (done["intra"],) = call(
            functools.partial(intra_body, heads, first, last),
            [done["queries"], keys, values, row, done["decays"][0], after, *before],
            [f32(rows, width)],
            "intra",
            flops=2 * large * (last - first) // TEAM,
            in_specs=[VMEM] * 5 + [ANY] + [VMEM] * len(before),
            alias={6: 0} if before else None,
        )
        return done["intra"]

    def probs_and_intra(after):
        return intra_beside(probs_beside(after))

    def dscaled_beside(after):
        done["dscaled"] = call(
            functools.partial(own_dscaled_body, heads, swaps),
            [gate, in_hbm(own), gain_row, done["queries"], row, after],
            [f32(rows, width), bf(width, rows)],
            "own_dscaled",
            [pltpu.VMEM((part, width), BF16), pltpu.SemaphoreType.DMA(())],
            small,
            [VMEM, HBM, VMEM, VMEM, VMEM, ANY],
        )
        (dscaled,) = call(
            functools.partial(got_dscaled_body, heads, swaps),
            [gate, arrived, gain_row, done["dscaled"][0]],
            [f32(rows, width)],
            "got_dscaled",
            alias={3: 0},
        )
        done["dscaled"] = dscaled, done["dscaled"][1]
        return dscaled

    work = {"pair": probs_beside, "one": probs_and_intra, "last": intra_beside, "pair_back": dscaled_beside}
    mine, got = scan(False, keep, give, work)
    queries = done["queries"]
    (col, growth), intra, (dscaled, turned) = done["decays"], done["intra"], done["dscaled"]
    tall = f32(rows, HEAD)
    wide_scratch = pltpu.VMEM((rows, 2 * HEAD), F32)
    att, squares, inner = call(
        functools.partial(attention_body, heads, True),
        [queries, intra, dscaled, growth, mine],
        [f32(rows, width), tall, tall],
        "attention",
        [wide_scratch],
        small // 2,
    )
    att, sums = call(
        functools.partial(attention_body, heads, False),
        [queries, intra, dscaled, growth, got, att, squares, inner],
        [f32(rows, width), f32(8, rows)],
        "attention",
        [pltpu.VMEM((rows, HEAD), F32)] * 2 + [wide_scratch],
        small // 2,
        alias={5: 0},
    )
    (unscaled_gate,) = call(
        functools.partial(unscaled_gate_body, heads),
        [gate, att, dscaled, intra],
        [f32(rows, width)],
        "unscaled_gate",
        in_specs=[VMEM] * 3 + [ANY],
        alias={3: 0},
    )
    if swaps:
        others = lax.ppermute(sums, "tp", [(0, 1), (1, 0)])
    else:
        others = lax.psum(sums, "tp") - sums
    dattn, give, scale, coef = call(
        functools.partial(dattn_body, heads, channels, False),
        [att, dscaled, turned, gain_row, row, sums, others, unscaled_gate],
        [bf(rows, width), narrow2, tall, tall],
        "sent_dattn",
        flops=small // 2,
        in_specs=[VMEM] * 7 + [ANY],
    )
    dattn, keep = call(
        functools.partial(dattn_body, heads, channels, True),
        [att, dscaled, turned, gain_row, row, scale, coef, dattn],
        [bf(rows, width), wide2],
        "kept_dattn",
        flops=small // 2,
        alias={7: 0},
    )
    out_scratch = [pltpu.VMEM((TEAM, rows, hq * HEAD), BF16), pltpu.SemaphoreType.DMA((TEAM,))]

    def gate_beside(after):
        done["gate"], token = call(
            functools.partial(gate_body, heads),
            [unscaled_gate, scale, after],
            [bf(rows, width), f32(SIDE, HEAD)],
            "gate",
            out_scratch,
            small,
            [VMEM] * 2 + [ANY],
            [HBM, VMEM],
        )
        return token

    units = heads // min(hq, 2)
    cuts = [0, units // 4, 5 * units // 8, units]

    def key_value_beside(after, carried=()):
        before = done.get("key_value", [])
        piece = done.get("piece", 0)
        done["piece"] = piece + 1
        inputs = [queries, values, dattn, *done["probs"], after, *carried, *before]
        results = call(
            functools.partial(key_value_body, heads, cuts[piece], cuts[piece + 1], len(carried)),
            inputs,
            [f32(rows, width)] * 2 + [bf(rows, width)] * len(carried),
            "key_value",
            [pltpu.SemaphoreType.DMA((rows // HEAD,))] * len(carried),
            4 * large * (cuts[piece + 1] - cuts[piece]) // units,
            [VMEM] * 7 + [ANY] + [VMEM] * (len(carried) + len(before)),
            [VMEM] * 2 + [HBM] * len(carried),
            {8 + len(carried) + i: i for i in range(len(before))},
        )
        done["key_value"] = results[:2]
        return results[0], results[-1]

    def gate_and_key_value(after):
        return key_value_beside(gate_beside(after))[0]

    def query_beside(after):
        (done["query"],) = call(
            functools.partial(query_body, heads),
            [keys, values, dattn, row, col, growth, mine, got, after],
            [bf(rows, width)],
            "query",
            flops=2 * large + small,
            in_specs=[VMEM] * 8 + [ANY],
        )
        return done["query"]

    def key_value_last(after):
        dk, done["query"] = key_value_beside(after, [done["query"]])
        return dk

    work = {"pair": gate_and_key_value, "one": lambda after: key_value_beside(after)[0], "last": query_beside, "pair_back": key_value_last}
    back_mine, back_got = scan(True, keep, give, work)
    gate_grad, query_grad, (dk, dv) = done["gate"], done["query"], done["key_value"]
    both = bf(2, rows, hq * HEAD)
    own_key, own_value, own_gain = call(
        functools.partial(own_final_body, heads),
        [keys, values, dk, dv, col, back_mine],
        [both, both, f32(1, width)],
        "own_final",
        flops=small,
    )
    key_grad, value_grad, gain_grad = call(
        functools.partial(final_body, heads),
        [keys, values, dk, dv, col, back_got, own_key, own_value, own_gain],
        [bf(rows, width), bf(rows, width), f32(1, width)],
        "final",
        [pltpu.VMEM((1, width), F32)]
        + [pltpu.VMEM(both.shape, BF16)] * 2
        + [pltpu.SemaphoreType.DMA((8 * hq + 1,))],
        small,
        out_specs=[HBM, HBM, HBM],
    )
    return query_grad, key_grad, value_grad, gate_grad, gain_grad.reshape(width)


def solution(mesh):
    return jax.shard_map(
        local,
        mesh=mesh,
        in_specs=(
            P("ctx", "tp"),
            P("ctx", "tp"),
            P("ctx", "tp"),
            P("tp", "ctx"),
            P("ctx", "tp"),
            P("tp"),
            P(("ctx", "tp"), None),
        ),
        out_specs=(P("ctx", "tp"), P("ctx", "tp"), P("ctx", "tp"), P("ctx", "tp"), P("tp")),
        check_vma=False,
    )
```

```python
import functools

import jax
import jax.numpy as jnp
from jax import lax
from jax.experimental import pallas as pl
from jax.experimental.pallas import tpu as pltpu
from jax.sharding import PartitionSpec as P

HEAD = 128
BLOCK = 512
HALF = BLOCK // 2
TEAM = 4
SIDE = 8
EXTRA = 16
EPSILON = 1e-06
F32 = jnp.float32
BF16 = jnp.bfloat16
GRANT = 5 * 1024 * 1024
VMEM = pl.BlockSpec(memory_space=pltpu.VMEM)
HBM = pl.BlockSpec(memory_space=pltpu.HBM)
ANY = pl.BlockSpec(memory_space=pl.ANY)


def nt(a, b, precision=None):
    return lax.dot_general(a, b, (((1,), (1,)), ((), ())), preferred_element_type=F32, precision=precision)


def nn(a, b):
    return lax.dot_general(a, b, (((1,), (0,)), ((), ())), preferred_element_type=F32)


def half(i):
    return slice(i * HALF, (i + 1) * HALF)


def chunk(i):
    return slice(i * HEAD, (i + 1) * HEAD)


def split_terms(x, count):
    terms = []
    for _ in range(count):
        term = x.astype(BF16)
        terms.append(term)
        x = x - term.astype(F32)
    return terms


def read_wide(ref, hq):
    base = hq * HEAD
    return [
        (ref[chunk(j), :], ref[base + j : base + j + 1, :], ref[base + TEAM + j : base + TEAM + j + 1, :])
        for j in range(hq)
    ]


def write_wide(ref, hq, items):
    base = hq * HEAD
    at = lax.broadcasted_iota(jnp.int32, (SIDE, HEAD), 0)
    side = jnp.zeros((SIDE, HEAD), F32)
    for j, (term, edge, gain) in enumerate(items):
        ref[chunk(j), :] = term
        side = jnp.where(at == j, edge, side)
        side = jnp.where(at == TEAM + j, gain, side)
    ref[base : base + SIDE, :] = side


def read_narrow(ref, hq):
    base = hq * HEAD
    side = ref[base : base + EXTRA, :].astype(F32)
    row = lambda i: side[i : i + 1, :] + side[i + 1 : i + 2, :]
    return [(ref[chunk(j), :].astype(F32), row(2 * j), row(2 * TEAM + 2 * j)) for j in range(hq)]


def write_narrow(ref, hq, items):
    base = hq * HEAD
    at = lax.broadcasted_iota(jnp.int32, (EXTRA, HEAD), 0)
    side = jnp.zeros((EXTRA, HEAD), F32)
    for j, (term, edge, gain) in enumerate(items):
        ref[chunk(j), :] = term.astype(BF16)
        for first, value in ((2 * j, edge), (2 * TEAM + 2 * j, gain)):
            for i, part in enumerate(split_terms(value, 2)):
                side = jnp.where(at == first + i, part.astype(F32), side)
    ref[base : base + EXTRA, :] = side.astype(BF16)


def core():
    return lax.rem(lax.axis_index("ctx"), 2)


def pair():
    return lax.rem(lax.axis_index("ctx") // 2, 2)


def group():
    return lax.axis_index("ctx") // TEAM


def quarter_of(y, same):
    return 2 * y + (core() if same else 1 - core())


def head_at(quarter, hq, j):
    h = quarter * hq + j
    return h, pl.ds(pl.multiple_of(h * HEAD, HEAD), HEAD)


def transposed(x):
    shape = (x.shape[1], x.shape[1])
    eye = (lax.broadcasted_iota(jnp.int32, shape, 0) == lax.broadcasted_iota(jnp.int32, shape, 1)).astype(BF16)
    return nt(eye, x)


def several(quarter, hq):
    count = min(hq, 2)
    for j in range(0, hq, count):
        h = quarter * hq + j
        yield j, h, count, pl.ds(pl.multiple_of(h * HEAD, HEAD), count * HEAD)


def call(body, inputs, out_shape, name, scratch=(), flops=0, in_specs=None, out_specs=None, alias=None):
    nbytes = sum(x.size * x.dtype.itemsize for x in inputs)
    nbytes += sum(x.size * x.dtype.itemsize for x in out_shape)
    out_shape = list(out_shape)
    for o in (alias or {}).values():
        out_shape[o] = pltpu.VMEM(out_shape[o].shape, out_shape[o].dtype)
    return pl.pallas_call(
        body,
        in_specs=in_specs or [VMEM] * len(inputs),
        out_specs=out_specs or [VMEM] * len(out_shape),
        out_shape=out_shape,
        scratch_shapes=list(scratch),
        input_output_aliases=alias or {},
        compiler_params=pltpu.CompilerParams(vmem_limit_bytes=GRANT),
        cost_estimate=pl.CostEstimate(flops=flops, bytes_accessed=nbytes, transcendentals=0),
        name=name,
    )(*inputs)


def joined(mine, other, mine_is_first, reverse):
    out = []
    for (a, ea, ga), (b, eb, gb) in zip(mine, other):
        near = mine_is_first if reverse else jnp.logical_not(mine_is_first)
        wa = jnp.where(near, 1.0, jnp.exp(eb))
        wb = jnp.where(near, jnp.exp(ea), 1.0)
        out.append((a * wa + b * wb, ea + eb, ga + gb))
    return out


def chip_total_body(reverse, hq, keep, got, own, send):
    first = core() == 0
    read_got = read_narrow if reverse else read_wide
    here, there = pair(), 1 - pair()
    own_items = joined(read_wide(keep.at[here], hq), read_got(got.at[here], hq), first, reverse)
    write_wide(own, hq, own_items)
    send_items = joined(read_wide(keep.at[there], hq), read_got(got.at[there], hq), first, reverse)
    write_narrow(send, hq, send_items)


def group_total_body(reverse, hq, own, got, *refs):
    total, send = refs[-2:]
    items = joined(read_wide(own, hq), read_narrow(got, hq), pair() == 0, reverse)
    write_wide(total, hq, items)
    write_narrow(send, hq, items)


def met(reverse, step, before, other):
    near = lax.rem(group() // step, 2) == (0 if reverse else 1)
    out = []
    for old, (term, edge, gain) in zip(before, other):
        term = jnp.where(near, term, 0.0)
        edge = jnp.where(near, edge, 0.0)
        if old is None:
            out.append((term, edge, gain))
        else:
            out.append((old[0] + jnp.exp(old[1]) * term, old[1] + edge, gain))
    return out


def window_body(reverse, hq, step, total, *refs):
    so_far, whole, send = refs[-3:]
    if step == 1:
        got = refs[0]
        before = [None] * hq
    else:
        got = refs[1]
        before = read_wide(refs[0], hq)
    other = read_narrow(got, hq)
    write_wide(so_far, hq, met(reverse, step, before, other))
    items = joined(read_wide(total, hq), other, lax.rem(group() // step, 2) == 0, reverse)
    write_wide(whole, hq, items)
    write_narrow(send, hq, items)


def into_chips_body(reverse, hq, step, own, got_pair, total, so_far, got, *refs):
    keep, send = refs[-2:]
    before = read_wide(so_far, hq) if step > 1 else [None] * hq
    entering = met(reverse, step, before, read_narrow(got, hq))
    mine_near = pair() == (1 if reverse else 0)
    kept, sent = [], []
    for (r, _, gr), (c, ec, _), (o, eo, _), (_, _, gt) in zip(
        entering, read_wide(own, hq), read_narrow(got_pair, hq), read_wide(total, hq)
    ):
        gain = gr + gt
        zero = jnp.zeros_like(ec)
        kept.append((jnp.where(mine_near, r, jnp.exp(eo) * r + o), zero, gain))
        sent.append((jnp.where(mine_near, jnp.exp(ec) * r + c, r), zero, gain))
    write_wide(keep, hq, kept)
    write_narrow(send, hq, sent)


def into_cores_body(reverse, hq, keep, got, own, other, *refs):
    mine, send = refs[-2:]
    mine_near = core() == (1 if reverse else 0)
    read_got = read_narrow if reverse else read_wide
    for y in range(2):
        a, b = read_wide(own, hq), read_narrow(other, hq)
        here = pair() == y
        items_mine, items_send = [], []
        for p, q, (k, ek, _), (g, eg, _) in zip(a, b, read_wide(keep.at[y], hq), read_got(got.at[y], hq)):
            r = jnp.where(here, p[0], q[0])
            gain = jnp.where(here, p[2], q[2])
            zero = jnp.zeros_like(ek)
            items_mine.append((jnp.where(mine_near, r, jnp.exp(eg) * r + g), zero, gain))
            items_send.append((jnp.where(mine_near, jnp.exp(ek) * r + k, r), zero, gain))
        write_narrow(mine.at[y], hq, items_mine)
        write_narrow(send.at[y], hq, items_send)


def block_states(hq, y, same, k, v, row, out):
    items = []
    for j, h, count, c in several(quarter_of(y, same), hq):
        turned = transposed(k[:, c])
        lines = [row[pl.ds(h + m, 1), :] for m in range(count)]
        edges = [line[:, BLOCK - 1 : BLOCK] for line in lines]
        faded = [turned[chunk(m)] * jnp.exp(edges[m] - lines[m]) for m in range(count)]
        both = nn(jnp.concatenate([x.astype(BF16) for x in faded], axis=0), v[:, c])
        for m in range(count):
            items.append((both[chunk(m), chunk(m)], jnp.broadcast_to(edges[m], (1, HEAD)), jnp.zeros((1, HEAD), F32)))
    write_wide(out.at[y], hq, items)


def sent_states_body(heads, swaps, k_hbm, v_hbm, ld_hbm, *refs):
    hq = heads // TEAM
    w = hq * HEAD
    if swaps:
        grad, give, row, k, v, away, ld, sems, side_sems = refs
        width = heads * HEAD
        there = pl.ds(pl.multiple_of((1 - lax.axis_index("tp")) * width, HEAD), width)
        side_copies = [pltpu.make_async_copy(grad.at[:, there], away, side_sems.at[1])]
    else:
        give, row, k, v, ld, sems, side_sems = refs
        side_copies = []
    first = pltpu.make_async_copy(ld_hbm, ld, side_sems.at[0])
    first.start()
    order = [(0, False), (1, False), (0, True), (1, True)]
    copies = []
    for slot, (y, same) in enumerate(order):
        cols_d = pl.ds(pl.multiple_of(quarter_of(y, same) * w, HEAD), w)
        both = [
            pltpu.make_async_copy(k_hbm.at[:, cols_d], k.at[:, cols_d], sems.at[0, slot]),
            pltpu.make_async_copy(v_hbm.at[:, cols_d], v.at[:, cols_d], sems.at[1, slot]),
        ]
        for c in both:
            c.start()
        copies.append(both)
    for c in side_copies:
        c.start()
    at = lax.broadcasted_iota(jnp.int32, (BLOCK, BLOCK), 0)
    other = lax.broadcasted_iota(jnp.int32, (BLOCK, BLOCK), 1)
    tri = (at <= other).astype(BF16)
    first.wait()
    x = ld[...]
    if heads < EXTRA:
        x = jnp.concatenate([x, jnp.zeros((EXTRA - heads, BLOCK), F32)], axis=0)
    sums = nn(jnp.concatenate(split_terms(x, 3), axis=0), tri)
    row[...] = sums[0:EXTRA] + (sums[EXTRA : 2 * EXTRA] + sums[2 * EXTRA : 3 * EXTRA])
    for slot, (y, same) in enumerate(order):
        for c in copies[slot]:
            c.wait()
        if not same:
            block_states(hq, y, same, k, v, row, give)
    for c in side_copies:
        c.wait()


def kept_states_body(heads, k, v, row, keep):
    for y in range(2):
        block_states(heads // TEAM, y, True, k, v, row, keep)


def decays_body(heads, row, q_hbm, _, col, growth, q, sem):
    hq = heads // TEAM
    copy = pltpu.make_async_copy(q_hbm, q, sem)
    copy.start()
    for g in range(TEAM):
        rows = row[g * hq : (g + 1) * hq, :]
        across = jnp.concatenate([rows, jnp.zeros((HEAD - hq, BLOCK), F32)], axis=0).T
        col[g] = across
        growth[g] = jnp.exp(across)
    copy.wait()


def decay_table(high, low, lower):
    table = jnp.exp(high - low)
    at = lax.broadcasted_iota(jnp.int32, (HALF, HALF), 0)
    other = lax.broadcasted_iota(jnp.int32, (HALF, HALF), 1)
    if lower:
        cut = jnp.where(at >= other, table[:, -HALF:], 0.0)
        return cut if table.shape[1] == HALF else jnp.concatenate([table[:, :HALF], cut], axis=1)
    cut = jnp.where(at <= other, table[:, :HALF], 0.0)
    return cut if table.shape[1] == HALF else jnp.concatenate([cut, table[:, HALF:]], axis=1)


def turned_probs_body(heads, first, q, k, row, col, _, *refs):
    hq = heads // TEAM
    tables, probs = refs[-4:-2], refs[-2:]

    def one(g, _):
        for j in range(hq):
            h, c = head_at(g, hq, j)
            line = row[pl.ds(h, 1), :]
            for i in range(2):
                t = slice(i * HALF, BLOCK)
                table = decay_table(line[:, t], col[g, half(i), j : j + 1], False)
                tables[i][h] = table
                probs[i][h] = (nt(k[half(i), c], q[t, c]) * table).astype(BF16)
        return 0

    lax.fori_loop(first, first + TEAM // 2, one, 0)


def intra_body(heads, first, last, q, k, v, row, col, *refs):
    hq = heads // TEAM
    intra = refs[-1]

    def one(g, _):
        for j in range(hq):
            h, c = head_at(g, hq, j)
            line = row[pl.ds(h, 1), :]
            for i in range(2):
                u = slice(0, (i + 1) * HALF)
                table = decay_table(col[g, half(i), j : j + 1], line[:, u], True)
                probs = (nt(q[half(i), c], k[u, c]) * table).astype(BF16)
                intra[half(i), c] = nn(probs, v[u, c])
        return 0

    lax.fori_loop(first, last, one, 0)


def dscaled_rows(heads, where, gate, ref, gain, dscaled):
    part = ref.shape[0]
    rows = pl.ds(pl.multiple_of(where * part, part), part)

    def one(g, _):
        for j in range(heads // TEAM):
            _, c = head_at(g, heads // TEAM, j)
            opened = jax.nn.sigmoid(gate[rows, c].astype(F32))
            dscaled[rows, c] = ref[:, c].astype(F32) * opened * gain[:, c]
        return 0

    lax.fori_loop(0, TEAM, one, 0)


def own_dscaled_body(heads, swaps, gate, grad, gain, q, row, _, dscaled, turned, own, sem):
    width = heads * HEAD
    mine = lax.axis_index("tp") if swaps else 0
    here = pl.ds(pl.multiple_of(mine * width, HEAD), width)
    copy = pltpu.make_async_copy(grad.at[:, here], own, sem)
    copy.start()

    def one(g, _):
        for j, h, count, c in several(g, heads // TEAM):
            both = transposed(q[:, c])
            for m in range(count):
                rows = pl.ds(pl.multiple_of((h + m) * HEAD, HEAD), HEAD)
                turned[rows, :] = (both[chunk(m)] * jnp.exp(row[pl.ds(h + m, 1), :])).astype(BF16)
        return 0

    lax.fori_loop(0, TEAM, one, 0)
    copy.wait()
    dscaled_rows(heads, mine, gate, own, gain, dscaled)


def got_dscaled_body(heads, swaps, gate, got, gain, _, dscaled):
    dscaled_rows(heads, 1 - lax.axis_index("tp") if swaps else 1, gate, got, gain, dscaled)


def states_of(state, j, count):
    if count == 1:
        return state[chunk(j), :]
    zero = jnp.zeros((HEAD, HEAD), BF16)
    upper = jnp.concatenate([state[chunk(j), :], zero], axis=1)
    lower = jnp.concatenate([zero, state[chunk(j + 1), :]], axis=1)
    return jnp.concatenate([upper, lower], axis=0)


def attention_body(heads, same, q, intra, dscaled, growth, state, *refs):
    hq = heads // TEAM
    if same:
        att, sq, inn, both = refs
    else:
        _, sq_before, inn_before, att, sums, sq, inn, both = refs
        sq[...] = sq_before[...]
        inn[...] = inn_before[...]
    for y in range(2):
        g = quarter_of(y, same)
        for j, h, count, c in several(g, hq):
            both[:, 0 : count * HEAD] = nn(q[:, c], states_of(state.at[y], j, count))
            for i in range(BLOCK // HEAD):
                r = chunk(i)
                a_sq = a_in = 0.0
                for m in range(count):
                    _, c = head_at(g, hq, j + m)
                    a = intra[r, c] + both[r, chunk(m)] * growth[g, r, j + m : j + m + 1]
                    att[r, c] = a
                    a_sq = a_sq + a * a
                    a_in = a_in + a * dscaled[r, c]
                if same and y == 0 and j == 0:
                    sq[r, :] = a_sq
                    inn[r, :] = a_in
                else:
                    sq[r, :] += a_sq
                    inn[r, :] += a_in
    if not same:
        ones = jnp.ones((8, HEAD), F32)
        a = nt(ones, sq[...], lax.Precision.HIGHEST)
        b = nt(ones, inn[...], lax.Precision.HIGHEST)
        sums[...] = jnp.where(lax.broadcasted_iota(jnp.int32, (8, BLOCK), 0) == 0, a, b)


def dattn_body(heads, channels, same, att, dscaled, turned, gain, row, *refs):
    hq = heads // TEAM
    if same:
        rsb, coefb, _, dattn, out = refs
    else:
        sum_a, sum_b, _, dattn, out, rsb, coefb = refs
        total = sum_a[...] + sum_b[...]
        rs = lax.rsqrt(total[0:1, :] / channels + EPSILON)
        coef = total[1:2, :] * (rs * rs * rs) / channels
        down = jnp.concatenate([rs, coef, jnp.zeros((HEAD - 2, BLOCK), F32)], axis=0).T
        rsb[...] = jnp.broadcast_to(down[:, 0:1], (BLOCK, HEAD))
        coefb[...] = jnp.broadcast_to(down[:, 1:2], (BLOCK, HEAD))
    for y in range(2):
        items = []
        for j, h, count, cols in several(quarter_of(y, same), hq):
            parts = []
            for m in range(count):
                _, c = head_at(quarter_of(y, same), hq, j + m)
                gsum = jnp.zeros((8, HEAD), F32)
                for i in range(BLOCK // HEAD):
                    r = chunk(i)
                    a = att[r, c]
                    t = dscaled[r, c] * rsb[r, :]
                    dattn[r, c] = (t - a * coefb[r, :]).astype(BF16)
                    gsum = gsum + jnp.sum((t * a).reshape(HEAD // 8, 8, HEAD), axis=0)
                parts.append(jnp.sum(gsum, axis=0, keepdims=True) / gain[:, c])
            both = nn(turned[pl.ds(pl.multiple_of(h * HEAD, HEAD), count * HEAD), :], dattn[:, cols])
            for m in range(count):
                edge = jnp.broadcast_to(row[pl.ds(h + m, 1), :][:, BLOCK - 1 : BLOCK], (1, HEAD))
                items.append((both[chunk(m), chunk(m)], edge, parts[m]))
        (write_wide if same else write_narrow)(out.at[y], hq, items)


def unscaled_gate_body(heads, gate, att, dscaled, _, out):
    hq = heads // TEAM
    for g in range(TEAM):
        for j in range(hq):
            _, c = head_at(g, hq, j)
            closed = jax.nn.sigmoid(-gate[:, c].astype(F32))
            out[:, c] = dscaled[:, c] * att[:, c] * closed


def leave(out, ref, sems, g, w):
    cols = pl.ds(pl.multiple_of(g * w, HEAD), w)
    copy = pltpu.make_async_copy(out, ref.at[:, cols], sems)
    copy.start()
    return copy


def gate_body(heads, unscaled, scale, _, gate_grad, token, out, sems):
    hq = heads // TEAM
    token[...] = jnp.zeros_like(token)
    copies = []
    for g in range(TEAM):
        for j in range(hq):
            _, c = head_at(g, hq, j)
            out[g, :, chunk(j)] = (unscaled[:, c] * scale[...]).astype(BF16)
        copies.append(leave(out.at[g], gate_grad, sems.at[g], g, hq * HEAD))
    for copy in copies:
        copy.wait()


def by_quarter(mine, got):
    return [(ref.at[y], quarter_of(y, same)) for ref, same in ((mine, True), (got, False)) for y in range(2)]


def query_body(heads, k, v, dattn, row, col, growth, mine, got, _, query_grad):
    hq = heads // TEAM
    for state, g in by_quarter(mine, got):
        for j in range(hq):
            h, c = head_at(g, hq, j)
            line = row[pl.ds(h, 1), :]
            for i in range(2):
                d = dattn[half(i), c]
                u = slice(0, (i + 1) * HALF)
                table = decay_table(col[g, half(i), j : j + 1], line[:, u], True)
                dscores = (nt(d, v[u, c]) * table).astype(BF16)
                inter = nt(d, state[chunk(j), :]) * growth[g, half(i), j : j + 1]
                query_grad[half(i), c] = (inter + nn(dscores, k[u, c])).astype(BF16)


def key_value_body(heads, first, last, carries, q, v, dattn, table0, table1, probs0, probs1, _, *refs):
    hq = heads // TEAM
    count = min(hq, 2)
    if carries:
        dk, dv, outside, sems = refs[-4:]
        rows = [slice(i * HEAD, (i + 1) * HEAD) for i in range(BLOCK // HEAD)]
        copies = [pltpu.make_async_copy(refs[0].at[r], outside.at[r], sems.at[i]) for i, r in enumerate(rows)]
    else:
        dk, dv = refs[-2:]
        copies = []
    for copy in copies:
        copy.start()

    def one(step, _):
        for m in range(count):
            h = step * count + m
            _, c = head_at(h, 1, 0)
            for i, (table, probs) in enumerate(((table0, probs0), (table1, probs1))):
                t = slice(i * HALF, BLOCK)
                dscores = (nt(v[half(i), c], dattn[t, c]) * table[h]).astype(BF16)
                dk[half(i), c] = nn(dscores, q[t, c])
                dv[half(i), c] = nn(probs[h], dattn[t, c])
        return 0

    lax.fori_loop(first, last, one, 0)
    for copy in copies:
        copy.wait()


def fades(col, y, same):
    sums = col[quarter_of(y, same)]
    return jnp.exp(sums[BLOCK - 1 : BLOCK, :] - sums)


def final_rows(hq, y, j, count, c, k, v, dk, dv, shrink, state, key_out, value_out):
    after = states_of(state.at[y], j, count)
    key_side, value_side = nt(v[:, c], after), nn(k[:, c], after)
    for m in range(count):
        fade = shrink[:, j + m : j + m + 1]
        own = pl.ds(pl.multiple_of(c.start + m * HEAD, HEAD), HEAD)
        key_out[y, :, chunk(j + m)] = (dk[:, own] + key_side[:, chunk(m)] * fade).astype(BF16)
        value_out[y, :, chunk(j + m)] = (dv[:, own] + value_side[:, chunk(m)] * fade).astype(BF16)


def own_final_body(heads, k, v, dk, dv, col, state, key_out, value_out, gain_grad):
    hq = heads // TEAM
    for y in range(2):
        items = read_narrow(state.at[y], hq)
        shrink = fades(col, y, True)
        for j, _, count, c in several(quarter_of(y, True), hq):
            final_rows(hq, y, j, count, c, k, v, dk, dv, shrink, state, key_out, value_out)
            for m in range(j, j + count):
                gain_grad[:, head_at(quarter_of(y, True), hq, m)[1]] = items[m][2]


def final_body(heads, k, v, dk, dv, col, state, own_key, own_value, own_gain, *refs):
    hq = heads // TEAM
    key_grad, value_grad, gain_grad, gains, key_out, value_out, sems = refs
    copies = []

    def send(src, dst, cols):
        copy = pltpu.make_async_copy(src, dst.at[:, cols], sems.at[len(copies)])
        copy.start()
        copies.append(copy)

    gains[...] = own_gain[...]
    for y in range(2):
        for j, (_, _, total) in enumerate(read_narrow(state.at[y], hq)):
            gains[:, head_at(quarter_of(y, False), hq, j)[1]] = total
    send(gains, gain_grad, slice(None))
    for y in range(2):
        for j, _, count, c in several(quarter_of(y, True), hq):
            place = slice(j * HEAD, (j + count) * HEAD)
            send(own_key.at[y, :, place], key_grad, c)
            send(own_value.at[y, :, place], value_grad, c)
    for y in range(2):
        shrink = fades(col, y, False)
        for j, _, count, c in several(quarter_of(y, False), hq):
            final_rows(hq, y, j, count, c, k, v, dk, dv, shrink, state, key_out, value_out)
            place = slice(j * HEAD, (j + count) * HEAD)
            send(key_out.at[y, :, place], key_grad, c)
            send(value_out.at[y, :, place], value_grad, c)
    for copy in copies:
        copy.wait()


def in_hbm(x):
    return pltpu.with_memory_space_constraint(x, pltpu.HBM)


def swap(x, bit):
    n = lax.axis_size("ctx")
    return lax.ppermute(x, "ctx", [(i, i ^ bit) for i in range(n)])


def local(queries, keys, values, log_decay, gate, gain, grad_out):
    rows, width = queries.shape
    heads = width // HEAD
    hq = heads // TEAM
    tp = lax.axis_size("tp")
    n = lax.axis_size("ctx")
    groups = n // TEAM
    channels = width * tp
    bf = lambda *shape: jax.ShapeDtypeStruct(shape, BF16)
    f32 = lambda *shape: jax.ShapeDtypeStruct(shape, F32)
    swaps = tp == 2
    part = rows // 2
    small = 2 * heads * rows * HEAD * HEAD
    large = 2 * heads * rows * rows * HEAD
    wide = f32(hq * HEAD + SIDE, HEAD)
    wide2 = f32(2, hq * HEAD + SIDE, HEAD)
    narrow = bf(hq * HEAD + EXTRA, HEAD)
    narrow2 = bf(2, hq * HEAD + EXTRA, HEAD)
    table = f32(TEAM, rows, HEAD)
    gain_row = gain.reshape(1, width)

    def beside(work, after, name):
        return [work[name](after)] if name in work else []

    def step_call(body, reverse, inputs, unread, shapes, name, *sizes):
        return call(
            functools.partial(body, reverse, hq, *sizes),
            [*inputs, *unread],
            shapes,
            name,
            in_specs=[VMEM] * len(inputs) + [ANY] * len(unread),
        )

    def scan(reverse, keep, give, work):
        got = swap(give, 1)
        own, send = step_call(chip_total_body, reverse, [keep, got], [], [wide, narrow], "chip_total")
        got_pair = swap(send, 2)
        unread = beside(work, send, "pair")
        total, send = step_call(group_total_body, reverse, [own, got_pair], unread, [wide, narrow], "group_total")
        so_far, step = total, 1
        while 2 * step < groups:
            far = swap(send, TEAM * step)
            unread = beside(work, send, "one") if step == 1 else []
            before = [] if step == 1 else [so_far]
            so_far, total, send = step_call(
                window_body, reverse, [total, *before, far], unread, [wide, wide, narrow], "window", step
            )
            step *= 2
        far = swap(send, TEAM * step)
        unread = beside(work, send, "last")
        kept, send = step_call(
            into_chips_body, reverse, [own, got_pair, total, so_far, far], unread, [wide, narrow], "into_chips", step
        )
        other = swap(send, 2)
        unread = beside(work, send, "pair_back")
        mine, send = step_call(
            into_cores_body, reverse, [keep, got, kept, other], unread, [narrow2, narrow2], "into_cores"
        )
        return mine, swap(send, 1)

    outs = call(
        functools.partial(sent_states_body, heads, swaps),
        [in_hbm(keys), in_hbm(values), in_hbm(log_decay)] + [in_hbm(grad_out)] * swaps,
        [wide2, f32(EXTRA, rows), bf(rows, width), bf(rows, width)] + [bf(part, width)] * swaps,
        "sent_states",
        [
            pltpu.VMEM(log_decay.shape, F32),
            pltpu.SemaphoreType.DMA((2, TEAM)),
            pltpu.SemaphoreType.DMA((2,)),
        ],
        small // 2,
        [HBM] * (3 + swaps),
        [VMEM] * 4 + [HBM] * swaps,
    )
    give, row, keys, values = outs[:4]
    if swaps:
        arrived = lax.ppermute(outs[4], "tp", [(0, 1), (1, 0)])
        own = grad_out
    else:
        every = lax.all_to_all(grad_out, "tp", split_axis=1, concat_axis=0, tiled=True)
        own, arrived = every[:part], every[part:]
    (keep,) = call(
        functools.partial(kept_states_body, heads), [keys, values, row], [wide2], "kept_states", flops=small // 2
    )
    done = {}

    def probs_beside(after):
        if "decays" not in done:
            *done["decays"], done["queries"] = call(
                functools.partial(decays_body, heads),
                [row, in_hbm(queries), after],
                [table] * 2 + [bf(rows, width)],
                "decays",
                [pltpu.SemaphoreType.DMA(())],
                in_specs=[VMEM, HBM, ANY],
            )
        before = done.get("probs", [])
        done["probs"] = call(
            functools.partial(turned_probs_body, heads, TEAM // 2 if before else 0),
            [done["queries"], keys, row, done["decays"][0], after, *before],
            [f32(heads, HALF, BLOCK), f32(heads, HALF, HALF), bf(heads, HALF, BLOCK), bf(heads, HALF, HALF)],
            "turned_probs",
            flops=large // 2,
            in_specs=[VMEM] * 4 + [ANY] + [VMEM] * len(before),
            alias={5 + i: i for i in range(len(before))},
        )
        return done["probs"][3]

    def intra_beside(after):
        before = [done["intra"]] if "intra" in done else []
        first, last = (1, TEAM) if before else (0, 1)
        (done["intra"],) = call(
            functools.partial(intra_body, heads, first, last),
            [done["queries"], keys, values, row, done["decays"][0], after, *before],
            [f32(rows, width)],
            "intra",
            flops=2 * large * (last - first) // TEAM,
            in_specs=[VMEM] * 5 + [ANY] + [VMEM] * len(before),
            alias={6: 0} if before else None,
        )
        return done["intra"]

    def probs_and_intra(after):
        return intra_beside(probs_beside(after))

    def dscaled_beside(after):
        done["dscaled"] = call(
            functools.partial(own_dscaled_body, heads, swaps),
            [gate, in_hbm(own), gain_row, done["queries"], row, after],
            [f32(rows, width), bf(width, rows)],
            "own_dscaled",
            [pltpu.VMEM((part, width), BF16), pltpu.SemaphoreType.DMA(())],
            small,
            [VMEM, HBM, VMEM, VMEM, VMEM, ANY],
        )
        (dscaled,) = call(
            functools.partial(got_dscaled_body, heads, swaps),
            [gate, arrived, gain_row, done["dscaled"][0]],
            [f32(rows, width)],
            "got_dscaled",
            alias={3: 0},
        )
        done["dscaled"] = dscaled, done["dscaled"][1]
        return dscaled

    work = {"pair": probs_beside, "one": probs_and_intra, "last": intra_beside, "pair_back": dscaled_beside}
    mine, got = scan(False, keep, give, work)
    queries = done["queries"]
    (col, growth), intra, (dscaled, turned) = done["decays"], done["intra"], done["dscaled"]
    tall = f32(rows, HEAD)
    wide_scratch = pltpu.VMEM((rows, 2 * HEAD), F32)
    att, squares, inner = call(
        functools.partial(attention_body, heads, True),
        [queries, intra, dscaled, growth, mine],
        [f32(rows, width), tall, tall],
        "attention",
        [wide_scratch],
        small // 2,
    )
    att, sums = call(
        functools.partial(attention_body, heads, False),
        [queries, intra, dscaled, growth, got, att, squares, inner],
        [f32(rows, width), f32(8, rows)],
        "attention",
        [pltpu.VMEM((rows, HEAD), F32)] * 2 + [wide_scratch],
        small // 2,
        alias={5: 0},
    )
    (unscaled_gate,) = call(
        functools.partial(unscaled_gate_body, heads),
        [gate, att, dscaled, intra],
        [f32(rows, width)],
        "unscaled_gate",
        in_specs=[VMEM] * 3 + [ANY],
        alias={3: 0},
    )
    if swaps:
        others = lax.ppermute(sums, "tp", [(0, 1), (1, 0)])
    else:
        others = lax.psum(sums, "tp") - sums
    dattn, give, scale, coef = call(
        functools.partial(dattn_body, heads, channels, False),
        [att, dscaled, turned, gain_row, row, sums, others, unscaled_gate],
        [bf(rows, width), narrow2, tall, tall],
        "sent_dattn",
        flops=small // 2,
        in_specs=[VMEM] * 7 + [ANY],
    )
    dattn, keep = call(
        functools.partial(dattn_body, heads, channels, True),
        [att, dscaled, turned, gain_row, row, scale, coef, dattn],
        [bf(rows, width), wide2],
        "kept_dattn",
        flops=small // 2,
        alias={7: 0},
    )
    out_scratch = [pltpu.VMEM((TEAM, rows, hq * HEAD), BF16), pltpu.SemaphoreType.DMA((TEAM,))]

    def gate_beside(after):
        done["gate"], token = call(
            functools.partial(gate_body, heads),
            [unscaled_gate, scale, after],
            [bf(rows, width), f32(SIDE, HEAD)],
            "gate",
            out_scratch,
            small,
            [VMEM] * 2 + [ANY],
            [HBM, VMEM],
        )
        return token

    units = heads // min(hq, 2)
    cuts = [0, units // 4, 5 * units // 8, units]

    def key_value_beside(after, carried=()):
        before = done.get("key_value", [unscaled_gate, dscaled])
        piece = done.get("piece", 0)
        done["piece"] = piece + 1
        inputs = [queries, values, dattn, *done["probs"], after, *carried, *before]
        results = call(
            functools.partial(key_value_body, heads, cuts[piece], cuts[piece + 1], len(carried)),
            inputs,
            [f32(rows, width)] * 2 + [bf(rows, width)] * len(carried),
            "key_value",
            [pltpu.SemaphoreType.DMA((rows // HEAD,))] * len(carried),
            4 * large * (cuts[piece + 1] - cuts[piece]) // units,
            [VMEM] * 7 + [ANY] + [VMEM] * (len(carried) + len(before)),
            [VMEM] * 2 + [HBM] * len(carried),
            {8 + len(carried) + i: i for i in range(len(before))},
        )
        done["key_value"] = results[:2]
        return results[0], results[-1]

    def gate_and_key_value(after):
        return key_value_beside(gate_beside(after))[0]

    def query_beside(after):
        (done["query"],) = call(
            functools.partial(query_body, heads),
            [keys, values, dattn, row, col, growth, mine, got, after],
            [bf(rows, width)],
            "query",
            flops=2 * large + small,
            in_specs=[VMEM] * 8 + [ANY],
        )
        return done["query"]

    def key_value_last(after):
        dk, done["query"] = key_value_beside(after, [done["query"]])
        return dk

    work = {"pair": gate_and_key_value, "one": lambda after: key_value_beside(after)[0], "last": query_beside, "pair_back": key_value_last}
    back_mine, back_got = scan(True, keep, give, work)
    gate_grad, query_grad, (dk, dv) = done["gate"], done["query"], done["key_value"]
    both = bf(2, rows, hq * HEAD)
    own_key, own_value, own_gain = call(
        functools.partial(own_final_body, heads),
        [keys, values, dk, dv, col, back_mine],
        [both, both, f32(1, width)],
        "own_final",
        flops=small,
    )
    key_grad, value_grad, gain_grad = call(
        functools.partial(final_body, heads),
        [keys, values, dk, dv, col, back_got, own_key, own_value, own_gain],
        [bf(rows, width), bf(rows, width), f32(1, width)],
        "final",
        [pltpu.VMEM((1, width), F32)]
        + [pltpu.VMEM(both.shape, BF16)] * 2
        + [pltpu.SemaphoreType.DMA((8 * hq + 1,))],
        small,
        out_specs=[HBM, HBM, HBM],
    )
    return query_grad, key_grad, value_grad, gate_grad, gain_grad.reshape(width)


def solution(mesh):
    return jax.shard_map(
        local,
        mesh=mesh,
        in_specs=(
            P("ctx", "tp"),
            P("ctx", "tp"),
            P("ctx", "tp"),
            P("tp", "ctx"),
            P("ctx", "tp"),
            P("tp"),
            P(("ctx", "tp"), None),
        ),
        out_specs=(P("ctx", "tp"), P("ctx", "tp"), P("ctx", "tp"), P("ctx", "tp"), P("tp")),
        check_vma=False,
    )
```

```python
import functools

import jax
import jax.numpy as jnp
from jax import lax
from jax.experimental import pallas as pl
from jax.experimental.pallas import tpu as pltpu
from jax.sharding import PartitionSpec as P

HEAD = 128
BLOCK = 512
HALF = BLOCK // 2
TEAM = 4
SIDE = 8
EXTRA = 16
EPSILON = 1e-06
F32 = jnp.float32
BF16 = jnp.bfloat16
GRANT = 5 * 1024 * 1024
VMEM = pl.BlockSpec(memory_space=pltpu.VMEM)
HBM = pl.BlockSpec(memory_space=pltpu.HBM)
ANY = pl.BlockSpec(memory_space=pl.ANY)


def nt(a, b, precision=None):
    return lax.dot_general(a, b, (((1,), (1,)), ((), ())), preferred_element_type=F32, precision=precision)


def nn(a, b):
    return lax.dot_general(a, b, (((1,), (0,)), ((), ())), preferred_element_type=F32)


def half(i):
    return slice(i * HALF, (i + 1) * HALF)


def chunk(i):
    return slice(i * HEAD, (i + 1) * HEAD)


def split_terms(x, count):
    terms = []
    for _ in range(count):
        term = x.astype(BF16)
        terms.append(term)
        x = x - term.astype(F32)
    return terms


def read_wide(ref, hq):
    base = hq * HEAD
    return [
        (ref[chunk(j), :], ref[base + j : base + j + 1, :], ref[base + TEAM + j : base + TEAM + j + 1, :])
        for j in range(hq)
    ]


def write_wide(ref, hq, items):
    base = hq * HEAD
    at = lax.broadcasted_iota(jnp.int32, (SIDE, HEAD), 0)
    side = jnp.zeros((SIDE, HEAD), F32)
    for j, (term, edge, gain) in enumerate(items):
        ref[chunk(j), :] = term
        side = jnp.where(at == j, edge, side)
        side = jnp.where(at == TEAM + j, gain, side)
    ref[base : base + SIDE, :] = side


def read_narrow(ref, hq):
    base = hq * HEAD
    side = ref[base : base + EXTRA, :].astype(F32)
    row = lambda i: side[i : i + 1, :] + side[i + 1 : i + 2, :]
    return [(ref[chunk(j), :].astype(F32), row(2 * j), row(2 * TEAM + 2 * j)) for j in range(hq)]


def write_narrow(ref, hq, items):
    base = hq * HEAD
    at = lax.broadcasted_iota(jnp.int32, (EXTRA, HEAD), 0)
    side = jnp.zeros((EXTRA, HEAD), F32)
    for j, (term, edge, gain) in enumerate(items):
        ref[chunk(j), :] = term.astype(BF16)
        for first, value in ((2 * j, edge), (2 * TEAM + 2 * j, gain)):
            for i, part in enumerate(split_terms(value, 2)):
                side = jnp.where(at == first + i, part.astype(F32), side)
    ref[base : base + EXTRA, :] = side.astype(BF16)


def core():
    return lax.rem(lax.axis_index("ctx"), 2)


def pair():
    return lax.rem(lax.axis_index("ctx") // 2, 2)


def group():
    return lax.axis_index("ctx") // TEAM


def quarter_of(y, same):
    return 2 * y + (core() if same else 1 - core())


def head_at(quarter, hq, j):
    h = quarter * hq + j
    return h, pl.ds(pl.multiple_of(h * HEAD, HEAD), HEAD)


def transposed(x):
    shape = (x.shape[1], x.shape[1])
    eye = (lax.broadcasted_iota(jnp.int32, shape, 0) == lax.broadcasted_iota(jnp.int32, shape, 1)).astype(BF16)
    return nt(eye, x)


def several(quarter, hq):
    count = min(hq, 2)
    for j in range(0, hq, count):
        h = quarter * hq + j
        yield j, h, count, pl.ds(pl.multiple_of(h * HEAD, HEAD), count * HEAD)


def call(body, inputs, out_shape, name, scratch=(), flops=0, in_specs=None, out_specs=None, alias=None):
    nbytes = sum(x.size * x.dtype.itemsize for x in inputs)
    nbytes += sum(x.size * x.dtype.itemsize for x in out_shape)
    out_shape = list(out_shape)
    for o in (alias or {}).values():
        out_shape[o] = pltpu.VMEM(out_shape[o].shape, out_shape[o].dtype)
    return pl.pallas_call(
        body,
        in_specs=in_specs or [VMEM] * len(inputs),
        out_specs=out_specs or [VMEM] * len(out_shape),
        out_shape=out_shape,
        scratch_shapes=list(scratch),
        input_output_aliases=alias or {},
        compiler_params=pltpu.CompilerParams(vmem_limit_bytes=GRANT),
        cost_estimate=pl.CostEstimate(flops=flops, bytes_accessed=nbytes, transcendentals=0),
        name=name,
    )(*inputs)


def joined(mine, other, mine_is_first, reverse):
    out = []
    for (a, ea, ga), (b, eb, gb) in zip(mine, other):
        near = mine_is_first if reverse else jnp.logical_not(mine_is_first)
        wa = jnp.where(near, 1.0, jnp.exp(eb))
        wb = jnp.where(near, jnp.exp(ea), 1.0)
        out.append((a * wa + b * wb, ea + eb, ga + gb))
    return out


def chip_total_body(reverse, hq, keep, got, own, send):
    first = core() == 0
    read_got = read_narrow if reverse else read_wide
    here, there = pair(), 1 - pair()
    own_items = joined(read_wide(keep.at[here], hq), read_got(got.at[here], hq), first, reverse)
    write_wide(own, hq, own_items)
    send_items = joined(read_wide(keep.at[there], hq), read_got(got.at[there], hq), first, reverse)
    write_narrow(send, hq, send_items)


def group_total_body(reverse, hq, own, got, *refs):
    total, send = refs[-2:]
    items = joined(read_wide(own, hq), read_narrow(got, hq), pair() == 0, reverse)
    write_wide(total, hq, items)
    write_narrow(send, hq, items)


def met(reverse, step, before, other):
    near = lax.rem(group() // step, 2) == (0 if reverse else 1)
    out = []
    for old, (term, edge, gain) in zip(before, other):
        term = jnp.where(near, term, 0.0)
        edge = jnp.where(near, edge, 0.0)
        if old is None:
            out.append((term, edge, gain))
        else:
            out.append((old[0] + jnp.exp(old[1]) * term, old[1] + edge, gain))
    return out


def window_body(reverse, hq, step, total, *refs):
    so_far, whole, send = refs[-3:]
    if step == 1:
        got = refs[0]
        before = [None] * hq
    else:
        got = refs[1]
        before = read_wide(refs[0], hq)
    other = read_narrow(got, hq)
    write_wide(so_far, hq, met(reverse, step, before, other))
    items = joined(read_wide(total, hq), other, lax.rem(group() // step, 2) == 0, reverse)
    write_wide(whole, hq, items)
    write_narrow(send, hq, items)


def into_chips_body(reverse, hq, step, own, got_pair, total, so_far, got, *refs):
    keep, send = refs[-2:]
    before = read_wide(so_far, hq) if step > 1 else [None] * hq
    entering = met(reverse, step, before, read_narrow(got, hq))
    mine_near = pair() == (1 if reverse else 0)
    kept, sent = [], []
    for (r, _, gr), (c, ec, _), (o, eo, _), (_, _, gt) in zip(
        entering, read_wide(own, hq), read_narrow(got_pair, hq), read_wide(total, hq)
    ):
        gain = gr + gt
        zero = jnp.zeros_like(ec)
        kept.append((jnp.where(mine_near, r, jnp.exp(eo) * r + o), zero, gain))
        sent.append((jnp.where(mine_near, jnp.exp(ec) * r + c, r), zero, gain))
    write_wide(keep, hq, kept)
    write_narrow(send, hq, sent)


def into_cores_body(reverse, hq, keep, got, own, other, *refs):
    mine, send = refs[-2:]
    mine_near = core() == (1 if reverse else 0)
    read_got = read_narrow if reverse else read_wide
    for y in range(2):
        a, b = read_wide(own, hq), read_narrow(other, hq)
        here = pair() == y
        items_mine, items_send = [], []
        for p, q, (k, ek, _), (g, eg, _) in zip(a, b, read_wide(keep.at[y], hq), read_got(got.at[y], hq)):
            r = jnp.where(here, p[0], q[0])
            gain = jnp.where(here, p[2], q[2])
            zero = jnp.zeros_like(ek)
            items_mine.append((jnp.where(mine_near, r, jnp.exp(eg) * r + g), zero, gain))
            items_send.append((jnp.where(mine_near, jnp.exp(ek) * r + k, r), zero, gain))
        write_narrow(mine.at[y], hq, items_mine)
        write_narrow(send.at[y], hq, items_send)


def block_states(hq, y, same, k, v, row, out):
    items = []
    for j, h, count, c in several(quarter_of(y, same), hq):
        turned = transposed(k[:, c])
        lines = [row[pl.ds(h + m, 1), :] for m in range(count)]
        edges = [line[:, BLOCK - 1 : BLOCK] for line in lines]
        faded = [turned[chunk(m)] * jnp.exp(edges[m] - lines[m]) for m in range(count)]
        both = nn(jnp.concatenate([x.astype(BF16) for x in faded], axis=0), v[:, c])
        for m in range(count):
            items.append((both[chunk(m), chunk(m)], jnp.broadcast_to(edges[m], (1, HEAD)), jnp.zeros((1, HEAD), F32)))
    write_wide(out.at[y], hq, items)


def sent_states_body(heads, swaps, k_hbm, v_hbm, ld_hbm, *refs):
    hq = heads // TEAM
    w = hq * HEAD
    if swaps:
        grad, give, row, k, v, away, ld, sems, side_sems = refs
        width = heads * HEAD
        there = pl.ds(pl.multiple_of((1 - lax.axis_index("tp")) * width, HEAD), width)
        side_copies = [pltpu.make_async_copy(grad.at[:, there], away, side_sems.at[1])]
    else:
        give, row, k, v, ld, sems, side_sems = refs
        side_copies = []
    first = pltpu.make_async_copy(ld_hbm, ld, side_sems.at[0])
    first.start()
    order = [(0, False), (1, False), (0, True), (1, True)]
    copies = []
    for slot, (y, same) in enumerate(order):
        cols_d = pl.ds(pl.multiple_of(quarter_of(y, same) * w, HEAD), w)
        both = [
            pltpu.make_async_copy(k_hbm.at[:, cols_d], k.at[:, cols_d], sems.at[0, slot]),
            pltpu.make_async_copy(v_hbm.at[:, cols_d], v.at[:, cols_d], sems.at[1, slot]),
        ]
        for c in both:
            c.start()
        copies.append(both)
    for c in side_copies:
        c.start()
    at = lax.broadcasted_iota(jnp.int32, (BLOCK, BLOCK), 0)
    other = lax.broadcasted_iota(jnp.int32, (BLOCK, BLOCK), 1)
    tri = (at <= other).astype(BF16)
    first.wait()
    x = ld[...]
    if heads < EXTRA:
        x = jnp.concatenate([x, jnp.zeros((EXTRA - heads, BLOCK), F32)], axis=0)
    sums = nn(jnp.concatenate(split_terms(x, 3), axis=0), tri)
    row[...] = sums[0:EXTRA] + (sums[EXTRA : 2 * EXTRA] + sums[2 * EXTRA : 3 * EXTRA])
    for slot, (y, same) in enumerate(order):
        for c in copies[slot]:
            c.wait()
        if not same:
            block_states(hq, y, same, k, v, row, give)
    for c in side_copies:
        c.wait()


def kept_states_body(heads, k, v, row, keep):
    for y in range(2):
        block_states(heads // TEAM, y, True, k, v, row, keep)


def decays_body(heads, row, q_hbm, _, col, growth, q, sem):
    hq = heads // TEAM
    copy = pltpu.make_async_copy(q_hbm, q, sem)
    copy.start()
    for g in range(TEAM):
        rows = row[g * hq : (g + 1) * hq, :]
        across = jnp.concatenate([rows, jnp.zeros((HEAD - hq, BLOCK), F32)], axis=0).T
        col[g] = across
        growth[g] = jnp.exp(across)
    copy.wait()


def decay_table(high, low, lower):
    table = jnp.exp(high - low)
    at = lax.broadcasted_iota(jnp.int32, (HALF, HALF), 0)
    other = lax.broadcasted_iota(jnp.int32, (HALF, HALF), 1)
    if lower:
        cut = jnp.where(at >= other, table[:, -HALF:], 0.0)
        return cut if table.shape[1] == HALF else jnp.concatenate([table[:, :HALF], cut], axis=1)
    cut = jnp.where(at <= other, table[:, :HALF], 0.0)
    return cut if table.shape[1] == HALF else jnp.concatenate([cut, table[:, HALF:]], axis=1)


def turned_probs_body(heads, first, q, k, row, col, _, *refs):
    hq = heads // TEAM
    tables, probs = refs[-4:-2], refs[-2:]

    def one(g, _):
        for j in range(hq):
            h, c = head_at(g, hq, j)
            line = row[pl.ds(h, 1), :]
            for i in range(2):
                t = slice(i * HALF, BLOCK)
                table = decay_table(line[:, t], col[g, half(i), j : j + 1], False)
                tables[i][h] = table
                probs[i][h] = (nt(k[half(i), c], q[t, c]) * table).astype(BF16)
        return 0

    lax.fori_loop(first, first + TEAM // 2, one, 0)


def intra_body(heads, first, last, q, k, v, row, col, *refs):
    hq = heads // TEAM
    intra = refs[-1]

    def one(g, _):
        for j in range(hq):
            h, c = head_at(g, hq, j)
            line = row[pl.ds(h, 1), :]
            for i in range(2):
                u = slice(0, (i + 1) * HALF)
                table = decay_table(col[g, half(i), j : j + 1], line[:, u], True)
                probs = (nt(q[half(i), c], k[u, c]) * table).astype(BF16)
                intra[half(i), c] = nn(probs, v[u, c])
        return 0

    lax.fori_loop(first, last, one, 0)


def dscaled_rows(heads, where, gate, ref, gain, dscaled):
    part = ref.shape[0]
    rows = pl.ds(pl.multiple_of(where * part, part), part)

    def one(g, _):
        for j in range(heads // TEAM):
            _, c = head_at(g, heads // TEAM, j)
            opened = jax.nn.sigmoid(gate[rows, c].astype(F32))
            dscaled[rows, c] = ref[:, c].astype(F32) * opened * gain[:, c]
        return 0

    lax.fori_loop(0, TEAM, one, 0)


def own_dscaled_body(heads, swaps, gate, grad, gain, q, row, _, dscaled, turned, own, sem):
    width = heads * HEAD
    mine = lax.axis_index("tp") if swaps else 0
    here = pl.ds(pl.multiple_of(mine * width, HEAD), width)
    copy = pltpu.make_async_copy(grad.at[:, here], own, sem)
    copy.start()

    def one(g, _):
        for j, h, count, c in several(g, heads // TEAM):
            both = transposed(q[:, c])
            for m in range(count):
                rows = pl.ds(pl.multiple_of((h + m) * HEAD, HEAD), HEAD)
                turned[rows, :] = (both[chunk(m)] * jnp.exp(row[pl.ds(h + m, 1), :])).astype(BF16)
        return 0

    lax.fori_loop(0, TEAM, one, 0)
    copy.wait()
    dscaled_rows(heads, mine, gate, own, gain, dscaled)


def got_dscaled_body(heads, swaps, gate, got, gain, _, dscaled):
    dscaled_rows(heads, 1 - lax.axis_index("tp") if swaps else 1, gate, got, gain, dscaled)


def states_of(state, j, count):
    if count == 1:
        return state[chunk(j), :]
    zero = jnp.zeros((HEAD, HEAD), BF16)
    upper = jnp.concatenate([state[chunk(j), :], zero], axis=1)
    lower = jnp.concatenate([zero, state[chunk(j + 1), :]], axis=1)
    return jnp.concatenate([upper, lower], axis=0)


def attention_body(heads, same, q, intra, dscaled, growth, state, *refs):
    hq = heads // TEAM
    if same:
        att, sq, inn, both = refs
    else:
        _, sq_before, inn_before, att, sums, sq, inn, both = refs
        sq[...] = sq_before[...]
        inn[...] = inn_before[...]
    for y in range(2):
        g = quarter_of(y, same)
        for j, h, count, c in several(g, hq):
            both[:, 0 : count * HEAD] = nn(q[:, c], states_of(state.at[y], j, count))
            for i in range(BLOCK // HEAD):
                r = chunk(i)
                a_sq = a_in = 0.0
                for m in range(count):
                    _, c = head_at(g, hq, j + m)
                    a = intra[r, c] + both[r, chunk(m)] * growth[g, r, j + m : j + m + 1]
                    att[r, c] = a
                    a_sq = a_sq + a * a
                    a_in = a_in + a * dscaled[r, c]
                if same and y == 0 and j == 0:
                    sq[r, :] = a_sq
                    inn[r, :] = a_in
                else:
                    sq[r, :] += a_sq
                    inn[r, :] += a_in
    if not same:
        ones = jnp.ones((8, HEAD), F32)
        a = nt(ones, sq[...], lax.Precision.HIGHEST)
        b = nt(ones, inn[...], lax.Precision.HIGHEST)
        sums[...] = jnp.where(lax.broadcasted_iota(jnp.int32, (8, BLOCK), 0) == 0, a, b)


def dattn_body(heads, channels, same, att, dscaled, turned, gain, row, *refs):
    hq = heads // TEAM
    if same:
        rsb, coefb, _, dattn, out = refs
    else:
        sum_a, sum_b, _, dattn, out, rsb, coefb = refs
        total = sum_a[...] + sum_b[...]
        rs = lax.rsqrt(total[0:1, :] / channels + EPSILON)
        coef = total[1:2, :] * (rs * rs * rs) / channels
        down = jnp.concatenate([rs, coef, jnp.zeros((HEAD - 2, BLOCK), F32)], axis=0).T
        rsb[...] = jnp.broadcast_to(down[:, 0:1], (BLOCK, HEAD))
        coefb[...] = jnp.broadcast_to(down[:, 1:2], (BLOCK, HEAD))
    for y in range(2):
        items = []
        for j, h, count, cols in several(quarter_of(y, same), hq):
            parts = []
            for m in range(count):
                _, c = head_at(quarter_of(y, same), hq, j + m)
                gsum = jnp.zeros((8, HEAD), F32)
                for i in range(BLOCK // HEAD):
                    r = chunk(i)
                    a = att[r, c]
                    t = dscaled[r, c] * rsb[r, :]
                    dattn[r, c] = (t - a * coefb[r, :]).astype(BF16)
                    gsum = gsum + jnp.sum((t * a).reshape(HEAD // 8, 8, HEAD), axis=0)
                parts.append(jnp.sum(gsum, axis=0, keepdims=True) / gain[:, c])
            both = nn(turned[pl.ds(pl.multiple_of(h * HEAD, HEAD), count * HEAD), :], dattn[:, cols])
            for m in range(count):
                edge = jnp.broadcast_to(row[pl.ds(h + m, 1), :][:, BLOCK - 1 : BLOCK], (1, HEAD))
                items.append((both[chunk(m), chunk(m)], edge, parts[m]))
        (write_wide if same else write_narrow)(out.at[y], hq, items)


def unscaled_gate_body(heads, gate, att, dscaled, _, out):
    hq = heads // TEAM
    for g in range(TEAM):
        for j in range(hq):
            _, c = head_at(g, hq, j)
            closed = jax.nn.sigmoid(-gate[:, c].astype(F32))
            out[:, c] = dscaled[:, c] * att[:, c] * closed


def leave(out, ref, sems, g, w):
    cols = pl.ds(pl.multiple_of(g * w, HEAD), w)
    copy = pltpu.make_async_copy(out, ref.at[:, cols], sems)
    copy.start()
    return copy


def gate_body(heads, unscaled, scale, _, gate_grad, token, out, sems):
    hq = heads // TEAM
    token[...] = jnp.zeros_like(token)
    copies = []
    for g in range(TEAM):
        for j in range(hq):
            _, c = head_at(g, hq, j)
            out[g, :, chunk(j)] = (unscaled[:, c] * scale[...]).astype(BF16)
        copies.append(leave(out.at[g], gate_grad, sems.at[g], g, hq * HEAD))
    for copy in copies:
        copy.wait()


def by_quarter(mine, got):
    return [(ref.at[y], quarter_of(y, same)) for ref, same in ((mine, True), (got, False)) for y in range(2)]


def query_body(heads, k, v, dattn, row, col, growth, mine, got, _, query_grad):
    hq = heads // TEAM
    for state, g in by_quarter(mine, got):
        for j in range(hq):
            h, c = head_at(g, hq, j)
            line = row[pl.ds(h, 1), :]
            for i in range(2):
                d = dattn[half(i), c]
                u = slice(0, (i + 1) * HALF)
                table = decay_table(col[g, half(i), j : j + 1], line[:, u], True)
                dscores = (nt(d, v[u, c]) * table).astype(BF16)
                inter = nt(d, state[chunk(j), :]) * growth[g, half(i), j : j + 1]
                query_grad[half(i), c] = (inter + nn(dscores, k[u, c])).astype(BF16)


def key_value_body(heads, first, last, carries, q, v, dattn, table0, table1, probs0, probs1, _, *refs):
    hq = heads // TEAM
    count = min(hq, 2)
    if carries:
        dk, dv, outside, sems = refs[-4:]
        rows = [slice(i * HEAD, (i + 1) * HEAD) for i in range(BLOCK // HEAD)]
        copies = [pltpu.make_async_copy(refs[0].at[r], outside.at[r], sems.at[i]) for i, r in enumerate(rows)]
    else:
        dk, dv = refs[-2:]
        copies = []
    for copy in copies:
        copy.start()

    def one(step, _):
        for m in range(count):
            h = step * count + m
            _, c = head_at(h, 1, 0)
            for i, (table, probs) in enumerate(((table0, probs0), (table1, probs1))):
                t = slice(i * HALF, BLOCK)
                dscores = (nt(v[half(i), c], dattn[t, c]) * table[h]).astype(BF16)
                dk[half(i), c] = nn(dscores, q[t, c])
                dv[half(i), c] = nn(probs[h], dattn[t, c])
        return 0

    lax.fori_loop(first, last, one, 0)
    for copy in copies:
        copy.wait()


def fades(col, y, same):
    sums = col[quarter_of(y, same)]
    return jnp.exp(sums[BLOCK - 1 : BLOCK, :] - sums)


def final_rows(hq, y, j, count, c, k, v, dk, dv, shrink, state, key_out, value_out):
    after = states_of(state.at[y], j, count)
    key_side, value_side = nt(v[:, c], after), nn(k[:, c], after)
    for m in range(count):
        fade = shrink[:, j + m : j + m + 1]
        own = pl.ds(pl.multiple_of(c.start + m * HEAD, HEAD), HEAD)
        key_out[y, :, chunk(j + m)] = (dk[:, own] + key_side[:, chunk(m)] * fade).astype(BF16)
        value_out[y, :, chunk(j + m)] = (dv[:, own] + value_side[:, chunk(m)] * fade).astype(BF16)


def own_final_body(heads, k, v, dk, dv, col, state, key_out, value_out, gain_grad):
    hq = heads // TEAM
    for y in range(2):
        items = read_narrow(state.at[y], hq)
        shrink = fades(col, y, True)
        for j, _, count, c in several(quarter_of(y, True), hq):
            final_rows(hq, y, j, count, c, k, v, dk, dv, shrink, state, key_out, value_out)
            for m in range(j, j + count):
                gain_grad[:, head_at(quarter_of(y, True), hq, m)[1]] = items[m][2]


def final_body(heads, k, v, dk, dv, col, state, own_key, own_value, own_gain, *refs):
    hq = heads // TEAM
    key_grad, value_grad, gain_grad, gains, key_out, value_out, sems = refs
    copies = []

    def send(src, dst, cols):
        copy = pltpu.make_async_copy(src, dst.at[:, cols], sems.at[len(copies)])
        copy.start()
        copies.append(copy)

    for y in range(2):
        for j, _, count, c in several(quarter_of(y, True), hq):
            place = slice(j * HEAD, (j + count) * HEAD)
            send(own_key.at[y, :, place], key_grad, c)
            send(own_value.at[y, :, place], value_grad, c)
    gains[...] = own_gain[...]
    for y in range(2):
        for j, (_, _, total) in enumerate(read_narrow(state.at[y], hq)):
            gains[:, head_at(quarter_of(y, False), hq, j)[1]] = total
    send(gains, gain_grad, slice(None))
    for y in range(2):
        shrink = fades(col, y, False)
        for j, _, count, c in several(quarter_of(y, False), hq):
            final_rows(hq, y, j, count, c, k, v, dk, dv, shrink, state, key_out, value_out)
            place = slice(j * HEAD, (j + count) * HEAD)
            send(key_out.at[y, :, place], key_grad, c)
            send(value_out.at[y, :, place], value_grad, c)
    for copy in copies:
        copy.wait()


def in_hbm(x):
    return pltpu.with_memory_space_constraint(x, pltpu.HBM)


def swap(x, bit):
    n = lax.axis_size("ctx")
    return lax.ppermute(x, "ctx", [(i, i ^ bit) for i in range(n)])


def local(queries, keys, values, log_decay, gate, gain, grad_out):
    rows, width = queries.shape
    heads = width // HEAD
    hq = heads // TEAM
    tp = lax.axis_size("tp")
    n = lax.axis_size("ctx")
    groups = n // TEAM
    channels = width * tp
    bf = lambda *shape: jax.ShapeDtypeStruct(shape, BF16)
    f32 = lambda *shape: jax.ShapeDtypeStruct(shape, F32)
    swaps = tp == 2
    part = rows // 2
    small = 2 * heads * rows * HEAD * HEAD
    large = 2 * heads * rows * rows * HEAD
    wide = f32(hq * HEAD + SIDE, HEAD)
    wide2 = f32(2, hq * HEAD + SIDE, HEAD)
    narrow = bf(hq * HEAD + EXTRA, HEAD)
    narrow2 = bf(2, hq * HEAD + EXTRA, HEAD)
    table = f32(TEAM, rows, HEAD)
    gain_row = gain.reshape(1, width)

    def beside(work, after, name):
        return [work[name](after)] if name in work else []

    def step_call(body, reverse, inputs, unread, shapes, name, *sizes):
        return call(
            functools.partial(body, reverse, hq, *sizes),
            [*inputs, *unread],
            shapes,
            name,
            in_specs=[VMEM] * len(inputs) + [ANY] * len(unread),
        )

    def scan(reverse, keep, give, work):
        got = swap(give, 1)
        own, send = step_call(chip_total_body, reverse, [keep, got], [], [wide, narrow], "chip_total")
        got_pair = swap(send, 2)
        unread = beside(work, send, "pair")
        total, send = step_call(group_total_body, reverse, [own, got_pair], unread, [wide, narrow], "group_total")
        so_far, step = total, 1
        while 2 * step < groups:
            far = swap(send, TEAM * step)
            unread = beside(work, send, "one") if step == 1 else []
            before = [] if step == 1 else [so_far]
            so_far, total, send = step_call(
                window_body, reverse, [total, *before, far], unread, [wide, wide, narrow], "window", step
            )
            step *= 2
        far = swap(send, TEAM * step)
        unread = beside(work, send, "last")
        kept, send = step_call(
            into_chips_body, reverse, [own, got_pair, total, so_far, far], unread, [wide, narrow], "into_chips", step
        )
        other = swap(send, 2)
        unread = beside(work, send, "pair_back")
        mine, send = step_call(
            into_cores_body, reverse, [keep, got, kept, other], unread, [narrow2, narrow2], "into_cores"
        )
        return mine, swap(send, 1)

    outs = call(
        functools.partial(sent_states_body, heads, swaps),
        [in_hbm(keys), in_hbm(values), in_hbm(log_decay)] + [in_hbm(grad_out)] * swaps,
        [wide2, f32(EXTRA, rows), bf(rows, width), bf(rows, width)] + [bf(part, width)] * swaps,
        "sent_states",
        [
            pltpu.VMEM(log_decay.shape, F32),
            pltpu.SemaphoreType.DMA((2, TEAM)),
            pltpu.SemaphoreType.DMA((2,)),
        ],
        small // 2,
        [HBM] * (3 + swaps),
        [VMEM] * 4 + [HBM] * swaps,
    )
    give, row, keys, values = outs[:4]
    if swaps:
        arrived = lax.ppermute(outs[4], "tp", [(0, 1), (1, 0)])
        own = grad_out
    else:
        every = lax.all_to_all(grad_out, "tp", split_axis=1, concat_axis=0, tiled=True)
        own, arrived = every[:part], every[part:]
    (keep,) = call(
        functools.partial(kept_states_body, heads), [keys, values, row], [wide2], "kept_states", flops=small // 2
    )
    done = {}

    def probs_beside(after):
        if "decays" not in done:
            *done["decays"], done["queries"] = call(
                functools.partial(decays_body, heads),
                [row, in_hbm(queries), after],
                [table] * 2 + [bf(rows, width)],
                "decays",
                [pltpu.SemaphoreType.DMA(())],
                in_specs=[VMEM, HBM, ANY],
            )
        before = done.get("probs", [])
        done["probs"] = call(
            functools.partial(turned_probs_body, heads, TEAM // 2 if before else 0),
            [done["queries"], keys, row, done["decays"][0], after, *before],
            [f32(heads, HALF, BLOCK), f32(heads, HALF, HALF), bf(heads, HALF, BLOCK), bf(heads, HALF, HALF)],
            "turned_probs",
            flops=large // 2,
            in_specs=[VMEM] * 4 + [ANY] + [VMEM] * len(before),
            alias={5 + i: i for i in range(len(before))},
        )
        return done["probs"][3]

    def intra_beside(after):
        before = [done["intra"]] if "intra" in done else []
        first, last = (1, TEAM) if before else (0, 1)
        (done["intra"],) = call(
            functools.partial(intra_body, heads, first, last),
            [done["queries"], keys, values, row, done["decays"][0], after, *before],
            [f32(rows, width)],
            "intra",
            flops=2 * large * (last - first) // TEAM,
            in_specs=[VMEM] * 5 + [ANY] + [VMEM] * len(before),
            alias={6: 0} if before else None,
        )
        return done["intra"]

    def probs_and_intra(after):
        return intra_beside(probs_beside(after))

    def dscaled_beside(after):
        done["dscaled"] = call(
            functools.partial(own_dscaled_body, heads, swaps),
            [gate, in_hbm(own), gain_row, done["queries"], row, after],
            [f32(rows, width), bf(width, rows)],
            "own_dscaled",
            [pltpu.VMEM((part, width), BF16), pltpu.SemaphoreType.DMA(())],
            small,
            [VMEM, HBM, VMEM, VMEM, VMEM, ANY],
        )
        (dscaled,) = call(
            functools.partial(got_dscaled_body, heads, swaps),
            [gate, arrived, gain_row, done["dscaled"][0]],
            [f32(rows, width)],
            "got_dscaled",
            alias={3: 0},
        )
        done["dscaled"] = dscaled, done["dscaled"][1]
        return dscaled

    work = {"pair": probs_beside, "one": probs_and_intra, "last": intra_beside, "pair_back": dscaled_beside}
    mine, got = scan(False, keep, give, work)
    queries = done["queries"]
    (col, growth), intra, (dscaled, turned) = done["decays"], done["intra"], done["dscaled"]
    tall = f32(rows, HEAD)
    wide_scratch = pltpu.VMEM((rows, 2 * HEAD), F32)
    att, squares, inner = call(
        functools.partial(attention_body, heads, True),
        [queries, intra, dscaled, growth, mine],
        [f32(rows, width), tall, tall],
        "attention",
        [wide_scratch],
        small // 2,
    )
    att, sums = call(
        functools.partial(attention_body, heads, False),
        [queries, intra, dscaled, growth, got, att, squares, inner],
        [f32(rows, width), f32(8, rows)],
        "attention",
        [pltpu.VMEM((rows, HEAD), F32)] * 2 + [wide_scratch],
        small // 2,
        alias={5: 0},
    )
    (unscaled_gate,) = call(
        functools.partial(unscaled_gate_body, heads),
        [gate, att, dscaled, intra],
        [f32(rows, width)],
        "unscaled_gate",
        in_specs=[VMEM] * 3 + [ANY],
        alias={3: 0},
    )
    if swaps:
        others = lax.ppermute(sums, "tp", [(0, 1), (1, 0)])
    else:
        others = lax.psum(sums, "tp") - sums
    dattn, give, scale, coef = call(
        functools.partial(dattn_body, heads, channels, False),
        [att, dscaled, turned, gain_row, row, sums, others, unscaled_gate],
        [bf(rows, width), narrow2, tall, tall],
        "sent_dattn",
        flops=small // 2,
        in_specs=[VMEM] * 7 + [ANY],
    )
    dattn, keep = call(
        functools.partial(dattn_body, heads, channels, True),
        [att, dscaled, turned, gain_row, row, scale, coef, dattn],
        [bf(rows, width), wide2],
        "kept_dattn",
        flops=small // 2,
        alias={7: 0},
    )
    out_scratch = [pltpu.VMEM((TEAM, rows, hq * HEAD), BF16), pltpu.SemaphoreType.DMA((TEAM,))]

    def gate_beside(after):
        done["gate"], token = call(
            functools.partial(gate_body, heads),
            [unscaled_gate, scale, after],
            [bf(rows, width), f32(SIDE, HEAD)],
            "gate",
            out_scratch,
            small,
            [VMEM] * 2 + [ANY],
            [HBM, VMEM],
        )
        return token

    units = heads // min(hq, 2)
    cuts = [0, units // 4, 5 * units // 8, units]

    def key_value_beside(after, carried=()):
        before = done.get("key_value", [])
        piece = done.get("piece", 0)
        done["piece"] = piece + 1
        inputs = [queries, values, dattn, *done["probs"], after, *carried, *before]
        results = call(
            functools.partial(key_value_body, heads, cuts[piece], cuts[piece + 1], len(carried)),
            inputs,
            [f32(rows, width)] * 2 + [bf(rows, width)] * len(carried),
            "key_value",
            [pltpu.SemaphoreType.DMA((rows // HEAD,))] * len(carried),
            4 * large * (cuts[piece + 1] - cuts[piece]) // units,
            [VMEM] * 7 + [ANY] + [VMEM] * (len(carried) + len(before)),
            [VMEM] * 2 + [HBM] * len(carried),
            {8 + len(carried) + i: i for i in range(len(before))},
        )
        done["key_value"] = results[:2]
        return results[0], results[-1]

    def gate_and_key_value(after):
        return key_value_beside(gate_beside(after))[0]

    def query_beside(after):
        (done["query"],) = call(
            functools.partial(query_body, heads),
            [keys, values, dattn, row, col, growth, mine, got, after],
            [bf(rows, width)],
            "query",
            flops=2 * large + small,
            in_specs=[VMEM] * 8 + [ANY],
        )
        return done["query"]

    def key_value_last(after):
        dk, done["query"] = key_value_beside(after, [done["query"]])
        return dk

    work = {"pair": gate_and_key_value, "one": lambda after: key_value_beside(after)[0], "last": query_beside, "pair_back": key_value_last}
    back_mine, back_got = scan(True, keep, give, work)
    gate_grad, query_grad, (dk, dv) = done["gate"], done["query"], done["key_value"]
    both = bf(2, rows, hq * HEAD)
    own_key, own_value, own_gain = call(
        functools.partial(own_final_body, heads),
        [keys, values, dk, dv, col, back_mine],
        [both, both, f32(1, width)],
        "own_final",
        flops=small,
    )
    key_grad, value_grad, gain_grad = call(
        functools.partial(final_body, heads),
        [keys, values, dk, dv, col, back_got, own_key, own_value, own_gain],
        [bf(rows, width), bf(rows, width), f32(1, width)],
        "final",
        [pltpu.VMEM((1, width), F32)]
        + [pltpu.VMEM(both.shape, BF16)] * 2
        + [pltpu.SemaphoreType.DMA((8 * hq + 1,))],
        small,
        out_specs=[HBM, HBM, HBM],
    )
    return query_grad, key_grad, value_grad, gate_grad, gain_grad.reshape(width)


def solution(mesh):
    return jax.shard_map(
        local,
        mesh=mesh,
        in_specs=(
            P("ctx", "tp"),
            P("ctx", "tp"),
            P("ctx", "tp"),
            P("tp", "ctx"),
            P("ctx", "tp"),
            P("tp"),
            P(("ctx", "tp"), None),
        ),
        out_specs=(P("ctx", "tp"), P("ctx", "tp"), P("ctx", "tp"), P("ctx", "tp"), P("tp")),
        check_vma=False,
    )
```
